32 devices in a mesh: tok: 8 (over y, x, core), kv: 4 (over z).
Axes of the slice: x: 2, y: 2, z: 4, core: 2. Of those that a mesh axis runs over, the one named last changes fastest.
Arguments:
- hidden_in: bfloat16 [8192, 1024], P(('tok', 'kv')), may hold values from -12 to 12
- qkv_weight: bfloat16 [1024, 3, 1024], P(None, None, 'kv'), may hold values from -1 to 1
- stretch_len: int32 [48], replicated, may hold values from 1 to 1024, 8192 in all
- out_weight: bfloat16 [1024, 1024], P('kv'), may hold values from -0.1875 to 0.1875
- ln1_gain: float32 [1024], replicated, may hold values from 0.5 to 1.5
- ln1_bias: float32 [1024], replicated, may hold values from -3 to 3
- up_weight: bfloat16 [1024, 4096], P(None, 'kv'), may hold values from -0.1875 to 0.1875
- down_weight: bfloat16 [4096, 1024], P('kv'), may hold values from -0.09375 to 0.09375
- ln2_gain: float32 [1024], replicated, may hold values from 0.5 to 1.5
- ln2_bias: float32 [1024], replicated, may hold values from -3 to 3
- dec_query: bfloat16 [64, 1024], P(('tok', 'kv')), may hold values from -12 to 12
- kv_cache: bfloat16 [2, 8, 24, 128, 1024], P(None, 'tok', 'kv'), may hold values from -12 to 12
- piece_req: int32 [8, 24], P('tok', 'kv'), may hold values from 0 to 7, as said below
- piece_used: int32 [8, 24], P('tok', 'kv'), may hold values from 0 to 128, as said below
Outputs:
- prefill_out: bfloat16 [8192, 1024], P(('tok', 'kv'))
- dec_out: bfloat16 [64, 1024], P(('tok', 'kv'))
The draws below stay inside these ranges and needn't reach their ends.
Inputs may be any that keep to these rules, and one draw needn't show every extreme that they name: `piece_req`: every request of an index of tok owns at least one piece of that index with a nonzero count. `piece_used`: slots with a count of 0 hold no tokens.
All inputs are finite; a program needn't handle non-finite values.
Results may differ from the reference program's by a relative error of at most 0.017.
Values may be sent and summed in bfloat16 or wider, within the bound.
No kernel may reach another device: no remote copies, remote signals or barrier semaphores. Data moves between devices by JAX's collectives and lax.ppermute only.
A program may use at most 64 MiB of HBM per device.

```python
import math
import jax
import jax.numpy as jnp
import numpy as np
from jax import lax

D = 1024
H = 16
HD = 64
FF = 4096
REACH = 256
BLK = 1024
PTOK = 8192
CLEN = 1024
NSEG = 48
PLEN = 128
PIECES_DEV = 6
RQ_DEV = 2
RQ_TOK = 8
REQ = 64
SLOTS = 24
N_TOK = 8
N_KV = 4


def draw_hidden_in(key, part):
    normals = jax.random.normal(jax.random.fold_in(key, 11), (PTOK, D), jnp.float32)
    return jnp.clip(normals, -12.0, 12.0).astype(jnp.bfloat16)


def draw_qkv_weight(key, part):
    normals = jax.random.normal(jax.random.fold_in(key, 51), (D, 3, D), jnp.float32)
    scales = jnp.array([1.5, 1.0, 3.0], jnp.float32).reshape(1, 3, 1) / math.sqrt(D)
    return jnp.clip(normals * scales, -1.0, 1.0).astype(jnp.bfloat16)


def draw_dec_query(key, part):
    normals = 5.0 * jax.random.normal(jax.random.fold_in(key, 21), (REQ, D), jnp.float32)
    return jnp.clip(normals, -12.0, 12.0).astype(jnp.bfloat16)


def draw_kv_cache(key, part):
    normals = jax.random.normal(jax.random.fold_in(key, 31), (2, N_TOK, SLOTS, PLEN, D), jnp.float32)
    normals = normals * jnp.array([1.0, 3.0], jnp.float32).reshape(2, 1, 1, 1, 1)
    return jnp.clip(normals, -12.0, 12.0).astype(jnp.bfloat16)


def piece_table(key):
    table_key = jax.random.fold_in(key, 41)
    requests = RQ_DEV * N_KV
    slot_count = PIECES_DEV * N_KV
    slot_ids = jnp.arange(slot_count, dtype=jnp.int32)[None, :]
    candidates = jax.random.randint(jax.random.fold_in(table_key, 1), (N_TOK, slot_count, 3), 0, requests)
    skewed = jnp.min(candidates, axis=2)
    owners = jnp.where(slot_ids < requests, slot_ids, skewed)
    slot_kind = jax.random.randint(jax.random.fold_in(table_key, 2), (N_TOK, slot_count), 0, 3)
    partial_value = jax.random.randint(jax.random.fold_in(table_key, 3), (N_TOK, slot_count), 1, PLEN + 1)
    filled = jnp.where(slot_kind == 0, 0, jnp.where(slot_kind == 1, PLEN, partial_value))
    filled = jnp.where((slot_ids < requests) & (filled == 0), partial_value, filled)
    filled = jnp.where(slot_ids == 0, PLEN, filled)
    filled = jnp.where(slot_ids == slot_count - 1, 0, filled)
    ranks = jax.random.randint(jax.random.fold_in(table_key, 4), (N_TOK, slot_count), 0, 1 << 20) * slot_count + slot_ids
    shuffle = jnp.argsort(ranks, axis=1)
    owners = jnp.take_along_axis(owners, shuffle, axis=1)
    filled = jnp.take_along_axis(filled, shuffle, axis=1)
    return (owners.astype(jnp.int32), filled.astype(jnp.int32))


def draw_piece_req(key, part):
    return piece_table(key)[0]


def draw_piece_used(key, part):
    return piece_table(key)[1]


def block_levels(own_key, dims, shards, low, largest):
    def one(axis_at, shards_of):
        steps = jax.random.uniform(jax.random.fold_in(jax.random.fold_in(own_key, 6), axis_at), (shards_of,), jnp.float32, low / len(shards), largest / len(shards))
        return jnp.repeat(jnp.exp(steps), dims[axis_at] // shards_of).reshape((-1,) + (1,) * (len(dims) - axis_at - 1))

    loudness = one(*shards[0])
    for cut in shards[1:]:
        loudness = loudness * one(*cut)
    return loudness


def profile(number_of, total, most, slope):
    loads = [(1 << 20) // math.isqrt(rank ** slope) + 1 for rank in range(2, number_of + 1)]
    spare, holding = total - most - (number_of - 1), [1] * (number_of - 1)
    while spare > 0:
        movable = [i for i in range(number_of - 1) if holding[i] < most]
        mass, remaining = sum([loads[i] for i in movable]), spare
        for i in movable:
            extra = min(most - holding[i], max(1, remaining * loads[i] // mass), spare)
            holding[i] = holding[i] + extra
            spare = spare - extra
    return np.array([most] + holding)


def uneven(own_key, number_of, total, limit, lean):
    if number_of == 2:
        one = jax.random.randint(own_key, (), max(1, total - limit), min(limit, total - 1) + 1)
        return jnp.stack([one, total - one])
    tallies = jnp.asarray(profile(number_of, total, limit, lean), jnp.int32)
    couples = (number_of - 1) // 2
    donor, receiver = tallies[1:1 + 2 * couples:2], tallies[2:2 + 2 * couples:2]
    margin = jnp.minimum(donor - 1, limit - receiver)
    moved = jax.random.randint(jax.random.fold_in(own_key, 1), (couples,), 0, 1 << 20) % (margin + 1)
    tallies = tallies.at[1:1 + 2 * couples:2].set(donor - moved).at[2:2 + 2 * couples:2].set(receiver + moved)
    return tallies[jax.random.permutation(jax.random.fold_in(own_key, 2), number_of)]


def centred(key, extent, width, limit, shards=(), kind=jnp.bfloat16):
    values = width * jax.random.normal(key, extent, jnp.float32)
    if shards:
        values = values * block_levels(key, extent, shards, -0.22, 0.18)
    return jnp.clip(values, -limit, limit).astype(kind)


def setup_inputs(seed: int = 0) -> dict:
    seeds = jax.random.split(jax.random.key(seed), 15)
    hidden_in = draw_hidden_in(jax.random.fold_in(seeds[14], 71), 0)
    qkv_weight = draw_qkv_weight(jax.random.fold_in(seeds[14], 71), 0)
    stretch_len = uneven(seeds[2], NSEG, PTOK, CLEN, 2).astype(jnp.int32)
    out_weight = centred(seeds[3], (D, D), D ** -0.5, 0.1875, ((0, 4),))
    ln1_gain = jnp.clip(1.0 + 0.1 * jax.random.normal(seeds[4], (D,), jnp.float32), 0.5, 1.5)
    ln1_bias = centred(seeds[5], (D,), 0.5, 3.0, (), jnp.float32)
    up_weight = centred(seeds[6], (D, FF), D ** -0.5, 0.1875, ((1, 4),))
    down_weight = centred(seeds[7], (FF, D), FF ** -0.5, 0.09375, ((0, 4),))
    ln2_gain = jnp.clip(1.0 + 0.1 * jax.random.normal(seeds[8], (D,), jnp.float32), 0.5, 1.5)
    ln2_bias = centred(seeds[9], (D,), 0.5, 3.0, (), jnp.float32)
    dec_query = draw_dec_query(jax.random.fold_in(seeds[14], 71), 0)
    kv_cache = draw_kv_cache(jax.random.fold_in(seeds[14], 71), 0)
    piece_req = draw_piece_req(jax.random.fold_in(seeds[14], 71), 0)
    piece_used = draw_piece_used(jax.random.fold_in(seeds[14], 71), 0)
    return {"hidden_in": hidden_in, "qkv_weight": qkv_weight, "stretch_len": stretch_len, "out_weight": out_weight, "ln1_gain": ln1_gain, "ln1_bias": ln1_bias, "up_weight": up_weight, "down_weight": down_weight, "ln2_gain": ln2_gain, "ln2_bias": ln2_bias, "dec_query": dec_query, "kv_cache": kv_cache, "piece_req": piece_req, "piece_used": piece_used}


NEG_FILL = -1e+30
LN_EPS = 1e-05

def segment_ids(row_ids, stretch_len):
    stretch_ends = jnp.cumsum(stretch_len).astype(jnp.int32)
    return lax.optimization_barrier(jnp.sum((row_ids[:, None] >= stretch_ends[None, :]).astype(jnp.int32), axis=1))

def layer_norm(values, gain, bias):
    center = values - lax.optimization_barrier(jnp.mean(values, axis=1, keepdims=True))
    spread = lax.optimization_barrier(jnp.mean(center * center, axis=1, keepdims=True))
    return center * lax.rsqrt(spread + LN_EPS) * gain + bias

def reference(hidden_in, qkv_weight, stretch_len, out_weight, ln1_gain, ln1_bias, up_weight, down_weight, ln2_gain, ln2_bias, dec_query, kv_cache, piece_req, piece_used):
    inv_scale = 1.0 / math.sqrt(HD)
    qblock = min(512, BLK)
    span = qblock + 2 * REACH
    prefill_qkv = jnp.stack([jnp.dot(hidden_in, qkv_weight[:, part_index, :], preferred_element_type=jnp.float32).astype(jnp.bfloat16) for part_index in range(3)])
    all_rows = jnp.arange(PTOK, dtype=jnp.int32)
    segment = segment_ids(all_rows, stretch_len)
    padded = jnp.pad(prefill_qkv[1:], ((0, 0), (REACH, REACH), (0, 0)))
    padded_seg = jnp.pad(segment, (REACH, REACH), constant_values=-1)
    distance = jnp.arange(span, dtype=jnp.int32)[None, :] - REACH - jnp.arange(qblock, dtype=jnp.int32)[:, None]

    def prefill_block(block_index):
        first_row = (block_index * qblock).astype(jnp.int32)
        queries = lax.dynamic_slice_in_dim(prefill_qkv[0], first_row, qblock, 0).astype(jnp.float32).reshape(qblock, H, HD)
        both = lax.dynamic_slice_in_dim(padded, first_row, span, 1).astype(jnp.float32)
        key_rows = both[0].reshape(span, H, HD)
        value_rows = both[1].reshape(span, H, HD)
        key_seg = lax.dynamic_slice_in_dim(padded_seg, first_row, span, 0)
        query_seg = lax.dynamic_slice_in_dim(segment, first_row, qblock, 0)
        allowed = (key_seg[None, :] == query_seg[:, None]) & (jnp.abs(distance) <= REACH)
        scores = jnp.einsum('ihd,jhd->hij', queries, key_rows) * inv_scale
        scores = jnp.where(allowed[None], scores, NEG_FILL)
        row_max = lax.optimization_barrier(jnp.max(scores, axis=2, keepdims=True))
        weights = jnp.where(allowed[None], jnp.exp(scores - row_max), 0.0)
        totals = lax.optimization_barrier(jnp.sum(weights, axis=2))
        rounded = weights.astype(jnp.bfloat16).astype(jnp.float32)
        summed = jnp.einsum('hij,jhd->ihd', rounded, value_rows)
        return (summed / jnp.transpose(totals)[:, :, None]).astype(jnp.bfloat16).reshape(qblock, D)
    attention = lax.map(prefill_block, jnp.arange(PTOK // qblock, dtype=jnp.int32)).reshape(PTOK, D)
    projected = jnp.dot(attention, out_weight, preferred_element_type=jnp.float32)
    normed = layer_norm(hidden_in.astype(jnp.float32) + projected, ln1_gain, ln1_bias).astype(jnp.bfloat16)
    units = jax.nn.gelu(jnp.dot(normed, up_weight, preferred_element_type=jnp.float32), approximate=False).astype(jnp.bfloat16)
    ffn = jnp.dot(units, down_weight, preferred_element_type=jnp.float32)
    prefill_out = layer_norm(normed.astype(jnp.float32) + ffn, ln2_gain, ln2_bias).astype(jnp.bfloat16)

    def decode_group(group_index):
        first_req = (group_index * RQ_TOK).astype(jnp.int32)
        queries = lax.dynamic_slice_in_dim(dec_query, first_req, RQ_TOK, 0).astype(jnp.float32)
        owners = piece_req[group_index]
        filled = piece_used[group_index]
        key_rows = kv_cache[0, group_index].astype(jnp.float32).reshape(SLOTS, PLEN, H, HD)
        value_rows = kv_cache[1, group_index].astype(jnp.float32).reshape(SLOTS, PLEN, H, HD)
        chosen = queries[owners].reshape(SLOTS, H, HD)
        scores = jnp.einsum('phd,pthd->pht', chosen, key_rows) * inv_scale
        active = jnp.arange(PLEN, dtype=jnp.int32)[None, :] < filled[:, None]
        scores = jnp.where(active[:, None, :], scores, NEG_FILL)
        piece_max = lax.optimization_barrier(jnp.max(scores, axis=2))
        weights = jnp.where(active[:, None, :], jnp.exp(scores - piece_max[:, :, None]), 0.0)
        totals = lax.optimization_barrier(jnp.sum(weights, axis=2))
        partial_value = jnp.einsum('pht,pthd->phd', weights.astype(jnp.bfloat16).astype(jnp.float32), value_rows)
        member = (owners[None, :] == jnp.arange(RQ_TOK, dtype=jnp.int32)[:, None]) & (filled[None, :] > 0)
        highest = lax.optimization_barrier(jnp.max(jnp.where(member[:, :, None], piece_max[None], NEG_FILL), axis=1))
        factor = jnp.where(member[:, :, None], jnp.exp(piece_max[None] - highest[:, None, :]), 0.0)
        denom = lax.optimization_barrier(jnp.sum(factor * totals[None], axis=1))
        weighted = jnp.einsum('rph,phd->rhd', factor, partial_value)
        return (weighted / denom[:, :, None]).astype(jnp.bfloat16).reshape(RQ_TOK, D)
    dec_out = lax.map(decode_group, jnp.arange(N_TOK, dtype=jnp.int32)).reshape(REQ, D)
    return (prefill_out, dec_out)
```

```python
import functools
import math

import jax
import jax.numpy as jnp
from jax import lax
from jax.experimental import pallas as pl
from jax.experimental.pallas import tpu as pltpu
from jax.sharding import PartitionSpec as P

H = 16
HD = 64
WIN = 512
PLEN = 128


NEG_FILL = -1e30
LN_EPS = 1e-05
BF16 = jnp.bfloat16
F32 = jnp.float32
VMEM_LIMIT = 56 * 1024 * 1024
ANY = pl.BlockSpec(memory_space=pl.ANY)
VMEM = pl.BlockSpec(memory_space=pltpu.VMEM)
SMEM = pl.BlockSpec(memory_space=pltpu.SMEM)


def swapped(value, axis, flip):
    count = lax.axis_size(axis)
    return lax.ppermute(value, axis, [(i, i ^ flip) for i in range(count)])


def after(value, *earlier):
    return lax.optimization_barrier((value,) + earlier)[0]


def spread_in_plane(first):
    half = first.shape[-2] // 2
    low = lambda a: lax.slice_in_dim(a, 0, half, axis=a.ndim - 2)
    high = lambda a: lax.slice_in_dim(a, half, 2 * half, axis=a.ndim - 2)
    from_x = swapped(first, "tok", 2)
    from_y = swapped(first, "tok", 4)
    far_low = swapped(low(from_y), "tok", 2)
    far_high = swapped(high(from_x), "tok", 4)
    held = [(0, None, first), (2, None, from_x), (4, None, from_y), (6, 0, far_low), (6, 1, far_high)]
    other = [(flip ^ 1, part, swapped(value, "tok", 1)) for flip, part, value in held]
    return held + other


def normalized(values, gain, bias):
    center = values - jnp.mean(values, axis=1, keepdims=True)
    spread = jnp.mean(center * center, axis=1, keepdims=True)
    return center * lax.rsqrt(spread + LN_EPS) * gain + bias


def prepare(place_ref, starts_ref, ends_ref, before_ref, own_ref, behind_ref, rows_ref, bias_ref):
    count = own_ref.shape[0]
    reach = WIN // 2
    rows_ref[0:count] = before_ref[...]
    rows_ref[count : 2 * count] = own_ref[...]
    rows_ref[2 * count : 3 * count] = behind_ref[...]
    first = place_ref[0]
    query = first + lax.broadcasted_iota(jnp.int32, (count, 1), 0)
    starts = starts_ref[...]
    ends = ends_ref[...]
    low = jnp.max(jnp.where(starts <= query, starts, 0), axis=1, keepdims=True)
    high = jnp.min(jnp.where(ends > query, ends, 1 << 30), axis=1, keepdims=True)
    low = jnp.maximum(low, query - reach)
    high = jnp.minimum(high, query + reach + 1)
    key = first - count + lax.broadcasted_iota(jnp.int32, (count, 3 * count), 1)
    bias_ref[...] = jnp.where((key >= low) & (key < high), 0.0, NEG_FILL)


def attend(rows_ref, bias_ref, weight, out_weight):
    count = bias_ref.shape[0]
    width = weight.shape[1] // 3
    own = rows_ref[count : 2 * count]
    rows = rows_ref[...]
    scale = 1.0 / math.sqrt(HD)
    query = (jnp.dot(own, weight[:, :width], preferred_element_type=F32) * scale).astype(BF16)
    keys = jnp.dot(rows, weight[:, width : 2 * width], preferred_element_type=F32).astype(BF16)
    values = jnp.dot(rows, weight[:, 2 * width :], preferred_element_type=F32).astype(BF16)
    lane = lax.broadcasted_iota(jnp.int32, (count, 2 * HD), 1)
    bias = bias_ref[...]
    pairs = []
    for start in range(0, width, 2 * HD):
        pair = slice(start, start + 2 * HD)
        halves = []
        for side in range(2):
            inside = (lane < HD) if side == 0 else (lane >= HD)
            only = jnp.where(inside, query[:, pair], jnp.zeros((), BF16))
            scores = lax.dot_general(only, keys[:, pair], (((1,), (1,)), ((), ())), preferred_element_type=F32)
            scores = scores + bias
            highest = jnp.max(scores, axis=1, keepdims=True)
            weights = jnp.exp(scores - highest)
            total = jnp.sum(weights, axis=1, keepdims=True)
            summed = jnp.dot(weights.astype(BF16), values[:, pair], preferred_element_type=F32)
            halves.append(summed / total)
        pairs.append(jnp.where(lane < HD, halves[0], halves[1]).astype(BF16))
    attention = jnp.concatenate(pairs, axis=1)
    return jnp.dot(attention, out_weight, preferred_element_type=F32)


def attend_own_kernel(
    place_ref, starts_ref, ends_ref, before_ref, own_ref, behind_ref, weight_ref, out_ref, sum_ref, rows_ref, bias_ref
):
    prepare(place_ref, starts_ref, ends_ref, before_ref, own_ref, behind_ref, rows_ref, bias_ref)
    sum_ref[...] = attend(rows_ref, bias_ref, weight_ref[...], out_ref[...])


def attend_rest_kernel(layout, quarters, *refs):
    count = len(layout)
    place_ref, starts_ref, ends_ref, before_ref, own_ref, behind_ref, sum_ref, gain_ref, bias1_ref = refs[:9]
    pieces = refs[9 : 9 + count]
    normed_ref, rows_ref, bias_ref, weight_ref, out_ref, total_ref, sems = refs[9 + count :]
    tok = place_ref[1]
    wide = weight_ref.shape[2]
    block = 128
    copies = []
    for (flip, part), piece in zip(layout, pieces):
        eighth = tok ^ flip
        size = piece.shape[1]
        shift = 0 if part is None else part * size
        at = pl.multiple_of(eighth * block, block)
        moves = [(piece.at[:, :, 0:wide], weight_ref.at[:, pl.ds(at + shift, size), :])]
        for side in range(2):
            columns = pl.ds(wide + side * block, block)
            moves.append((piece.at[:, :, columns], out_ref.at[:, pl.ds(side * block + shift, size), pl.ds(at, block)]))
        for source, target in moves:
            copies.append(pltpu.make_async_copy(source, target, sems.at[len(copies)]))
    for copy in copies:
        copy.start()
    prepare(place_ref, starts_ref, ends_ref, before_ref, own_ref, behind_ref, rows_ref, bias_ref)
    total_ref[...] = sum_ref[...]
    for copy in copies:
        copy.wait()

    def step(index, carry):
        total_ref[...] += attend(rows_ref, bias_ref, weight_ref[index], out_ref[index])
        return carry

    lax.fori_loop(0, quarters, step, 0)
    mixed = own_ref[...].astype(F32) + total_ref[...]
    normed_ref[...] = normalized(mixed, gain_ref[...], bias1_ref[...]).astype(BF16)


def attend_cost(rows, width, heads_width):
    flops = 2 * rows * width * heads_width * 8 + 4 * rows * 3 * rows * heads_width * 4
    return pl.CostEstimate(flops=flops, bytes_accessed=4 * width * heads_width * 2, transcendentals=0)


def attend_own(place, starts, ends, before, own, behind, weight, out_weight):
    rows, width = own.shape
    return pl.pallas_call(
        attend_own_kernel,
        out_shape=jax.ShapeDtypeStruct((rows, width), F32),
        in_specs=[SMEM] + [VMEM] * 7,
        out_specs=VMEM,
        scratch_shapes=[pltpu.VMEM((3 * rows, width), BF16), pltpu.VMEM((rows, 3 * rows), F32)],
        compiler_params=pltpu.CompilerParams(vmem_limit_bytes=VMEM_LIMIT),
        cost_estimate=attend_cost(rows, width, out_weight.shape[0]),
        name="attend_own",
    )(place, starts, ends, before, own, behind, weight, out_weight)


def attend_rest(place, starts, ends, before, own, behind, summed, gain, bias, pieces, heads_width):
    rows, width = own.shape
    layout = tuple((flip, part) for flip, part, _ in pieces)
    quarters = pieces[0][2].shape[0]
    return pl.pallas_call(
        functools.partial(attend_rest_kernel, layout, quarters),
        out_shape=jax.ShapeDtypeStruct((rows, width), BF16),
        in_specs=[SMEM] + [VMEM] * 8 + [ANY] * len(pieces),
        out_specs=VMEM,
        scratch_shapes=[
            pltpu.VMEM((3 * rows, width), BF16),
            pltpu.VMEM((rows, 3 * rows), F32),
            pltpu.VMEM((quarters, width, 3 * heads_width), BF16),
            pltpu.VMEM((quarters, heads_width, width), BF16),
            pltpu.VMEM((rows, width), F32),
            pltpu.SemaphoreType.DMA((3 * len(pieces),)),
        ],
        compiler_params=pltpu.CompilerParams(vmem_limit_bytes=VMEM_LIMIT),
        cost_estimate=attend_cost(rows, width, quarters * heads_width),
        name="attend_rest",
    )(place, starts, ends, before, own, behind, summed, gain, bias, *[value for _, _, value in pieces])


def gelu(values):
    return 0.5 * values * (1.0 + lax.erf(values * math.sqrt(0.5)))


def feed_kernel(layout, *refs):
    count = len(layout)
    place_ref, rows_ref, up_ref, down_ref = refs[:4]
    pieces = refs[4 : 4 + count]
    sum_ref, far_up_ref, far_down_ref, total_ref, sems = refs[4 + count :]
    tok = place_ref[1]
    block = 128
    copies = []
    for (flip, part), piece in zip(layout, pieces):
        at = pl.multiple_of((tok ^ flip) * block, block)
        if part in (None, 0):
            copies.append(
                pltpu.make_async_copy(piece.at[0:block], far_up_ref.at[pl.ds(at, block)], sems.at[len(copies)])
            )
        if part in (None, 1):
            shift = block if part is None else 0
            copies.append(
                pltpu.make_async_copy(
                    piece.at[shift : shift + block], far_down_ref.at[pl.ds(at, block)], sems.at[len(copies)]
                )
            )
    for copy in copies:
        copy.start()
    rows = rows_ref[...]
    chunk = 512
    total_ref[...] = jnp.zeros_like(total_ref)

    def through(up, down):
        for at in range(0, up.shape[1], chunk):
            units = gelu(jnp.dot(rows, up[:, at : at + chunk], preferred_element_type=F32)).astype(BF16)
            total_ref[...] += jnp.dot(units, down[at : at + chunk, :], preferred_element_type=F32)

    through(up_ref, down_ref)
    for copy in copies:
        copy.wait()
    through(far_up_ref, far_down_ref)
    sum_ref[...] = total_ref[...].astype(sum_ref.dtype)


def feed(place, rows, up_weight, down_weight, pieces, dtype, name):
    count, width = rows.shape
    units = up_weight.shape[1]
    layout = tuple((flip, part) for flip, part, _ in pieces)
    copies = sum(2 if part is None else 1 for _, part in layout)
    return pl.pallas_call(
        functools.partial(feed_kernel, layout),
        out_shape=jax.ShapeDtypeStruct((count, width), dtype),
        in_specs=[SMEM] + [VMEM] * 3 + [ANY] * len(pieces),
        out_specs=VMEM,
        scratch_shapes=[
            pltpu.VMEM((width, units), BF16),
            pltpu.VMEM((units, width), BF16),
            pltpu.VMEM((count, width), F32),
            pltpu.SemaphoreType.DMA((copies,)),
        ],
        compiler_params=pltpu.CompilerParams(vmem_limit_bytes=VMEM_LIMIT),
        cost_estimate=pl.CostEstimate(
            flops=8 * count * width * units, bytes_accessed=8 * width * units, transcendentals=2 * count * units
        ),
        name=name,
    )(place, rows, up_weight, down_weight, *[value for _, _, value in pieces])


def finish_kernel(normed_ref, near_ref, far_ref, gain_ref, bias_ref, out_ref):
    mixed = normed_ref[...].astype(F32) + near_ref[...] + far_ref[...].astype(F32)
    out_ref[...] = normalized(mixed, gain_ref[...], bias_ref[...]).astype(out_ref.dtype)


def finish(normed, near, far, gain, bias):
    return pl.pallas_call(
        finish_kernel,
        out_shape=jax.ShapeDtypeStruct(normed.shape, BF16),
        in_specs=[VMEM] * 5,
        out_specs=VMEM,
        compiler_params=pltpu.CompilerParams(vmem_limit_bytes=VMEM_LIMIT),
        name="finish",
    )(normed, near, far, gain, bias)


def decode_kernel(slot_ref, filled_ref, query_ref, cache_ref, out_ref, high_ref, total_ref, sum_ref):
    step = pl.program_id(0)

    @pl.when(step == 0)
    def _():
        high_ref[...] = jnp.full(high_ref.shape, NEG_FILL, F32)
        total_ref[...] = jnp.zeros_like(total_ref)
        sum_ref[...] = jnp.zeros_like(sum_ref)

    row = slot_ref[step]
    filled = filled_ref[step]
    width = query_ref.shape[1]
    head = lax.broadcasted_iota(jnp.int32, (H, width), 0)
    inside = head == lax.broadcasted_iota(jnp.int32, (H, width), 1) // HD
    query = jnp.where(inside, query_ref[pl.ds(row, 1), :], 0.0).astype(BF16)
    scores = lax.dot_general(query, cache_ref[0, 0, 0], (((1,), (1,)), ((), ())), preferred_element_type=F32)
    live = lax.broadcasted_iota(jnp.int32, scores.shape, 1) < filled
    scores = jnp.where(live, scores * (1.0 / math.sqrt(HD)), NEG_FILL)
    high = jnp.max(scores, axis=1, keepdims=True)
    weights = jnp.where(live, jnp.exp(scores - high), 0.0)
    total = jnp.sum(weights, axis=1, keepdims=True)
    summed = jnp.dot(weights.astype(BF16), cache_ref[1, 0, 0], preferred_element_type=F32)
    along = lambda column: jnp.sum(jnp.where(inside, column, 0.0), axis=0, keepdims=True)
    high, total, summed = along(high), along(total), along(summed)
    used = filled > 0
    at = pl.ds(row, 1)
    old = high_ref[at, :]
    new = jnp.where(used, jnp.maximum(old, high), old)
    left = jnp.exp(old - new)
    right = jnp.where(used, jnp.exp(high - new), 0.0)
    high_ref[at, :] = new
    total_ref[at, :] = total_ref[at, :] * left + total * right
    sum_ref[at, :] = sum_ref[at, :] * left + summed * right

    @pl.when(step == pl.num_programs(0) - 1)
    def _():
        out_ref[0] = high_ref[...]
        out_ref[1] = total_ref[...]
        out_ref[2] = sum_ref[...]


def decode(slots, filled, queries, kv_cache):
    requests, width = queries.shape
    pieces = kv_cache.shape[2]
    state = pltpu.VMEM((requests, width), F32)
    return pl.pallas_call(
        decode_kernel,
        grid=(pieces,),
        out_shape=jax.ShapeDtypeStruct((3, requests, width), F32),
        in_specs=[
            SMEM,
            SMEM,
            pl.BlockSpec((requests, width), lambda i: (0, 0)),
            pl.BlockSpec((2, 1, 1, PLEN, width), lambda i: (0, 0, i, 0, 0)),
        ],
        out_specs=pl.BlockSpec((3, requests, width), lambda i: (0, 0, 0)),
        scratch_shapes=[state, state, state],
        compiler_params=pltpu.CompilerParams(vmem_limit_bytes=VMEM_LIMIT),
        cost_estimate=pl.CostEstimate(flops=0, bytes_accessed=kv_cache.size * 2, transcendentals=0),
        name="decode",
    )(slots, filled, queries, kv_cache)


def decode_rows(dec_query, kv_cache, piece_req, piece_used):
    own = dec_query.shape[0]
    kv = lax.axis_index("kv")
    count = lax.axis_size("kv")
    queries = jnp.concatenate([dec_query] + [swapped(dec_query, "kv", flip) for flip in range(1, count)])
    owners = piece_req[0]
    slots = ((owners // own) ^ kv) * own + owners % own
    partial = decode(slots, piece_used[0], queries.astype(F32), kv_cache)
    parts = [partial[:, :own]]
    for flip in range(1, count):
        parts.append(swapped(partial[:, flip * own : (flip + 1) * own], "kv", flip))
    high = functools.reduce(jnp.maximum, [part[0] for part in parts])
    factors = [jnp.exp(part[0] - high) for part in parts]
    total = sum(part[1] * factor for part, factor in zip(parts, factors))
    summed = sum(part[2] * factor for part, factor in zip(parts, factors))
    return (summed / total).astype(BF16)


def routed_body(
    hidden_in,
    qkv_weight,
    stretch_len,
    out_weight,
    ln1_gain,
    ln1_bias,
    up_weight,
    down_weight,
    ln2_gain,
    ln2_bias,
    dec_query,
    kv_cache,
    piece_req,
    piece_used,
):
    tok = lax.axis_index("tok")
    kv = lax.axis_index("kv")
    toks, kvs = lax.axis_size("tok"), lax.axis_size("kv")
    rows, width = hidden_in.shape
    heads_width = out_weight.shape[0]
    block = width // toks

    eighth = lambda value, axis: lax.dynamic_slice_in_dim(value, tok * block, block, axis)
    out_part = eighth(out_weight, 1)
    bundle = jnp.concatenate(
        [eighth(qkv_weight, 0).reshape(block, 3 * heads_width), out_part[:block], out_part[block:]], axis=1
    )
    foreign = [swapped(bundle, "kv", flip) for flip in range(1, kvs)]

    hidden_late = after(hidden_in, *foreign)
    flat = toks * kvs
    before = lax.ppermute(hidden_late, ("tok", "kv"), [(i, i + 1) for i in range(flat - 1)])
    behind = lax.ppermute(hidden_late, ("tok", "kv"), [(i + 1, i) for i in range(flat - 1)])

    pieces = spread_in_plane(jnp.stack(foreign))

    feed_part = jnp.concatenate([eighth(up_weight, 0), eighth(down_weight, 0)], axis=0)
    feed_part = after(feed_part, before, behind)
    feed_pieces = spread_in_plane(swapped(feed_part, "kv", 2))

    place = jnp.stack([(tok * kvs + kv) * rows, tok]).astype(jnp.int32)
    order = jnp.arange(stretch_len.shape[0])
    ends = jnp.sum(jnp.where(order[:, None] <= order[None, :], stretch_len[:, None], 0), axis=0, dtype=jnp.int32)
    starts = (ends - stretch_len)[None, :]
    ends = ends[None, :]

    own_weight = qkv_weight.reshape(width, 3 * heads_width)
    summed = attend_own(place, starts, ends, before, hidden_in, behind, own_weight, out_weight)
    normed = attend_rest(
        place,
        starts,
        ends,
        before,
        hidden_in,
        behind,
        summed,
        ln1_gain[None, :],
        ln1_bias[None, :],
        pieces,
        heads_width,
    )

    partner = swapped(normed, "kv", 1)
    near = feed(place, normed, up_weight, down_weight, feed_pieces, F32, "feed_own")
    away = feed(place, partner, up_weight, down_weight, feed_pieces, BF16, "feed_partner")
    far = swapped(away, "kv", 1)
    prefill_out = finish(normed, near, far, ln2_gain[None, :], ln2_bias[None, :])

    return prefill_out, decode_rows(dec_query, kv_cache, piece_req, piece_used)


def extended(value, sides, width):
    for axis, dim in sides:
        count, length = (lax.axis_size(axis), value.shape[dim])
        up = [(i, (i + 1) % count) for i in range(count - 1)]
        down = [(j, i) for i, j in up]
        last = lax.slice_in_dim(value, length - width, length, axis=dim)
        leading = lax.slice_in_dim(value, 0, width, axis=dim)
        before = lax.ppermute(last, axis, up)
        after = lax.ppermute(leading, axis, down)
        value = jnp.concatenate([before, value, after], axis=dim)
    return value


def merged(value, axis, join):
    pieces = jax.tree.map(lambda part: lax.all_gather(part, axis), value)
    head = jax.tree.map(lambda part: part[0], pieces)
    tail = jax.tree.map(lambda part: part[1:], pieces)
    subtotal, _ = lax.scan(lambda subtotal, section: (join(subtotal, section), None), head, tail)
    return subtotal


def segment_ids(row_ids, stretch_len):
    stretch_ends = jnp.cumsum(stretch_len)
    return jnp.sum((row_ids[:, None] >= stretch_ends[None, :]).astype(jnp.int32), axis=1)


def layer_norm(values, gain, bias):
    center = values - jnp.mean(values, axis=1, keepdims=True)
    spread = jnp.mean(center * center, axis=1, keepdims=True)
    return center * lax.rsqrt(spread + LN_EPS) * gain + bias


def merge_partials(earlier, later):
    highest = jnp.maximum(earlier[0], later[0])
    left_factor = jnp.exp(earlier[0] - highest)
    right_factor = jnp.exp(later[0] - highest)
    totals = earlier[1] * left_factor + later[1] * right_factor
    weighted = earlier[2] * left_factor[..., None] + later[2] * right_factor[..., None]
    return (highest, totals, weighted)


def row_folder(source, shard_rows):
    return jnp.dot(source, shard_rows, preferred_element_type=jnp.float32)


def general_body(
    hidden_in,
    qkv_weight,
    stretch_len,
    out_weight,
    ln1_gain,
    ln1_bias,
    up_weight,
    down_weight,
    ln2_gain,
    ln2_bias,
    dec_query,
    kv_cache,
    piece_req,
    piece_used,
):
    inv_scale = 1.0 / math.sqrt(HD)
    reach = WIN // 2
    local_width = qkv_weight.shape[2]
    head_count = local_width // HD
    flat_weight = qkv_weight.reshape(qkv_weight.shape[0], 3 * local_width)
    qkv_rows = jnp.dot(
        lax.all_gather(hidden_in, "kv", axis=0, tiled=True),
        flat_weight,
        preferred_element_type=jnp.float32,
    ).astype(jnp.bfloat16)
    row_count = qkv_rows.shape[0]
    query_rows = qkv_rows[:, :local_width]
    keyval_rows = qkv_rows[:, local_width:]
    padded = extended(keyval_rows, (("tok", 0),), reach)
    first_row = lax.axis_index("tok") * row_count
    total_rows = row_count * lax.axis_size("tok")
    qblock = min(512, row_count)
    span = qblock + 2 * reach
    block_count = row_count // qblock

    def attend(block_index):
        start = block_index * qblock
        query_ids = first_row + start + jnp.arange(qblock, dtype=jnp.int32)
        key_ids = first_row + start - reach + jnp.arange(span, dtype=jnp.int32)
        query_seg = segment_ids(query_ids, stretch_len)
        inside = (key_ids >= 0) & (key_ids < total_rows)
        key_seg = jnp.where(inside, segment_ids(key_ids, stretch_len), -1)
        allowed = (key_seg[None, :] == query_seg[:, None]) & (
            jnp.abs(key_ids[None, :] - query_ids[:, None]) <= reach
        )
        queries = lax.dynamic_slice_in_dim(query_rows, start, qblock, 0).reshape(
            qblock, head_count, HD
        )
        both = lax.dynamic_slice_in_dim(padded, start, span, 0)
        key_rows = both[:, :local_width].reshape(span, head_count, HD)
        value_rows = both[:, local_width:].reshape(span, head_count, HD)
        scores = (
            jnp.einsum("ihd,jhd->hij", queries, key_rows, preferred_element_type=jnp.float32)
            * inv_scale
        )
        scores = jnp.where(allowed[None], scores, NEG_FILL)
        row_max = jnp.max(scores, axis=2, keepdims=True)
        weights = jnp.where(allowed[None], jnp.exp(scores - row_max), 0.0)
        totals = jnp.sum(weights, axis=2)
        summed = jnp.einsum(
            "hij,jhd->ihd",
            weights.astype(jnp.bfloat16),
            value_rows,
            preferred_element_type=jnp.float32,
        )
        return (
            (summed / jnp.transpose(totals)[:, :, None])
            .astype(jnp.bfloat16)
            .reshape(qblock, local_width)
        )

    attention = lax.map(attend, jnp.arange(block_count, dtype=jnp.int32)).reshape(
        row_count, local_width
    )
    token_major = lax.all_to_all(attention, "kv", split_axis=0, concat_axis=1, tiled=True)
    projected = row_folder(token_major, lax.all_gather(out_weight, "kv", axis=0, tiled=True))
    normed = layer_norm(hidden_in.astype(jnp.float32) + projected, ln1_gain, ln1_bias).astype(
        jnp.bfloat16
    )
    units = jax.nn.gelu(
        jnp.dot(
            lax.all_gather(normed, "kv", axis=0, tiled=True),
            up_weight,
            preferred_element_type=jnp.float32,
        ),
        approximate=False,
    ).astype(jnp.bfloat16)
    ffn = lax.psum_scatter(
        jnp.dot(units, down_weight, preferred_element_type=jnp.float32).astype(jnp.bfloat16),
        "kv",
        scatter_dimension=0,
        tiled=True,
    ).astype(jnp.float32)
    prefill_out = layer_norm(normed.astype(jnp.float32) + ffn, ln2_gain, ln2_bias).astype(
        jnp.bfloat16
    )
    group_queries = lax.all_gather(dec_query, "kv", axis=0, tiled=True)
    request_count = group_queries.shape[0]
    owners = piece_req[0]
    filled = piece_used[0]
    slot_count = owners.shape[0]
    request_ids = jnp.arange(request_count, dtype=jnp.int32)
    selector = (owners[:, None] == request_ids[None, :]).astype(jnp.bfloat16)
    chosen = jnp.dot(selector, group_queries, preferred_element_type=jnp.float32).astype(
        jnp.bfloat16
    )
    chosen = chosen.reshape(slot_count, H, HD)
    cache_keys = kv_cache[0, 0].reshape(slot_count, PLEN, H, HD)
    cache_values = kv_cache[1, 0].reshape(slot_count, PLEN, H, HD)
    piece_scores = (
        jnp.einsum("phd,pthd->pht", chosen, cache_keys, preferred_element_type=jnp.float32)
        * inv_scale
    )
    active = jnp.arange(PLEN, dtype=jnp.int32)[None, :] < filled[:, None]
    piece_scores = jnp.where(active[:, None, :], piece_scores, NEG_FILL)
    piece_max = jnp.max(piece_scores, axis=2)
    piece_weights = jnp.where(
        active[:, None, :], jnp.exp(piece_scores - piece_max[:, :, None]), 0.0
    )
    piece_totals = jnp.sum(piece_weights, axis=2)
    partial_value = jnp.einsum(
        "pht,pthd->phd",
        piece_weights.astype(jnp.bfloat16),
        cache_values,
        preferred_element_type=jnp.float32,
    )
    member = (owners[None, :] == request_ids[:, None]) & (filled[None, :] > 0)
    highest = jnp.max(jnp.where(member[:, :, None], piece_max[None], NEG_FILL), axis=1)
    factor = jnp.where(member[:, :, None], jnp.exp(piece_max[None] - highest[:, None, :]), 0.0)
    denom = jnp.sum(factor * piece_totals[None], axis=1)
    weighted = jnp.einsum("rph,phd->rhd", factor, partial_value)
    own_requests = dec_query.shape[0]
    joined = merged((highest, denom, weighted), "kv", merge_partials)
    begin = lax.axis_index("kv") * own_requests
    final_denom = lax.dynamic_slice_in_dim(joined[1], begin, own_requests, 0)
    final_weighted = lax.dynamic_slice_in_dim(joined[2], begin, own_requests, 0)
    dec_out = (
        (final_weighted / final_denom[:, :, None])
        .astype(jnp.bfloat16)
        .reshape(own_requests, H * HD)
    )
    return (prefill_out, dec_out)


def solution(mesh):
    placed = (
        P(("tok", "kv"), None),
        P(None, None, "kv"),
        P(),
        P("kv", None),
        P(),
        P(),
        P(None, "kv"),
        P("kv", None),
        P(),
        P(),
        P(("tok", "kv"), None),
        P(None, "tok", "kv", None, None),
        P("tok", "kv"),
        P("tok", "kv"),
    )
    routed = mesh.shape["tok"] == 8 and mesh.shape["kv"] == 4
    return jax.shard_map(
        routed_body if routed else general_body,
        mesh=mesh,
        in_specs=placed,
        out_specs=(P(("tok", "kv"), None), P(("tok", "kv"), None)),
        check_vma=False,
    )
```

```python
import functools
import math

import jax
import jax.numpy as jnp
from jax import lax
from jax.experimental import pallas as pl
from jax.experimental.pallas import tpu as pltpu
from jax.sharding import PartitionSpec as P

H = 16
HD = 64
WIN = 512
PLEN = 128


NEG_FILL = -1e30
LN_EPS = 1e-05
BF16 = jnp.bfloat16
F32 = jnp.float32
VMEM_LIMIT = 56 * 1024 * 1024
ANY = pl.BlockSpec(memory_space=pl.ANY)
VMEM = pl.BlockSpec(memory_space=pltpu.VMEM)
SMEM = pl.BlockSpec(memory_space=pltpu.SMEM)


def swapped(value, axis, flip):
    count = lax.axis_size(axis)
    return lax.ppermute(value, axis, [(i, i ^ flip) for i in range(count)])


def after(value, *earlier):
    return lax.optimization_barrier((value,) + earlier)[0]


def spread_in_plane(first):
    half = first.shape[-2] // 2
    low = lambda a: lax.slice_in_dim(a, 0, half, axis=a.ndim - 2)
    high = lambda a: lax.slice_in_dim(a, half, 2 * half, axis=a.ndim - 2)
    from_x = swapped(first, "tok", 2)
    from_y = swapped(first, "tok", 4)
    far_low = swapped(low(from_y), "tok", 2)
    far_high = swapped(high(from_x), "tok", 4)
    held = [(0, None, first), (2, None, from_x), (4, None, from_y), (6, 0, far_low), (6, 1, far_high)]
    other = [(flip ^ 1, part, swapped(value, "tok", 1)) for flip, part, value in held]
    return held + other


def normalized(values, gain, bias):
    center = values - jnp.mean(values, axis=1, keepdims=True)
    spread = jnp.mean(center * center, axis=1, keepdims=True)
    return center * lax.rsqrt(spread + LN_EPS) * gain + bias


def prepare(place_ref, starts_ref, ends_ref, before_ref, own_ref, behind_ref, rows_ref, bias_ref):
    count = own_ref.shape[0]
    reach = WIN // 2
    rows_ref[0:count] = before_ref[...]
    rows_ref[count : 2 * count] = own_ref[...]
    rows_ref[2 * count : 3 * count] = behind_ref[...]
    first = place_ref[0]
    query = first + lax.broadcasted_iota(jnp.int32, (count, 1), 0)
    starts = starts_ref[...]
    ends = ends_ref[...]
    low = jnp.max(jnp.where(starts <= query, starts, 0), axis=1, keepdims=True)
    high = jnp.min(jnp.where(ends > query, ends, 1 << 30), axis=1, keepdims=True)
    low = jnp.maximum(low, query - reach)
    high = jnp.minimum(high, query + reach + 1)
    key = first - count + lax.broadcasted_iota(jnp.int32, (count, 3 * count), 1)
    bias_ref[...] = jnp.where((key >= low) & (key < high), 0.0, NEG_FILL)


def attend(rows_ref, bias_ref, weight_ref, out_weight):
    count = bias_ref.shape[0]
    width = weight_ref.shape[2]
    own = rows_ref[count : 2 * count]
    rows = rows_ref[...]
    scale = 1.0 / math.sqrt(HD)
    query = (jnp.dot(own, weight_ref[0], preferred_element_type=F32) * scale).astype(BF16)
    keys = jnp.dot(rows, weight_ref[1], preferred_element_type=F32).astype(BF16)
    values = jnp.dot(rows, weight_ref[2], preferred_element_type=F32).astype(BF16)
    lane = lax.broadcasted_iota(jnp.int32, (count, 2 * HD), 1)
    bias = bias_ref[...]
    pairs = []
    for start in range(0, width, 2 * HD):
        pair = slice(start, start + 2 * HD)
        halves = []
        for side in range(2):
            inside = (lane < HD) if side == 0 else (lane >= HD)
            only = jnp.where(inside, query[:, pair], jnp.zeros((), BF16))
            scores = lax.dot_general(only, keys[:, pair], (((1,), (1,)), ((), ())), preferred_element_type=F32)
            scores = scores + bias
            highest = jnp.max(scores, axis=1, keepdims=True)
            weights = jnp.exp(scores - highest)
            total = jnp.sum(weights, axis=1, keepdims=True)
            summed = jnp.dot(weights.astype(BF16), values[:, pair], preferred_element_type=F32)
            halves.append(summed / total)
        pairs.append(jnp.where(lane < HD, halves[0], halves[1]).astype(BF16))
    attention = jnp.concatenate(pairs, axis=1)
    return jnp.dot(attention, out_weight, preferred_element_type=F32)


def attend_own_kernel(
    place_ref, starts_ref, ends_ref, before_ref, own_ref, behind_ref, weight_ref, out_ref, sum_ref, rows_ref, bias_ref
):
    prepare(place_ref, starts_ref, ends_ref, before_ref, own_ref, behind_ref, rows_ref, bias_ref)
    sum_ref[...] = attend(rows_ref, bias_ref, weight_ref, out_ref[...])


def attend_next_kernel(layout, last, *refs):
    count = len(layout)
    place_ref, starts_ref, ends_ref, before_ref, own_ref, behind_ref, sum_ref, gain_ref, shift_ref = refs[:9]
    pieces = refs[9 : 9 + count]
    result_ref, rows_ref, bias_ref, weight_ref, out_ref, sems = refs[9 + count :]
    tok = place_ref[1]
    block = 128
    copies = []
    for (flip, part), piece in zip(layout, pieces):
        size = piece.shape[1]
        shift = 0 if part is None else part * size
        at = pl.multiple_of((tok ^ flip) * block, block)
        moves = [(piece.at[0:3], weight_ref.at[:, pl.ds(at + shift, size), :])]
        for side in range(2):
            columns = slice(side * block, (side + 1) * block)
            moves.append((piece.at[3, :, columns], out_ref.at[pl.ds(side * block + shift, size), pl.ds(at, block)]))
        for source, target in moves:
            copies.append(pltpu.make_async_copy(source, target, sems.at[len(copies)]))
    for copy in copies:
        copy.start()
    prepare(place_ref, starts_ref, ends_ref, before_ref, own_ref, behind_ref, rows_ref, bias_ref)
    for copy in copies:
        copy.wait()
    total = sum_ref[...] + attend(rows_ref, bias_ref, weight_ref, out_ref[...])
    if last:
        mixed = own_ref[...].astype(F32) + total
        result_ref[...] = normalized(mixed, gain_ref[...], shift_ref[...]).astype(BF16)
    else:
        result_ref[...] = total


def attend_cost(rows, width, heads_width):
    flops = 2 * rows * width * heads_width * 8 + 4 * rows * 3 * rows * heads_width * 4
    return pl.CostEstimate(flops=flops, bytes_accessed=4 * width * heads_width * 2, transcendentals=0)


def attend_own(shards, weight, out_weight):
    rows, width = shards[4].shape
    return pl.pallas_call(
        attend_own_kernel,
        out_shape=jax.ShapeDtypeStruct((rows, width), F32),
        in_specs=[SMEM] + [VMEM] * 7,
        out_specs=VMEM,
        scratch_shapes=[pltpu.VMEM((3 * rows, width), BF16), pltpu.VMEM((rows, 3 * rows), F32)],
        compiler_params=pltpu.CompilerParams(vmem_limit_bytes=VMEM_LIMIT),
        cost_estimate=attend_cost(rows, width, out_weight.shape[0]),
        name="attend_own",
    )(*shards, weight, out_weight)


def attend_next(shards, summed, gain, bias, pieces, heads_width, last, name):
    rows, width = shards[4].shape
    layout = tuple((flip, part) for flip, part, _ in pieces)
    return pl.pallas_call(
        functools.partial(attend_next_kernel, layout, last),
        out_shape=jax.ShapeDtypeStruct((rows, width), BF16 if last else F32),
        in_specs=[SMEM] + [VMEM] * 8 + [ANY] * len(pieces),
        out_specs=VMEM,
        scratch_shapes=[
            pltpu.VMEM((3 * rows, width), BF16),
            pltpu.VMEM((rows, 3 * rows), F32),
            pltpu.VMEM((3, width, heads_width), BF16),
            pltpu.VMEM((heads_width, width), BF16),
            pltpu.SemaphoreType.DMA((3 * len(pieces),)),
        ],
        compiler_params=pltpu.CompilerParams(vmem_limit_bytes=VMEM_LIMIT),
        cost_estimate=attend_cost(rows, width, heads_width),
        name=name,
    )(*shards, summed, gain, bias, *[value for _, _, value in pieces])


def gelu(values):
    return 0.5 * values * (1.0 + lax.erf(values * math.sqrt(0.5)))


def feed_into(total_ref, rows, up_ref, down_ref):
    chunk = 512
    for at in range(0, up_ref.shape[1], chunk):
        units = gelu(jnp.dot(rows, up_ref[:, at : at + chunk], preferred_element_type=F32)).astype(BF16)
        total_ref[...] += jnp.dot(units, down_ref[at : at + chunk, :], preferred_element_type=F32)


def feed_near_kernel(rows_ref, up_ref, down_ref, sum_ref):
    sum_ref[...] = jnp.zeros_like(sum_ref)
    feed_into(sum_ref, rows_ref[...], up_ref, down_ref)


def feed_cost(count, width, units):
    return pl.CostEstimate(
        flops=4 * count * width * units, bytes_accessed=4 * width * units, transcendentals=count * units
    )


def feed_near(rows, up_weight, down_weight, name):
    count, width = rows.shape
    return pl.pallas_call(
        feed_near_kernel,
        out_shape=jax.ShapeDtypeStruct((count, width), F32),
        in_specs=[VMEM] * 3,
        out_specs=VMEM,
        compiler_params=pltpu.CompilerParams(vmem_limit_bytes=VMEM_LIMIT),
        cost_estimate=feed_cost(count, width, up_weight.shape[1]),
        name=name,
    )(rows, up_weight, down_weight)


def feed_far_kernel(layout, *refs):
    count = len(layout)
    place_ref, rows_ref, near_ref = refs[:3]
    pieces = refs[3 : 3 + count]
    sum_ref, up_ref, down_ref, total_ref, sems = refs[3 + count :]
    tok = place_ref[1]
    block = 128
    copies = []
    for (flip, part), piece in zip(layout, pieces):
        at = pl.multiple_of((tok ^ flip) * block, block)
        if part in (None, 0):
            copies.append(pltpu.make_async_copy(piece.at[0:block], up_ref.at[pl.ds(at, block)], sems.at[len(copies)]))
        if part in (None, 1):
            shift = block if part is None else 0
            copies.append(
                pltpu.make_async_copy(
                    piece.at[shift : shift + block], down_ref.at[pl.ds(at, block)], sems.at[len(copies)]
                )
            )
    for copy in copies:
        copy.start()
    total_ref[...] = near_ref[...]
    for copy in copies:
        copy.wait()
    feed_into(total_ref, rows_ref[...], up_ref, down_ref)
    sum_ref[...] = total_ref[...].astype(sum_ref.dtype)


def feed_far(place, rows, near, pieces, units, dtype, name):
    count, width = rows.shape
    layout = tuple((flip, part) for flip, part, _ in pieces)
    copies = sum(2 if part is None else 1 for _, part in layout)
    return pl.pallas_call(
        functools.partial(feed_far_kernel, layout),
        out_shape=jax.ShapeDtypeStruct((count, width), dtype),
        in_specs=[SMEM] + [VMEM] * 2 + [ANY] * len(pieces),
        out_specs=VMEM,
        scratch_shapes=[
            pltpu.VMEM((width, units), BF16),
            pltpu.VMEM((units, width), BF16),
            pltpu.VMEM((count, width), F32),
            pltpu.SemaphoreType.DMA((copies,)),
        ],
        compiler_params=pltpu.CompilerParams(vmem_limit_bytes=VMEM_LIMIT),
        cost_estimate=feed_cost(count, width, units),
        name=name,
    )(place, rows, near, *[value for _, _, value in pieces])


def finish_kernel(normed_ref, near_ref, far_ref, gain_ref, bias_ref, out_ref):
    mixed = normed_ref[...].astype(F32) + near_ref[...] + far_ref[...].astype(F32)
    out_ref[...] = normalized(mixed, gain_ref[...], bias_ref[...]).astype(out_ref.dtype)


def finish(normed, near, far, gain, bias):
    return pl.pallas_call(
        finish_kernel,
        out_shape=jax.ShapeDtypeStruct(normed.shape, BF16),
        in_specs=[VMEM] * 5,
        out_specs=VMEM,
        compiler_params=pltpu.CompilerParams(vmem_limit_bytes=VMEM_LIMIT),
        name="finish",
    )(normed, near, far, gain, bias)


def decode_kernel(slot_ref, filled_ref, query_ref, cache_ref, out_ref, high_ref, total_ref, sum_ref):
    step = pl.program_id(0)

    @pl.when(step == 0)
    def _():
        high_ref[...] = jnp.full(high_ref.shape, NEG_FILL, F32)
        total_ref[...] = jnp.zeros_like(total_ref)
        sum_ref[...] = jnp.zeros_like(sum_ref)

    row = slot_ref[step]
    filled = filled_ref[step]
    width = query_ref.shape[1]
    head = lax.broadcasted_iota(jnp.int32, (H, width), 0)
    inside = head == lax.broadcasted_iota(jnp.int32, (H, width), 1) // HD
    query = jnp.where(inside, query_ref[pl.ds(row, 1), :], 0.0).astype(BF16)
    scores = lax.dot_general(query, cache_ref[0, 0, 0], (((1,), (1,)), ((), ())), preferred_element_type=F32)
    live = lax.broadcasted_iota(jnp.int32, scores.shape, 1) < filled
    scores = jnp.where(live, scores * (1.0 / math.sqrt(HD)), NEG_FILL)
    high = jnp.max(scores, axis=1, keepdims=True)
    weights = jnp.where(live, jnp.exp(scores - high), 0.0)
    total = jnp.sum(weights, axis=1, keepdims=True)
    summed = jnp.dot(weights.astype(BF16), cache_ref[1, 0, 0], preferred_element_type=F32)
    along = lambda column: jnp.sum(jnp.where(inside, column, 0.0), axis=0, keepdims=True)
    high, total, summed = along(high), along(total), along(summed)
    used = filled > 0
    at = pl.ds(row, 1)
    old = high_ref[at, :]
    new = jnp.where(used, jnp.maximum(old, high), old)
    left = jnp.exp(old - new)
    right = jnp.where(used, jnp.exp(high - new), 0.0)
    high_ref[at, :] = new
    total_ref[at, :] = total_ref[at, :] * left + total * right
    sum_ref[at, :] = sum_ref[at, :] * left + summed * right

    @pl.when(step == pl.num_programs(0) - 1)
    def _():
        out_ref[0] = high_ref[...]
        out_ref[1] = total_ref[...]
        out_ref[2] = sum_ref[...]


def decode(slots, filled, queries, kv_cache):
    requests, width = queries.shape
    pieces = kv_cache.shape[2]
    state = pltpu.VMEM((requests, width), F32)
    return pl.pallas_call(
        decode_kernel,
        grid=(pieces,),
        out_shape=jax.ShapeDtypeStruct((3, requests, width), F32),
        in_specs=[
            SMEM,
            SMEM,
            pl.BlockSpec((requests, width), lambda i: (0, 0)),
            pl.BlockSpec((2, 1, 1, PLEN, width), lambda i: (0, 0, i, 0, 0)),
        ],
        out_specs=pl.BlockSpec((3, requests, width), lambda i: (0, 0, 0)),
        scratch_shapes=[state, state, state],
        compiler_params=pltpu.CompilerParams(vmem_limit_bytes=VMEM_LIMIT),
        cost_estimate=pl.CostEstimate(flops=0, bytes_accessed=kv_cache.size * 2, transcendentals=0),
        name="decode",
    )(slots, filled, queries, kv_cache)


def gathered_queries(dec_query):
    flips = range(1, lax.axis_size("kv"))
    return [dec_query] + [swapped(dec_query, "kv", flip) for flip in flips]


def decode_partial(queries, kv_cache, piece_req, piece_used):
    own = queries[0].shape[0]
    owners = piece_req[0]
    slots = ((owners // own) ^ lax.axis_index("kv")) * own + owners % own
    return decode(slots, piece_used[0], jnp.concatenate(queries).astype(F32), kv_cache)


def decode_merged(partial, own):
    parts = [partial[:, :own]]
    for flip in range(1, lax.axis_size("kv")):
        parts.append(swapped(partial[:, flip * own : (flip + 1) * own], "kv", flip))
    high = functools.reduce(jnp.maximum, [part[0] for part in parts])
    factors = [jnp.exp(part[0] - high) for part in parts]
    total = sum(part[1] * factor for part, factor in zip(parts, factors))
    summed = sum(part[2] * factor for part, factor in zip(parts, factors))
    return (summed / total).astype(BF16)


def routed_body(
    hidden_in,
    qkv_weight,
    stretch_len,
    out_weight,
    ln1_gain,
    ln1_bias,
    up_weight,
    down_weight,
    ln2_gain,
    ln2_bias,
    dec_query,
    kv_cache,
    piece_req,
    piece_used,
):
    tok = lax.axis_index("tok")
    kv = lax.axis_index("kv")
    toks, kvs = lax.axis_size("tok"), lax.axis_size("kv")
    rows, width = hidden_in.shape
    heads_width = out_weight.shape[0]
    block = width // toks

    queries = gathered_queries(dec_query)
    flat = toks * kvs
    before = lax.ppermute(hidden_in, ("tok", "kv"), [(i, i + 1) for i in range(flat - 1)])
    behind = lax.ppermute(hidden_in, ("tok", "kv"), [(i + 1, i) for i in range(flat - 1)])

    eighth = lambda value, axis: lax.dynamic_slice_in_dim(value, tok * block, block, axis)
    out_part = eighth(out_weight, 1)
    qkv_part = lax.optimization_barrier(eighth(qkv_weight, 0))
    bundle = jnp.concatenate(
        [
            jnp.transpose(qkv_part, (1, 0, 2)),
            jnp.concatenate([out_part[:block], out_part[block:]], axis=1)[None],
        ],
        axis=0,
    )
    bundle = after(bundle, *queries)
    foreign = [swapped(bundle, "kv", flip) for flip in range(1, kvs)]
    feed_part = jnp.concatenate([eighth(up_weight, 0), eighth(down_weight, 0)], axis=0)
    feed_foreign = swapped(feed_part, "kv", 2)

    partial = decode_partial(queries, kv_cache, piece_req, piece_used)
    pieces = [spread_in_plane(foreign[0])]
    turn = partial
    for value in foreign[1:]:
        pieces.append(spread_in_plane(after(value, turn)))
        turn = pieces[-1][1][2]
    feed_pieces = spread_in_plane(after(feed_foreign, turn))

    place = jnp.stack([(tok * kvs + kv) * rows, tok]).astype(jnp.int32)
    order = jnp.arange(stretch_len.shape[0])
    ends = jnp.sum(jnp.where(order[:, None] <= order[None, :], stretch_len[:, None], 0), axis=0, dtype=jnp.int32)
    starts = (ends - stretch_len)[None, :]
    shards = (place, starts, ends[None, :], before, hidden_in, behind)

    total = attend_own(shards, jnp.transpose(qkv_weight, (1, 0, 2)), out_weight)
    for index, quarter in enumerate(pieces):
        last = index == len(pieces) - 1
        partial = after(partial, total) if last else partial
        total = attend_next(
            shards, total, ln1_gain[None, :], ln1_bias[None, :], quarter, heads_width, last, "attend_%d" % (index + 1)
        )
    normed = total

    units = up_weight.shape[1]
    partner = swapped(normed, "kv", 1)
    near = feed_near(normed, up_weight, down_weight, "feed_near_own")
    partner = after(partner, near)
    near_away = feed_near(partner, up_weight, down_weight, "feed_near_partner")
    away = feed_far(place, partner, near_away, feed_pieces, units, BF16, "feed_far_partner")
    arrived = swapped(away, "kv", 1)
    mine = feed_far(place, after(normed, away), near, feed_pieces, units, F32, "feed_far_own")
    prefill_out = finish(normed, mine, arrived, ln2_gain[None, :], ln2_bias[None, :])

    return prefill_out, decode_merged(partial, dec_query.shape[0])


def extended(value, sides, width):
    for axis, dim in sides:
        count, length = (lax.axis_size(axis), value.shape[dim])
        up = [(i, (i + 1) % count) for i in range(count - 1)]
        down = [(j, i) for i, j in up]
        last = lax.slice_in_dim(value, length - width, length, axis=dim)
        leading = lax.slice_in_dim(value, 0, width, axis=dim)
        before = lax.ppermute(last, axis, up)
        after = lax.ppermute(leading, axis, down)
        value = jnp.concatenate([before, value, after], axis=dim)
    return value


def merged(value, axis, join):
    pieces = jax.tree.map(lambda part: lax.all_gather(part, axis), value)
    head = jax.tree.map(lambda part: part[0], pieces)
    tail = jax.tree.map(lambda part: part[1:], pieces)
    subtotal, _ = lax.scan(lambda subtotal, section: (join(subtotal, section), None), head, tail)
    return subtotal


def segment_ids(row_ids, stretch_len):
    stretch_ends = jnp.cumsum(stretch_len)
    return jnp.sum((row_ids[:, None] >= stretch_ends[None, :]).astype(jnp.int32), axis=1)


def layer_norm(values, gain, bias):
    center = values - jnp.mean(values, axis=1, keepdims=True)
    spread = jnp.mean(center * center, axis=1, keepdims=True)
    return center * lax.rsqrt(spread + LN_EPS) * gain + bias


def merge_partials(earlier, later):
    highest = jnp.maximum(earlier[0], later[0])
    left_factor = jnp.exp(earlier[0] - highest)
    right_factor = jnp.exp(later[0] - highest)
    totals = earlier[1] * left_factor + later[1] * right_factor
    weighted = earlier[2] * left_factor[..., None] + later[2] * right_factor[..., None]
    return (highest, totals, weighted)


def row_folder(source, shard_rows):
    return jnp.dot(source, shard_rows, preferred_element_type=jnp.float32)


def general_body(
    hidden_in,
    qkv_weight,
    stretch_len,
    out_weight,
    ln1_gain,
    ln1_bias,
    up_weight,
    down_weight,
    ln2_gain,
    ln2_bias,
    dec_query,
    kv_cache,
    piece_req,
    piece_used,
):
    inv_scale = 1.0 / math.sqrt(HD)
    reach = WIN // 2
    local_width = qkv_weight.shape[2]
    head_count = local_width // HD
    flat_weight = qkv_weight.reshape(qkv_weight.shape[0], 3 * local_width)
    qkv_rows = jnp.dot(
        lax.all_gather(hidden_in, "kv", axis=0, tiled=True),
        flat_weight,
        preferred_element_type=jnp.float32,
    ).astype(jnp.bfloat16)
    row_count = qkv_rows.shape[0]
    query_rows = qkv_rows[:, :local_width]
    keyval_rows = qkv_rows[:, local_width:]
    padded = extended(keyval_rows, (("tok", 0),), reach)
    first_row = lax.axis_index("tok") * row_count
    total_rows = row_count * lax.axis_size("tok")
    qblock = min(512, row_count)
    span = qblock + 2 * reach
    block_count = row_count // qblock

    def attend(block_index):
        start = block_index * qblock
        query_ids = first_row + start + jnp.arange(qblock, dtype=jnp.int32)
        key_ids = first_row + start - reach + jnp.arange(span, dtype=jnp.int32)
        query_seg = segment_ids(query_ids, stretch_len)
        inside = (key_ids >= 0) & (key_ids < total_rows)
        key_seg = jnp.where(inside, segment_ids(key_ids, stretch_len), -1)
        allowed = (key_seg[None, :] == query_seg[:, None]) & (
            jnp.abs(key_ids[None, :] - query_ids[:, None]) <= reach
        )
        queries = lax.dynamic_slice_in_dim(query_rows, start, qblock, 0).reshape(
            qblock, head_count, HD
        )
        both = lax.dynamic_slice_in_dim(padded, start, span, 0)
        key_rows = both[:, :local_width].reshape(span, head_count, HD)
        value_rows = both[:, local_width:].reshape(span, head_count, HD)
        scores = (
            jnp.einsum("ihd,jhd->hij", queries, key_rows, preferred_element_type=jnp.float32)
            * inv_scale
        )
        scores = jnp.where(allowed[None], scores, NEG_FILL)
        row_max = jnp.max(scores, axis=2, keepdims=True)
        weights = jnp.where(allowed[None], jnp.exp(scores - row_max), 0.0)
        totals = jnp.sum(weights, axis=2)
        summed = jnp.einsum(
            "hij,jhd->ihd",
            weights.astype(jnp.bfloat16),
            value_rows,
            preferred_element_type=jnp.float32,
        )
        return (
            (summed / jnp.transpose(totals)[:, :, None])
            .astype(jnp.bfloat16)
            .reshape(qblock, local_width)
        )

    attention = lax.map(attend, jnp.arange(block_count, dtype=jnp.int32)).reshape(
        row_count, local_width
    )
    token_major = lax.all_to_all(attention, "kv", split_axis=0, concat_axis=1, tiled=True)
    projected = row_folder(token_major, lax.all_gather(out_weight, "kv", axis=0, tiled=True))
    normed = layer_norm(hidden_in.astype(jnp.float32) + projected, ln1_gain, ln1_bias).astype(
        jnp.bfloat16
    )
    units = jax.nn.gelu(
        jnp.dot(
            lax.all_gather(normed, "kv", axis=0, tiled=True),
            up_weight,
            preferred_element_type=jnp.float32,
        ),
        approximate=False,
    ).astype(jnp.bfloat16)
    ffn = lax.psum_scatter(
        jnp.dot(units, down_weight, preferred_element_type=jnp.float32).astype(jnp.bfloat16),
        "kv",
        scatter_dimension=0,
        tiled=True,
    ).astype(jnp.float32)
    prefill_out = layer_norm(normed.astype(jnp.float32) + ffn, ln2_gain, ln2_bias).astype(
        jnp.bfloat16
    )
    group_queries = lax.all_gather(dec_query, "kv", axis=0, tiled=True)
    request_count = group_queries.shape[0]
    owners = piece_req[0]
    filled = piece_used[0]
    slot_count = owners.shape[0]
    request_ids = jnp.arange(request_count, dtype=jnp.int32)
    selector = (owners[:, None] == request_ids[None, :]).astype(jnp.bfloat16)
    chosen = jnp.dot(selector, group_queries, preferred_element_type=jnp.float32).astype(
        jnp.bfloat16
    )
    chosen = chosen.reshape(slot_count, H, HD)
    cache_keys = kv_cache[0, 0].reshape(slot_count, PLEN, H, HD)
    cache_values = kv_cache[1, 0].reshape(slot_count, PLEN, H, HD)
    piece_scores = (
        jnp.einsum("phd,pthd->pht", chosen, cache_keys, preferred_element_type=jnp.float32)
        * inv_scale
    )
    active = jnp.arange(PLEN, dtype=jnp.int32)[None, :] < filled[:, None]
    piece_scores = jnp.where(active[:, None, :], piece_scores, NEG_FILL)
    piece_max = jnp.max(piece_scores, axis=2)
    piece_weights = jnp.where(
        active[:, None, :], jnp.exp(piece_scores - piece_max[:, :, None]), 0.0
    )
    piece_totals = jnp.sum(piece_weights, axis=2)
    partial_value = jnp.einsum(
        "pht,pthd->phd",
        piece_weights.astype(jnp.bfloat16),
        cache_values,
        preferred_element_type=jnp.float32,
    )
    member = (owners[None, :] == request_ids[:, None]) & (filled[None, :] > 0)
    highest = jnp.max(jnp.where(member[:, :, None], piece_max[None], NEG_FILL), axis=1)
    factor = jnp.where(member[:, :, None], jnp.exp(piece_max[None] - highest[:, None, :]), 0.0)
    denom = jnp.sum(factor * piece_totals[None], axis=1)
    weighted = jnp.einsum("rph,phd->rhd", factor, partial_value)
    own_requests = dec_query.shape[0]
    joined = merged((highest, denom, weighted), "kv", merge_partials)
    begin = lax.axis_index("kv") * own_requests
    final_denom = lax.dynamic_slice_in_dim(joined[1], begin, own_requests, 0)
    final_weighted = lax.dynamic_slice_in_dim(joined[2], begin, own_requests, 0)
    dec_out = (
        (final_weighted / final_denom[:, :, None])
        .astype(jnp.bfloat16)
        .reshape(own_requests, H * HD)
    )
    return (prefill_out, dec_out)


def solution(mesh):
    placed = (
        P(("tok", "kv"), None),
        P(None, None, "kv"),
        P(),
        P("kv", None),
        P(),
        P(),
        P(None, "kv"),
        P("kv", None),
        P(),
        P(),
        P(("tok", "kv"), None),
        P(None, "tok", "kv", None, None),
        P("tok", "kv"),
        P("tok", "kv"),
    )
    routed = mesh.shape["tok"] == 8 and mesh.shape["kv"] == 4
    return jax.shard_map(
        routed_body if routed else general_body,
        mesh=mesh,
        in_specs=placed,
        out_specs=(P(("tok", "kv"), None), P(("tok", "kv"), None)),
        check_vma=False,
    )
```

```python
import functools
import math

import jax
import jax.numpy as jnp
from jax import lax
from jax.experimental import pallas as pl
from jax.experimental.pallas import tpu as pltpu
from jax.sharding import PartitionSpec as P

H = 16
HD = 64
WIN = 512
PLEN = 128


NEG_FILL = -1e30
LN_EPS = 1e-05
BF16 = jnp.bfloat16
F32 = jnp.float32
VMEM_LIMIT = 56 * 1024 * 1024
ANY = pl.BlockSpec(memory_space=pl.ANY)
VMEM = pl.BlockSpec(memory_space=pltpu.VMEM)
SMEM = pl.BlockSpec(memory_space=pltpu.SMEM)


def swapped(value, axis, flip):
    count = lax.axis_size(axis)
    return lax.ppermute(value, axis, [(i, i ^ flip) for i in range(count)])


def after(value, *earlier):
    return lax.optimization_barrier((value,) + earlier)[0]


def normalized(values, gain, bias):
    center = values - jnp.mean(values, axis=1, keepdims=True)
    spread = jnp.mean(center * center, axis=1, keepdims=True)
    return center * lax.rsqrt(spread + LN_EPS) * gain + bias


def project_kernel(place_ref, weight_ref, *refs):
    shards, (query_ref, keyval_ref, top_ref, bottom_ref, rows_ref, sems) = refs[:-6], refs[-6:]
    kv = place_ref[1]
    count = shards[0].shape[0]
    steps = (len(shards) - 1) // 2
    width = weight_ref.shape[2]
    moves = [(shards[0], kv, None)]
    for step in range(1, steps + 1):
        moves.append((shards[step], kv - step, kv >= step))
        moves.append((shards[steps + step], kv + step, kv + step <= steps))

    def guarded(needed, act):
        if needed is None:
            act()
        else:
            pl.when(needed)(act)

    copies = []
    for index, (source, owner, needed) in enumerate(moves):
        safe = owner if needed is None else jnp.where(needed, owner, 0)
        at = pl.ds(pl.multiple_of(safe * count, count), count)
        copies.append((needed, pltpu.make_async_copy(source, rows_ref.at[at], sems.at[index])))
    for needed, copy in copies:
        guarded(needed, copy.start)
    for needed, copy in copies:
        guarded(needed, copy.wait)
    scale = 1.0 / math.sqrt(HD)
    for block in range(steps + 1):
        at = slice(block * count, (block + 1) * count)
        rows = rows_ref[at]
        query = jnp.dot(rows, weight_ref[0], preferred_element_type=F32) * scale
        query_ref[at] = query.astype(BF16)
        keys = jnp.dot(rows, weight_ref[1], preferred_element_type=F32).astype(BF16)
        values = jnp.dot(rows, weight_ref[2], preferred_element_type=F32).astype(BF16)
        keyval_ref[at, :width] = keys
        keyval_ref[at, width:] = values
        for edge, edge_ref in ((0, top_ref), (steps, bottom_ref)):
            if block == edge:
                edge_ref[:, :width] = keys
                edge_ref[:, width:] = values


def project(place, weight, shards):
    rows, width = shards[0].shape
    heads_width = weight.shape[2]
    blocks = (len(shards) + 1) // 2
    edge = jax.ShapeDtypeStruct((rows, 2 * heads_width), BF16)
    return pl.pallas_call(
        project_kernel,
        out_shape=(
            jax.ShapeDtypeStruct((blocks * rows, heads_width), BF16),
            jax.ShapeDtypeStruct((blocks * rows, 2 * heads_width), BF16),
            edge,
            edge,
        ),
        in_specs=[SMEM, VMEM] + [ANY] * len(shards),
        out_specs=(VMEM,) * 4,
        scratch_shapes=[pltpu.VMEM((blocks * rows, width), BF16), pltpu.SemaphoreType.DMA((len(shards),))],
        compiler_params=pltpu.CompilerParams(vmem_limit_bytes=VMEM_LIMIT),
        cost_estimate=pl.CostEstimate(
            flops=6 * blocks * rows * width * heads_width, bytes_accessed=6 * width * heads_width, transcendentals=0
        ),
        name="project",
    )(place, weight, *shards)


def window_bias(first, count, starts, ends):
    reach = WIN // 2
    query = first + lax.broadcasted_iota(jnp.int32, (count, 1), 0)
    low = jnp.max(jnp.where(starts <= query, starts, 0), axis=1, keepdims=True)
    high = jnp.min(jnp.where(ends > query, ends, 1 << 30), axis=1, keepdims=True)
    low = jnp.maximum(low, query - reach)
    high = jnp.minimum(high, query + reach + 1)
    key = first - count + lax.broadcasted_iota(jnp.int32, (count, 3 * count), 1)
    return jnp.where((key >= low) & (key < high), 0.0, NEG_FILL)


def attend(query, keyval_ref, bias):
    count, width = query.shape
    lane = lax.broadcasted_iota(jnp.int32, (count, 2 * HD), 1)
    pairs = []
    for start in range(0, width, 2 * HD):
        keys = keyval_ref[:, start : start + 2 * HD]
        values = keyval_ref[:, width + start : width + start + 2 * HD]
        halves = []
        for side in range(2):
            inside = (lane < HD) if side == 0 else (lane >= HD)
            only = jnp.where(inside, query[:, start : start + 2 * HD], jnp.zeros((), BF16))
            scores = lax.dot_general(only, keys, (((1,), (1,)), ((), ())), preferred_element_type=F32)
            scores = scores + bias
            highest = jnp.max(scores, axis=1, keepdims=True)
            weights = jnp.exp(scores - highest)
            total = jnp.sum(weights, axis=1, keepdims=True)
            summed = jnp.dot(weights.astype(BF16), values, preferred_element_type=F32)
            halves.append(summed / total)
        pairs.append(jnp.where(lane < HD, halves[0], halves[1]).astype(BF16))
    return jnp.concatenate(pairs, axis=1)


def attend_kernel(flips, place_ref, starts_ref, ends_ref, query_ref, before_ref, keyval_ref, behind_ref, *refs):
    outs, (window_ref, sems) = refs[: len(flips)], refs[len(flips) :]
    tok, kv = place_ref[0], place_ref[1]
    count = outs[0].shape[0]
    blocks = query_ref.shape[0] // count
    copies = []
    for index, flip in enumerate(flips):
        block = kv ^ flip
        for part in range(3):
            target = window_ref.at[index, part * count : (part + 1) * count]
            sem = sems.at[index, part]
            at = block + part - 1
            inner = (at >= 0) & (at < blocks)
            safe = jnp.where(inner, at, 0)
            source = keyval_ref.at[pl.ds(pl.multiple_of(safe * count, count), count)]
            copies.append((index, inner, pltpu.make_async_copy(source, target, sem)))
            if part == 0:
                copies.append((index, at < 0, pltpu.make_async_copy(before_ref, target, sem)))
            if part == 2:
                copies.append((index, at >= blocks, pltpu.make_async_copy(behind_ref, target, sem)))
    for _, needed, copy in copies:
        pl.when(needed)(copy.start)
    for index, flip in enumerate(flips):
        block = kv ^ flip
        first = (tok * blocks + block) * count
        bias = window_bias(first, count, starts_ref[...], ends_ref[...])
        for owner, needed, copy in copies:
            if owner == index:
                pl.when(needed)(copy.wait)
        query = query_ref[pl.ds(pl.multiple_of(block * count, count), count)]
        outs[index][...] = attend(query, window_ref.at[index], bias)


def attend_blocks(place, starts, ends, query, before, keyval, behind, rows, flips, name):
    heads_width = query.shape[1]
    pairs = rows * 3 * rows * heads_width * len(flips)
    return pl.pallas_call(
        functools.partial(attend_kernel, flips),
        out_shape=tuple(jax.ShapeDtypeStruct((rows, heads_width), BF16) for _ in flips),
        in_specs=[SMEM, VMEM, VMEM, VMEM, ANY, ANY, ANY],
        out_specs=(VMEM,) * len(flips),
        scratch_shapes=[
            pltpu.VMEM((len(flips), 3 * rows, 2 * heads_width), BF16),
            pltpu.SemaphoreType.DMA((len(flips), 3)),
        ],
        compiler_params=pltpu.CompilerParams(vmem_limit_bytes=VMEM_LIMIT),
        cost_estimate=pl.CostEstimate(flops=32 * pairs, bytes_accessed=8 * rows * heads_width, transcendentals=0),
        name=name,
    )(place, starts, ends, query, before, keyval, behind)


def first_norm_kernel(place_ref, hidden_ref, out_ref, gain_ref, bias_ref, *refs):
    parts, (normed_ref, all_ref, weight_ref, sems) = refs[:-4], refs[-4:]
    kv = place_ref[1]
    eighths, quarters, depth, width = out_ref.shape
    copies = []
    for index in range(eighths):
        target = weight_ref.at[:, index * depth : (index + 1) * depth]
        copies.append(pltpu.make_async_copy(out_ref.at[index], target, sems.at[index]))
    for copy in copies:
        copy.start()
    heads_width = eighths * depth
    for flip, part_ref in enumerate(parts):
        at = pl.multiple_of((kv ^ flip) * heads_width, heads_width)
        all_ref[:, pl.ds(at, heads_width)] = part_ref[...]
    for copy in copies:
        copy.wait()
    weight = weight_ref[...].reshape(quarters * heads_width, width)
    projected = jnp.dot(all_ref[...], weight, preferred_element_type=F32)
    mixed = hidden_ref[...].astype(F32) + projected
    normed_ref[...] = normalized(mixed, gain_ref[...], bias_ref[...]).astype(BF16)


def first_norm(place, hidden, out_pieces, gain, bias, parts):
    rows, width = hidden.shape
    eighths, quarters, depth, _ = out_pieces.shape
    return pl.pallas_call(
        first_norm_kernel,
        out_shape=jax.ShapeDtypeStruct((rows, width), BF16),
        in_specs=[SMEM, VMEM, ANY, VMEM, VMEM] + [VMEM] * len(parts),
        out_specs=VMEM,
        scratch_shapes=[
            pltpu.VMEM((rows, width), BF16),
            pltpu.VMEM((quarters, eighths * depth, width), BF16),
            pltpu.SemaphoreType.DMA((eighths,)),
        ],
        compiler_params=pltpu.CompilerParams(vmem_limit_bytes=VMEM_LIMIT),
        cost_estimate=pl.CostEstimate(
            flops=2 * rows * width * width, bytes_accessed=2 * width * width, transcendentals=0
        ),
        name="first_norm",
    )(place, hidden, out_pieces, gain, bias, *parts)


def gelu(values):
    return 0.5 * values * (1.0 + lax.erf(values * math.sqrt(0.5)))


def feed_into(total_ref, rows, up_ref, down_ref):
    chunk = 512
    for at in range(0, up_ref.shape[1], chunk):
        units = gelu(jnp.dot(rows, up_ref[:, at : at + chunk], preferred_element_type=F32)).astype(BF16)
        total_ref[...] += jnp.dot(units, down_ref[at : at + chunk, :], preferred_element_type=F32)


def feed_near_kernel(rows_ref, up_ref, down_ref, sum_ref):
    sum_ref[...] = jnp.zeros_like(sum_ref)
    feed_into(sum_ref, rows_ref[...], up_ref, down_ref)


def feed_cost(count, width, units):
    return pl.CostEstimate(
        flops=4 * count * width * units, bytes_accessed=4 * width * units, transcendentals=count * units
    )


def feed_near(rows, up_weight, down_weight, name):
    count, width = rows.shape
    return pl.pallas_call(
        feed_near_kernel,
        out_shape=jax.ShapeDtypeStruct((count, width), F32),
        in_specs=[VMEM] * 3,
        out_specs=VMEM,
        compiler_params=pltpu.CompilerParams(vmem_limit_bytes=VMEM_LIMIT),
        cost_estimate=feed_cost(count, width, up_weight.shape[1]),
        name=name,
    )(rows, up_weight, down_weight)


def feed_far_kernel(layout, *refs):
    count = len(layout)
    place_ref, rows_ref, near_ref = refs[:3]
    pieces = refs[3 : 3 + count]
    sum_ref, up_ref, down_ref, total_ref, sems = refs[3 + count :]
    tok = place_ref[0]
    block = 128
    copies = []
    for (flip, part), piece in zip(layout, pieces):
        at = pl.multiple_of((tok ^ flip) * block, block)
        if part in (None, 0):
            copies.append(pltpu.make_async_copy(piece.at[0:block], up_ref.at[pl.ds(at, block)], sems.at[len(copies)]))
        if part in (None, 1):
            shift = block if part is None else 0
            copies.append(
                pltpu.make_async_copy(
                    piece.at[shift : shift + block], down_ref.at[pl.ds(at, block)], sems.at[len(copies)]
                )
            )
    for copy in copies:
        copy.start()
    total_ref[...] = near_ref[...]
    for copy in copies:
        copy.wait()
    feed_into(total_ref, rows_ref[...], up_ref, down_ref)
    sum_ref[...] = total_ref[...].astype(sum_ref.dtype)


def feed_far(place, rows, near, pieces, units, dtype, name):
    count, width = rows.shape
    layout = tuple((flip, part) for flip, part, _ in pieces)
    copies = sum(2 if part is None else 1 for _, part in layout)
    return pl.pallas_call(
        functools.partial(feed_far_kernel, layout),
        out_shape=jax.ShapeDtypeStruct((count, width), dtype),
        in_specs=[SMEM] + [VMEM] * 2 + [ANY] * len(pieces),
        out_specs=VMEM,
        scratch_shapes=[
            pltpu.VMEM((width, units), BF16),
            pltpu.VMEM((units, width), BF16),
            pltpu.VMEM((count, width), F32),
            pltpu.SemaphoreType.DMA((copies,)),
        ],
        compiler_params=pltpu.CompilerParams(vmem_limit_bytes=VMEM_LIMIT),
        cost_estimate=feed_cost(count, width, units),
        name=name,
    )(place, rows, near, *[value for _, _, value in pieces])


def finish_kernel(normed_ref, near_ref, far_ref, gain_ref, bias_ref, out_ref):
    mixed = normed_ref[...].astype(F32) + near_ref[...] + far_ref[...].astype(F32)
    out_ref[...] = normalized(mixed, gain_ref[...], bias_ref[...]).astype(out_ref.dtype)


def finish(normed, near, far, gain, bias):
    return pl.pallas_call(
        finish_kernel,
        out_shape=jax.ShapeDtypeStruct(normed.shape, BF16),
        in_specs=[VMEM] * 5,
        out_specs=VMEM,
        compiler_params=pltpu.CompilerParams(vmem_limit_bytes=VMEM_LIMIT),
        name="finish",
    )(normed, near, far, gain, bias)


def decode_kernel(slot_ref, filled_ref, query_ref, cache_ref, out_ref, high_ref, total_ref, sum_ref):
    step = pl.program_id(0)

    @pl.when(step == 0)
    def _():
        high_ref[...] = jnp.full(high_ref.shape, NEG_FILL, F32)
        total_ref[...] = jnp.zeros_like(total_ref)
        sum_ref[...] = jnp.zeros_like(sum_ref)

    row = slot_ref[step]
    filled = filled_ref[step]
    width = query_ref.shape[1]
    head = lax.broadcasted_iota(jnp.int32, (H, width), 0)
    inside = head == lax.broadcasted_iota(jnp.int32, (H, width), 1) // HD
    query = jnp.where(inside, query_ref[pl.ds(row, 1), :], 0.0).astype(BF16)
    scores = lax.dot_general(query, cache_ref[0, 0, 0], (((1,), (1,)), ((), ())), preferred_element_type=F32)
    live = lax.broadcasted_iota(jnp.int32, scores.shape, 1) < filled
    scores = jnp.where(live, scores * (1.0 / math.sqrt(HD)), NEG_FILL)
    high = jnp.max(scores, axis=1, keepdims=True)
    weights = jnp.where(live, jnp.exp(scores - high), 0.0)
    total = jnp.sum(weights, axis=1, keepdims=True)
    summed = jnp.dot(weights.astype(BF16), cache_ref[1, 0, 0], preferred_element_type=F32)
    along = lambda column: jnp.sum(jnp.where(inside, column, 0.0), axis=0, keepdims=True)
    high, total, summed = along(high), along(total), along(summed)
    used = filled > 0
    at = pl.ds(row, 1)
    old = high_ref[at, :]
    new = jnp.where(used, jnp.maximum(old, high), old)
    left = jnp.exp(old - new)
    right = jnp.where(used, jnp.exp(high - new), 0.0)
    high_ref[at, :] = new
    total_ref[at, :] = total_ref[at, :] * left + total * right
    sum_ref[at, :] = sum_ref[at, :] * left + summed * right

    @pl.when(step == pl.num_programs(0) - 1)
    def _():
        out_ref[0] = high_ref[...]
        out_ref[1] = total_ref[...]
        out_ref[2] = sum_ref[...]


def decode(slots, filled, queries, kv_cache):
    requests, width = queries.shape
    pieces = kv_cache.shape[2]
    state = pltpu.VMEM((requests, width), F32)
    return pl.pallas_call(
        decode_kernel,
        grid=(pieces,),
        out_shape=jax.ShapeDtypeStruct((3, requests, width), F32),
        in_specs=[
            SMEM,
            SMEM,
            pl.BlockSpec((requests, width), lambda i: (0, 0)),
            pl.BlockSpec((2, 1, 1, PLEN, width), lambda i: (0, 0, i, 0, 0)),
        ],
        out_specs=pl.BlockSpec((3, requests, width), lambda i: (0, 0, 0)),
        scratch_shapes=[state, state, state],
        compiler_params=pltpu.CompilerParams(vmem_limit_bytes=VMEM_LIMIT),
        cost_estimate=pl.CostEstimate(flops=0, bytes_accessed=kv_cache.size * 2, transcendentals=0),
        name="decode",
    )(slots, filled, queries, kv_cache)


def gathered_queries(dec_query):
    flips = range(1, lax.axis_size("kv"))
    return [dec_query] + [swapped(dec_query, "kv", flip) for flip in flips]


def decode_partial(queries, kv_cache, piece_req, piece_used):
    own = queries[0].shape[0]
    owners = piece_req[0]
    slots = ((owners // own) ^ lax.axis_index("kv")) * own + owners % own
    return decode(slots, piece_used[0], jnp.concatenate(queries).astype(F32), kv_cache)


def exchanged_partials(partial, own):
    parts = [partial[:, :own]]
    for flip in range(1, lax.axis_size("kv")):
        parts.append(swapped(partial[:, flip * own : (flip + 1) * own], "kv", flip))
    return parts


def merged_partials(parts):
    high = functools.reduce(jnp.maximum, [part[0] for part in parts])
    factors = [jnp.exp(part[0] - high) for part in parts]
    total = sum(part[1] * factor for part, factor in zip(parts, factors))
    summed = sum(part[2] * factor for part, factor in zip(parts, factors))
    return (summed / total).astype(BF16)


def routed_body(
    hidden_in,
    qkv_weight,
    stretch_len,
    out_weight,
    ln1_gain,
    ln1_bias,
    up_weight,
    down_weight,
    ln2_gain,
    ln2_bias,
    dec_query,
    kv_cache,
    piece_req,
    piece_used,
):
    tok = lax.axis_index("tok")
    kv = lax.axis_index("kv")
    toks, kvs = lax.axis_size("tok"), lax.axis_size("kv")
    rows, width = hidden_in.shape
    place = jnp.stack([tok, kv]).astype(jnp.int32)
    eighth = lambda value: lax.dynamic_slice_in_dim(value, tok * (value.shape[0] // toks), value.shape[0] // toks, 0)

    queries = gathered_queries(dec_query)
    partial = decode_partial(queries, kv_cache, piece_req, piece_used)
    from_below, from_above = [], []
    rising = falling = hidden_in
    for step in range(1, kvs):
        links = range(step - 1, kvs - 1)
        rising = lax.ppermute(rising, "kv", [(i, i + 1) for i in links])
        falling = lax.ppermute(falling, "kv", [(kvs - 1 - i, kvs - 2 - i) for i in links])
        from_below.append(rising)
        from_above.append(falling)
        if step == 1:
            rising, falling = after(rising, partial), after(falling, partial)

    out_pieces = lax.all_gather(lax.all_gather(eighth(out_weight), "kv"), "tok")

    feed_part = jnp.concatenate([eighth(up_weight), eighth(down_weight)], axis=0)
    feed_here = swapped(after(feed_part, from_below[1], from_above[1]), "kv", 2)

    order = jnp.arange(stretch_len.shape[0])
    ends = jnp.sum(jnp.where(order[:, None] <= order[None, :], stretch_len[:, None], 0), axis=0, dtype=jnp.int32)
    starts = (ends - stretch_len)[None, :]
    ends = ends[None, :]

    shards = [hidden_in] + from_below + from_above
    query, keyval, top, bottom = project(place, jnp.transpose(qkv_weight, (1, 0, 2)), shards)
    before = lax.ppermute(bottom, "tok", [(i, i + 1) for i in range(toks - 1)])
    behind = lax.ppermute(top, "tok", [(i + 1, i) for i in range(toks - 1)])
    window = (place, starts, ends, query, before, keyval, behind, rows)
    parts = [None] * kvs
    parts[3], parts[2] = attend_blocks(*window, (3, 2), "attend_far")
    feed_here = after(feed_here, parts[3], parts[2])
    parts[3], parts[2] = swapped(parts[3], "kv", 3), swapped(parts[2], "kv", 2)
    feed_x, feed_y = swapped(feed_here, "tok", 2), swapped(feed_here, "tok", 4)
    window = (place, starts, ends, after(query, feed_here), before, keyval, behind, rows)
    parts[1], parts[0] = attend_blocks(*window, (1, 0), "attend_near")
    parts[1] = swapped(parts[1], "kv", 1)
    half = feed_here.shape[0] // 2
    far_up = swapped(after(feed_y, parts[0])[:half], "tok", 2)
    far_down = swapped(after(feed_x, parts[0])[half:], "tok", 4)
    normed = first_norm(place, hidden_in, out_pieces, ln1_gain[None, :], ln1_bias[None, :], parts)

    partner = swapped(normed, "kv", 1)
    held = [(0, None, feed_here), (2, None, feed_x), (4, None, feed_y), (6, 0, far_up), (6, 1, far_down)]
    feed_pieces = held + [(flip ^ 1, part, swapped(after(value, normed), "tok", 1)) for flip, part, value in held]
    units = up_weight.shape[1]
    near = feed_near(normed, up_weight, down_weight, "feed_near_own")
    dec_out = merged_partials(exchanged_partials(after(partial, normed), dec_query.shape[0]))
    partner = after(partner, near, dec_out)
    near_away = feed_near(partner, up_weight, down_weight, "feed_near_partner")
    away = feed_far(place, partner, near_away, feed_pieces, units, BF16, "feed_far_partner")
    arrived = swapped(away, "kv", 1)
    mine = feed_far(place, after(normed, away), near, feed_pieces, units, F32, "feed_far_own")
    prefill_out = finish(normed, mine, arrived, ln2_gain[None, :], ln2_bias[None, :])

    return prefill_out, dec_out


def extended(value, sides, width):
    for axis, dim in sides:
        count, length = (lax.axis_size(axis), value.shape[dim])
        up = [(i, (i + 1) % count) for i in range(count - 1)]
        down = [(j, i) for i, j in up]
        last = lax.slice_in_dim(value, length - width, length, axis=dim)
        leading = lax.slice_in_dim(value, 0, width, axis=dim)
        before = lax.ppermute(last, axis, up)
        after = lax.ppermute(leading, axis, down)
        value = jnp.concatenate([before, value, after], axis=dim)
    return value


def merged(value, axis, join):
    pieces = jax.tree.map(lambda part: lax.all_gather(part, axis), value)
    head = jax.tree.map(lambda part: part[0], pieces)
    tail = jax.tree.map(lambda part: part[1:], pieces)
    subtotal, _ = lax.scan(lambda subtotal, section: (join(subtotal, section), None), head, tail)
    return subtotal


def segment_ids(row_ids, stretch_len):
    stretch_ends = jnp.cumsum(stretch_len)
    return jnp.sum((row_ids[:, None] >= stretch_ends[None, :]).astype(jnp.int32), axis=1)


def layer_norm(values, gain, bias):
    center = values - jnp.mean(values, axis=1, keepdims=True)
    spread = jnp.mean(center * center, axis=1, keepdims=True)
    return center * lax.rsqrt(spread + LN_EPS) * gain + bias


def merge_partials(earlier, later):
    highest = jnp.maximum(earlier[0], later[0])
    left_factor = jnp.exp(earlier[0] - highest)
    right_factor = jnp.exp(later[0] - highest)
    totals = earlier[1] * left_factor + later[1] * right_factor
    weighted = earlier[2] * left_factor[..., None] + later[2] * right_factor[..., None]
    return (highest, totals, weighted)


def row_folder(source, shard_rows):
    return jnp.dot(source, shard_rows, preferred_element_type=jnp.float32)


def general_body(
    hidden_in,
    qkv_weight,
    stretch_len,
    out_weight,
    ln1_gain,
    ln1_bias,
    up_weight,
    down_weight,
    ln2_gain,
    ln2_bias,
    dec_query,
    kv_cache,
    piece_req,
    piece_used,
):
    inv_scale = 1.0 / math.sqrt(HD)
    reach = WIN // 2
    local_width = qkv_weight.shape[2]
    head_count = local_width // HD
    flat_weight = qkv_weight.reshape(qkv_weight.shape[0], 3 * local_width)
    qkv_rows = jnp.dot(
        lax.all_gather(hidden_in, "kv", axis=0, tiled=True),
        flat_weight,
        preferred_element_type=jnp.float32,
    ).astype(jnp.bfloat16)
    row_count = qkv_rows.shape[0]
    query_rows = qkv_rows[:, :local_width]
    keyval_rows = qkv_rows[:, local_width:]
    padded = extended(keyval_rows, (("tok", 0),), reach)
    first_row = lax.axis_index("tok") * row_count
    total_rows = row_count * lax.axis_size("tok")
    qblock = min(512, row_count)
    span = qblock + 2 * reach
    block_count = row_count // qblock

    def attend(block_index):
        start = block_index * qblock
        query_ids = first_row + start + jnp.arange(qblock, dtype=jnp.int32)
        key_ids = first_row + start - reach + jnp.arange(span, dtype=jnp.int32)
        query_seg = segment_ids(query_ids, stretch_len)
        inside = (key_ids >= 0) & (key_ids < total_rows)
        key_seg = jnp.where(inside, segment_ids(key_ids, stretch_len), -1)
        allowed = (key_seg[None, :] == query_seg[:, None]) & (
            jnp.abs(key_ids[None, :] - query_ids[:, None]) <= reach
        )
        queries = lax.dynamic_slice_in_dim(query_rows, start, qblock, 0).reshape(
            qblock, head_count, HD
        )
        both = lax.dynamic_slice_in_dim(padded, start, span, 0)
        key_rows = both[:, :local_width].reshape(span, head_count, HD)
        value_rows = both[:, local_width:].reshape(span, head_count, HD)
        scores = (
            jnp.einsum("ihd,jhd->hij", queries, key_rows, preferred_element_type=jnp.float32)
            * inv_scale
        )
        scores = jnp.where(allowed[None], scores, NEG_FILL)
        row_max = jnp.max(scores, axis=2, keepdims=True)
        weights = jnp.where(allowed[None], jnp.exp(scores - row_max), 0.0)
        totals = jnp.sum(weights, axis=2)
        summed = jnp.einsum(
            "hij,jhd->ihd",
            weights.astype(jnp.bfloat16),
            value_rows,
            preferred_element_type=jnp.float32,
        )
        return (
            (summed / jnp.transpose(totals)[:, :, None])
            .astype(jnp.bfloat16)
            .reshape(qblock, local_width)
        )

    attention = lax.map(attend, jnp.arange(block_count, dtype=jnp.int32)).reshape(
        row_count, local_width
    )
    token_major = lax.all_to_all(attention, "kv", split_axis=0, concat_axis=1, tiled=True)
    projected = row_folder(token_major, lax.all_gather(out_weight, "kv", axis=0, tiled=True))
    normed = layer_norm(hidden_in.astype(jnp.float32) + projected, ln1_gain, ln1_bias).astype(
        jnp.bfloat16
    )
    units = jax.nn.gelu(
        jnp.dot(
            lax.all_gather(normed, "kv", axis=0, tiled=True),
            up_weight,
            preferred_element_type=jnp.float32,
        ),
        approximate=False,
    ).astype(jnp.bfloat16)
    ffn = lax.psum_scatter(
        jnp.dot(units, down_weight, preferred_element_type=jnp.float32).astype(jnp.bfloat16),
        "kv",
        scatter_dimension=0,
        tiled=True,
    ).astype(jnp.float32)
    prefill_out = layer_norm(normed.astype(jnp.float32) + ffn, ln2_gain, ln2_bias).astype(
        jnp.bfloat16
    )
    group_queries = lax.all_gather(dec_query, "kv", axis=0, tiled=True)
    request_count = group_queries.shape[0]
    owners = piece_req[0]
    filled = piece_used[0]
    slot_count = owners.shape[0]
    request_ids = jnp.arange(request_count, dtype=jnp.int32)
    selector = (owners[:, None] == request_ids[None, :]).astype(jnp.bfloat16)
    chosen = jnp.dot(selector, group_queries, preferred_element_type=jnp.float32).astype(
        jnp.bfloat16
    )
    chosen = chosen.reshape(slot_count, H, HD)
    cache_keys = kv_cache[0, 0].reshape(slot_count, PLEN, H, HD)
    cache_values = kv_cache[1, 0].reshape(slot_count, PLEN, H, HD)
    piece_scores = (
        jnp.einsum("phd,pthd->pht", chosen, cache_keys, preferred_element_type=jnp.float32)
        * inv_scale
    )
    active = jnp.arange(PLEN, dtype=jnp.int32)[None, :] < filled[:, None]
    piece_scores = jnp.where(active[:, None, :], piece_scores, NEG_FILL)
    piece_max = jnp.max(piece_scores, axis=2)
    piece_weights = jnp.where(
        active[:, None, :], jnp.exp(piece_scores - piece_max[:, :, None]), 0.0
    )
    piece_totals = jnp.sum(piece_weights, axis=2)
    partial_value = jnp.einsum(
        "pht,pthd->phd",
        piece_weights.astype(jnp.bfloat16),
        cache_values,
        preferred_element_type=jnp.float32,
    )
    member = (owners[None, :] == request_ids[:, None]) & (filled[None, :] > 0)
    highest = jnp.max(jnp.where(member[:, :, None], piece_max[None], NEG_FILL), axis=1)
    factor = jnp.where(member[:, :, None], jnp.exp(piece_max[None] - highest[:, None, :]), 0.0)
    denom = jnp.sum(factor * piece_totals[None], axis=1)
    weighted = jnp.einsum("rph,phd->rhd", factor, partial_value)
    own_requests = dec_query.shape[0]
    joined = merged((highest, denom, weighted), "kv", merge_partials)
    begin = lax.axis_index("kv") * own_requests
    final_denom = lax.dynamic_slice_in_dim(joined[1], begin, own_requests, 0)
    final_weighted = lax.dynamic_slice_in_dim(joined[2], begin, own_requests, 0)
    dec_out = (
        (final_weighted / final_denom[:, :, None])
        .astype(jnp.bfloat16)
        .reshape(own_requests, H * HD)
    )
    return (prefill_out, dec_out)


def solution(mesh):
    placed = (
        P(("tok", "kv"), None),
        P(None, None, "kv"),
        P(),
        P("kv", None),
        P(),
        P(),
        P(None, "kv"),
        P("kv", None),
        P(),
        P(),
        P(("tok", "kv"), None),
        P(None, "tok", "kv", None, None),
        P("tok", "kv"),
        P("tok", "kv"),
    )
    routed = mesh.shape["tok"] == 8 and mesh.shape["kv"] == 4
    return jax.shard_map(
        routed_body if routed else general_body,
        mesh=mesh,
        in_specs=placed,
        out_specs=(P(("tok", "kv"), None), P(("tok", "kv"), None)),
        check_vma=False,
    )
```

```python
import functools
import math

import jax
import jax.numpy as jnp
from jax import lax
from jax.experimental import pallas as pl
from jax.experimental.pallas import tpu as pltpu
from jax.sharding import PartitionSpec as P

H = 16
HD = 64
WIN = 512
PLEN = 128


NEG_FILL = -1e30
LN_EPS = 1e-05
BF16 = jnp.bfloat16
F32 = jnp.float32
STRIP = 32
VMEM_LIMIT = 56 * 1024 * 1024
ANY = pl.BlockSpec(memory_space=pl.ANY)
VMEM = pl.BlockSpec(memory_space=pltpu.VMEM)
SMEM = pl.BlockSpec(memory_space=pltpu.SMEM)
SHORT = pl.CostEstimate(flops=1, bytes_accessed=1, transcendentals=0)


def swapped(value, axis, flip):
    count = lax.axis_size(axis)
    return lax.ppermute(value, axis, [(i, i ^ flip) for i in range(count)])


def after(value, *earlier):
    return lax.optimization_barrier((value,) + earlier)[0]


def normalized(values, gain, bias):
    center = values - jnp.mean(values, axis=1, keepdims=True)
    spread = jnp.mean(center * center, axis=1, keepdims=True)
    return center * lax.rsqrt(spread + LN_EPS) * gain + bias


def project_kernel(place_ref, weight_ref, *refs):
    shards, (query_ref, keyval_ref, top_ref, bottom_ref, rows_ref, sems) = refs[:-6], refs[-6:]
    kv = place_ref[1]
    count = shards[0].shape[0]
    steps = (len(shards) - 1) // 2
    width = weight_ref.shape[2]
    moves = [(shards[0], kv, None)]
    for step in range(1, steps + 1):
        moves.append((shards[step], kv - step, kv >= step))
        moves.append((shards[steps + step], kv + step, kv + step <= steps))

    def guarded(needed, act):
        if needed is None:
            act()
        else:
            pl.when(needed)(act)

    copies = []
    for index, (source, owner, needed) in enumerate(moves):
        safe = owner if needed is None else jnp.where(needed, owner, 0)
        at = pl.ds(pl.multiple_of(safe * count, count), count)
        copies.append((needed, pltpu.make_async_copy(source, rows_ref.at[at], sems.at[index])))
    for needed, copy in copies:
        guarded(needed, copy.start)
    for needed, copy in copies:
        guarded(needed, copy.wait)
    rows = rows_ref[...]
    query = jnp.dot(rows, weight_ref[0], preferred_element_type=F32) * (1.0 / math.sqrt(HD))
    query_ref[...] = query.astype(BF16)
    for part in range(2):
        at = slice(part * width, (part + 1) * width)
        keyval_ref[:, at] = jnp.dot(rows, weight_ref[part + 1], preferred_element_type=F32).astype(BF16)
    top_ref[...] = keyval_ref[:count]
    bottom_ref[...] = keyval_ref[steps * count :]


def project(place, weight, shards):
    rows, width = shards[0].shape
    heads_width = weight.shape[2]
    blocks = (len(shards) + 1) // 2
    edge = jax.ShapeDtypeStruct((rows, 2 * heads_width), BF16)
    return pl.pallas_call(
        project_kernel,
        out_shape=(
            jax.ShapeDtypeStruct((blocks * rows, heads_width), BF16),
            jax.ShapeDtypeStruct((blocks * rows, 2 * heads_width), BF16),
            edge,
            edge,
        ),
        in_specs=[SMEM, VMEM] + [ANY] * len(shards),
        out_specs=(VMEM,) * 4,
        scratch_shapes=[pltpu.VMEM((blocks * rows, width), BF16), pltpu.SemaphoreType.DMA((len(shards),))],
        compiler_params=pltpu.CompilerParams(vmem_limit_bytes=VMEM_LIMIT),
        cost_estimate=SHORT,
        name="project",
    )(place, weight, *shards)


def window_bias(first, count, starts, ends):
    reach = WIN // 2
    query = first + lax.broadcasted_iota(jnp.int32, (count, 1), 0)
    low = jnp.max(jnp.where(starts <= query, starts, 0), axis=1, keepdims=True)
    high = jnp.min(jnp.where(ends > query, ends, 1 << 30), axis=1, keepdims=True)
    low = jnp.maximum(low, query - reach)
    high = jnp.minimum(high, query + reach + 1)
    key = first - count + lax.broadcasted_iota(jnp.int32, (count, 3 * count), 1)
    return jnp.where((key >= low) & (key < high), 0.0, NEG_FILL)


def attend(query, keyval_ref, bias_ref, scores_ref, weights_ref, out_ref):
    count, width = query.shape
    lane = lax.broadcasted_iota(jnp.int32, (count, 2 * HD), 1)
    for start in range(0, width, 2 * HD):
        values = keyval_ref[:, width + start : width + start + 2 * HD]
        halves = []
        for side in range(2):
            head = start // HD + side
            inside = (lane < HD) if side == 0 else (lane >= HD)
            only = jnp.where(inside, query[:, start : start + 2 * HD], jnp.zeros((), BF16))
            scores_ref[head] = lax.dot_general(
                only, keyval_ref[:, start : start + 2 * HD], (((1,), (1,)), ((), ())), preferred_element_type=F32
            )
            totals = []
            for row in range(0, count, STRIP):
                at = slice(row, row + STRIP)
                scores = scores_ref[head, at] + bias_ref[at]
                weights = jnp.exp(scores - jnp.max(scores, axis=1, keepdims=True))
                totals.append(jnp.sum(weights, axis=1, keepdims=True))
                weights_ref[head, at] = weights.astype(BF16)
            summed = jnp.dot(weights_ref[head], values, preferred_element_type=F32)
            halves.append(summed / jnp.concatenate(totals, axis=0))
        out_ref[:, start : start + 2 * HD] = jnp.where(lane < HD, halves[0], halves[1]).astype(BF16)


def attend_kernel(flips, place_ref, starts_ref, ends_ref, query_ref, before_ref, keyval_ref, behind_ref, *refs):
    outs = refs[: len(flips)]
    window_ref, bias_ref, scores_ref, weights_ref, sems = refs[len(flips) :]
    tok, kv = place_ref[0], place_ref[1]
    count = outs[0].shape[0]
    blocks = query_ref.shape[0] // count
    copies = []
    for index, flip in enumerate(flips):
        block = kv ^ flip
        for part in range(3):
            target = window_ref.at[index, part * count : (part + 1) * count]
            sem = sems.at[index, part]
            at = block + part - 1
            inner = (at >= 0) & (at < blocks)
            safe = jnp.where(inner, at, 0)
            source = keyval_ref.at[pl.ds(pl.multiple_of(safe * count, count), count)]
            copies.append((index, inner, pltpu.make_async_copy(source, target, sem)))
            if part == 0:
                copies.append((index, at < 0, pltpu.make_async_copy(before_ref, target, sem)))
            if part == 2:
                copies.append((index, at >= blocks, pltpu.make_async_copy(behind_ref, target, sem)))
    for _, needed, copy in copies:
        pl.when(needed)(copy.start)
    for index, flip in enumerate(flips):
        block = kv ^ flip
        first = (tok * blocks + block) * count
        bias_ref[...] = window_bias(first, count, starts_ref[...], ends_ref[...])
        for owner, needed, copy in copies:
            if owner == index:
                pl.when(needed)(copy.wait)
        query = query_ref[pl.ds(pl.multiple_of(block * count, count), count)]
        attend(query, window_ref.at[index], bias_ref, scores_ref, weights_ref, outs[index])


def attend_blocks(place, starts, ends, query, before, keyval, behind, rows, flips, name):
    heads_width = query.shape[1]
    return pl.pallas_call(
        functools.partial(attend_kernel, flips),
        out_shape=tuple(jax.ShapeDtypeStruct((rows, heads_width), BF16) for _ in flips),
        in_specs=[SMEM, VMEM, VMEM, VMEM, ANY, ANY, ANY],
        out_specs=(VMEM,) * len(flips),
        scratch_shapes=[
            pltpu.VMEM((len(flips), 3 * rows, 2 * heads_width), BF16),
            pltpu.VMEM((rows, 3 * rows), F32),
            pltpu.VMEM((heads_width // HD, rows, 3 * rows), F32),
            pltpu.VMEM((heads_width // HD, rows, 3 * rows), BF16),
            pltpu.SemaphoreType.DMA((len(flips), 3)),
        ],
        compiler_params=pltpu.CompilerParams(vmem_limit_bytes=VMEM_LIMIT),
        cost_estimate=SHORT,
        name=name,
    )(place, starts, ends, query, before, keyval, behind)


def first_norm_kernel(layout, place_ref, hidden_ref, own_out_ref, gain_ref, bias_ref, *refs):
    parts, pieces = refs[: -5 - len(layout)], refs[-5 - len(layout) : -5]
    normed_ref, all_ref, weight_ref, mixed_ref, sems = refs[-5:]
    tok = place_ref[0]
    quarters, heads_width, width = weight_ref.shape
    copies = [pltpu.make_async_copy(own_out_ref, weight_ref.at[0], sems.at[0])]
    for flips, piece in zip(layout, pieces):
        for index, flip in enumerate(flips):
            depth = piece.shape[2]
            at = pl.multiple_of((tok ^ flip) * depth, depth)
            target = weight_ref.at[1:quarters, pl.ds(at, depth)]
            copies.append(pltpu.make_async_copy(piece.at[index], target, sems.at[len(copies)]))
    for copy in copies:
        copy.start()
    for flip, part_ref in enumerate(parts):
        all_ref[:, flip * heads_width : (flip + 1) * heads_width] = part_ref[...]
    for copy in copies:
        copy.wait()
    weight = weight_ref[...].reshape(quarters * heads_width, width)
    mixed_ref[...] = jnp.dot(all_ref[...], weight, preferred_element_type=F32)
    for row in range(0, hidden_ref.shape[0], STRIP):
        at = slice(row, row + STRIP)
        mixed = hidden_ref[at].astype(F32) + mixed_ref[at]
        normed_ref[at] = normalized(mixed, gain_ref[...], bias_ref[...]).astype(BF16)


def first_norm(place, hidden, own_out, gain, bias, parts, pieces):
    rows, width = hidden.shape
    heads_width = own_out.shape[0]
    layout = tuple(flips for flips, _ in pieces)
    return pl.pallas_call(
        functools.partial(first_norm_kernel, layout),
        out_shape=jax.ShapeDtypeStruct((rows, width), BF16),
        in_specs=[SMEM, VMEM, ANY, VMEM, VMEM] + [VMEM] * len(parts) + [ANY] * len(pieces),
        out_specs=VMEM,
        scratch_shapes=[
            pltpu.VMEM((rows, width), BF16),
            pltpu.VMEM((len(parts), heads_width, width), BF16),
            pltpu.VMEM((rows, width), F32),
            pltpu.SemaphoreType.DMA((1 + sum(len(flips) for flips in layout),)),
        ],
        compiler_params=pltpu.CompilerParams(vmem_limit_bytes=VMEM_LIMIT),
        cost_estimate=SHORT,
        name="first_norm",
    )(place, hidden, own_out, gain, bias, *parts, *[value for _, value in pieces])


def gelu(values):
    return 0.5 * values * (1.0 + lax.erf(values * math.sqrt(0.5)))


def feed_kernel(layout, *refs):
    count = len(layout)
    place_ref, rows_ref, up_near_ref, down_near_ref = refs[:4]
    pieces = refs[4 : 4 + count]
    sum_ref, up_ref, down_ref, wide_ref, units_ref, total_ref, near_sems, sems = refs[4 + count :]
    tok = place_ref[0]
    block = 128
    chunk = wide_ref.shape[2]
    chunks = up_ref.shape[2] // chunk
    near = []
    for index in range(chunks):
        at = slice(index * chunk, (index + 1) * chunk)
        near.append(
            (
                pltpu.make_async_copy(up_near_ref.at[:, at], up_ref.at[0, :, at], near_sems.at[0, index]),
                pltpu.make_async_copy(down_near_ref.at[at], down_ref.at[0, at], near_sems.at[1, index]),
            )
        )
    far = []
    for (flip, part), piece in zip(layout, pieces):
        at = pl.ds(pl.multiple_of((tok ^ flip) * block, block), block)
        if part in (None, 0):
            far.append(pltpu.make_async_copy(piece.at[0:block], up_ref.at[1, at], sems.at[len(far)]))
        if part in (None, 1):
            shift = block if part is None else 0
            far.append(pltpu.make_async_copy(piece.at[shift : shift + block], down_ref.at[1, at], sems.at[len(far)]))
    for pair in near:
        for copy in pair:
            copy.start()
    for copy in far:
        copy.start()
    rows = rows_ref[...]
    for side in range(2):
        for index in range(chunks):
            at = slice(index * chunk, (index + 1) * chunk)
            slot = index % 2
            if side == 0:
                near[index][0].wait()
            elif index == 0:
                for copy in far:
                    copy.wait()
            wide_ref[slot] = jnp.dot(rows, up_ref[side, :, at], preferred_element_type=F32)
            for row in range(0, rows.shape[0], STRIP):
                strip = slice(row, row + STRIP)
                units_ref[slot, strip] = gelu(wide_ref[slot, strip]).astype(BF16)
            if side == 0:
                near[index][1].wait()
            product = jnp.dot(units_ref[slot], down_ref[side, at], preferred_element_type=F32)
            if side == 0 and index == 0:
                total_ref[...] = product
            elif side == 1 and index == chunks - 1:
                sum_ref[...] = (total_ref[...] + product).astype(sum_ref.dtype)
            else:
                total_ref[...] += product


def feed(place, rows, up_weight, down_weight, pieces, dtype, name):
    count, width = rows.shape
    units = up_weight.shape[1]
    chunk = 512
    layout = tuple((flip, part) for flip, part, _ in pieces)
    copies = sum(2 if part is None else 1 for _, part in layout)
    return pl.pallas_call(
        functools.partial(feed_kernel, layout),
        out_shape=jax.ShapeDtypeStruct((count, width), dtype),
        in_specs=[SMEM, VMEM, ANY, ANY] + [ANY] * len(pieces),
        out_specs=VMEM,
        scratch_shapes=[
            pltpu.VMEM((2, width, units), BF16),
            pltpu.VMEM((2, units, width), BF16),
            pltpu.VMEM((2, count, chunk), F32),
            pltpu.VMEM((2, count, chunk), BF16),
            pltpu.VMEM((count, width), F32),
            pltpu.SemaphoreType.DMA((2, units // chunk)),
            pltpu.SemaphoreType.DMA((copies,)),
        ],
        compiler_params=pltpu.CompilerParams(vmem_limit_bytes=VMEM_LIMIT),
        cost_estimate=SHORT,
        name=name,
    )(place, rows, up_weight, down_weight, *[value for _, _, value in pieces])


def finish_kernel(normed_ref, near_ref, far_ref, gain_ref, bias_ref, out_ref):
    for row in range(0, normed_ref.shape[0], STRIP):
        at = slice(row, row + STRIP)
        mixed = normed_ref[at].astype(F32) + near_ref[at] + far_ref[at].astype(F32)
        out_ref[at] = normalized(mixed, gain_ref[...], bias_ref[...]).astype(out_ref.dtype)


def finish(normed, near, far, gain, bias):
    return pl.pallas_call(
        finish_kernel,
        out_shape=jax.ShapeDtypeStruct(normed.shape, BF16),
        in_specs=[VMEM] * 5,
        out_specs=VMEM,
        compiler_params=pltpu.CompilerParams(vmem_limit_bytes=VMEM_LIMIT),
        name="finish",
    )(normed, near, far, gain, bias)


def decode_kernel(slot_ref, filled_ref, query_ref, cache_ref, out_ref, high_ref, total_ref, sum_ref):
    step = pl.program_id(0)

    @pl.when(step == 0)
    def _():
        high_ref[...] = jnp.full(high_ref.shape, NEG_FILL, F32)
        total_ref[...] = jnp.zeros_like(total_ref)
        sum_ref[...] = jnp.zeros_like(sum_ref)

    row = slot_ref[step]
    filled = filled_ref[step]
    width = query_ref.shape[1]
    head = lax.broadcasted_iota(jnp.int32, (H, width), 0)
    inside = head == lax.broadcasted_iota(jnp.int32, (H, width), 1) // HD
    query = jnp.where(inside, query_ref[pl.ds(row, 1), :], 0.0).astype(BF16)
    scores = lax.dot_general(query, cache_ref[0, 0, 0], (((1,), (1,)), ((), ())), preferred_element_type=F32)
    live = lax.broadcasted_iota(jnp.int32, scores.shape, 1) < filled
    scores = jnp.where(live, scores * (1.0 / math.sqrt(HD)), NEG_FILL)
    high = jnp.max(scores, axis=1, keepdims=True)
    weights = jnp.where(live, jnp.exp(scores - high), 0.0)
    total = jnp.sum(weights, axis=1, keepdims=True)
    summed = jnp.dot(weights.astype(BF16), cache_ref[1, 0, 0], preferred_element_type=F32)
    along = lambda column: jnp.sum(jnp.where(inside, column, 0.0), axis=0, keepdims=True)
    high, total, summed = along(high), along(total), along(summed)
    used = filled > 0
    at = pl.ds(row, 1)
    old = high_ref[at, :]
    new = jnp.where(used, jnp.maximum(old, high), old)
    left = jnp.exp(old - new)
    right = jnp.where(used, jnp.exp(high - new), 0.0)
    high_ref[at, :] = new
    total_ref[at, :] = total_ref[at, :] * left + total * right
    sum_ref[at, :] = sum_ref[at, :] * left + summed * right

    @pl.when(step == pl.num_programs(0) - 1)
    def _():
        out_ref[0] = high_ref[...]
        out_ref[1] = total_ref[...]
        out_ref[2] = sum_ref[...]


def decode(slots, filled, queries, kv_cache):
    requests, width = queries.shape
    pieces = kv_cache.shape[2]
    state = pltpu.VMEM((requests, width), F32)
    return pl.pallas_call(
        decode_kernel,
        grid=(pieces,),
        out_shape=jax.ShapeDtypeStruct((3, requests, width), F32),
        in_specs=[
            SMEM,
            SMEM,
            pl.BlockSpec((requests, width), lambda i: (0, 0)),
            pl.BlockSpec((2, 1, 1, PLEN, width), lambda i: (0, 0, i, 0, 0)),
        ],
        out_specs=pl.BlockSpec((3, requests, width), lambda i: (0, 0, 0)),
        scratch_shapes=[state, state, state],
        compiler_params=pltpu.CompilerParams(vmem_limit_bytes=VMEM_LIMIT),
        cost_estimate=SHORT,
        name="decode",
    )(slots, filled, queries, kv_cache)


def gathered_queries(dec_query):
    flips = range(1, lax.axis_size("kv"))
    return [dec_query] + [swapped(dec_query, "kv", flip) for flip in flips]


def decode_partial(queries, kv_cache, piece_req, piece_used):
    own = queries[0].shape[0]
    owners = piece_req[0]
    slots = ((owners // own) ^ lax.axis_index("kv")) * own + owners % own
    return decode(slots, piece_used[0], jnp.concatenate(queries).astype(F32), kv_cache)


def exchanged_partials(partial, own):
    parts = [partial[:, :own]]
    for flip in range(1, lax.axis_size("kv")):
        parts.append(swapped(partial[:, flip * own : (flip + 1) * own], "kv", flip))
    return parts


def merged_partials(parts):
    high = functools.reduce(jnp.maximum, [part[0] for part in parts])
    factors = [jnp.exp(part[0] - high) for part in parts]
    total = sum(part[1] * factor for part, factor in zip(parts, factors))
    summed = sum(part[2] * factor for part, factor in zip(parts, factors))
    return (summed / total).astype(BF16)


def routed_body(
    hidden_in,
    qkv_weight,
    stretch_len,
    out_weight,
    ln1_gain,
    ln1_bias,
    up_weight,
    down_weight,
    ln2_gain,
    ln2_bias,
    dec_query,
    kv_cache,
    piece_req,
    piece_used,
):
    tok = lax.axis_index("tok")
    kv = lax.axis_index("kv")
    toks, kvs = lax.axis_size("tok"), lax.axis_size("kv")
    rows, width = hidden_in.shape
    place = jnp.stack([tok, kv]).astype(jnp.int32)
    eighth = lambda value: lax.dynamic_slice_in_dim(value, tok * (value.shape[0] // toks), value.shape[0] // toks, 0)

    queries = gathered_queries(dec_query)
    partial = decode_partial(queries, kv_cache, piece_req, piece_used)
    from_below, from_above = [], []
    rising = falling = hidden_in
    for step in range(1, kvs):
        links = range(step - 1, kvs - 1)
        rising = lax.ppermute(rising, "kv", [(i, i + 1) for i in links])
        falling = lax.ppermute(falling, "kv", [(kvs - 1 - i, kvs - 2 - i) for i in links])
        from_below.append(rising)
        from_above.append(falling)
        if step == 1:
            out_part = after(eighth(out_weight), rising, falling)
            out_here = jnp.stack([swapped(out_part, "kv", flip) for flip in range(1, kvs)])
        if step == 2:
            rising, falling = after(rising, partial, out_here), after(falling, partial, out_here)
    out_x, out_y = swapped(out_here, "tok", 2), swapped(out_here, "tok", 4)
    out_far = swapped(after(out_y, rising), "tok", 2)

    feed_part = jnp.concatenate([eighth(up_weight), eighth(down_weight)], axis=0)
    feed_here = swapped(after(feed_part, from_below[1], from_above[1]), "kv", 2)

    order = jnp.arange(stretch_len.shape[0])
    ends = jnp.sum(jnp.where(order[:, None] <= order[None, :], stretch_len[:, None], 0), axis=0, dtype=jnp.int32)
    starts = (ends - stretch_len)[None, :]
    ends = ends[None, :]

    shards = [hidden_in] + from_below + from_above
    query, keyval, top, bottom = project(place, jnp.transpose(qkv_weight, (1, 0, 2)), shards)
    before = lax.ppermute(bottom, "tok", [(i, i + 1) for i in range(toks - 1)])
    behind = lax.ppermute(top, "tok", [(i + 1, i) for i in range(toks - 1)])
    window = (place, starts, ends, query, before, keyval, behind, rows)
    parts = [None] * kvs
    parts[3], parts[2] = attend_blocks(*window, (3, 2), "attend_far")
    out_all = jnp.stack([out_here, out_x, out_y, after(out_far, parts[3])])
    out_core = swapped(out_all, "tok", 1)
    feed_here = after(feed_here, parts[3], parts[2])
    parts[3], parts[2] = swapped(parts[3], "kv", 3), swapped(parts[2], "kv", 2)
    feed_x, feed_y = swapped(feed_here, "tok", 2), swapped(feed_here, "tok", 4)
    window = (place, starts, ends, after(query, feed_here), before, keyval, behind, rows)
    parts[1], parts[0] = attend_blocks(*window, (1, 0), "attend_near")
    half = feed_here.shape[0] // 2
    far_up = swapped(after(feed_y, parts[0])[:half], "tok", 2)
    far_down = swapped(after(feed_x, parts[0])[half:], "tok", 4)
    parts[1] = swapped(parts[1], "kv", 1)
    out_pieces = [((0, 2, 4, 6), out_all), ((1, 3, 5, 7), out_core)]
    normed = first_norm(place, hidden_in, out_weight, ln1_gain[None, :], ln1_bias[None, :], parts, out_pieces)

    partner = swapped(normed, "kv", 1)
    held = [(0, None, feed_here), (2, None, feed_x), (4, None, feed_y), (6, 0, far_up), (6, 1, far_down)]
    feed_pieces = held + [(flip ^ 1, part, swapped(after(value, normed), "tok", 1)) for flip, part, value in held]
    dec_out = merged_partials(exchanged_partials(after(partial, normed), dec_query.shape[0]))
    partner = after(partner, dec_out)
    away = feed(place, partner, up_weight, down_weight, feed_pieces, BF16, "feed_partner")
    arrived = swapped(away, "kv", 1)
    mine = feed(place, after(normed, away), up_weight, down_weight, feed_pieces, F32, "feed_own")
    prefill_out = finish(normed, mine, arrived, ln2_gain[None, :], ln2_bias[None, :])

    return prefill_out, dec_out


def extended(value, sides, width):
    for axis, dim in sides:
        count, length = (lax.axis_size(axis), value.shape[dim])
        up = [(i, (i + 1) % count) for i in range(count - 1)]
        down = [(j, i) for i, j in up]
        last = lax.slice_in_dim(value, length - width, length, axis=dim)
        leading = lax.slice_in_dim(value, 0, width, axis=dim)
        before = lax.ppermute(last, axis, up)
        after = lax.ppermute(leading, axis, down)
        value = jnp.concatenate([before, value, after], axis=dim)
    return value


def merged(value, axis, join):
    pieces = jax.tree.map(lambda part: lax.all_gather(part, axis), value)
    head = jax.tree.map(lambda part: part[0], pieces)
    tail = jax.tree.map(lambda part: part[1:], pieces)
    subtotal, _ = lax.scan(lambda subtotal, section: (join(subtotal, section), None), head, tail)
    return subtotal


def segment_ids(row_ids, stretch_len):
    stretch_ends = jnp.cumsum(stretch_len)
    return jnp.sum((row_ids[:, None] >= stretch_ends[None, :]).astype(jnp.int32), axis=1)


def layer_norm(values, gain, bias):
    center = values - jnp.mean(values, axis=1, keepdims=True)
    spread = jnp.mean(center * center, axis=1, keepdims=True)
    return center * lax.rsqrt(spread + LN_EPS) * gain + bias


def merge_partials(earlier, later):
    highest = jnp.maximum(earlier[0], later[0])
    left_factor = jnp.exp(earlier[0] - highest)
    right_factor = jnp.exp(later[0] - highest)
    totals = earlier[1] * left_factor + later[1] * right_factor
    weighted = earlier[2] * left_factor[..., None] + later[2] * right_factor[..., None]
    return (highest, totals, weighted)


def row_folder(source, shard_rows):
    return jnp.dot(source, shard_rows, preferred_element_type=jnp.float32)


def general_body(
    hidden_in,
    qkv_weight,
    stretch_len,
    out_weight,
    ln1_gain,
    ln1_bias,
    up_weight,
    down_weight,
    ln2_gain,
    ln2_bias,
    dec_query,
    kv_cache,
    piece_req,
    piece_used,
):
    inv_scale = 1.0 / math.sqrt(HD)
    reach = WIN // 2
    local_width = qkv_weight.shape[2]
    head_count = local_width // HD
    flat_weight = qkv_weight.reshape(qkv_weight.shape[0], 3 * local_width)
    qkv_rows = jnp.dot(
        lax.all_gather(hidden_in, "kv", axis=0, tiled=True),
        flat_weight,
        preferred_element_type=jnp.float32,
    ).astype(jnp.bfloat16)
    row_count = qkv_rows.shape[0]
    query_rows = qkv_rows[:, :local_width]
    keyval_rows = qkv_rows[:, local_width:]
    padded = extended(keyval_rows, (("tok", 0),), reach)
    first_row = lax.axis_index("tok") * row_count
    total_rows = row_count * lax.axis_size("tok")
    qblock = min(512, row_count)
    span = qblock + 2 * reach
    block_count = row_count // qblock

    def attend(block_index):
        start = block_index * qblock
        query_ids = first_row + start + jnp.arange(qblock, dtype=jnp.int32)
        key_ids = first_row + start - reach + jnp.arange(span, dtype=jnp.int32)
        query_seg = segment_ids(query_ids, stretch_len)
        inside = (key_ids >= 0) & (key_ids < total_rows)
        key_seg = jnp.where(inside, segment_ids(key_ids, stretch_len), -1)
        allowed = (key_seg[None, :] == query_seg[:, None]) & (
            jnp.abs(key_ids[None, :] - query_ids[:, None]) <= reach
        )
        queries = lax.dynamic_slice_in_dim(query_rows, start, qblock, 0).reshape(
            qblock, head_count, HD
        )
        both = lax.dynamic_slice_in_dim(padded, start, span, 0)
        key_rows = both[:, :local_width].reshape(span, head_count, HD)
        value_rows = both[:, local_width:].reshape(span, head_count, HD)
        scores = (
            jnp.einsum("ihd,jhd->hij", queries, key_rows, preferred_element_type=jnp.float32)
            * inv_scale
        )
        scores = jnp.where(allowed[None], scores, NEG_FILL)
        row_max = jnp.max(scores, axis=2, keepdims=True)
        weights = jnp.where(allowed[None], jnp.exp(scores - row_max), 0.0)
        totals = jnp.sum(weights, axis=2)
        summed = jnp.einsum(
            "hij,jhd->ihd",
            weights.astype(jnp.bfloat16),
            value_rows,
            preferred_element_type=jnp.float32,
        )
        return (
            (summed / jnp.transpose(totals)[:, :, None])
            .astype(jnp.bfloat16)
            .reshape(qblock, local_width)
        )

    attention = lax.map(attend, jnp.arange(block_count, dtype=jnp.int32)).reshape(
        row_count, local_width
    )
    token_major = lax.all_to_all(attention, "kv", split_axis=0, concat_axis=1, tiled=True)
    projected = row_folder(token_major, lax.all_gather(out_weight, "kv", axis=0, tiled=True))
    normed = layer_norm(hidden_in.astype(jnp.float32) + projected, ln1_gain, ln1_bias).astype(
        jnp.bfloat16
    )
    units = jax.nn.gelu(
        jnp.dot(
            lax.all_gather(normed, "kv", axis=0, tiled=True),
            up_weight,
            preferred_element_type=jnp.float32,
        ),
        approximate=False,
    ).astype(jnp.bfloat16)
    ffn = lax.psum_scatter(
        jnp.dot(units, down_weight, preferred_element_type=jnp.float32).astype(jnp.bfloat16),
        "kv",
        scatter_dimension=0,
        tiled=True,
    ).astype(jnp.float32)
    prefill_out = layer_norm(normed.astype(jnp.float32) + ffn, ln2_gain, ln2_bias).astype(
        jnp.bfloat16
    )
    group_queries = lax.all_gather(dec_query, "kv", axis=0, tiled=True)
    request_count = group_queries.shape[0]
    owners = piece_req[0]
    filled = piece_used[0]
    slot_count = owners.shape[0]
    request_ids = jnp.arange(request_count, dtype=jnp.int32)
    selector = (owners[:, None] == request_ids[None, :]).astype(jnp.bfloat16)
    chosen = jnp.dot(selector, group_queries, preferred_element_type=jnp.float32).astype(
        jnp.bfloat16
    )
    chosen = chosen.reshape(slot_count, H, HD)
    cache_keys = kv_cache[0, 0].reshape(slot_count, PLEN, H, HD)
    cache_values = kv_cache[1, 0].reshape(slot_count, PLEN, H, HD)
    piece_scores = (
        jnp.einsum("phd,pthd->pht", chosen, cache_keys, preferred_element_type=jnp.float32)
        * inv_scale
    )
    active = jnp.arange(PLEN, dtype=jnp.int32)[None, :] < filled[:, None]
    piece_scores = jnp.where(active[:, None, :], piece_scores, NEG_FILL)
    piece_max = jnp.max(piece_scores, axis=2)
    piece_weights = jnp.where(
        active[:, None, :], jnp.exp(piece_scores - piece_max[:, :, None]), 0.0
    )
    piece_totals = jnp.sum(piece_weights, axis=2)
    partial_value = jnp.einsum(
        "pht,pthd->phd",
        piece_weights.astype(jnp.bfloat16),
        cache_values,
        preferred_element_type=jnp.float32,
    )
    member = (owners[None, :] == request_ids[:, None]) & (filled[None, :] > 0)
    highest = jnp.max(jnp.where(member[:, :, None], piece_max[None], NEG_FILL), axis=1)
    factor = jnp.where(member[:, :, None], jnp.exp(piece_max[None] - highest[:, None, :]), 0.0)
    denom = jnp.sum(factor * piece_totals[None], axis=1)
    weighted = jnp.einsum("rph,phd->rhd", factor, partial_value)
    own_requests = dec_query.shape[0]
    joined = merged((highest, denom, weighted), "kv", merge_partials)
    begin = lax.axis_index("kv") * own_requests
    final_denom = lax.dynamic_slice_in_dim(joined[1], begin, own_requests, 0)
    final_weighted = lax.dynamic_slice_in_dim(joined[2], begin, own_requests, 0)
    dec_out = (
        (final_weighted / final_denom[:, :, None])
        .astype(jnp.bfloat16)
        .reshape(own_requests, H * HD)
    )
    return (prefill_out, dec_out)


def solution(mesh):
    placed = (
        P(("tok", "kv"), None),
        P(None, None, "kv"),
        P(),
        P("kv", None),
        P(),
        P(),
        P(None, "kv"),
        P("kv", None),
        P(),
        P(),
        P(("tok", "kv"), None),
        P(None, "tok", "kv", None, None),
        P("tok", "kv"),
        P("tok", "kv"),
    )
    routed = mesh.shape["tok"] == 8 and mesh.shape["kv"] == 4
    return jax.shard_map(
        routed_body if routed else general_body,
        mesh=mesh,
        in_specs=placed,
        out_specs=(P(("tok", "kv"), None), P(("tok", "kv"), None)),
        check_vma=False,
    )
```

```python
import functools
import math

import jax
import jax.numpy as jnp
from jax import lax
from jax.experimental import pallas as pl
from jax.experimental.pallas import tpu as pltpu
from jax.sharding import PartitionSpec as P

H = 16
HD = 64
WIN = 512
PLEN = 128


NEG_FILL = -1e30
LN_EPS = 1e-05
BF16 = jnp.bfloat16
F32 = jnp.float32
STRIP = 32
MIB = 1024 * 1024
ANY = pl.BlockSpec(memory_space=pl.ANY)
VMEM = pl.BlockSpec(memory_space=pltpu.VMEM)
SMEM = pl.BlockSpec(memory_space=pltpu.SMEM)
SHORT = pl.CostEstimate(flops=1, bytes_accessed=1, transcendentals=0)


def swapped(value, axis, flip):
    count = lax.axis_size(axis)
    return lax.ppermute(value, axis, [(i, i ^ flip) for i in range(count)])


def after(value, *earlier):
    return lax.optimization_barrier((value,) + earlier)[0]


def normalized(values, gain, bias):
    center = values - jnp.mean(values, axis=1, keepdims=True)
    spread = jnp.mean(center * center, axis=1, keepdims=True)
    return center * lax.rsqrt(spread + LN_EPS) * gain + bias


def project_kernel(place_ref, weight_ref, *refs):
    shards, (query_ref, keyval_ref, top_ref, bottom_ref, rows_ref, sems) = refs[:-6], refs[-6:]
    kv = place_ref[1]
    count = shards[0].shape[0]
    steps = (len(shards) - 1) // 2
    width = weight_ref.shape[2]
    moves = [(shards[0], kv, None)]
    for step in range(1, steps + 1):
        moves.append((shards[step], kv - step, kv >= step))
        moves.append((shards[steps + step], kv + step, kv + step <= steps))

    def guarded(needed, act):
        if needed is None:
            act()
        else:
            pl.when(needed)(act)

    copies = []
    for index, (source, owner, needed) in enumerate(moves):
        safe = owner if needed is None else jnp.where(needed, owner, 0)
        at = pl.ds(pl.multiple_of(safe * count, count), count)
        copies.append((needed, pltpu.make_async_copy(source, rows_ref.at[at], sems.at[index])))
    for needed, copy in copies:
        guarded(needed, copy.start)
    for needed, copy in copies:
        guarded(needed, copy.wait)
    rows = rows_ref[...]
    query = jnp.dot(rows, weight_ref[0], preferred_element_type=F32) * (1.0 / math.sqrt(HD))
    query_ref[...] = query.astype(BF16)
    for part in range(2):
        at = slice(part * width, (part + 1) * width)
        keyval_ref[:, at] = jnp.dot(rows, weight_ref[part + 1], preferred_element_type=F32).astype(BF16)
    top_ref[...] = keyval_ref[:count]
    bottom_ref[...] = keyval_ref[steps * count :]


def project(place, weight, shards):
    rows, width = shards[0].shape
    heads_width = weight.shape[2]
    blocks = (len(shards) + 1) // 2
    edge = jax.ShapeDtypeStruct((rows, 2 * heads_width), BF16)
    return pl.pallas_call(
        project_kernel,
        out_shape=(
            jax.ShapeDtypeStruct((blocks * rows, heads_width), BF16),
            jax.ShapeDtypeStruct((blocks * rows, 2 * heads_width), BF16),
            edge,
            edge,
        ),
        in_specs=[SMEM, VMEM] + [ANY] * len(shards),
        out_specs=(VMEM,) * 4,
        scratch_shapes=[pltpu.VMEM((blocks * rows, width), BF16), pltpu.SemaphoreType.DMA((len(shards),))],
        compiler_params=pltpu.CompilerParams(vmem_limit_bytes=14 * MIB),
        cost_estimate=SHORT,
        name="project",
    )(place, weight, *shards)


def window_bias(first, count, starts, ends):
    reach = WIN // 2
    query = first + lax.broadcasted_iota(jnp.int32, (count, 1), 0)
    low = jnp.max(jnp.where(starts <= query, starts, 0), axis=1, keepdims=True)
    high = jnp.min(jnp.where(ends > query, ends, 1 << 30), axis=1, keepdims=True)
    low = jnp.maximum(low, query - reach)
    high = jnp.minimum(high, query + reach + 1)
    key = first - count + lax.broadcasted_iota(jnp.int32, (count, 3 * count), 1)
    return jnp.where((key >= low) & (key < high), 0.0, NEG_FILL)


def attend(query, keyval_ref, bias_ref, scores_ref, weights_ref, out_ref):
    count, width = query.shape
    lane = lax.broadcasted_iota(jnp.int32, (count, 2 * HD), 1)
    for start in range(0, width, 2 * HD):
        values = keyval_ref[:, width + start : width + start + 2 * HD]
        halves = []
        for side in range(2):
            head = start // HD + side
            inside = (lane < HD) if side == 0 else (lane >= HD)
            only = jnp.where(inside, query[:, start : start + 2 * HD], jnp.zeros((), BF16))
            scores_ref[head] = lax.dot_general(
                only, keyval_ref[:, start : start + 2 * HD], (((1,), (1,)), ((), ())), preferred_element_type=F32
            )
            totals = []
            for row in range(0, count, STRIP):
                at = slice(row, row + STRIP)
                scores = scores_ref[head, at] + bias_ref[at]
                weights = jnp.exp(scores - jnp.max(scores, axis=1, keepdims=True))
                totals.append(jnp.sum(weights, axis=1, keepdims=True))
                weights_ref[head, at] = weights.astype(BF16)
            summed = jnp.dot(weights_ref[head], values, preferred_element_type=F32)
            halves.append(summed / jnp.concatenate(totals, axis=0))
        out_ref[:, start : start + 2 * HD] = jnp.where(lane < HD, halves[0], halves[1]).astype(BF16)


def attend_kernel(flips, place_ref, starts_ref, ends_ref, query_ref, before_ref, keyval_ref, behind_ref, *refs):
    outs = refs[: len(flips)]
    window_ref, bias_ref, scores_ref, weights_ref, sems = refs[len(flips) :]
    tok, kv = place_ref[0], place_ref[1]
    count = outs[0].shape[0]
    blocks = query_ref.shape[0] // count
    copies = []
    for index, flip in enumerate(flips):
        block = kv ^ flip
        for part in range(3):
            target = window_ref.at[index, part * count : (part + 1) * count]
            sem = sems.at[index, part]
            at = block + part - 1
            inner = (at >= 0) & (at < blocks)
            safe = jnp.where(inner, at, 0)
            source = keyval_ref.at[pl.ds(pl.multiple_of(safe * count, count), count)]
            copies.append((index, inner, pltpu.make_async_copy(source, target, sem)))
            if part == 0:
                copies.append((index, at < 0, pltpu.make_async_copy(before_ref, target, sem)))
            if part == 2:
                copies.append((index, at >= blocks, pltpu.make_async_copy(behind_ref, target, sem)))
    for _, needed, copy in copies:
        pl.when(needed)(copy.start)
    for index, flip in enumerate(flips):
        block = kv ^ flip
        first = (tok * blocks + block) * count
        bias_ref[...] = window_bias(first, count, starts_ref[...], ends_ref[...])
        for owner, needed, copy in copies:
            if owner == index:
                pl.when(needed)(copy.wait)
        query = query_ref[pl.ds(pl.multiple_of(block * count, count), count)]
        attend(query, window_ref.at[index], bias_ref, scores_ref, weights_ref, outs[index])


def attend_blocks(place, starts, ends, query, before, keyval, behind, rows, flips, name):
    heads_width = query.shape[1]
    return pl.pallas_call(
        functools.partial(attend_kernel, flips),
        out_shape=tuple(jax.ShapeDtypeStruct((rows, heads_width), BF16) for _ in flips),
        in_specs=[SMEM, VMEM, VMEM, VMEM, ANY, ANY, ANY],
        out_specs=(VMEM,) * len(flips),
        scratch_shapes=[
            pltpu.VMEM((len(flips), 3 * rows, 2 * heads_width), BF16),
            pltpu.VMEM((rows, 3 * rows), F32),
            pltpu.VMEM((heads_width // HD, rows, 3 * rows), F32),
            pltpu.VMEM((heads_width // HD, rows, 3 * rows), BF16),
            pltpu.SemaphoreType.DMA((len(flips), 3)),
        ],
        compiler_params=pltpu.CompilerParams(vmem_limit_bytes=14 * MIB),
        cost_estimate=SHORT,
        name=name,
    )(place, starts, ends, query, before, keyval, behind)


def first_norm_kernel(layout, place_ref, hidden_ref, own_out_ref, gain_ref, bias_ref, *refs):
    parts, pieces = refs[: -5 - len(layout)], refs[-5 - len(layout) : -5]
    normed_ref, all_ref, weight_ref, mixed_ref, sems = refs[-5:]
    tok = place_ref[0]
    quarters, heads_width, width = weight_ref.shape
    copies = [pltpu.make_async_copy(own_out_ref, weight_ref.at[0], sems.at[0])]
    for flips, piece in zip(layout, pieces):
        for index, flip in enumerate(flips):
            depth = piece.shape[2]
            at = pl.multiple_of((tok ^ flip) * depth, depth)
            target = weight_ref.at[1:quarters, pl.ds(at, depth)]
            copies.append(pltpu.make_async_copy(piece.at[index], target, sems.at[len(copies)]))
    for copy in copies:
        copy.start()
    for flip, part_ref in enumerate(parts):
        all_ref[:, flip * heads_width : (flip + 1) * heads_width] = part_ref[...]
    for copy in copies:
        copy.wait()
    weight = weight_ref[...].reshape(quarters * heads_width, width)
    mixed_ref[...] = jnp.dot(all_ref[...], weight, preferred_element_type=F32)
    for row in range(0, hidden_ref.shape[0], STRIP):
        at = slice(row, row + STRIP)
        mixed = hidden_ref[at].astype(F32) + mixed_ref[at]
        normed_ref[at] = normalized(mixed, gain_ref[...], bias_ref[...]).astype(BF16)


def first_norm(place, hidden, own_out, gain, bias, parts, pieces):
    rows, width = hidden.shape
    heads_width = own_out.shape[0]
    layout = tuple(flips for flips, _ in pieces)
    return pl.pallas_call(
        functools.partial(first_norm_kernel, layout),
        out_shape=jax.ShapeDtypeStruct((rows, width), BF16),
        in_specs=[SMEM, VMEM, ANY, VMEM, VMEM] + [VMEM] * len(parts) + [ANY] * len(pieces),
        out_specs=VMEM,
        scratch_shapes=[
            pltpu.VMEM((rows, width), BF16),
            pltpu.VMEM((len(parts), heads_width, width), BF16),
            pltpu.VMEM((rows, width), F32),
            pltpu.SemaphoreType.DMA((1 + sum(len(flips) for flips in layout),)),
        ],
        compiler_params=pltpu.CompilerParams(vmem_limit_bytes=11 * MIB),
        cost_estimate=SHORT,
        name="first_norm",
    )(place, hidden, own_out, gain, bias, *parts, *[value for _, value in pieces])


def gelu(values):
    return 0.5 * values * (1.0 + lax.erf(values * math.sqrt(0.5)))


def feed_kernel(layout, *refs):
    count = len(layout)
    place_ref, rows_ref, up_near_ref, down_near_ref = refs[:4]
    pieces = refs[4 : 4 + count]
    sum_ref, up_ref, down_ref, wide_ref, units_ref, total_ref, near_sems, sems = refs[4 + count :]
    tok = place_ref[0]
    block = 128
    chunk = wide_ref.shape[2]
    chunks = up_ref.shape[2] // chunk
    near = []
    for index in range(chunks):
        at = slice(index * chunk, (index + 1) * chunk)
        near.append(
            (
                pltpu.make_async_copy(up_near_ref.at[:, at], up_ref.at[0, :, at], near_sems.at[0, index]),
                pltpu.make_async_copy(down_near_ref.at[at], down_ref.at[0, at], near_sems.at[1, index]),
            )
        )
    far = []
    for (flip, part), piece in zip(layout, pieces):
        at = pl.ds(pl.multiple_of((tok ^ flip) * block, block), block)
        if part in (None, 0):
            far.append(pltpu.make_async_copy(piece.at[0:block], up_ref.at[1, at], sems.at[len(far)]))
        if part in (None, 1):
            shift = block if part is None else 0
            far.append(pltpu.make_async_copy(piece.at[shift : shift + block], down_ref.at[1, at], sems.at[len(far)]))
    for pair in near:
        for copy in pair:
            copy.start()
    for copy in far:
        copy.start()
    rows = rows_ref[...]
    for side in range(2):
        for index in range(chunks):
            at = slice(index * chunk, (index + 1) * chunk)
            slot = index % 2
            if side == 0:
                near[index][0].wait()
            elif index == 0:
                for copy in far:
                    copy.wait()
            wide_ref[slot] = jnp.dot(rows, up_ref[side, :, at], preferred_element_type=F32)
            for row in range(0, rows.shape[0], STRIP):
                strip = slice(row, row + STRIP)
                units_ref[slot, strip] = gelu(wide_ref[slot, strip]).astype(BF16)
            if side == 0:
                near[index][1].wait()
            product = jnp.dot(units_ref[slot], down_ref[side, at], preferred_element_type=F32)
            if side == 0 and index == 0:
                total_ref[...] = product
            elif side == 1 and index == chunks - 1:
                sum_ref[...] = (total_ref[...] + product).astype(sum_ref.dtype)
            else:
                total_ref[...] += product


def feed(place, rows, up_weight, down_weight, pieces, dtype, name):
    count, width = rows.shape
    units = up_weight.shape[1]
    chunk = 512
    layout = tuple((flip, part) for flip, part, _ in pieces)
    copies = sum(2 if part is None else 1 for _, part in layout)
    return pl.pallas_call(
        functools.partial(feed_kernel, layout),
        out_shape=jax.ShapeDtypeStruct((count, width), dtype),
        in_specs=[SMEM, VMEM, ANY, ANY] + [ANY] * len(pieces),
        out_specs=VMEM,
        scratch_shapes=[
            pltpu.VMEM((2, width, units), BF16),
            pltpu.VMEM((2, units, width), BF16),
            pltpu.VMEM((2, count, chunk), F32),
            pltpu.VMEM((2, count, chunk), BF16),
            pltpu.VMEM((count, width), F32),
            pltpu.SemaphoreType.DMA((2, units // chunk)),
            pltpu.SemaphoreType.DMA((copies,)),
        ],
        compiler_params=pltpu.CompilerParams(vmem_limit_bytes=20 * MIB),
        cost_estimate=SHORT,
        name=name,
    )(place, rows, up_weight, down_weight, *[value for _, _, value in pieces])


def finish_kernel(normed_ref, near_ref, far_ref, gain_ref, bias_ref, out_ref):
    for row in range(0, normed_ref.shape[0], STRIP):
        at = slice(row, row + STRIP)
        mixed = normed_ref[at].astype(F32) + near_ref[at] + far_ref[at].astype(F32)
        out_ref[at] = normalized(mixed, gain_ref[...], bias_ref[...]).astype(out_ref.dtype)


def finish(normed, near, far, gain, bias):
    return pl.pallas_call(
        finish_kernel,
        out_shape=jax.ShapeDtypeStruct(normed.shape, BF16),
        in_specs=[VMEM] * 5,
        out_specs=VMEM,
        compiler_params=pltpu.CompilerParams(vmem_limit_bytes=6 * MIB),
        name="finish",
    )(normed, near, far, gain, bias)


def decode_kernel(slot_ref, filled_ref, query_ref, cache_ref, out_ref, high_ref, total_ref, sum_ref):
    step = pl.program_id(0)

    @pl.when(step == 0)
    def _():
        high_ref[...] = jnp.full(high_ref.shape, NEG_FILL, F32)
        total_ref[...] = jnp.zeros_like(total_ref)
        sum_ref[...] = jnp.zeros_like(sum_ref)

    row = slot_ref[step]
    filled = filled_ref[step]
    width = query_ref.shape[1]
    head = lax.broadcasted_iota(jnp.int32, (H, width), 0)
    inside = head == lax.broadcasted_iota(jnp.int32, (H, width), 1) // HD
    query = jnp.where(inside, query_ref[pl.ds(row, 1), :], 0.0).astype(BF16)
    scores = lax.dot_general(query, cache_ref[0, 0, 0], (((1,), (1,)), ((), ())), preferred_element_type=F32)
    live = lax.broadcasted_iota(jnp.int32, scores.shape, 1) < filled
    scores = jnp.where(live, scores * (1.0 / math.sqrt(HD)), NEG_FILL)
    high = jnp.max(scores, axis=1, keepdims=True)
    weights = jnp.where(live, jnp.exp(scores - high), 0.0)
    total = jnp.sum(weights, axis=1, keepdims=True)
    summed = jnp.dot(weights.astype(BF16), cache_ref[1, 0, 0], preferred_element_type=F32)
    along = lambda column: jnp.sum(jnp.where(inside, column, 0.0), axis=0, keepdims=True)
    high, total, summed = along(high), along(total), along(summed)
    used = filled > 0
    at = pl.ds(row, 1)
    old = high_ref[at, :]
    new = jnp.where(used, jnp.maximum(old, high), old)
    left = jnp.exp(old - new)
    right = jnp.where(used, jnp.exp(high - new), 0.0)
    high_ref[at, :] = new
    total_ref[at, :] = total_ref[at, :] * left + total * right
    sum_ref[at, :] = sum_ref[at, :] * left + summed * right

    @pl.when(step == pl.num_programs(0) - 1)
    def _():
        out_ref[0] = high_ref[...]
        out_ref[1] = total_ref[...]
        out_ref[2] = sum_ref[...]


def decode(slots, filled, queries, kv_cache):
    requests, width = queries.shape
    pieces = kv_cache.shape[2]
    state = pltpu.VMEM((requests, width), F32)
    return pl.pallas_call(
        decode_kernel,
        grid=(pieces,),
        out_shape=jax.ShapeDtypeStruct((3, requests, width), F32),
        in_specs=[
            SMEM,
            SMEM,
            pl.BlockSpec((requests, width), lambda i: (0, 0)),
            pl.BlockSpec((2, 1, 1, PLEN, width), lambda i: (0, 0, i, 0, 0)),
        ],
        out_specs=pl.BlockSpec((3, requests, width), lambda i: (0, 0, 0)),
        scratch_shapes=[state, state, state],
        compiler_params=pltpu.CompilerParams(vmem_limit_bytes=8 * MIB),
        cost_estimate=SHORT,
        name="decode",
    )(slots, filled, queries, kv_cache)


def gathered_queries(dec_query):
    flips = range(1, lax.axis_size("kv"))
    return [dec_query] + [swapped(dec_query, "kv", flip) for flip in flips]


def decode_partial(queries, kv_cache, piece_req, piece_used):
    own = queries[0].shape[0]
    owners = piece_req[0]
    slots = ((owners // own) ^ lax.axis_index("kv")) * own + owners % own
    return decode(slots, piece_used[0], jnp.concatenate(queries).astype(F32), kv_cache)


def exchanged_partials(partial, own):
    parts = [partial[:, :own]]
    for flip in range(1, lax.axis_size("kv")):
        parts.append(swapped(partial[:, flip * own : (flip + 1) * own], "kv", flip))
    return parts


def merged_partials(parts):
    high = functools.reduce(jnp.maximum, [part[0] for part in parts])
    factors = [jnp.exp(part[0] - high) for part in parts]
    total = sum(part[1] * factor for part, factor in zip(parts, factors))
    summed = sum(part[2] * factor for part, factor in zip(parts, factors))
    return (summed / total).astype(BF16)


def routed_body(
    hidden_in,
    qkv_weight,
    stretch_len,
    out_weight,
    ln1_gain,
    ln1_bias,
    up_weight,
    down_weight,
    ln2_gain,
    ln2_bias,
    dec_query,
    kv_cache,
    piece_req,
    piece_used,
):
    tok = lax.axis_index("tok")
    kv = lax.axis_index("kv")
    toks, kvs = lax.axis_size("tok"), lax.axis_size("kv")
    rows, width = hidden_in.shape
    place = jnp.stack([tok, kv]).astype(jnp.int32)
    eighth = lambda value: lax.dynamic_slice_in_dim(value, tok * (value.shape[0] // toks), value.shape[0] // toks, 0)

    queries = gathered_queries(dec_query)
    partial = decode_partial(queries, kv_cache, piece_req, piece_used)
    from_below, from_above = [], []
    rising = falling = hidden_in
    for step in range(1, kvs):
        links = range(step - 1, kvs - 1)
        rising = lax.ppermute(rising, "kv", [(i, i + 1) for i in links])
        falling = lax.ppermute(falling, "kv", [(kvs - 1 - i, kvs - 2 - i) for i in links])
        from_below.append(rising)
        from_above.append(falling)
        if step == 2:
            rising, falling = after(rising, partial), after(falling, partial)
    dec_parts = exchanged_partials(partial, dec_query.shape[0])

    out_part = after(eighth(out_weight), from_below[1], from_above[1])
    feed_part = jnp.concatenate([eighth(up_weight), eighth(down_weight), eighth(out_weight)], axis=0)
    feed_here = swapped(after(feed_part, from_below[1], from_above[1]), "kv", 2)
    out_near, out_far = swapped(out_part, "kv", 1), swapped(out_part, "kv", 3)

    order = jnp.arange(stretch_len.shape[0])
    ends = jnp.sum(jnp.where(order[:, None] <= order[None, :], stretch_len[:, None], 0), axis=0, dtype=jnp.int32)
    starts = (ends - stretch_len)[None, :]
    ends = ends[None, :]

    shards = [after(hidden_in, *dec_parts)] + from_below + from_above
    query, keyval, top, bottom = project(place, jnp.transpose(qkv_weight, (1, 0, 2)), shards)
    before = lax.ppermute(bottom, "tok", [(i, i + 1) for i in range(toks - 1)])
    behind = lax.ppermute(top, "tok", [(i + 1, i) for i in range(toks - 1)])
    window = (place, starts, ends, query, before, keyval, behind, rows)
    parts = [None] * kvs
    parts[3], parts[2] = attend_blocks(*window, (3, 2), "attend_far")
    feed_here = after(feed_here, parts[3], parts[2])
    parts[3], parts[2] = swapped(parts[3], "kv", 3), swapped(parts[2], "kv", 2)
    depth = out_part.shape[0]
    out_here = jnp.stack([out_near, feed_here[-depth:], out_far])
    feed_here = feed_here[:-depth]
    out_x, out_y = swapped(out_here, "tok", 2), swapped(out_here, "tok", 4)
    feed_x, feed_y = swapped(feed_here, "tok", 2), swapped(feed_here, "tok", 4)
    window = (place, starts, ends, after(query, out_here), before, keyval, behind, rows)
    parts[1], parts[0] = attend_blocks(*window, (1, 0), "attend_near")
    out_all = jnp.stack([out_here, out_x, out_y, swapped(after(out_y, parts[0]), "tok", 2)])
    out_core = swapped(out_all, "tok", 1)
    half = feed_here.shape[0] // 2
    far_up = swapped(after(feed_y, parts[0])[:half], "tok", 2)
    far_down = swapped(after(feed_x, parts[0])[half:], "tok", 4)
    parts[1] = swapped(parts[1], "kv", 1)
    out_pieces = [((0, 2, 4, 6), out_all), ((1, 3, 5, 7), out_core)]
    normed = first_norm(place, hidden_in, out_weight, ln1_gain[None, :], ln1_bias[None, :], parts, out_pieces)

    partner = swapped(normed, "kv", 1)
    held = [(0, None, feed_here), (2, None, feed_x), (4, None, feed_y), (6, 0, far_up), (6, 1, far_down)]
    feed_pieces = held + [(flip ^ 1, part, swapped(after(value, normed), "tok", 1)) for flip, part, value in held]
    away = feed(place, partner, up_weight, down_weight, feed_pieces, BF16, "feed_partner")
    arrived = swapped(away, "kv", 1)
    mine = feed(place, after(normed, away), up_weight, down_weight, feed_pieces, F32, "feed_own")
    prefill_out = finish(normed, mine, arrived, ln2_gain[None, :], ln2_bias[None, :])

    return prefill_out, merged_partials(dec_parts)


def extended(value, sides, width):
    for axis, dim in sides:
        count, length = (lax.axis_size(axis), value.shape[dim])
        up = [(i, (i + 1) % count) for i in range(count - 1)]
        down = [(j, i) for i, j in up]
        last = lax.slice_in_dim(value, length - width, length, axis=dim)
        leading = lax.slice_in_dim(value, 0, width, axis=dim)
        before = lax.ppermute(last, axis, up)
        after = lax.ppermute(leading, axis, down)
        value = jnp.concatenate([before, value, after], axis=dim)
    return value


def merged(value, axis, join):
    pieces = jax.tree.map(lambda part: lax.all_gather(part, axis), value)
    head = jax.tree.map(lambda part: part[0], pieces)
    tail = jax.tree.map(lambda part: part[1:], pieces)
    subtotal, _ = lax.scan(lambda subtotal, section: (join(subtotal, section), None), head, tail)
    return subtotal


def segment_ids(row_ids, stretch_len):
    stretch_ends = jnp.cumsum(stretch_len)
    return jnp.sum((row_ids[:, None] >= stretch_ends[None, :]).astype(jnp.int32), axis=1)


def layer_norm(values, gain, bias):
    center = values - jnp.mean(values, axis=1, keepdims=True)
    spread = jnp.mean(center * center, axis=1, keepdims=True)
    return center * lax.rsqrt(spread + LN_EPS) * gain + bias


def merge_partials(earlier, later):
    highest = jnp.maximum(earlier[0], later[0])
    left_factor = jnp.exp(earlier[0] - highest)
    right_factor = jnp.exp(later[0] - highest)
    totals = earlier[1] * left_factor + later[1] * right_factor
    weighted = earlier[2] * left_factor[..., None] + later[2] * right_factor[..., None]
    return (highest, totals, weighted)


def row_folder(source, shard_rows):
    return jnp.dot(source, shard_rows, preferred_element_type=jnp.float32)


def general_body(
    hidden_in,
    qkv_weight,
    stretch_len,
    out_weight,
    ln1_gain,
    ln1_bias,
    up_weight,
    down_weight,
    ln2_gain,
    ln2_bias,
    dec_query,
    kv_cache,
    piece_req,
    piece_used,
):
    inv_scale = 1.0 / math.sqrt(HD)
    reach = WIN // 2
    local_width = qkv_weight.shape[2]
    head_count = local_width // HD
    flat_weight = qkv_weight.reshape(qkv_weight.shape[0], 3 * local_width)
    qkv_rows = jnp.dot(
        lax.all_gather(hidden_in, "kv", axis=0, tiled=True),
        flat_weight,
        preferred_element_type=jnp.float32,
    ).astype(jnp.bfloat16)
    row_count = qkv_rows.shape[0]
    query_rows = qkv_rows[:, :local_width]
    keyval_rows = qkv_rows[:, local_width:]
    padded = extended(keyval_rows, (("tok", 0),), reach)
    first_row = lax.axis_index("tok") * row_count
    total_rows = row_count * lax.axis_size("tok")
    qblock = min(512, row_count)
    span = qblock + 2 * reach
    block_count = row_count // qblock

    def attend(block_index):
        start = block_index * qblock
        query_ids = first_row + start + jnp.arange(qblock, dtype=jnp.int32)
        key_ids = first_row + start - reach + jnp.arange(span, dtype=jnp.int32)
        query_seg = segment_ids(query_ids, stretch_len)
        inside = (key_ids >= 0) & (key_ids < total_rows)
        key_seg = jnp.where(inside, segment_ids(key_ids, stretch_len), -1)
        allowed = (key_seg[None, :] == query_seg[:, None]) & (
            jnp.abs(key_ids[None, :] - query_ids[:, None]) <= reach
        )
        queries = lax.dynamic_slice_in_dim(query_rows, start, qblock, 0).reshape(
            qblock, head_count, HD
        )
        both = lax.dynamic_slice_in_dim(padded, start, span, 0)
        key_rows = both[:, :local_width].reshape(span, head_count, HD)
        value_rows = both[:, local_width:].reshape(span, head_count, HD)
        scores = (
            jnp.einsum("ihd,jhd->hij", queries, key_rows, preferred_element_type=jnp.float32)
            * inv_scale
        )
        scores = jnp.where(allowed[None], scores, NEG_FILL)
        row_max = jnp.max(scores, axis=2, keepdims=True)
        weights = jnp.where(allowed[None], jnp.exp(scores - row_max), 0.0)
        totals = jnp.sum(weights, axis=2)
        summed = jnp.einsum(
            "hij,jhd->ihd",
            weights.astype(jnp.bfloat16),
            value_rows,
            preferred_element_type=jnp.float32,
        )
        return (
            (summed / jnp.transpose(totals)[:, :, None])
            .astype(jnp.bfloat16)
            .reshape(qblock, local_width)
        )

    attention = lax.map(attend, jnp.arange(block_count, dtype=jnp.int32)).reshape(
        row_count, local_width
    )
    token_major = lax.all_to_all(attention, "kv", split_axis=0, concat_axis=1, tiled=True)
    projected = row_folder(token_major, lax.all_gather(out_weight, "kv", axis=0, tiled=True))
    normed = layer_norm(hidden_in.astype(jnp.float32) + projected, ln1_gain, ln1_bias).astype(
        jnp.bfloat16
    )
    units = jax.nn.gelu(
        jnp.dot(
            lax.all_gather(normed, "kv", axis=0, tiled=True),
            up_weight,
            preferred_element_type=jnp.float32,
        ),
        approximate=False,
    ).astype(jnp.bfloat16)
    ffn = lax.psum_scatter(
        jnp.dot(units, down_weight, preferred_element_type=jnp.float32).astype(jnp.bfloat16),
        "kv",
        scatter_dimension=0,
        tiled=True,
    ).astype(jnp.float32)
    prefill_out = layer_norm(normed.astype(jnp.float32) + ffn, ln2_gain, ln2_bias).astype(
        jnp.bfloat16
    )
    group_queries = lax.all_gather(dec_query, "kv", axis=0, tiled=True)
    request_count = group_queries.shape[0]
    owners = piece_req[0]
    filled = piece_used[0]
    slot_count = owners.shape[0]
    request_ids = jnp.arange(request_count, dtype=jnp.int32)
    selector = (owners[:, None] == request_ids[None, :]).astype(jnp.bfloat16)
    chosen = jnp.dot(selector, group_queries, preferred_element_type=jnp.float32).astype(
        jnp.bfloat16
    )
    chosen = chosen.reshape(slot_count, H, HD)
    cache_keys = kv_cache[0, 0].reshape(slot_count, PLEN, H, HD)
    cache_values = kv_cache[1, 0].reshape(slot_count, PLEN, H, HD)
    piece_scores = (
        jnp.einsum("phd,pthd->pht", chosen, cache_keys, preferred_element_type=jnp.float32)
        * inv_scale
    )
    active = jnp.arange(PLEN, dtype=jnp.int32)[None, :] < filled[:, None]
    piece_scores = jnp.where(active[:, None, :], piece_scores, NEG_FILL)
    piece_max = jnp.max(piece_scores, axis=2)
    piece_weights = jnp.where(
        active[:, None, :], jnp.exp(piece_scores - piece_max[:, :, None]), 0.0
    )
    piece_totals = jnp.sum(piece_weights, axis=2)
    partial_value = jnp.einsum(
        "pht,pthd->phd",
        piece_weights.astype(jnp.bfloat16),
        cache_values,
        preferred_element_type=jnp.float32,
    )
    member = (owners[None, :] == request_ids[:, None]) & (filled[None, :] > 0)
    highest = jnp.max(jnp.where(member[:, :, None], piece_max[None], NEG_FILL), axis=1)
    factor = jnp.where(member[:, :, None], jnp.exp(piece_max[None] - highest[:, None, :]), 0.0)
    denom = jnp.sum(factor * piece_totals[None], axis=1)
    weighted = jnp.einsum("rph,phd->rhd", factor, partial_value)
    own_requests = dec_query.shape[0]
    joined = merged((highest, denom, weighted), "kv", merge_partials)
    begin = lax.axis_index("kv") * own_requests
    final_denom = lax.dynamic_slice_in_dim(joined[1], begin, own_requests, 0)
    final_weighted = lax.dynamic_slice_in_dim(joined[2], begin, own_requests, 0)
    dec_out = (
        (final_weighted / final_denom[:, :, None])
        .astype(jnp.bfloat16)
        .reshape(own_requests, H * HD)
    )
    return (prefill_out, dec_out)


def solution(mesh):
    placed = (
        P(("tok", "kv"), None),
        P(None, None, "kv"),
        P(),
        P("kv", None),
        P(),
        P(),
        P(None, "kv"),
        P("kv", None),
        P(),
        P(),
        P(("tok", "kv"), None),
        P(None, "tok", "kv", None, None),
        P("tok", "kv"),
        P("tok", "kv"),
    )
    routed = mesh.shape["tok"] == 8 and mesh.shape["kv"] == 4
    return jax.shard_map(
        routed_body if routed else general_body,
        mesh=mesh,
        in_specs=placed,
        out_specs=(P(("tok", "kv"), None), P(("tok", "kv"), None)),
        check_vma=False,
    )
```

```python
import functools
import math

import jax
import jax.numpy as jnp
from jax import lax
from jax.experimental import pallas as pl
from jax.experimental.pallas import tpu as pltpu
from jax.sharding import PartitionSpec as P

H = 16
HD = 64
WIN = 512
PLEN = 128


NEG_FILL = -1e30
LN_EPS = 1e-05
BF16 = jnp.bfloat16
F32 = jnp.float32
STRIP = 32
MIB = 1024 * 1024
ANY = pl.BlockSpec(memory_space=pl.ANY)
VMEM = pl.BlockSpec(memory_space=pltpu.VMEM)
SMEM = pl.BlockSpec(memory_space=pltpu.SMEM)
SHORT = pl.CostEstimate(flops=1, bytes_accessed=1, transcendentals=0)


def swapped(value, axis, flip):
    count = lax.axis_size(axis)
    return lax.ppermute(value, axis, [(i, i ^ flip) for i in range(count)])


def after(value, *earlier):
    return lax.optimization_barrier((value,) + earlier)[0]


def normalized(values, gain, bias):
    center = values - jnp.mean(values, axis=1, keepdims=True)
    spread = jnp.mean(center * center, axis=1, keepdims=True)
    return center * lax.rsqrt(spread + LN_EPS) * gain + bias


def project_kernel(place_ref, weight_ref, *refs):
    shards, (query_ref, keyval_ref, top_ref, bottom_ref, rows_ref, sems) = refs[:-6], refs[-6:]
    kv = place_ref[1]
    count = shards[0].shape[0]
    steps = (len(shards) - 1) // 2
    width = weight_ref.shape[2]
    moves = [(shards[0], kv, None)]
    for step in range(1, steps + 1):
        moves.append((shards[step], kv - step, kv >= step))
        moves.append((shards[steps + step], kv + step, kv + step <= steps))

    def guarded(needed, act):
        if needed is None:
            act()
        else:
            pl.when(needed)(act)

    copies = []
    for index, (source, owner, needed) in enumerate(moves):
        safe = owner if needed is None else jnp.where(needed, owner, 0)
        at = pl.ds(pl.multiple_of(safe * count, count), count)
        copies.append((needed, pltpu.make_async_copy(source, rows_ref.at[at], sems.at[index])))
    for needed, copy in copies:
        guarded(needed, copy.start)
    for needed, copy in copies:
        guarded(needed, copy.wait)
    rows = rows_ref[...]
    query = jnp.dot(rows, weight_ref[0], preferred_element_type=F32) * (1.0 / math.sqrt(HD))
    query_ref[...] = query.astype(BF16)
    for part in range(2):
        at = slice(part * width, (part + 1) * width)
        keyval_ref[:, at] = jnp.dot(rows, weight_ref[part + 1], preferred_element_type=F32).astype(BF16)
    top_ref[...] = keyval_ref[:count]
    bottom_ref[...] = keyval_ref[steps * count :]


def project(place, weight, shards):
    rows, width = shards[0].shape
    heads_width = weight.shape[2]
    blocks = (len(shards) + 1) // 2
    edge = jax.ShapeDtypeStruct((rows, 2 * heads_width), BF16)
    return pl.pallas_call(
        project_kernel,
        out_shape=(
            jax.ShapeDtypeStruct((blocks * rows, heads_width), BF16),
            jax.ShapeDtypeStruct((blocks * rows, 2 * heads_width), BF16),
            edge,
            edge,
        ),
        in_specs=[SMEM, VMEM] + [ANY] * len(shards),
        out_specs=(VMEM,) * 4,
        scratch_shapes=[pltpu.VMEM((blocks * rows, width), BF16), pltpu.SemaphoreType.DMA((len(shards),))],
        compiler_params=pltpu.CompilerParams(vmem_limit_bytes=14 * MIB),
        cost_estimate=SHORT,
        name="project",
    )(place, weight, *shards)


def window_bias(first, count, starts, ends):
    reach = WIN // 2
    query = first + lax.broadcasted_iota(jnp.int32, (count, 1), 0)
    low = jnp.max(jnp.where(starts <= query, starts, 0), axis=1, keepdims=True)
    high = jnp.min(jnp.where(ends > query, ends, 1 << 30), axis=1, keepdims=True)
    low = jnp.maximum(low, query - reach)
    high = jnp.minimum(high, query + reach + 1)
    key = first - count + lax.broadcasted_iota(jnp.int32, (count, 3 * count), 1)
    return jnp.where((key >= low) & (key < high), 0.0, NEG_FILL)


def attend(query, keyval_ref, bias_ref, scores_ref, weights_ref, out_ref):
    count, width = query.shape
    lane = lax.broadcasted_iota(jnp.int32, (count, 2 * HD), 1)
    for start in range(0, width, 2 * HD):
        values = keyval_ref[:, width + start : width + start + 2 * HD]
        halves = []
        for side in range(2):
            head = start // HD + side
            inside = (lane < HD) if side == 0 else (lane >= HD)
            only = jnp.where(inside, query[:, start : start + 2 * HD], jnp.zeros((), BF16))
            scores_ref[head] = lax.dot_general(
                only, keyval_ref[:, start : start + 2 * HD], (((1,), (1,)), ((), ())), preferred_element_type=F32
            )
            totals = []
            for row in range(0, count, STRIP):
                at = slice(row, row + STRIP)
                scores = scores_ref[head, at] + bias_ref[at]
                weights = jnp.exp(scores - jnp.max(scores, axis=1, keepdims=True))
                totals.append(jnp.sum(weights, axis=1, keepdims=True))
                weights_ref[head, at] = weights.astype(BF16)
            summed = jnp.dot(weights_ref[head], values, preferred_element_type=F32)
            halves.append(summed / jnp.concatenate(totals, axis=0))
        out_ref[:, start : start + 2 * HD] = jnp.where(lane < HD, halves[0], halves[1]).astype(BF16)


def attend_kernel(flips, place_ref, starts_ref, ends_ref, query_ref, before_ref, keyval_ref, behind_ref, *refs):
    outs = refs[: len(flips)]
    window_ref, bias_ref, scores_ref, weights_ref, sems = refs[len(flips) :]
    tok, kv = place_ref[0], place_ref[1]
    count = outs[0].shape[0]
    blocks = query_ref.shape[0] // count
    copies = []
    for index, flip in enumerate(flips):
        block = kv ^ flip
        for part in range(3):
            target = window_ref.at[index, part * count : (part + 1) * count]
            sem = sems.at[index, part]
            at = block + part - 1
            inner = (at >= 0) & (at < blocks)
            safe = jnp.where(inner, at, 0)
            source = keyval_ref.at[pl.ds(pl.multiple_of(safe * count, count), count)]
            copies.append((index, inner, pltpu.make_async_copy(source, target, sem)))
            if part == 0:
                copies.append((index, at < 0, pltpu.make_async_copy(before_ref, target, sem)))
            if part == 2:
                copies.append((index, at >= blocks, pltpu.make_async_copy(behind_ref, target, sem)))
    for _, needed, copy in copies:
        pl.when(needed)(copy.start)
    for index, flip in enumerate(flips):
        block = kv ^ flip
        first = (tok * blocks + block) * count
        bias_ref[...] = window_bias(first, count, starts_ref[...], ends_ref[...])
        for owner, needed, copy in copies:
            if owner == index:
                pl.when(needed)(copy.wait)
        query = query_ref[pl.ds(pl.multiple_of(block * count, count), count)]
        attend(query, window_ref.at[index], bias_ref, scores_ref, weights_ref, outs[index])


def attend_blocks(place, starts, ends, query, before, keyval, behind, rows, flips, name):
    heads_width = query.shape[1]
    return pl.pallas_call(
        functools.partial(attend_kernel, flips),
        out_shape=tuple(jax.ShapeDtypeStruct((rows, heads_width), BF16) for _ in flips),
        in_specs=[SMEM, VMEM, VMEM, VMEM, ANY, ANY, ANY],
        out_specs=(VMEM,) * len(flips),
        scratch_shapes=[
            pltpu.VMEM((len(flips), 3 * rows, 2 * heads_width), BF16),
            pltpu.VMEM((rows, 3 * rows), F32),
            pltpu.VMEM((heads_width // HD, rows, 3 * rows), F32),
            pltpu.VMEM((heads_width // HD, rows, 3 * rows), BF16),
            pltpu.SemaphoreType.DMA((len(flips), 3)),
        ],
        compiler_params=pltpu.CompilerParams(vmem_limit_bytes=14 * MIB),
        cost_estimate=SHORT,
        name=name,
    )(place, starts, ends, query, before, keyval, behind)


def first_norm_kernel(layout, place_ref, hidden_ref, own_out_ref, gain_ref, bias_ref, *refs):
    parts, pieces = refs[: -5 - len(layout)], refs[-5 - len(layout) : -5]
    normed_ref, all_ref, weight_ref, mixed_ref, sems = refs[-5:]
    tok = place_ref[0]
    quarters, heads_width, width = weight_ref.shape
    copies = [pltpu.make_async_copy(own_out_ref, weight_ref.at[0], sems.at[0])]
    for flips, piece in zip(layout, pieces):
        for index, flip in enumerate(flips):
            depth = piece.shape[2]
            at = pl.multiple_of((tok ^ flip) * depth, depth)
            target = weight_ref.at[1:quarters, pl.ds(at, depth)]
            copies.append(pltpu.make_async_copy(piece.at[index], target, sems.at[len(copies)]))
    for copy in copies:
        copy.start()
    for flip, part_ref in enumerate(parts):
        all_ref[:, flip * heads_width : (flip + 1) * heads_width] = part_ref[...]
    for copy in copies:
        copy.wait()
    weight = weight_ref[...].reshape(quarters * heads_width, width)
    mixed_ref[...] = jnp.dot(all_ref[...], weight, preferred_element_type=F32)
    for row in range(0, hidden_ref.shape[0], STRIP):
        at = slice(row, row + STRIP)
        mixed = hidden_ref[at].astype(F32) + mixed_ref[at]
        normed_ref[at] = normalized(mixed, gain_ref[...], bias_ref[...]).astype(BF16)


def first_norm(place, hidden, own_out, gain, bias, parts, pieces):
    rows, width = hidden.shape
    heads_width = own_out.shape[0]
    layout = tuple(flips for flips, _ in pieces)
    return pl.pallas_call(
        functools.partial(first_norm_kernel, layout),
        out_shape=jax.ShapeDtypeStruct((rows, width), BF16),
        in_specs=[SMEM, VMEM, ANY, VMEM, VMEM] + [VMEM] * len(parts) + [ANY] * len(pieces),
        out_specs=VMEM,
        scratch_shapes=[
            pltpu.VMEM((rows, width), BF16),
            pltpu.VMEM((len(parts), heads_width, width), BF16),
            pltpu.VMEM((rows, width), F32),
            pltpu.SemaphoreType.DMA((1 + sum(len(flips) for flips in layout),)),
        ],
        compiler_params=pltpu.CompilerParams(vmem_limit_bytes=11 * MIB),
        cost_estimate=SHORT,
        name="first_norm",
    )(place, hidden, own_out, gain, bias, *parts, *[value for _, value in pieces])


def gelu(values):
    return 0.5 * values * (1.0 + lax.erf(values * math.sqrt(0.5)))


CHUNK = 512


def feed_chunk(rows, up, down_ref, wide_ref, units_ref):
    wide_ref[...] = jnp.dot(rows, up, preferred_element_type=F32)
    for row in range(0, rows.shape[0], STRIP):
        strip = slice(row, row + STRIP)
        units_ref[strip] = gelu(wide_ref[strip]).astype(BF16)
    return jnp.dot(units_ref[...], down_ref[...], preferred_element_type=F32)


def far_copies(tok, held_ref, core_ref, up_ref, down_ref, sems):
    block = 128
    copies = []
    for side, piece in enumerate((held_ref, core_ref)):
        for index in range(4):
            at = pl.ds(pl.multiple_of((tok ^ (2 * index + side)) * block, block), block)
            for part, target in enumerate((up_ref, down_ref)):
                source = piece.at[pl.ds((2 * index + part) * block, block)]
                copies.append(pltpu.make_async_copy(source, target.at[at], sems.at[len(copies)]))
    return copies


def feed_near_kernel(rows_ref, up_ref, down_ref, sum_ref, wide_ref, units_ref):
    rows = rows_ref[...]
    for index in range(up_ref.shape[1] // CHUNK):
        at = slice(index * CHUNK, (index + 1) * CHUNK)
        product = feed_chunk(rows, up_ref[:, at], down_ref.at[at], wide_ref.at[index % 2], units_ref.at[index % 2])
        if index == 0:
            sum_ref[...] = product
        else:
            sum_ref[...] += product


def feed_far_kernel(
    place_ref, rows_ref, near_ref, held_ref, core_ref, sum_ref, up_ref, down_ref, wide_ref, units_ref, total_ref, sems
):
    copies = far_copies(place_ref[0], held_ref, core_ref, up_ref, down_ref, sems)
    for copy in copies:
        copy.start()
    rows = rows_ref[...]
    total_ref[...] = near_ref[...]
    for copy in copies:
        copy.wait()
    for index in range(up_ref.shape[1] // CHUNK):
        at = slice(index * CHUNK, (index + 1) * CHUNK)
        slot = index % 2
        total_ref[...] += feed_chunk(rows, up_ref[:, at], down_ref.at[at], wide_ref.at[slot], units_ref.at[slot])
    sum_ref[...] = total_ref[...].astype(sum_ref.dtype)


def feed_kernel(
    place_ref, rows_ref, up_near_ref, down_near_ref, held_ref, core_ref, sum_ref, up_ref, down_ref, wide_ref, units_ref, sems
):
    copies = far_copies(place_ref[0], held_ref, core_ref, up_ref, down_ref, sems)
    for copy in copies:
        copy.start()
    feed_near_kernel(rows_ref, up_near_ref, down_near_ref, sum_ref, wide_ref, units_ref)
    rows = rows_ref[...]
    for copy in copies:
        copy.wait()
    for index in range(up_ref.shape[1] // CHUNK):
        at = slice(index * CHUNK, (index + 1) * CHUNK)
        slot = index % 2
        sum_ref[...] += feed_chunk(rows, up_ref[:, at], down_ref.at[at], wide_ref.at[slot], units_ref.at[slot])


def feed_scratch(count):
    return [pltpu.VMEM((2, count, CHUNK), F32), pltpu.VMEM((2, count, CHUNK), BF16)]


def feed_near(rows, up_weight, down_weight):
    return pl.pallas_call(
        feed_near_kernel,
        out_shape=jax.ShapeDtypeStruct(rows.shape, F32),
        in_specs=[VMEM] * 3,
        out_specs=VMEM,
        scratch_shapes=feed_scratch(rows.shape[0]),
        compiler_params=pltpu.CompilerParams(vmem_limit_bytes=14 * MIB),
        cost_estimate=SHORT,
        name="feed_near",
    )(rows, up_weight, down_weight)


def feed_far(place, rows, near, pieces):
    count, width = rows.shape
    units = pieces[0].shape[0]
    return pl.pallas_call(
        feed_far_kernel,
        out_shape=jax.ShapeDtypeStruct((count, width), BF16),
        in_specs=[SMEM] + [VMEM] * 2 + [ANY] * 2,
        out_specs=VMEM,
        scratch_shapes=[pltpu.VMEM((width, units), BF16), pltpu.VMEM((units, width), BF16)]
        + feed_scratch(count)
        + [pltpu.VMEM((count, width), F32), pltpu.SemaphoreType.DMA((16,))],
        compiler_params=pltpu.CompilerParams(vmem_limit_bytes=14 * MIB),
        cost_estimate=SHORT,
        name="feed_far",
    )(place, rows, near, *pieces)


def feed(place, rows, up_weight, down_weight, pieces):
    count, width = rows.shape
    units = up_weight.shape[1]
    return pl.pallas_call(
        feed_kernel,
        out_shape=jax.ShapeDtypeStruct((count, width), F32),
        in_specs=[SMEM] + [VMEM] * 3 + [ANY] * 2,
        out_specs=VMEM,
        scratch_shapes=[pltpu.VMEM((width, units), BF16), pltpu.VMEM((units, width), BF16)]
        + feed_scratch(count)
        + [pltpu.SemaphoreType.DMA((16,))],
        compiler_params=pltpu.CompilerParams(vmem_limit_bytes=18 * MIB),
        cost_estimate=SHORT,
        name="feed_own",
    )(place, rows, up_weight, down_weight, *pieces)


def finish_kernel(normed_ref, near_ref, far_ref, gain_ref, bias_ref, out_ref):
    for row in range(0, normed_ref.shape[0], STRIP):
        at = slice(row, row + STRIP)
        mixed = normed_ref[at].astype(F32) + near_ref[at] + far_ref[at].astype(F32)
        out_ref[at] = normalized(mixed, gain_ref[...], bias_ref[...]).astype(out_ref.dtype)


def finish(normed, near, far, gain, bias):
    return pl.pallas_call(
        finish_kernel,
        out_shape=jax.ShapeDtypeStruct(normed.shape, BF16),
        in_specs=[VMEM] * 5,
        out_specs=VMEM,
        compiler_params=pltpu.CompilerParams(vmem_limit_bytes=6 * MIB),
        name="finish",
    )(normed, near, far, gain, bias)


def decode_kernel(slot_ref, filled_ref, query_ref, cache_ref, out_ref, high_ref, total_ref, sum_ref):
    step = pl.program_id(0)

    @pl.when(step == 0)
    def _():
        high_ref[...] = jnp.full(high_ref.shape, NEG_FILL, F32)
        total_ref[...] = jnp.zeros_like(total_ref)
        sum_ref[...] = jnp.zeros_like(sum_ref)

    row = slot_ref[step]
    filled = filled_ref[step]
    width = query_ref.shape[1]
    head = lax.broadcasted_iota(jnp.int32, (H, width), 0)
    inside = head == lax.broadcasted_iota(jnp.int32, (H, width), 1) // HD
    query = jnp.where(inside, query_ref[pl.ds(row, 1), :], 0.0).astype(BF16)
    scores = lax.dot_general(query, cache_ref[0, 0, 0], (((1,), (1,)), ((), ())), preferred_element_type=F32)
    live = lax.broadcasted_iota(jnp.int32, scores.shape, 1) < filled
    scores = jnp.where(live, scores * (1.0 / math.sqrt(HD)), NEG_FILL)
    high = jnp.max(scores, axis=1, keepdims=True)
    weights = jnp.where(live, jnp.exp(scores - high), 0.0)
    total = jnp.sum(weights, axis=1, keepdims=True)
    summed = jnp.dot(weights.astype(BF16), cache_ref[1, 0, 0], preferred_element_type=F32)
    along = lambda column: jnp.sum(jnp.where(inside, column, 0.0), axis=0, keepdims=True)
    high, total, summed = along(high), along(total), along(summed)
    used = filled > 0
    at = pl.ds(row, 1)
    old = high_ref[at, :]
    new = jnp.where(used, jnp.maximum(old, high), old)
    left = jnp.exp(old - new)
    right = jnp.where(used, jnp.exp(high - new), 0.0)
    high_ref[at, :] = new
    total_ref[at, :] = total_ref[at, :] * left + total * right
    sum_ref[at, :] = sum_ref[at, :] * left + summed * right

    @pl.when(step == pl.num_programs(0) - 1)
    def _():
        out_ref[0] = high_ref[...]
        out_ref[1] = total_ref[...]
        out_ref[2] = sum_ref[...]


def decode(slots, filled, queries, kv_cache):
    requests, width = queries.shape
    pieces = kv_cache.shape[2]
    state = pltpu.VMEM((requests, width), F32)
    return pl.pallas_call(
        decode_kernel,
        grid=(pieces,),
        out_shape=jax.ShapeDtypeStruct((3, requests, width), F32),
        in_specs=[
            SMEM,
            SMEM,
            pl.BlockSpec((requests, width), lambda i: (0, 0)),
            pl.BlockSpec((2, 1, 1, PLEN, width), lambda i: (0, 0, i, 0, 0)),
        ],
        out_specs=pl.BlockSpec((3, requests, width), lambda i: (0, 0, 0)),
        scratch_shapes=[state, state, state],
        compiler_params=pltpu.CompilerParams(vmem_limit_bytes=8 * MIB),
        cost_estimate=SHORT,
        name="decode",
    )(slots, filled, queries, kv_cache)


def gathered_queries(dec_query):
    flips = range(1, lax.axis_size("kv"))
    return [dec_query] + [swapped(dec_query, "kv", flip) for flip in flips]


def decode_partial(queries, kv_cache, piece_req, piece_used):
    own = queries[0].shape[0]
    owners = piece_req[0]
    slots = ((owners // own) ^ lax.axis_index("kv")) * own + owners % own
    return decode(slots, piece_used[0], jnp.concatenate(queries).astype(F32), kv_cache)


def exchanged_partials(partial, own):
    parts = [partial[:, :own]]
    for flip in range(1, lax.axis_size("kv")):
        parts.append(swapped(partial[:, flip * own : (flip + 1) * own], "kv", flip))
    return parts


def merged_partials(parts):
    high = functools.reduce(jnp.maximum, [part[0] for part in parts])
    factors = [jnp.exp(part[0] - high) for part in parts]
    total = sum(part[1] * factor for part, factor in zip(parts, factors))
    summed = sum(part[2] * factor for part, factor in zip(parts, factors))
    return (summed / total).astype(BF16)


def routed_body(
    hidden_in,
    qkv_weight,
    stretch_len,
    out_weight,
    ln1_gain,
    ln1_bias,
    up_weight,
    down_weight,
    ln2_gain,
    ln2_bias,
    dec_query,
    kv_cache,
    piece_req,
    piece_used,
):
    tok = lax.axis_index("tok")
    kv = lax.axis_index("kv")
    toks, kvs = lax.axis_size("tok"), lax.axis_size("kv")
    rows, width = hidden_in.shape
    place = jnp.stack([tok, kv]).astype(jnp.int32)
    eighth = lambda value: lax.dynamic_slice_in_dim(value, tok * (value.shape[0] // toks), value.shape[0] // toks, 0)

    queries = gathered_queries(dec_query)
    partial = decode_partial(queries, kv_cache, piece_req, piece_used)
    early = {2: queries[1:], 3: [partial]}
    from_below, from_above = [], []
    rising = falling = hidden_in
    for step in range(1, kvs):
        rising, falling = after(rising, *early.get(step, ())), after(falling, *early.get(step, ()))
        links = range(step - 1, kvs - 1)
        rising = lax.ppermute(rising, "kv", [(i, i + 1) for i in links])
        falling = lax.ppermute(falling, "kv", [(kvs - 1 - i, kvs - 2 - i) for i in links])
        from_below.append(rising)
        from_above.append(falling)

    feed_part = jnp.concatenate([eighth(up_weight), eighth(down_weight), eighth(out_weight)], axis=0)
    feed_inner = lax.ppermute(after(feed_part, from_below[1], from_above[1], partial), "kv", [(0, 2), (3, 1)])
    feed_outer = lax.ppermute(after(feed_part, rising, falling, feed_inner), "kv", [(1, 3), (2, 0)])
    out_part = after(eighth(out_weight), rising, falling)
    out_near, out_far = swapped(out_part, "kv", 1), swapped(out_part, "kv", 3)

    order = jnp.arange(stretch_len.shape[0])
    ends = jnp.sum(jnp.where(order[:, None] <= order[None, :], stretch_len[:, None], 0), axis=0, dtype=jnp.int32)
    starts = (ends - stretch_len)[None, :]
    ends = ends[None, :]

    shards = [after(hidden_in, feed_inner)] + from_below + from_above
    query, keyval, top, bottom = project(place, jnp.transpose(qkv_weight, (1, 0, 2)), shards)
    before = lax.ppermute(bottom, "tok", [(i, i + 1) for i in range(toks - 1)])
    behind = lax.ppermute(top, "tok", [(i + 1, i) for i in range(toks - 1)])
    window = (place, starts, ends, query, before, keyval, behind, rows)
    parts = [None] * kvs
    parts[3], parts[2] = attend_blocks(*window, (3, 2), "attend_far")
    depth = out_part.shape[0]
    inner = (kv == 1) | (kv == 2)
    feed_here = jnp.where(inner, feed_inner, after(feed_outer, parts[3], parts[2]))
    out_here = jnp.stack([out_near, feed_here[-depth:], out_far])
    feed_here = feed_here[:-depth]
    parts[3], parts[2] = swapped(parts[3], "kv", 3), swapped(parts[2], "kv", 2)
    out_x, out_y = swapped(out_here, "tok", 2), swapped(out_here, "tok", 4)
    window = (place, starts, ends, after(query, out_here), before, keyval, behind, rows)
    parts[1], parts[0] = attend_blocks(*window, (1, 0), "attend_near")
    feed_here = after(feed_here, parts[0])
    parts[1] = swapped(parts[1], "kv", 1)
    out_all = jnp.stack([out_here, out_x, out_y, swapped(after(out_y, parts[0], parts[3], parts[2]), "tok", 2)])
    out_core = swapped(out_all, "tok", 1)
    feed_x, feed_y = swapped(feed_here, "tok", 2), swapped(feed_here, "tok", 4)
    out_pieces = [((0, 2, 4, 6), out_all), ((1, 3, 5, 7), out_core)]
    normed = first_norm(place, hidden_in, out_weight, ln1_gain[None, :], ln1_bias[None, :], parts, out_pieces)

    partner = swapped(normed, "kv", 1)
    half = feed_here.shape[0] // 2
    far_up = swapped(after(feed_y, normed)[:half], "tok", 2)
    far_down = swapped(after(feed_x, normed)[half:], "tok", 4)
    held = jnp.concatenate([feed_here, feed_x, feed_y, far_up, far_down], axis=0)
    near_away = feed_near(partner, up_weight, down_weight)
    feed_pieces = (held, swapped(after(held, partner), "tok", 1))
    away = feed_far(place, partner, near_away, feed_pieces)
    arrived = swapped(away, "kv", 1)
    dec_parts = exchanged_partials(after(partial, away), dec_query.shape[0])
    mine = feed(place, after(normed, away), up_weight, down_weight, feed_pieces)
    prefill_out = finish(normed, mine, arrived, ln2_gain[None, :], ln2_bias[None, :])

    return prefill_out, merged_partials(after(tuple(dec_parts), mine))


def extended(value, sides, width):
    for axis, dim in sides:
        count, length = (lax.axis_size(axis), value.shape[dim])
        up = [(i, (i + 1) % count) for i in range(count - 1)]
        down = [(j, i) for i, j in up]
        last = lax.slice_in_dim(value, length - width, length, axis=dim)
        leading = lax.slice_in_dim(value, 0, width, axis=dim)
        before = lax.ppermute(last, axis, up)
        after = lax.ppermute(leading, axis, down)
        value = jnp.concatenate([before, value, after], axis=dim)
    return value


def merged(value, axis, join):
    pieces = jax.tree.map(lambda part: lax.all_gather(part, axis), value)
    head = jax.tree.map(lambda part: part[0], pieces)
    tail = jax.tree.map(lambda part: part[1:], pieces)
    subtotal, _ = lax.scan(lambda subtotal, section: (join(subtotal, section), None), head, tail)
    return subtotal


def segment_ids(row_ids, stretch_len):
    stretch_ends = jnp.cumsum(stretch_len)
    return jnp.sum((row_ids[:, None] >= stretch_ends[None, :]).astype(jnp.int32), axis=1)


def layer_norm(values, gain, bias):
    center = values - jnp.mean(values, axis=1, keepdims=True)
    spread = jnp.mean(center * center, axis=1, keepdims=True)
    return center * lax.rsqrt(spread + LN_EPS) * gain + bias


def merge_partials(earlier, later):
    highest = jnp.maximum(earlier[0], later[0])
    left_factor = jnp.exp(earlier[0] - highest)
    right_factor = jnp.exp(later[0] - highest)
    totals = earlier[1] * left_factor + later[1] * right_factor
    weighted = earlier[2] * left_factor[..., None] + later[2] * right_factor[..., None]
    return (highest, totals, weighted)


def row_folder(source, shard_rows):
    return jnp.dot(source, shard_rows, preferred_element_type=jnp.float32)


def general_body(
    hidden_in,
    qkv_weight,
    stretch_len,
    out_weight,
    ln1_gain,
    ln1_bias,
    up_weight,
    down_weight,
    ln2_gain,
    ln2_bias,
    dec_query,
    kv_cache,
    piece_req,
    piece_used,
):
    inv_scale = 1.0 / math.sqrt(HD)
    reach = WIN // 2
    local_width = qkv_weight.shape[2]
    head_count = local_width // HD
    flat_weight = qkv_weight.reshape(qkv_weight.shape[0], 3 * local_width)
    qkv_rows = jnp.dot(
        lax.all_gather(hidden_in, "kv", axis=0, tiled=True),
        flat_weight,
        preferred_element_type=jnp.float32,
    ).astype(jnp.bfloat16)
    row_count = qkv_rows.shape[0]
    query_rows = qkv_rows[:, :local_width]
    keyval_rows = qkv_rows[:, local_width:]
    padded = extended(keyval_rows, (("tok", 0),), reach)
    first_row = lax.axis_index("tok") * row_count
    total_rows = row_count * lax.axis_size("tok")
    qblock = min(512, row_count)
    span = qblock + 2 * reach
    block_count = row_count // qblock

    def attend(block_index):
        start = block_index * qblock
        query_ids = first_row + start + jnp.arange(qblock, dtype=jnp.int32)
        key_ids = first_row + start - reach + jnp.arange(span, dtype=jnp.int32)
        query_seg = segment_ids(query_ids, stretch_len)
        inside = (key_ids >= 0) & (key_ids < total_rows)
        key_seg = jnp.where(inside, segment_ids(key_ids, stretch_len), -1)
        allowed = (key_seg[None, :] == query_seg[:, None]) & (
            jnp.abs(key_ids[None, :] - query_ids[:, None]) <= reach
        )
        queries = lax.dynamic_slice_in_dim(query_rows, start, qblock, 0).reshape(
            qblock, head_count, HD
        )
        both = lax.dynamic_slice_in_dim(padded, start, span, 0)
        key_rows = both[:, :local_width].reshape(span, head_count, HD)
        value_rows = both[:, local_width:].reshape(span, head_count, HD)
        scores = (
            jnp.einsum("ihd,jhd->hij", queries, key_rows, preferred_element_type=jnp.float32)
            * inv_scale
        )
        scores = jnp.where(allowed[None], scores, NEG_FILL)
        row_max = jnp.max(scores, axis=2, keepdims=True)
        weights = jnp.where(allowed[None], jnp.exp(scores - row_max), 0.0)
        totals = jnp.sum(weights, axis=2)
        summed = jnp.einsum(
            "hij,jhd->ihd",
            weights.astype(jnp.bfloat16),
            value_rows,
            preferred_element_type=jnp.float32,
        )
        return (
            (summed / jnp.transpose(totals)[:, :, None])
            .astype(jnp.bfloat16)
            .reshape(qblock, local_width)
        )

    attention = lax.map(attend, jnp.arange(block_count, dtype=jnp.int32)).reshape(
        row_count, local_width
    )
    token_major = lax.all_to_all(attention, "kv", split_axis=0, concat_axis=1, tiled=True)
    projected = row_folder(token_major, lax.all_gather(out_weight, "kv", axis=0, tiled=True))
    normed = layer_norm(hidden_in.astype(jnp.float32) + projected, ln1_gain, ln1_bias).astype(
        jnp.bfloat16
    )
    units = jax.nn.gelu(
        jnp.dot(
            lax.all_gather(normed, "kv", axis=0, tiled=True),
            up_weight,
            preferred_element_type=jnp.float32,
        ),
        approximate=False,
    ).astype(jnp.bfloat16)
    ffn = lax.psum_scatter(
        jnp.dot(units, down_weight, preferred_element_type=jnp.float32).astype(jnp.bfloat16),
        "kv",
        scatter_dimension=0,
        tiled=True,
    ).astype(jnp.float32)
    prefill_out = layer_norm(normed.astype(jnp.float32) + ffn, ln2_gain, ln2_bias).astype(
        jnp.bfloat16
    )
    group_queries = lax.all_gather(dec_query, "kv", axis=0, tiled=True)
    request_count = group_queries.shape[0]
    owners = piece_req[0]
    filled = piece_used[0]
    slot_count = owners.shape[0]
    request_ids = jnp.arange(request_count, dtype=jnp.int32)
    selector = (owners[:, None] == request_ids[None, :]).astype(jnp.bfloat16)
    chosen = jnp.dot(selector, group_queries, preferred_element_type=jnp.float32).astype(
        jnp.bfloat16
    )
    chosen = chosen.reshape(slot_count, H, HD)
    cache_keys = kv_cache[0, 0].reshape(slot_count, PLEN, H, HD)
    cache_values = kv_cache[1, 0].reshape(slot_count, PLEN, H, HD)
    piece_scores = (
        jnp.einsum("phd,pthd->pht", chosen, cache_keys, preferred_element_type=jnp.float32)
        * inv_scale
    )
    active = jnp.arange(PLEN, dtype=jnp.int32)[None, :] < filled[:, None]
    piece_scores = jnp.where(active[:, None, :], piece_scores, NEG_FILL)
    piece_max = jnp.max(piece_scores, axis=2)
    piece_weights = jnp.where(
        active[:, None, :], jnp.exp(piece_scores - piece_max[:, :, None]), 0.0
    )
    piece_totals = jnp.sum(piece_weights, axis=2)
    partial_value = jnp.einsum(
        "pht,pthd->phd",
        piece_weights.astype(jnp.bfloat16),
        cache_values,
        preferred_element_type=jnp.float32,
    )
    member = (owners[None, :] == request_ids[:, None]) & (filled[None, :] > 0)
    highest = jnp.max(jnp.where(member[:, :, None], piece_max[None], NEG_FILL), axis=1)
    factor = jnp.where(member[:, :, None], jnp.exp(piece_max[None] - highest[:, None, :]), 0.0)
    denom = jnp.sum(factor * piece_totals[None], axis=1)
    weighted = jnp.einsum("rph,phd->rhd", factor, partial_value)
    own_requests = dec_query.shape[0]
    joined = merged((highest, denom, weighted), "kv", merge_partials)
    begin = lax.axis_index("kv") * own_requests
    final_denom = lax.dynamic_slice_in_dim(joined[1], begin, own_requests, 0)
    final_weighted = lax.dynamic_slice_in_dim(joined[2], begin, own_requests, 0)
    dec_out = (
        (final_weighted / final_denom[:, :, None])
        .astype(jnp.bfloat16)
        .reshape(own_requests, H * HD)
    )
    return (prefill_out, dec_out)


def solution(mesh):
    placed = (
        P(("tok", "kv"), None),
        P(None, None, "kv"),
        P(),
        P("kv", None),
        P(),
        P(),
        P(None, "kv"),
        P("kv", None),
        P(),
        P(),
        P(("tok", "kv"), None),
        P(None, "tok", "kv", None, None),
        P("tok", "kv"),
        P("tok", "kv"),
    )
    routed = mesh.shape["tok"] == 8 and mesh.shape["kv"] == 4
    return jax.shard_map(
        routed_body if routed else general_body,
        mesh=mesh,
        in_specs=placed,
        out_specs=(P(("tok", "kv"), None), P(("tok", "kv"), None)),
        check_vma=False,
    )
```

```python
import functools
import math

import jax
import jax.numpy as jnp
from jax import lax
from jax.experimental import pallas as pl
from jax.experimental.pallas import tpu as pltpu
from jax.sharding import PartitionSpec as P

H = 16
HD = 64
WIN = 512
PLEN = 128


NEG_FILL = -1e30
LN_EPS = 1e-05
BF16 = jnp.bfloat16
F32 = jnp.float32
STRIP = 32
MIB = 1024 * 1024
ANY = pl.BlockSpec(memory_space=pl.ANY)
VMEM = pl.BlockSpec(memory_space=pltpu.VMEM)
SMEM = pl.BlockSpec(memory_space=pltpu.SMEM)
SHORT = pl.CostEstimate(flops=1, bytes_accessed=1, transcendentals=0)


def swapped(value, axis, flip):
    count = lax.axis_size(axis)
    return lax.ppermute(value, axis, [(i, i ^ flip) for i in range(count)])


def after(value, *earlier):
    return lax.optimization_barrier((value,) + earlier)[0]


def normalized(values, gain, bias):
    center = values - jnp.mean(values, axis=1, keepdims=True)
    spread = jnp.mean(center * center, axis=1, keepdims=True)
    return center * lax.rsqrt(spread + LN_EPS) * gain + bias


def project_kernel(place_ref, weight_ref, *refs):
    shards, (query_ref, keyval_ref, top_ref, bottom_ref, rows_ref, sems) = refs[:-6], refs[-6:]
    kv = place_ref[1]
    count = top_ref.shape[0]
    steps = (len(shards) - 1) // 2
    width = weight_ref.shape[2]
    moves = [(shards[0], kv, None)]
    for step in range(1, steps + 1):
        moves.append((shards[step], kv - step, kv >= step))
        moves.append((shards[steps + step], kv + step, kv + step <= steps))

    def guarded(needed, act):
        if needed is None:
            act()
        else:
            pl.when(needed)(act)

    copies = []
    for index, (source, owner, needed) in enumerate(moves):
        safe = owner if needed is None else jnp.where(needed, owner, 0)
        at = pl.ds(pl.multiple_of(safe * count, count), count)
        copies.append((needed, pltpu.make_async_copy(source.at[0:count], rows_ref.at[at], sems.at[index])))
    for needed, copy in copies:
        guarded(needed, copy.start)
    for needed, copy in copies:
        guarded(needed, copy.wait)
    rows = rows_ref[...]
    query = jnp.dot(rows, weight_ref[0], preferred_element_type=F32) * (1.0 / math.sqrt(HD))
    query_ref[...] = query.astype(BF16)
    for part in range(2):
        at = slice(part * width, (part + 1) * width)
        keyval_ref[:, at] = jnp.dot(rows, weight_ref[part + 1], preferred_element_type=F32).astype(BF16)
    top_ref[...] = keyval_ref[:count]
    bottom_ref[...] = keyval_ref[steps * count :]


def project(place, weight, shards):
    rows, width = shards[0].shape
    heads_width = weight.shape[2]
    blocks = (len(shards) + 1) // 2
    edge = jax.ShapeDtypeStruct((rows, 2 * heads_width), BF16)
    return pl.pallas_call(
        project_kernel,
        out_shape=(
            jax.ShapeDtypeStruct((blocks * rows, heads_width), BF16),
            jax.ShapeDtypeStruct((blocks * rows, 2 * heads_width), BF16),
            edge,
            edge,
        ),
        in_specs=[SMEM, VMEM] + [ANY] * len(shards),
        out_specs=(VMEM,) * 4,
        scratch_shapes=[pltpu.VMEM((blocks * rows, width), BF16), pltpu.SemaphoreType.DMA((len(shards),))],
        compiler_params=pltpu.CompilerParams(vmem_limit_bytes=14 * MIB),
        cost_estimate=SHORT,
        name="project",
    )(place, weight, *shards)


def window_bias(first, count, starts, ends):
    reach = WIN // 2
    query = first + lax.broadcasted_iota(jnp.int32, (count, 1), 0)
    low = jnp.max(jnp.where(starts <= query, starts, 0), axis=1, keepdims=True)
    high = jnp.min(jnp.where(ends > query, ends, 1 << 30), axis=1, keepdims=True)
    low = jnp.maximum(low, query - reach)
    high = jnp.minimum(high, query + reach + 1)
    key = first - count + lax.broadcasted_iota(jnp.int32, (count, 3 * count), 1)
    return jnp.where((key >= low) & (key < high), 0.0, NEG_FILL)


def attend(query, keyval_ref, bias_ref, scores_ref, weights_ref, out_ref):
    count, width = query.shape
    lane = lax.broadcasted_iota(jnp.int32, (count, 2 * HD), 1)
    for start in range(0, width, 2 * HD):
        values = keyval_ref[:, width + start : width + start + 2 * HD]
        halves = []
        for side in range(2):
            head = start // HD + side
            inside = (lane < HD) if side == 0 else (lane >= HD)
            only = jnp.where(inside, query[:, start : start + 2 * HD], jnp.zeros((), BF16))
            scores_ref[head] = lax.dot_general(
                only, keyval_ref[:, start : start + 2 * HD], (((1,), (1,)), ((), ())), preferred_element_type=F32
            )
            totals = []
            for row in range(0, count, STRIP):
                at = slice(row, row + STRIP)
                scores = scores_ref[head, at] + bias_ref[at]
                weights = jnp.exp(scores - jnp.max(scores, axis=1, keepdims=True))
                totals.append(jnp.sum(weights, axis=1, keepdims=True))
                weights_ref[head, at] = weights.astype(BF16)
            summed = jnp.dot(weights_ref[head], values, preferred_element_type=F32)
            halves.append(summed / jnp.concatenate(totals, axis=0))
        out_ref[:, start : start + 2 * HD] = jnp.where(lane < HD, halves[0], halves[1]).astype(BF16)


def attend_kernel(flips, place_ref, starts_ref, ends_ref, query_ref, before_ref, keyval_ref, behind_ref, *refs):
    outs = refs[: len(flips)]
    window_ref, bias_ref, scores_ref, weights_ref, sems = refs[len(flips) :]
    tok, kv = place_ref[0], place_ref[1]
    count = outs[0].shape[0]
    blocks = query_ref.shape[0] // count
    copies = []
    for index, flip in enumerate(flips):
        block = kv ^ flip
        for part in range(3):
            target = window_ref.at[index, part * count : (part + 1) * count]
            sem = sems.at[index, part]
            at = block + part - 1
            inner = (at >= 0) & (at < blocks)
            safe = jnp.where(inner, at, 0)
            source = keyval_ref.at[pl.ds(pl.multiple_of(safe * count, count), count)]
            copies.append((index, inner, pltpu.make_async_copy(source, target, sem)))
            if part == 0:
                copies.append((index, at < 0, pltpu.make_async_copy(before_ref, target, sem)))
            if part == 2:
                copies.append((index, at >= blocks, pltpu.make_async_copy(behind_ref, target, sem)))
    for _, needed, copy in copies:
        pl.when(needed)(copy.start)
    for index, flip in enumerate(flips):
        block = kv ^ flip
        first = (tok * blocks + block) * count
        bias_ref[...] = window_bias(first, count, starts_ref[...], ends_ref[...])
        for owner, needed, copy in copies:
            if owner == index:
                pl.when(needed)(copy.wait)
        query = query_ref[pl.ds(pl.multiple_of(block * count, count), count)]
        attend(query, window_ref.at[index], bias_ref, scores_ref, weights_ref, outs[index])


def attend_blocks(place, starts, ends, query, before, keyval, behind, rows, flips, name):
    heads_width = query.shape[1]
    return pl.pallas_call(
        functools.partial(attend_kernel, flips),
        out_shape=tuple(jax.ShapeDtypeStruct((rows, heads_width), BF16) for _ in flips),
        in_specs=[SMEM, VMEM, VMEM, VMEM, ANY, ANY, ANY],
        out_specs=(VMEM,) * len(flips),
        scratch_shapes=[
            pltpu.VMEM((len(flips), 3 * rows, 2 * heads_width), BF16),
            pltpu.VMEM((rows, 3 * rows), F32),
            pltpu.VMEM((heads_width // HD, rows, 3 * rows), F32),
            pltpu.VMEM((heads_width // HD, rows, 3 * rows), BF16),
            pltpu.SemaphoreType.DMA((len(flips), 3)),
        ],
        compiler_params=pltpu.CompilerParams(vmem_limit_bytes=14 * MIB),
        cost_estimate=SHORT,
        name=name,
    )(place, starts, ends, query, before, keyval, behind)


def first_norm_kernel(layout, place_ref, hidden_ref, own_out_ref, gain_ref, bias_ref, *refs):
    parts, pieces = refs[: -5 - len(layout)], refs[-5 - len(layout) : -5]
    normed_ref, all_ref, weight_ref, mixed_ref, sems = refs[-5:]
    tok = place_ref[0]
    quarters, heads_width, width = weight_ref.shape
    copies = [pltpu.make_async_copy(own_out_ref, weight_ref.at[0], sems.at[0])]
    for flips, piece in zip(layout, pieces):
        for index, flip in enumerate(flips):
            depth = piece.shape[2]
            at = pl.multiple_of((tok ^ flip) * depth, depth)
            target = weight_ref.at[1:quarters, pl.ds(at, depth)]
            copies.append(pltpu.make_async_copy(piece.at[index], target, sems.at[len(copies)]))
    for copy in copies:
        copy.start()
    for flip, part_ref in enumerate(parts):
        all_ref[:, flip * heads_width : (flip + 1) * heads_width] = part_ref[...]
    for copy in copies:
        copy.wait()
    weight = weight_ref[...].reshape(quarters * heads_width, width)
    mixed_ref[...] = jnp.dot(all_ref[...], weight, preferred_element_type=F32)
    for row in range(0, hidden_ref.shape[0], STRIP):
        at = slice(row, row + STRIP)
        mixed = hidden_ref[at].astype(F32) + mixed_ref[at]
        normed_ref[at] = normalized(mixed, gain_ref[...], bias_ref[...]).astype(BF16)


def first_norm(place, hidden, own_out, gain, bias, parts, pieces):
    rows, width = hidden.shape
    heads_width = own_out.shape[0]
    layout = tuple(flips for flips, _ in pieces)
    return pl.pallas_call(
        functools.partial(first_norm_kernel, layout),
        out_shape=jax.ShapeDtypeStruct((rows, width), BF16),
        in_specs=[SMEM, VMEM, ANY, VMEM, VMEM] + [VMEM] * len(parts) + [ANY] * len(pieces),
        out_specs=VMEM,
        scratch_shapes=[
            pltpu.VMEM((rows, width), BF16),
            pltpu.VMEM((len(parts), heads_width, width), BF16),
            pltpu.VMEM((rows, width), F32),
            pltpu.SemaphoreType.DMA((1 + sum(len(flips) for flips in layout),)),
        ],
        compiler_params=pltpu.CompilerParams(vmem_limit_bytes=11 * MIB),
        cost_estimate=SHORT,
        name="first_norm",
    )(place, hidden, own_out, gain, bias, *parts, *[value for _, value in pieces])


def gelu(values):
    return 0.5 * values * (1.0 + lax.erf(values * math.sqrt(0.5)))


CHUNK = 512


def feed_chunk(rows, up, down_ref, wide_ref, units_ref):
    wide_ref[...] = jnp.dot(rows, up, preferred_element_type=F32)
    for row in range(0, rows.shape[0], STRIP):
        strip = slice(row, row + STRIP)
        units_ref[strip] = gelu(wide_ref[strip]).astype(BF16)
    return jnp.dot(units_ref[...], down_ref[...], preferred_element_type=F32)


def far_copies(tok, held_ref, core_ref, up_ref, down_ref, sems):
    block = 128
    copies = []
    for side, piece in enumerate((held_ref, core_ref)):
        for index in range(4):
            at = pl.ds(pl.multiple_of((tok ^ (2 * index + side)) * block, block), block)
            for part, target in enumerate((up_ref, down_ref)):
                source = piece.at[pl.ds((2 * index + part) * block, block)]
                copies.append(pltpu.make_async_copy(source, target.at[at], sems.at[len(copies)]))
    return copies


def feed_near_kernel(rows_ref, up_ref, down_ref, sum_ref, wide_ref, units_ref):
    rows = rows_ref[...]
    for index in range(up_ref.shape[1] // CHUNK):
        at = slice(index * CHUNK, (index + 1) * CHUNK)
        product = feed_chunk(rows, up_ref[:, at], down_ref.at[at], wide_ref.at[index % 2], units_ref.at[index % 2])
        if index == 0:
            sum_ref[...] = product
        else:
            sum_ref[...] += product


def feed_far_kernel(
    place_ref, rows_ref, near_ref, held_ref, core_ref, sum_ref, up_ref, down_ref, wide_ref, units_ref, total_ref, sems
):
    copies = far_copies(place_ref[0], held_ref, core_ref, up_ref, down_ref, sems)
    for copy in copies:
        copy.start()
    rows = rows_ref[...]
    total_ref[...] = near_ref[...]
    for copy in copies:
        copy.wait()
    for index in range(up_ref.shape[1] // CHUNK):
        at = slice(index * CHUNK, (index + 1) * CHUNK)
        slot = index % 2
        total_ref[...] += feed_chunk(rows, up_ref[:, at], down_ref.at[at], wide_ref.at[slot], units_ref.at[slot])
    sum_ref[...] = total_ref[...].astype(sum_ref.dtype)


def feed_kernel(
    place_ref, rows_ref, up_near_ref, down_near_ref, held_ref, core_ref, sum_ref, up_ref, down_ref, wide_ref, units_ref, sems
):
    copies = far_copies(place_ref[0], held_ref, core_ref, up_ref, down_ref, sems)
    for copy in copies:
        copy.start()
    feed_near_kernel(rows_ref, up_near_ref, down_near_ref, sum_ref, wide_ref, units_ref)
    rows = rows_ref[...]
    for copy in copies:
        copy.wait()
    for index in range(up_ref.shape[1] // CHUNK):
        at = slice(index * CHUNK, (index + 1) * CHUNK)
        slot = index % 2
        sum_ref[...] += feed_chunk(rows, up_ref[:, at], down_ref.at[at], wide_ref.at[slot], units_ref.at[slot])


def feed_scratch(count):
    return [pltpu.VMEM((2, count, CHUNK), F32), pltpu.VMEM((2, count, CHUNK), BF16)]


def feed_near(rows, up_weight, down_weight):
    return pl.pallas_call(
        feed_near_kernel,
        out_shape=jax.ShapeDtypeStruct(rows.shape, F32),
        in_specs=[VMEM] * 3,
        out_specs=VMEM,
        scratch_shapes=feed_scratch(rows.shape[0]),
        compiler_params=pltpu.CompilerParams(vmem_limit_bytes=14 * MIB),
        cost_estimate=SHORT,
        name="feed_near",
    )(rows, up_weight, down_weight)


def feed_far(place, rows, near, pieces):
    count, width = rows.shape
    units = pieces[0].shape[0]
    return pl.pallas_call(
        feed_far_kernel,
        out_shape=jax.ShapeDtypeStruct((count, width), BF16),
        in_specs=[SMEM] + [VMEM] * 2 + [ANY] * 2,
        out_specs=VMEM,
        scratch_shapes=[pltpu.VMEM((width, units), BF16), pltpu.VMEM((units, width), BF16)]
        + feed_scratch(count)
        + [pltpu.VMEM((count, width), F32), pltpu.SemaphoreType.DMA((16,))],
        compiler_params=pltpu.CompilerParams(vmem_limit_bytes=14 * MIB),
        cost_estimate=SHORT,
        name="feed_far",
    )(place, rows, near, *pieces)


def feed(place, rows, up_weight, down_weight, pieces):
    count, width = rows.shape
    units = up_weight.shape[1]
    return pl.pallas_call(
        feed_kernel,
        out_shape=jax.ShapeDtypeStruct((count, width), F32),
        in_specs=[SMEM] + [VMEM] * 3 + [ANY] * 2,
        out_specs=VMEM,
        scratch_shapes=[pltpu.VMEM((width, units), BF16), pltpu.VMEM((units, width), BF16)]
        + feed_scratch(count)
        + [pltpu.SemaphoreType.DMA((16,))],
        compiler_params=pltpu.CompilerParams(vmem_limit_bytes=18 * MIB),
        cost_estimate=SHORT,
        name="feed_own",
    )(place, rows, up_weight, down_weight, *pieces)


def finish_kernel(normed_ref, near_ref, far_ref, gain_ref, bias_ref, out_ref):
    for row in range(0, normed_ref.shape[0], STRIP):
        at = slice(row, row + STRIP)
        mixed = normed_ref[at].astype(F32) + near_ref[at] + far_ref[at].astype(F32)
        out_ref[at] = normalized(mixed, gain_ref[...], bias_ref[...]).astype(out_ref.dtype)


def finish(normed, near, far, gain, bias):
    return pl.pallas_call(
        finish_kernel,
        out_shape=jax.ShapeDtypeStruct(normed.shape, BF16),
        in_specs=[VMEM] * 5,
        out_specs=VMEM,
        compiler_params=pltpu.CompilerParams(vmem_limit_bytes=6 * MIB),
        name="finish",
    )(normed, near, far, gain, bias)


def decode_kernel(source_ref, slot_ref, filled_ref, query_ref, cache_ref, out_ref, high_ref, total_ref, sum_ref):
    step = pl.program_id(0)

    @pl.when(step == 0)
    def _():
        high_ref[...] = jnp.full(high_ref.shape, NEG_FILL, F32)
        total_ref[...] = jnp.zeros_like(total_ref)
        sum_ref[...] = jnp.zeros_like(sum_ref)

    row = slot_ref[step]
    filled = filled_ref[step]
    width = query_ref.shape[1]
    head = lax.broadcasted_iota(jnp.int32, (H, width), 0)
    inside = head == lax.broadcasted_iota(jnp.int32, (H, width), 1) // HD
    query = jnp.where(inside, query_ref[pl.ds(source_ref[step], 1), :], 0.0).astype(BF16)
    scores = lax.dot_general(query, cache_ref[0, 0, 0], (((1,), (1,)), ((), ())), preferred_element_type=F32)
    live = lax.broadcasted_iota(jnp.int32, scores.shape, 1) < filled
    scores = jnp.where(live, scores * (1.0 / math.sqrt(HD)), NEG_FILL)
    high = jnp.max(scores, axis=1, keepdims=True)
    weights = jnp.where(live, jnp.exp(scores - high), 0.0)
    total = jnp.sum(weights, axis=1, keepdims=True)
    summed = jnp.dot(weights.astype(BF16), cache_ref[1, 0, 0], preferred_element_type=F32)
    along = lambda column: jnp.sum(jnp.where(inside, column, 0.0), axis=0, keepdims=True)
    high, total, summed = along(high), along(total), along(summed)
    used = filled > 0
    at = pl.ds(row, 1)
    old = high_ref[at, :]
    new = jnp.where(used, jnp.maximum(old, high), old)
    left = jnp.exp(old - new)
    right = jnp.where(used, jnp.exp(high - new), 0.0)
    high_ref[at, :] = new
    total_ref[at, :] = total_ref[at, :] * left + total * right
    sum_ref[at, :] = sum_ref[at, :] * left + summed * right

    @pl.when(step == pl.num_programs(0) - 1)
    def _():
        out_ref[0] = high_ref[...]
        out_ref[1] = total_ref[...]
        out_ref[2] = sum_ref[...]


def decode(sources, slots, filled, queries, requests, kv_cache):
    count, width = queries.shape
    pieces = kv_cache.shape[2]
    state = pltpu.VMEM((requests, width), F32)
    return pl.pallas_call(
        decode_kernel,
        grid=(pieces,),
        out_shape=jax.ShapeDtypeStruct((3, requests, width), F32),
        in_specs=[
            SMEM,
            SMEM,
            SMEM,
            pl.BlockSpec((count, width), lambda i: (0, 0)),
            pl.BlockSpec((2, 1, 1, PLEN, width), lambda i: (0, 0, i, 0, 0)),
        ],
        out_specs=pl.BlockSpec((3, requests, width), lambda i: (0, 0, 0)),
        scratch_shapes=[state, state, state],
        compiler_params=pltpu.CompilerParams(vmem_limit_bytes=8 * MIB),
        cost_estimate=SHORT,
        name="decode",
    )(sources, slots, filled, queries, kv_cache)


def decode_partial(queries, own, kv_cache, piece_req, piece_used):
    kv = lax.axis_index("kv")
    owners = piece_req[0]
    home = owners // own
    place = jnp.where(home <= kv, kv - home, lax.axis_size("kv") - 1 + home - kv)
    sources = place * own + owners % own
    slots = (home ^ kv) * own + owners % own
    return decode(sources, slots, piece_used[0], queries, own * lax.axis_size("kv"), kv_cache)


def exchanged_partials(partial, own):
    parts = [partial[:, :own]]
    for flip in range(1, lax.axis_size("kv")):
        parts.append(swapped(partial[:, flip * own : (flip + 1) * own], "kv", flip))
    return parts


def merged_partials(parts):
    high = functools.reduce(jnp.maximum, [part[0] for part in parts])
    factors = [jnp.exp(part[0] - high) for part in parts]
    total = sum(part[1] * factor for part, factor in zip(parts, factors))
    summed = sum(part[2] * factor for part, factor in zip(parts, factors))
    return (summed / total).astype(BF16)


def routed_body(
    hidden_in,
    qkv_weight,
    stretch_len,
    out_weight,
    ln1_gain,
    ln1_bias,
    up_weight,
    down_weight,
    ln2_gain,
    ln2_bias,
    dec_query,
    kv_cache,
    piece_req,
    piece_used,
):
    tok = lax.axis_index("tok")
    kv = lax.axis_index("kv")
    toks, kvs = lax.axis_size("tok"), lax.axis_size("kv")
    rows, width = hidden_in.shape
    place = jnp.stack([tok, kv]).astype(jnp.int32)
    eighth = lambda value: lax.dynamic_slice_in_dim(value, tok * (value.shape[0] // toks), value.shape[0] // toks, 0)

    from_below, from_above = [], []
    rising = falling = jnp.concatenate([hidden_in, dec_query], axis=0)
    for step in range(1, kvs):
        links = range(step - 1, kvs - 1)
        rising = lax.ppermute(rising, "kv", [(i, i + 1) for i in links])
        falling = lax.ppermute(falling, "kv", [(kvs - 1 - i, kvs - 2 - i) for i in links])
        from_below.append(rising)
        from_above.append(falling)

    out_part = eighth(out_weight)
    depth = out_part.shape[0]
    out_one = swapped(after(out_part, from_below[0], from_above[0]), "kv", 1)
    out_two = swapped(after(jnp.concatenate([out_part, out_one], axis=0), from_below[1], from_above[1]), "kv", 2)
    out_here = jnp.concatenate([out_one, out_two], axis=0).reshape(kvs - 1, depth, width)
    feed_part = jnp.concatenate([eighth(up_weight), eighth(down_weight)], axis=0)
    feed_inner = lax.ppermute(after(feed_part, from_below[1], from_above[1]), "kv", [(0, 2), (3, 1)])
    feed_outer = lax.ppermute(after(feed_part, rising, falling, feed_inner, out_two), "kv", [(1, 3), (2, 0)])

    order = jnp.arange(stretch_len.shape[0])
    ends = jnp.sum(jnp.where(order[:, None] <= order[None, :], stretch_len[:, None], 0), axis=0, dtype=jnp.int32)
    starts = (ends - stretch_len)[None, :]
    ends = ends[None, :]

    shards = [after(hidden_in, feed_inner, out_two)] + from_below + from_above
    query, keyval, top, bottom = project(place, jnp.transpose(qkv_weight, (1, 0, 2)), shards)
    before = lax.ppermute(bottom, "tok", [(i, i + 1) for i in range(toks - 1)])
    behind = lax.ppermute(top, "tok", [(i + 1, i) for i in range(toks - 1)])
    out_here = after(out_here, query)
    out_x, out_y = swapped(out_here, "tok", 2), swapped(out_here, "tok", 4)
    window = (place, starts, ends, after(query, out_x, out_y), before, keyval, behind, rows)
    parts = [None] * kvs
    parts[3], parts[2] = attend_blocks(*window, (3, 2), "attend_far")
    out_all = jnp.stack([out_here, out_x, out_y, swapped(out_y, "tok", 2)])
    out_core = swapped(after(out_all, parts[3]), "tok", 1)
    inner = (kv == 1) | (kv == 2)
    feed_here = jnp.where(inner, feed_inner, after(feed_outer, parts[3], parts[2]))
    parts[3], parts[2] = swapped(parts[3], "kv", 3), swapped(parts[2], "kv", 2)
    window = (place, starts, ends, after(query, feed_here), before, keyval, behind, rows)
    parts[1], parts[0] = attend_blocks(*window, (1, 0), "attend_near")
    parts[1] = swapped(parts[1], "kv", 1)
    feed_x, feed_y = swapped(feed_here, "tok", 2), swapped(feed_here, "tok", 4)
    out_pieces = [((0, 2, 4, 6), out_all), ((1, 3, 5, 7), out_core)]
    normed = first_norm(place, hidden_in, out_weight, ln1_gain[None, :], ln1_bias[None, :], parts, out_pieces)

    partner = swapped(normed, "kv", 1)
    half = feed_here.shape[0] // 2
    far_up = swapped(after(feed_y, normed)[:half], "tok", 2)
    far_down = swapped(after(feed_x, normed)[half:], "tok", 4)
    own = dec_query.shape[0]
    queries = jnp.concatenate([dec_query] + [shard[rows:] for shard in from_below + from_above], axis=0)
    queries = after(queries.astype(F32), normed)
    partial = decode_partial(queries, own, kv_cache, piece_req, piece_used)
    dec_parts = exchanged_partials(after(partial, partner), own)
    held = jnp.concatenate([feed_here, feed_x, feed_y, after(far_up, partial), far_down], axis=0)
    near_away = feed_near(partner, up_weight, down_weight)
    near_away = after(near_away, *dec_parts)
    feed_pieces = (held, swapped(after(held, partner), "tok", 1))
    away = feed_far(place, partner, near_away, feed_pieces)
    arrived = swapped(away, "kv", 1)
    mine = feed(place, after(normed, away), up_weight, down_weight, feed_pieces)
    prefill_out = finish(normed, mine, arrived, ln2_gain[None, :], ln2_bias[None, :])

    return prefill_out, merged_partials(after(tuple(dec_parts), away))


def extended(value, sides, width):
    for axis, dim in sides:
        count, length = (lax.axis_size(axis), value.shape[dim])
        up = [(i, (i + 1) % count) for i in range(count - 1)]
        down = [(j, i) for i, j in up]
        last = lax.slice_in_dim(value, length - width, length, axis=dim)
        leading = lax.slice_in_dim(value, 0, width, axis=dim)
        before = lax.ppermute(last, axis, up)
        after = lax.ppermute(leading, axis, down)
        value = jnp.concatenate([before, value, after], axis=dim)
    return value


def merged(value, axis, join):
    pieces = jax.tree.map(lambda part: lax.all_gather(part, axis), value)
    head = jax.tree.map(lambda part: part[0], pieces)
    tail = jax.tree.map(lambda part: part[1:], pieces)
    subtotal, _ = lax.scan(lambda subtotal, section: (join(subtotal, section), None), head, tail)
    return subtotal


def segment_ids(row_ids, stretch_len):
    stretch_ends = jnp.cumsum(stretch_len)
    return jnp.sum((row_ids[:, None] >= stretch_ends[None, :]).astype(jnp.int32), axis=1)


def layer_norm(values, gain, bias):
    center = values - jnp.mean(values, axis=1, keepdims=True)
    spread = jnp.mean(center * center, axis=1, keepdims=True)
    return center * lax.rsqrt(spread + LN_EPS) * gain + bias


def merge_partials(earlier, later):
    highest = jnp.maximum(earlier[0], later[0])
    left_factor = jnp.exp(earlier[0] - highest)
    right_factor = jnp.exp(later[0] - highest)
    totals = earlier[1] * left_factor + later[1] * right_factor
    weighted = earlier[2] * left_factor[..., None] + later[2] * right_factor[..., None]
    return (highest, totals, weighted)


def row_folder(source, shard_rows):
    return jnp.dot(source, shard_rows, preferred_element_type=jnp.float32)


def general_body(
    hidden_in,
    qkv_weight,
    stretch_len,
    out_weight,
    ln1_gain,
    ln1_bias,
    up_weight,
    down_weight,
    ln2_gain,
    ln2_bias,
    dec_query,
    kv_cache,
    piece_req,
    piece_used,
):
    inv_scale = 1.0 / math.sqrt(HD)
    reach = WIN // 2
    local_width = qkv_weight.shape[2]
    head_count = local_width // HD
    flat_weight = qkv_weight.reshape(qkv_weight.shape[0], 3 * local_width)
    qkv_rows = jnp.dot(
        lax.all_gather(hidden_in, "kv", axis=0, tiled=True),
        flat_weight,
        preferred_element_type=jnp.float32,
    ).astype(jnp.bfloat16)
    row_count = qkv_rows.shape[0]
    query_rows = qkv_rows[:, :local_width]
    keyval_rows = qkv_rows[:, local_width:]
    padded = extended(keyval_rows, (("tok", 0),), reach)
    first_row = lax.axis_index("tok") * row_count
    total_rows = row_count * lax.axis_size("tok")
    qblock = min(512, row_count)
    span = qblock + 2 * reach
    block_count = row_count // qblock

    def attend(block_index):
        start = block_index * qblock
        query_ids = first_row + start + jnp.arange(qblock, dtype=jnp.int32)
        key_ids = first_row + start - reach + jnp.arange(span, dtype=jnp.int32)
        query_seg = segment_ids(query_ids, stretch_len)
        inside = (key_ids >= 0) & (key_ids < total_rows)
        key_seg = jnp.where(inside, segment_ids(key_ids, stretch_len), -1)
        allowed = (key_seg[None, :] == query_seg[:, None]) & (
            jnp.abs(key_ids[None, :] - query_ids[:, None]) <= reach
        )
        queries = lax.dynamic_slice_in_dim(query_rows, start, qblock, 0).reshape(
            qblock, head_count, HD
        )
        both = lax.dynamic_slice_in_dim(padded, start, span, 0)
        key_rows = both[:, :local_width].reshape(span, head_count, HD)
        value_rows = both[:, local_width:].reshape(span, head_count, HD)
        scores = (
            jnp.einsum("ihd,jhd->hij", queries, key_rows, preferred_element_type=jnp.float32)
            * inv_scale
        )
        scores = jnp.where(allowed[None], scores, NEG_FILL)
        row_max = jnp.max(scores, axis=2, keepdims=True)
        weights = jnp.where(allowed[None], jnp.exp(scores - row_max), 0.0)
        totals = jnp.sum(weights, axis=2)
        summed = jnp.einsum(
            "hij,jhd->ihd",
            weights.astype(jnp.bfloat16),
            value_rows,
            preferred_element_type=jnp.float32,
        )
        return (
            (summed / jnp.transpose(totals)[:, :, None])
            .astype(jnp.bfloat16)
            .reshape(qblock, local_width)
        )

    attention = lax.map(attend, jnp.arange(block_count, dtype=jnp.int32)).reshape(
        row_count, local_width
    )
    token_major = lax.all_to_all(attention, "kv", split_axis=0, concat_axis=1, tiled=True)
    projected = row_folder(token_major, lax.all_gather(out_weight, "kv", axis=0, tiled=True))
    normed = layer_norm(hidden_in.astype(jnp.float32) + projected, ln1_gain, ln1_bias).astype(
        jnp.bfloat16
    )
    units = jax.nn.gelu(
        jnp.dot(
            lax.all_gather(normed, "kv", axis=0, tiled=True),
            up_weight,
            preferred_element_type=jnp.float32,
        ),
        approximate=False,
    ).astype(jnp.bfloat16)
    ffn = lax.psum_scatter(
        jnp.dot(units, down_weight, preferred_element_type=jnp.float32).astype(jnp.bfloat16),
        "kv",
        scatter_dimension=0,
        tiled=True,
    ).astype(jnp.float32)
    prefill_out = layer_norm(normed.astype(jnp.float32) + ffn, ln2_gain, ln2_bias).astype(
        jnp.bfloat16
    )
    group_queries = lax.all_gather(dec_query, "kv", axis=0, tiled=True)
    request_count = group_queries.shape[0]
    owners = piece_req[0]
    filled = piece_used[0]
    slot_count = owners.shape[0]
    request_ids = jnp.arange(request_count, dtype=jnp.int32)
    selector = (owners[:, None] == request_ids[None, :]).astype(jnp.bfloat16)
    chosen = jnp.dot(selector, group_queries, preferred_element_type=jnp.float32).astype(
        jnp.bfloat16
    )
    chosen = chosen.reshape(slot_count, H, HD)
    cache_keys = kv_cache[0, 0].reshape(slot_count, PLEN, H, HD)
    cache_values = kv_cache[1, 0].reshape(slot_count, PLEN, H, HD)
    piece_scores = (
        jnp.einsum("phd,pthd->pht", chosen, cache_keys, preferred_element_type=jnp.float32)
        * inv_scale
    )
    active = jnp.arange(PLEN, dtype=jnp.int32)[None, :] < filled[:, None]
    piece_scores = jnp.where(active[:, None, :], piece_scores, NEG_FILL)
    piece_max = jnp.max(piece_scores, axis=2)
    piece_weights = jnp.where(
        active[:, None, :], jnp.exp(piece_scores - piece_max[:, :, None]), 0.0
    )
    piece_totals = jnp.sum(piece_weights, axis=2)
    partial_value = jnp.einsum(
        "pht,pthd->phd",
        piece_weights.astype(jnp.bfloat16),
        cache_values,
        preferred_element_type=jnp.float32,
    )
    member = (owners[None, :] == request_ids[:, None]) & (filled[None, :] > 0)
    highest = jnp.max(jnp.where(member[:, :, None], piece_max[None], NEG_FILL), axis=1)
    factor = jnp.where(member[:, :, None], jnp.exp(piece_max[None] - highest[:, None, :]), 0.0)
    denom = jnp.sum(factor * piece_totals[None], axis=1)
    weighted = jnp.einsum("rph,phd->rhd", factor, partial_value)
    own_requests = dec_query.shape[0]
    joined = merged((highest, denom, weighted), "kv", merge_partials)
    begin = lax.axis_index("kv") * own_requests
    final_denom = lax.dynamic_slice_in_dim(joined[1], begin, own_requests, 0)
    final_weighted = lax.dynamic_slice_in_dim(joined[2], begin, own_requests, 0)
    dec_out = (
        (final_weighted / final_denom[:, :, None])
        .astype(jnp.bfloat16)
        .reshape(own_requests, H * HD)
    )
    return (prefill_out, dec_out)


def solution(mesh):
    placed = (
        P(("tok", "kv"), None),
        P(None, None, "kv"),
        P(),
        P("kv", None),
        P(),
        P(),
        P(None, "kv"),
        P("kv", None),
        P(),
        P(),
        P(("tok", "kv"), None),
        P(None, "tok", "kv", None, None),
        P("tok", "kv"),
        P("tok", "kv"),
    )
    routed = mesh.shape["tok"] == 8 and mesh.shape["kv"] == 4
    return jax.shard_map(
        routed_body if routed else general_body,
        mesh=mesh,
        in_specs=placed,
        out_specs=(P(("tok", "kv"), None), P(("tok", "kv"), None)),
        check_vma=False,
    )
```

```python
import functools
import math

import jax
import jax.numpy as jnp
from jax import lax
from jax.experimental import pallas as pl
from jax.experimental.pallas import tpu as pltpu
from jax.sharding import PartitionSpec as P

H = 16
HD = 64
WIN = 512
PLEN = 128


NEG_FILL = -1e30
LN_EPS = 1e-05
BF16 = jnp.bfloat16
F32 = jnp.float32
STRIP = 32
MIB = 1024 * 1024
ANY = pl.BlockSpec(memory_space=pl.ANY)
VMEM = pl.BlockSpec(memory_space=pltpu.VMEM)
SMEM = pl.BlockSpec(memory_space=pltpu.SMEM)
SHORT = pl.CostEstimate(flops=1, bytes_accessed=1, transcendentals=0)


def swapped(value, axis, flip):
    count = lax.axis_size(axis)
    return lax.ppermute(value, axis, [(i, i ^ flip) for i in range(count)])


def after(value, *earlier):
    return lax.optimization_barrier((value,) + earlier)[0]


def normalized(values, gain, bias):
    center = values - jnp.mean(values, axis=1, keepdims=True)
    spread = jnp.mean(center * center, axis=1, keepdims=True)
    return center * lax.rsqrt(spread + LN_EPS) * gain + bias


def project_kernel(place_ref, weight_ref, *refs):
    shards, (query_ref, keyval_ref, top_ref, bottom_ref, riders_ref, rows_ref, sems, rider_sems) = refs[:-8], refs[-8:]
    kv = place_ref[1]
    count = top_ref.shape[0]
    steps = (len(shards) - 1) // 2
    width = weight_ref.shape[2]
    depth = riders_ref.shape[1]
    moves = [(shards[0], kv, None, None)]
    for step in range(1, steps + 1):
        moves.append((shards[step], kv - step, kv >= step, steps - step))
        moves.append((shards[steps + step], kv + step, kv + step <= steps, step - 1))

    def guarded(needed, act):
        if needed is None:
            act()
        else:
            pl.when(needed)(act)

    copies = []
    for index, (source, owner, needed, turn) in enumerate(moves):
        safe = owner if needed is None else jnp.where(needed, owner, 0)
        at = pl.ds(pl.multiple_of(safe * count, count), count)
        copies.append((needed, pltpu.make_async_copy(source.at[0:count], rows_ref.at[at], sems.at[index])))
        if turn is not None:
            rider = source.at[count : count + depth]
            copies.append((needed, pltpu.make_async_copy(rider, riders_ref.at[turn], rider_sems.at[index])))
    for needed, copy in copies:
        guarded(needed, copy.start)
    for needed, copy in copies:
        guarded(needed, copy.wait)
    rows = rows_ref[...]
    query = jnp.dot(rows, weight_ref[0], preferred_element_type=F32) * (1.0 / math.sqrt(HD))
    query_ref[...] = query.astype(BF16)
    for part in range(2):
        at = slice(part * width, (part + 1) * width)
        keyval_ref[:, at] = jnp.dot(rows, weight_ref[part + 1], preferred_element_type=F32).astype(BF16)
    top_ref[...] = keyval_ref[:count]
    bottom_ref[...] = keyval_ref[steps * count :]


def project(place, weight, shards, depth):
    rows, width = shards[0].shape
    heads_width = weight.shape[2]
    blocks = (len(shards) + 1) // 2
    edge = jax.ShapeDtypeStruct((rows, 2 * heads_width), BF16)
    return pl.pallas_call(
        project_kernel,
        out_shape=(
            jax.ShapeDtypeStruct((blocks * rows, heads_width), BF16),
            jax.ShapeDtypeStruct((blocks * rows, 2 * heads_width), BF16),
            edge,
            edge,
            jax.ShapeDtypeStruct((blocks - 1, depth, width), BF16),
        ),
        in_specs=[SMEM, VMEM] + [ANY] * len(shards),
        out_specs=(VMEM,) * 5,
        scratch_shapes=[pltpu.VMEM((blocks * rows, width), BF16)] + [pltpu.SemaphoreType.DMA((len(shards),))] * 2,
        compiler_params=pltpu.CompilerParams(vmem_limit_bytes=14 * MIB),
        cost_estimate=SHORT,
        name="project",
    )(place, weight, *shards)


def window_bias(first, count, starts, ends):
    reach = WIN // 2
    query = first + lax.broadcasted_iota(jnp.int32, (count, 1), 0)
    low = jnp.max(jnp.where(starts <= query, starts, 0), axis=1, keepdims=True)
    high = jnp.min(jnp.where(ends > query, ends, 1 << 30), axis=1, keepdims=True)
    low = jnp.maximum(low, query - reach)
    high = jnp.minimum(high, query + reach + 1)
    key = first - count + lax.broadcasted_iota(jnp.int32, (count, 3 * count), 1)
    return jnp.where((key >= low) & (key < high), 0.0, NEG_FILL)


def attend(query, keyval_ref, bias_ref, scores_ref, weights_ref, out_ref):
    count, width = query.shape
    lane = lax.broadcasted_iota(jnp.int32, (count, 2 * HD), 1)
    for start in range(0, width, 2 * HD):
        values = keyval_ref[:, width + start : width + start + 2 * HD]
        halves = []
        for side in range(2):
            head = start // HD + side
            inside = (lane < HD) if side == 0 else (lane >= HD)
            only = jnp.where(inside, query[:, start : start + 2 * HD], jnp.zeros((), BF16))
            scores_ref[head] = lax.dot_general(
                only, keyval_ref[:, start : start + 2 * HD], (((1,), (1,)), ((), ())), preferred_element_type=F32
            )
            totals = []
            for row in range(0, count, STRIP):
                at = slice(row, row + STRIP)
                scores = scores_ref[head, at] + bias_ref[at]
                weights = jnp.exp(scores - jnp.max(scores, axis=1, keepdims=True))
                totals.append(jnp.sum(weights, axis=1, keepdims=True))
                weights_ref[head, at] = weights.astype(BF16)
            summed = jnp.dot(weights_ref[head], values, preferred_element_type=F32)
            halves.append(summed / jnp.concatenate(totals, axis=0))
        out_ref[:, start : start + 2 * HD] = jnp.where(lane < HD, halves[0], halves[1]).astype(BF16)


def attend_kernel(flips, place_ref, starts_ref, ends_ref, query_ref, before_ref, keyval_ref, behind_ref, *refs):
    outs = refs[: len(flips)]
    window_ref, bias_ref, scores_ref, weights_ref, sems = refs[len(flips) :]
    tok, kv = place_ref[0], place_ref[1]
    count = outs[0].shape[0]
    blocks = query_ref.shape[0] // count
    copies = []
    for index, flip in enumerate(flips):
        block = kv ^ flip
        for part in range(3):
            target = window_ref.at[index, part * count : (part + 1) * count]
            sem = sems.at[index, part]
            at = block + part - 1
            inner = (at >= 0) & (at < blocks)
            safe = jnp.where(inner, at, 0)
            source = keyval_ref.at[pl.ds(pl.multiple_of(safe * count, count), count)]
            copies.append((index, inner, pltpu.make_async_copy(source, target, sem)))
            if part == 0:
                copies.append((index, at < 0, pltpu.make_async_copy(before_ref, target, sem)))
            if part == 2:
                copies.append((index, at >= blocks, pltpu.make_async_copy(behind_ref, target, sem)))
    for _, needed, copy in copies:
        pl.when(needed)(copy.start)
    for index, flip in enumerate(flips):
        block = kv ^ flip
        first = (tok * blocks + block) * count
        bias_ref[...] = window_bias(first, count, starts_ref[...], ends_ref[...])
        for owner, needed, copy in copies:
            if owner == index:
                pl.when(needed)(copy.wait)
        query = query_ref[pl.ds(pl.multiple_of(block * count, count), count)]
        attend(query, window_ref.at[index], bias_ref, scores_ref, weights_ref, outs[index])


def attend_blocks(place, starts, ends, query, before, keyval, behind, rows, flips, name):
    heads_width = query.shape[1]
    return pl.pallas_call(
        functools.partial(attend_kernel, flips),
        out_shape=tuple(jax.ShapeDtypeStruct((rows, heads_width), BF16) for _ in flips),
        in_specs=[SMEM, VMEM, VMEM, VMEM, ANY, ANY, ANY],
        out_specs=(VMEM,) * len(flips),
        scratch_shapes=[
            pltpu.VMEM((len(flips), 3 * rows, 2 * heads_width), BF16),
            pltpu.VMEM((rows, 3 * rows), F32),
            pltpu.VMEM((heads_width // HD, rows, 3 * rows), F32),
            pltpu.VMEM((heads_width // HD, rows, 3 * rows), BF16),
            pltpu.SemaphoreType.DMA((len(flips), 3)),
        ],
        compiler_params=pltpu.CompilerParams(vmem_limit_bytes=14 * MIB),
        cost_estimate=SHORT,
        name=name,
    )(place, starts, ends, query, before, keyval, behind)


def first_norm_kernel(layout, place_ref, hidden_ref, own_out_ref, gain_ref, bias_ref, *refs):
    parts, pieces = refs[: -5 - len(layout)], refs[-5 - len(layout) : -5]
    normed_ref, all_ref, weight_ref, mixed_ref, sems = refs[-5:]
    tok, kv = place_ref[0], place_ref[1]
    quarters, heads_width, width = weight_ref.shape
    copies = [pltpu.make_async_copy(own_out_ref, weight_ref.at[kv], sems.at[0])]
    for flips, piece in zip(layout, pieces):
        for index, flip in enumerate(flips):
            for turn in range(1, quarters):
                depth = piece.shape[2]
                at = pl.multiple_of((tok ^ flip) * depth, depth)
                target = weight_ref.at[lax.rem(kv + turn, quarters), pl.ds(at, depth)]
                copies.append(pltpu.make_async_copy(piece.at[index, turn - 1], target, sems.at[len(copies)]))
    for copy in copies:
        copy.start()
    for flip, part_ref in enumerate(parts):
        at = pl.multiple_of((kv ^ flip) * heads_width, heads_width)
        all_ref[:, pl.ds(at, heads_width)] = part_ref[...]
    for copy in copies:
        copy.wait()
    weight = weight_ref[...].reshape(quarters * heads_width, width)
    mixed_ref[...] = jnp.dot(all_ref[...], weight, preferred_element_type=F32)
    for row in range(0, hidden_ref.shape[0], STRIP):
        at = slice(row, row + STRIP)
        mixed = hidden_ref[at].astype(F32) + mixed_ref[at]
        normed_ref[at] = normalized(mixed, gain_ref[...], bias_ref[...]).astype(BF16)


def first_norm(place, hidden, own_out, gain, bias, parts, pieces):
    rows, width = hidden.shape
    heads_width = own_out.shape[0]
    layout = tuple(flips for flips, _ in pieces)
    return pl.pallas_call(
        functools.partial(first_norm_kernel, layout),
        out_shape=jax.ShapeDtypeStruct((rows, width), BF16),
        in_specs=[SMEM, VMEM, ANY, VMEM, VMEM] + [VMEM] * len(parts) + [ANY] * len(pieces),
        out_specs=VMEM,
        scratch_shapes=[
            pltpu.VMEM((rows, width), BF16),
            pltpu.VMEM((len(parts), heads_width, width), BF16),
            pltpu.VMEM((rows, width), F32),
            pltpu.SemaphoreType.DMA((1 + (len(parts) - 1) * sum(len(flips) for flips in layout),)),
        ],
        compiler_params=pltpu.CompilerParams(vmem_limit_bytes=11 * MIB),
        cost_estimate=SHORT,
        name="first_norm",
    )(place, hidden, own_out, gain, bias, *parts, *[value for _, value in pieces])


def gelu(values):
    return 0.5 * values * (1.0 + lax.erf(values * math.sqrt(0.5)))


CHUNK = 512


def feed_chunk(rows, up, down_ref, wide_ref, units_ref):
    wide_ref[...] = jnp.dot(rows, up, preferred_element_type=F32)
    for row in range(0, rows.shape[0], STRIP):
        strip = slice(row, row + STRIP)
        units_ref[strip] = gelu(wide_ref[strip]).astype(BF16)
    return jnp.dot(units_ref[...], down_ref[...], preferred_element_type=F32)


def far_copies(tok, held_ref, core_ref, up_ref, down_ref, sems):
    block = 128
    copies = []
    for side, piece in enumerate((held_ref, core_ref)):
        for index in range(4):
            at = pl.ds(pl.multiple_of((tok ^ (2 * index + side)) * block, block), block)
            for part, target in enumerate((up_ref, down_ref)):
                source = piece.at[pl.ds((2 * index + part) * block, block)]
                copies.append(pltpu.make_async_copy(source, target.at[at], sems.at[len(copies)]))
    return copies


def feed_near_kernel(rows_ref, up_ref, down_ref, sum_ref, wide_ref, units_ref):
    rows = rows_ref[...]
    for index in range(up_ref.shape[1] // CHUNK):
        at = slice(index * CHUNK, (index + 1) * CHUNK)
        product = feed_chunk(rows, up_ref[:, at], down_ref.at[at], wide_ref.at[index % 2], units_ref.at[index % 2])
        if index == 0:
            sum_ref[...] = product
        else:
            sum_ref[...] += product


def feed_far_kernel(
    place_ref, rows_ref, near_ref, held_ref, core_ref, sum_ref, up_ref, down_ref, wide_ref, units_ref, total_ref, sems
):
    copies = far_copies(place_ref[0], held_ref, core_ref, up_ref, down_ref, sems)
    for copy in copies:
        copy.start()
    rows = rows_ref[...]
    total_ref[...] = near_ref[...]
    for copy in copies:
        copy.wait()
    for index in range(up_ref.shape[1] // CHUNK):
        at = slice(index * CHUNK, (index + 1) * CHUNK)
        slot = index % 2
        total_ref[...] += feed_chunk(rows, up_ref[:, at], down_ref.at[at], wide_ref.at[slot], units_ref.at[slot])
    sum_ref[...] = total_ref[...].astype(sum_ref.dtype)


def feed_kernel(
    place_ref, rows_ref, up_near_ref, down_near_ref, held_ref, core_ref, sum_ref, up_ref, down_ref, wide_ref, units_ref, sems
):
    copies = far_copies(place_ref[0], held_ref, core_ref, up_ref, down_ref, sems)
    for copy in copies:
        copy.start()
    feed_near_kernel(rows_ref, up_near_ref, down_near_ref, sum_ref, wide_ref, units_ref)
    rows = rows_ref[...]
    for copy in copies:
        copy.wait()
    for index in range(up_ref.shape[1] // CHUNK):
        at = slice(index * CHUNK, (index + 1) * CHUNK)
        slot = index % 2
        sum_ref[...] += feed_chunk(rows, up_ref[:, at], down_ref.at[at], wide_ref.at[slot], units_ref.at[slot])


def feed_scratch(count):
    return [pltpu.VMEM((2, count, CHUNK), F32), pltpu.VMEM((2, count, CHUNK), BF16)]


def feed_near(rows, up_weight, down_weight):
    return pl.pallas_call(
        feed_near_kernel,
        out_shape=jax.ShapeDtypeStruct(rows.shape, F32),
        in_specs=[VMEM] * 3,
        out_specs=VMEM,
        scratch_shapes=feed_scratch(rows.shape[0]),
        compiler_params=pltpu.CompilerParams(vmem_limit_bytes=14 * MIB),
        cost_estimate=SHORT,
        name="feed_near",
    )(rows, up_weight, down_weight)


def feed_far(place, rows, near, pieces):
    count, width = rows.shape
    units = pieces[0].shape[0]
    return pl.pallas_call(
        feed_far_kernel,
        out_shape=jax.ShapeDtypeStruct((count, width), BF16),
        in_specs=[SMEM] + [VMEM] * 2 + [ANY] * 2,
        out_specs=VMEM,
        scratch_shapes=[pltpu.VMEM((width, units), BF16), pltpu.VMEM((units, width), BF16)]
        + feed_scratch(count)
        + [pltpu.VMEM((count, width), F32), pltpu.SemaphoreType.DMA((16,))],
        compiler_params=pltpu.CompilerParams(vmem_limit_bytes=14 * MIB),
        cost_estimate=SHORT,
        name="feed_far",
    )(place, rows, near, *pieces)


def feed(place, rows, up_weight, down_weight, pieces):
    count, width = rows.shape
    units = up_weight.shape[1]
    return pl.pallas_call(
        feed_kernel,
        out_shape=jax.ShapeDtypeStruct((count, width), F32),
        in_specs=[SMEM] + [VMEM] * 3 + [ANY] * 2,
        out_specs=VMEM,
        scratch_shapes=[pltpu.VMEM((width, units), BF16), pltpu.VMEM((units, width), BF16)]
        + feed_scratch(count)
        + [pltpu.SemaphoreType.DMA((16,))],
        compiler_params=pltpu.CompilerParams(vmem_limit_bytes=18 * MIB),
        cost_estimate=SHORT,
        name="feed_own",
    )(place, rows, up_weight, down_weight, *pieces)


def finish_kernel(normed_ref, near_ref, far_ref, gain_ref, bias_ref, out_ref):
    for row in range(0, normed_ref.shape[0], STRIP):
        at = slice(row, row + STRIP)
        mixed = normed_ref[at].astype(F32) + near_ref[at] + far_ref[at].astype(F32)
        out_ref[at] = normalized(mixed, gain_ref[...], bias_ref[...]).astype(out_ref.dtype)


def finish(normed, near, far, gain, bias):
    return pl.pallas_call(
        finish_kernel,
        out_shape=jax.ShapeDtypeStruct(normed.shape, BF16),
        in_specs=[VMEM] * 5,
        out_specs=VMEM,
        compiler_params=pltpu.CompilerParams(vmem_limit_bytes=6 * MIB),
        name="finish",
    )(normed, near, far, gain, bias)


def decode_kernel(source_ref, slot_ref, filled_ref, query_ref, cache_ref, out_ref, high_ref, total_ref, sum_ref):
    step = pl.program_id(0)

    @pl.when(step == 0)
    def _():
        high_ref[...] = jnp.full(high_ref.shape, NEG_FILL, F32)
        total_ref[...] = jnp.zeros_like(total_ref)
        sum_ref[...] = jnp.zeros_like(sum_ref)

    row = slot_ref[step]
    filled = filled_ref[step]
    width = query_ref.shape[1]
    head = lax.broadcasted_iota(jnp.int32, (H, width), 0)
    inside = head == lax.broadcasted_iota(jnp.int32, (H, width), 1) // HD
    query = jnp.where(inside, query_ref[pl.ds(source_ref[step], 1), :], 0.0).astype(BF16)
    scores = lax.dot_general(query, cache_ref[0, 0, 0], (((1,), (1,)), ((), ())), preferred_element_type=F32)
    live = lax.broadcasted_iota(jnp.int32, scores.shape, 1) < filled
    scores = jnp.where(live, scores * (1.0 / math.sqrt(HD)), NEG_FILL)
    high = jnp.max(scores, axis=1, keepdims=True)
    weights = jnp.where(live, jnp.exp(scores - high), 0.0)
    total = jnp.sum(weights, axis=1, keepdims=True)
    summed = jnp.dot(weights.astype(BF16), cache_ref[1, 0, 0], preferred_element_type=F32)
    along = lambda column: jnp.sum(jnp.where(inside, column, 0.0), axis=0, keepdims=True)
    high, total, summed = along(high), along(total), along(summed)
    used = filled > 0
    at = pl.ds(row, 1)
    old = high_ref[at, :]
    new = jnp.where(used, jnp.maximum(old, high), old)
    left = jnp.exp(old - new)
    right = jnp.where(used, jnp.exp(high - new), 0.0)
    high_ref[at, :] = new
    total_ref[at, :] = total_ref[at, :] * left + total * right
    sum_ref[at, :] = sum_ref[at, :] * left + summed * right

    @pl.when(step == pl.num_programs(0) - 1)
    def _():
        out_ref[0] = high_ref[...]
        out_ref[1] = total_ref[...]
        out_ref[2] = sum_ref[...]


def decode(sources, slots, filled, queries, requests, kv_cache):
    count, width = queries.shape
    pieces = kv_cache.shape[2]
    state = pltpu.VMEM((requests, width), F32)
    return pl.pallas_call(
        decode_kernel,
        grid=(pieces,),
        out_shape=jax.ShapeDtypeStruct((3, requests, width), F32),
        in_specs=[
            SMEM,
            SMEM,
            SMEM,
            pl.BlockSpec((count, width), lambda i: (0, 0)),
            pl.BlockSpec((2, 1, 1, PLEN, width), lambda i: (0, 0, i, 0, 0)),
        ],
        out_specs=pl.BlockSpec((3, requests, width), lambda i: (0, 0, 0)),
        scratch_shapes=[state, state, state],
        compiler_params=pltpu.CompilerParams(vmem_limit_bytes=8 * MIB),
        cost_estimate=SHORT,
        name="decode",
    )(sources, slots, filled, queries, kv_cache)


def decode_partial(queries, own, kv_cache, piece_req, piece_used):
    kv, kvs = lax.axis_index("kv"), lax.axis_size("kv")
    owners = piece_req[0]
    home = owners // own
    sources = ((home + kvs - kv) % kvs) * own + owners % own
    slots = (home ^ kv) * own + owners % own
    return decode(sources, slots, piece_used[0], queries, own * kvs, kv_cache)


def exchanged_partials(partial, own):
    parts = [partial[:, :own]]
    for flip in range(1, lax.axis_size("kv")):
        parts.append(swapped(partial[:, flip * own : (flip + 1) * own], "kv", flip))
    return parts


def merged_partials(parts):
    high = functools.reduce(jnp.maximum, [part[0] for part in parts])
    factors = [jnp.exp(part[0] - high) for part in parts]
    total = sum(part[1] * factor for part, factor in zip(parts, factors))
    summed = sum(part[2] * factor for part, factor in zip(parts, factors))
    return (summed / total).astype(BF16)


def routed_body(
    hidden_in,
    qkv_weight,
    stretch_len,
    out_weight,
    ln1_gain,
    ln1_bias,
    up_weight,
    down_weight,
    ln2_gain,
    ln2_bias,
    dec_query,
    kv_cache,
    piece_req,
    piece_used,
):
    tok = lax.axis_index("tok")
    kv = lax.axis_index("kv")
    toks, kvs = lax.axis_size("tok"), lax.axis_size("kv")
    rows, width = hidden_in.shape
    place = jnp.stack([tok, kv]).astype(jnp.int32)
    eighth = lambda value: lax.dynamic_slice_in_dim(value, tok * (value.shape[0] // toks), value.shape[0] // toks, 0)

    out_part = eighth(out_weight)
    depth = out_part.shape[0]
    from_below, from_above = [], []
    rising = falling = jnp.concatenate([hidden_in, out_part, dec_query], axis=0)
    for step in range(1, kvs):
        links = range(step - 1, kvs - 1)
        rising = lax.ppermute(rising, "kv", [(i, i + 1) for i in links])
        falling = lax.ppermute(falling, "kv", [(kvs - 1 - i, kvs - 2 - i) for i in links])
        from_below.append(rising)
        from_above.append(falling)
    feed_up, feed_down = after((eighth(up_weight), eighth(down_weight)), from_below[1], from_above[1])
    inner_up = lax.ppermute(feed_up, "kv", [(0, 2), (3, 1)])
    inner_down = lax.ppermute(feed_down, "kv", [(0, 2), (3, 1)])
    feed_part = after(jnp.concatenate([feed_up, feed_down], axis=0), rising, falling, inner_up, inner_down)
    feed_outer = lax.ppermute(feed_part, "kv", [(1, 3), (2, 0)])
    feed_inner = jnp.concatenate([inner_up, inner_down], axis=0)

    order = jnp.arange(stretch_len.shape[0])
    ends = jnp.sum(jnp.where(order[:, None] <= order[None, :], stretch_len[:, None], 0), axis=0, dtype=jnp.int32)
    starts = (ends - stretch_len)[None, :]
    ends = ends[None, :]

    shards = [after(hidden_in, inner_up, inner_down)] + from_below + from_above
    query, keyval, top, bottom, out_here = project(place, jnp.transpose(qkv_weight, (1, 0, 2)), shards, depth)
    before = lax.ppermute(bottom, "tok", [(i, i + 1) for i in range(toks - 1)])
    behind = lax.ppermute(top, "tok", [(i + 1, i) for i in range(toks - 1)])
    out_x, out_y = swapped(out_here, "tok", 2), swapped(out_here, "tok", 4)
    window = (place, starts, ends, query, before, keyval, behind, rows)
    parts = [None] * kvs
    parts[3], parts[2] = attend_blocks(*window, (3, 2), "attend_far")
    out_all = jnp.stack([out_here, out_x, out_y, swapped(after(out_y, parts[3]), "tok", 2)])
    out_core = swapped(out_all, "tok", 1)
    inner = (kv == 1) | (kv == 2)
    feed_here = jnp.where(inner, feed_inner, after(feed_outer, parts[3], parts[2]))
    parts[3], parts[2] = swapped(parts[3], "kv", 3), swapped(parts[2], "kv", 2)
    window = (place, starts, ends, after(query, feed_here), before, keyval, behind, rows)
    parts[1], parts[0] = attend_blocks(*window, (1, 0), "attend_near")
    parts[1] = swapped(parts[1], "kv", 1)
    feed_x, feed_y = swapped(feed_here, "tok", 2), swapped(feed_here, "tok", 4)
    out_pieces = [((0, 2, 4, 6), out_all), ((1, 3, 5, 7), out_core)]
    normed = first_norm(place, hidden_in, out_weight, ln1_gain[None, :], ln1_bias[None, :], parts, out_pieces)

    partner = swapped(normed, "kv", 1)
    half = feed_here.shape[0] // 2
    far_up = swapped(after(feed_y, normed)[:half], "tok", 2)
    far_down = swapped(after(feed_x, normed)[half:], "tok", 4)
    own = dec_query.shape[0]
    queries = [dec_query]
    for turn in range(1, kvs):
        above, below = from_above[turn - 1], from_below[kvs - 1 - turn]
        queries.append(jnp.where(kv + turn < kvs, above[rows + depth :], below[rows + depth :]))
    queries = after(jnp.concatenate(queries, axis=0).astype(F32), normed)
    partial = decode_partial(queries, own, kv_cache, piece_req, piece_used)
    dec_parts = exchanged_partials(after(partial, partner), own)
    held = jnp.concatenate([feed_here, feed_x, feed_y, after(far_up, partial), far_down], axis=0)
    near_away = feed_near(partner, up_weight, down_weight)
    near_away = after(near_away, *dec_parts)
    feed_pieces = (held, swapped(after(held, partner), "tok", 1))
    away = feed_far(place, partner, near_away, feed_pieces)
    arrived = swapped(away, "kv", 1)
    mine = feed(place, after(normed, away), up_weight, down_weight, feed_pieces)
    prefill_out = finish(normed, mine, arrived, ln2_gain[None, :], ln2_bias[None, :])

    return prefill_out, merged_partials(after(tuple(dec_parts), away))


def extended(value, sides, width):
    for axis, dim in sides:
        count, length = (lax.axis_size(axis), value.shape[dim])
        up = [(i, (i + 1) % count) for i in range(count - 1)]
        down = [(j, i) for i, j in up]
        last = lax.slice_in_dim(value, length - width, length, axis=dim)
        leading = lax.slice_in_dim(value, 0, width, axis=dim)
        before = lax.ppermute(last, axis, up)
        after = lax.ppermute(leading, axis, down)
        value = jnp.concatenate([before, value, after], axis=dim)
    return value


def merged(value, axis, join):
    pieces = jax.tree.map(lambda part: lax.all_gather(part, axis), value)
    head = jax.tree.map(lambda part: part[0], pieces)
    tail = jax.tree.map(lambda part: part[1:], pieces)
    subtotal, _ = lax.scan(lambda subtotal, section: (join(subtotal, section), None), head, tail)
    return subtotal


def segment_ids(row_ids, stretch_len):
    stretch_ends = jnp.cumsum(stretch_len)
    return jnp.sum((row_ids[:, None] >= stretch_ends[None, :]).astype(jnp.int32), axis=1)


def layer_norm(values, gain, bias):
    center = values - jnp.mean(values, axis=1, keepdims=True)
    spread = jnp.mean(center * center, axis=1, keepdims=True)
    return center * lax.rsqrt(spread + LN_EPS) * gain + bias


def merge_partials(earlier, later):
    highest = jnp.maximum(earlier[0], later[0])
    left_factor = jnp.exp(earlier[0] - highest)
    right_factor = jnp.exp(later[0] - highest)
    totals = earlier[1] * left_factor + later[1] * right_factor
    weighted = earlier[2] * left_factor[..., None] + later[2] * right_factor[..., None]
    return (highest, totals, weighted)


def row_folder(source, shard_rows):
    return jnp.dot(source, shard_rows, preferred_element_type=jnp.float32)


def general_body(
    hidden_in,
    qkv_weight,
    stretch_len,
    out_weight,
    ln1_gain,
    ln1_bias,
    up_weight,
    down_weight,
    ln2_gain,
    ln2_bias,
    dec_query,
    kv_cache,
    piece_req,
    piece_used,
):
    inv_scale = 1.0 / math.sqrt(HD)
    reach = WIN // 2
    local_width = qkv_weight.shape[2]
    head_count = local_width // HD
    flat_weight = qkv_weight.reshape(qkv_weight.shape[0], 3 * local_width)
    qkv_rows = jnp.dot(
        lax.all_gather(hidden_in, "kv", axis=0, tiled=True),
        flat_weight,
        preferred_element_type=jnp.float32,
    ).astype(jnp.bfloat16)
    row_count = qkv_rows.shape[0]
    query_rows = qkv_rows[:, :local_width]
    keyval_rows = qkv_rows[:, local_width:]
    padded = extended(keyval_rows, (("tok", 0),), reach)
    first_row = lax.axis_index("tok") * row_count
    total_rows = row_count * lax.axis_size("tok")
    qblock = min(512, row_count)
    span = qblock + 2 * reach
    block_count = row_count // qblock

    def attend(block_index):
        start = block_index * qblock
        query_ids = first_row + start + jnp.arange(qblock, dtype=jnp.int32)
        key_ids = first_row + start - reach + jnp.arange(span, dtype=jnp.int32)
        query_seg = segment_ids(query_ids, stretch_len)
        inside = (key_ids >= 0) & (key_ids < total_rows)
        key_seg = jnp.where(inside, segment_ids(key_ids, stretch_len), -1)
        allowed = (key_seg[None, :] == query_seg[:, None]) & (
            jnp.abs(key_ids[None, :] - query_ids[:, None]) <= reach
        )
        queries = lax.dynamic_slice_in_dim(query_rows, start, qblock, 0).reshape(
            qblock, head_count, HD
        )
        both = lax.dynamic_slice_in_dim(padded, start, span, 0)
        key_rows = both[:, :local_width].reshape(span, head_count, HD)
        value_rows = both[:, local_width:].reshape(span, head_count, HD)
        scores = (
            jnp.einsum("ihd,jhd->hij", queries, key_rows, preferred_element_type=jnp.float32)
            * inv_scale
        )
        scores = jnp.where(allowed[None], scores, NEG_FILL)
        row_max = jnp.max(scores, axis=2, keepdims=True)
        weights = jnp.where(allowed[None], jnp.exp(scores - row_max), 0.0)
        totals = jnp.sum(weights, axis=2)
        summed = jnp.einsum(
            "hij,jhd->ihd",
            weights.astype(jnp.bfloat16),
            value_rows,
            preferred_element_type=jnp.float32,
        )
        return (
            (summed / jnp.transpose(totals)[:, :, None])
            .astype(jnp.bfloat16)
            .reshape(qblock, local_width)
        )

    attention = lax.map(attend, jnp.arange(block_count, dtype=jnp.int32)).reshape(
        row_count, local_width
    )
    token_major = lax.all_to_all(attention, "kv", split_axis=0, concat_axis=1, tiled=True)
    projected = row_folder(token_major, lax.all_gather(out_weight, "kv", axis=0, tiled=True))
    normed = layer_norm(hidden_in.astype(jnp.float32) + projected, ln1_gain, ln1_bias).astype(
        jnp.bfloat16
    )
    units = jax.nn.gelu(
        jnp.dot(
            lax.all_gather(normed, "kv", axis=0, tiled=True),
            up_weight,
            preferred_element_type=jnp.float32,
        ),
        approximate=False,
    ).astype(jnp.bfloat16)
    ffn = lax.psum_scatter(
        jnp.dot(units, down_weight, preferred_element_type=jnp.float32).astype(jnp.bfloat16),
        "kv",
        scatter_dimension=0,
        tiled=True,
    ).astype(jnp.float32)
    prefill_out = layer_norm(normed.astype(jnp.float32) + ffn, ln2_gain, ln2_bias).astype(
        jnp.bfloat16
    )
    group_queries = lax.all_gather(dec_query, "kv", axis=0, tiled=True)
    request_count = group_queries.shape[0]
    owners = piece_req[0]
    filled = piece_used[0]
    slot_count = owners.shape[0]
    request_ids = jnp.arange(request_count, dtype=jnp.int32)
    selector = (owners[:, None] == request_ids[None, :]).astype(jnp.bfloat16)
    chosen = jnp.dot(selector, group_queries, preferred_element_type=jnp.float32).astype(
        jnp.bfloat16
    )
    chosen = chosen.reshape(slot_count, H, HD)
    cache_keys = kv_cache[0, 0].reshape(slot_count, PLEN, H, HD)
    cache_values = kv_cache[1, 0].reshape(slot_count, PLEN, H, HD)
    piece_scores = (
        jnp.einsum("phd,pthd->pht", chosen, cache_keys, preferred_element_type=jnp.float32)
        * inv_scale
    )
    active = jnp.arange(PLEN, dtype=jnp.int32)[None, :] < filled[:, None]
    piece_scores = jnp.where(active[:, None, :], piece_scores, NEG_FILL)
    piece_max = jnp.max(piece_scores, axis=2)
    piece_weights = jnp.where(
        active[:, None, :], jnp.exp(piece_scores - piece_max[:, :, None]), 0.0
    )
    piece_totals = jnp.sum(piece_weights, axis=2)
    partial_value = jnp.einsum(
        "pht,pthd->phd",
        piece_weights.astype(jnp.bfloat16),
        cache_values,
        preferred_element_type=jnp.float32,
    )
    member = (owners[None, :] == request_ids[:, None]) & (filled[None, :] > 0)
    highest = jnp.max(jnp.where(member[:, :, None], piece_max[None], NEG_FILL), axis=1)
    factor = jnp.where(member[:, :, None], jnp.exp(piece_max[None] - highest[:, None, :]), 0.0)
    denom = jnp.sum(factor * piece_totals[None], axis=1)
    weighted = jnp.einsum("rph,phd->rhd", factor, partial_value)
    own_requests = dec_query.shape[0]
    joined = merged((highest, denom, weighted), "kv", merge_partials)
    begin = lax.axis_index("kv") * own_requests
    final_denom = lax.dynamic_slice_in_dim(joined[1], begin, own_requests, 0)
    final_weighted = lax.dynamic_slice_in_dim(joined[2], begin, own_requests, 0)
    dec_out = (
        (final_weighted / final_denom[:, :, None])
        .astype(jnp.bfloat16)
        .reshape(own_requests, H * HD)
    )
    return (prefill_out, dec_out)


def solution(mesh):
    placed = (
        P(("tok", "kv"), None),
        P(None, None, "kv"),
        P(),
        P("kv", None),
        P(),
        P(),
        P(None, "kv"),
        P("kv", None),
        P(),
        P(),
        P(("tok", "kv"), None),
        P(None, "tok", "kv", None, None),
        P("tok", "kv"),
        P("tok", "kv"),
    )
    routed = mesh.shape["tok"] == 8 and mesh.shape["kv"] == 4
    return jax.shard_map(
        routed_body if routed else general_body,
        mesh=mesh,
        in_specs=placed,
        out_specs=(P(("tok", "kv"), None), P(("tok", "kv"), None)),
        check_vma=False,
    )
```

```python
import functools
import math

import jax
import jax.numpy as jnp
from jax import lax
from jax.experimental import pallas as pl
from jax.experimental.pallas import tpu as pltpu
from jax.sharding import PartitionSpec as P

H = 16
HD = 64
WIN = 512
PLEN = 128


NEG_FILL = -1e30
LN_EPS = 1e-05
BF16 = jnp.bfloat16
F32 = jnp.float32
STRIP = 32
MIB = 1024 * 1024
ANY = pl.BlockSpec(memory_space=pl.ANY)
VMEM = pl.BlockSpec(memory_space=pltpu.VMEM)
SMEM = pl.BlockSpec(memory_space=pltpu.SMEM)
SHORT = pl.CostEstimate(flops=1, bytes_accessed=1, transcendentals=0)


def swapped(value, axis, flip):
    count = lax.axis_size(axis)
    return lax.ppermute(value, axis, [(i, i ^ flip) for i in range(count)])


def after(value, *earlier):
    return lax.optimization_barrier((value,) + earlier)[0]


def normalized(values, gain, bias):
    center = values - jnp.mean(values, axis=1, keepdims=True)
    spread = jnp.mean(center * center, axis=1, keepdims=True)
    return center * lax.rsqrt(spread + LN_EPS) * gain + bias


def project_kernel(place_ref, weight_ref, *refs):
    shards, (query_ref, keyval_ref, top_ref, bottom_ref, rows_ref, sems) = refs[:-6], refs[-6:]
    kv = place_ref[1]
    count = top_ref.shape[0]
    steps = (len(shards) - 1) // 2
    width = weight_ref.shape[2]
    moves = [(shards[0], kv, None)]
    for step in range(1, steps + 1):
        moves.append((shards[step], kv - step, kv >= step))
        moves.append((shards[steps + step], kv + step, kv + step <= steps))

    def guarded(needed, act):
        if needed is None:
            act()
        else:
            pl.when(needed)(act)

    copies = []
    for index, (source, owner, needed) in enumerate(moves):
        safe = owner if needed is None else jnp.where(needed, owner, 0)
        at = pl.ds(pl.multiple_of(safe * count, count), count)
        copies.append((needed, pltpu.make_async_copy(source, rows_ref.at[at], sems.at[index])))
    for needed, copy in copies:
        guarded(needed, copy.start)
    for needed, copy in copies:
        guarded(needed, copy.wait)
    rows = rows_ref[...]
    query = jnp.dot(rows, weight_ref[0], preferred_element_type=F32) * (1.0 / math.sqrt(HD))
    query_ref[...] = query.astype(BF16)
    for part in range(2):
        at = slice(part * width, (part + 1) * width)
        keyval_ref[:, at] = jnp.dot(rows, weight_ref[part + 1], preferred_element_type=F32).astype(BF16)
    top_ref[...] = keyval_ref[:count]
    bottom_ref[...] = keyval_ref[steps * count :]


def project(place, weight, shards):
    rows, width = shards[0].shape
    heads_width = weight.shape[2]
    blocks = (len(shards) + 1) // 2
    edge = jax.ShapeDtypeStruct((rows, 2 * heads_width), BF16)
    return pl.pallas_call(
        project_kernel,
        out_shape=(
            jax.ShapeDtypeStruct((blocks * rows, heads_width), BF16),
            jax.ShapeDtypeStruct((blocks * rows, 2 * heads_width), BF16),
            edge,
            edge,
        ),
        in_specs=[SMEM, VMEM] + [ANY] * len(shards),
        out_specs=(VMEM,) * 4,
        scratch_shapes=[pltpu.VMEM((blocks * rows, width), BF16), pltpu.SemaphoreType.DMA((len(shards),))],
        compiler_params=pltpu.CompilerParams(vmem_limit_bytes=14 * MIB),
        cost_estimate=SHORT,
        name="project",
    )(place, weight, *shards)


def window_bias(first, count, starts, ends):
    reach = WIN // 2
    query = first + lax.broadcasted_iota(jnp.int32, (count, 1), 0)
    low = jnp.max(jnp.where(starts <= query, starts, 0), axis=1, keepdims=True)
    high = jnp.min(jnp.where(ends > query, ends, 1 << 30), axis=1, keepdims=True)
    low = jnp.maximum(low, query - reach)
    high = jnp.minimum(high, query + reach + 1)
    key = first - count + lax.broadcasted_iota(jnp.int32, (count, 3 * count), 1)
    return jnp.where((key >= low) & (key < high), 0.0, NEG_FILL)


def attend(query, keyval_ref, bias_ref, scores_ref, weights_ref, out_ref):
    count, width = query.shape
    lane = lax.broadcasted_iota(jnp.int32, (count, 2 * HD), 1)
    for start in range(0, width, 2 * HD):
        values = keyval_ref[:, width + start : width + start + 2 * HD]
        halves = []
        for side in range(2):
            head = start // HD + side
            inside = (lane < HD) if side == 0 else (lane >= HD)
            only = jnp.where(inside, query[:, start : start + 2 * HD], jnp.zeros((), BF16))
            scores_ref[head] = lax.dot_general(
                only, keyval_ref[:, start : start + 2 * HD], (((1,), (1,)), ((), ())), preferred_element_type=F32
            )
            totals = []
            for row in range(0, count, STRIP):
                at = slice(row, row + STRIP)
                scores = scores_ref[head, at] + bias_ref[at]
                weights = jnp.exp(scores - jnp.max(scores, axis=1, keepdims=True))
                totals.append(jnp.sum(weights, axis=1, keepdims=True))
                weights_ref[head, at] = weights.astype(BF16)
            summed = jnp.dot(weights_ref[head], values, preferred_element_type=F32)
            halves.append(summed / jnp.concatenate(totals, axis=0))
        out_ref[:, start : start + 2 * HD] = jnp.where(lane < HD, halves[0], halves[1]).astype(BF16)


def attend_kernel(flips, place_ref, starts_ref, ends_ref, query_ref, before_ref, keyval_ref, behind_ref, *refs):
    outs = refs[: len(flips)]
    window_ref, bias_ref, scores_ref, weights_ref, sems = refs[len(flips) :]
    tok, kv = place_ref[0], place_ref[1]
    count = outs[0].shape[0]
    blocks = query_ref.shape[0] // count
    copies = []
    for index, flip in enumerate(flips):
        block = kv ^ flip
        for part in range(3):
            target = window_ref.at[index, part * count : (part + 1) * count]
            sem = sems.at[index, part]
            at = block + part - 1
            inner = (at >= 0) & (at < blocks)
            safe = jnp.where(inner, at, 0)
            source = keyval_ref.at[pl.ds(pl.multiple_of(safe * count, count), count)]
            copies.append((index, inner, pltpu.make_async_copy(source, target, sem)))
            if part == 0:
                copies.append((index, at < 0, pltpu.make_async_copy(before_ref, target, sem)))
            if part == 2:
                copies.append((index, at >= blocks, pltpu.make_async_copy(behind_ref, target, sem)))
    for _, needed, copy in copies:
        pl.when(needed)(copy.start)
    for index, flip in enumerate(flips):
        block = kv ^ flip
        first = (tok * blocks + block) * count
        bias_ref[...] = window_bias(first, count, starts_ref[...], ends_ref[...])
        for owner, needed, copy in copies:
            if owner == index:
                pl.when(needed)(copy.wait)
        query = query_ref[pl.ds(pl.multiple_of(block * count, count), count)]
        attend(query, window_ref.at[index], bias_ref, scores_ref, weights_ref, outs[index])


def attend_blocks(place, starts, ends, query, before, keyval, behind, rows, flips, name):
    heads_width = query.shape[1]
    return pl.pallas_call(
        functools.partial(attend_kernel, flips),
        out_shape=tuple(jax.ShapeDtypeStruct((rows, heads_width), BF16) for _ in flips),
        in_specs=[SMEM, VMEM, VMEM, VMEM, ANY, ANY, ANY],
        out_specs=(VMEM,) * len(flips),
        scratch_shapes=[
            pltpu.VMEM((len(flips), 3 * rows, 2 * heads_width), BF16),
            pltpu.VMEM((rows, 3 * rows), F32),
            pltpu.VMEM((heads_width // HD, rows, 3 * rows), F32),
            pltpu.VMEM((heads_width // HD, rows, 3 * rows), BF16),
            pltpu.SemaphoreType.DMA((len(flips), 3)),
        ],
        compiler_params=pltpu.CompilerParams(vmem_limit_bytes=14 * MIB),
        cost_estimate=SHORT,
        name=name,
    )(place, starts, ends, query, before, keyval, behind)


def first_norm_kernel(layout, place_ref, hidden_ref, own_out_ref, gain_ref, bias_ref, *refs):
    parts, pieces = refs[: -5 - len(layout)], refs[-5 - len(layout) : -5]
    normed_ref, all_ref, weight_ref, mixed_ref, sems = refs[-5:]
    tok = place_ref[0]
    quarters, heads_width, width = weight_ref.shape
    copies = [pltpu.make_async_copy(own_out_ref, weight_ref.at[0], sems.at[0])]
    for flips, piece in zip(layout, pieces):
        for index, flip in enumerate(flips):
            depth = piece.shape[2]
            at = pl.multiple_of((tok ^ flip) * depth, depth)
            target = weight_ref.at[1:quarters, pl.ds(at, depth)]
            copies.append(pltpu.make_async_copy(piece.at[index], target, sems.at[len(copies)]))
    for copy in copies:
        copy.start()
    for flip, part_ref in enumerate(parts):
        all_ref[:, flip * heads_width : (flip + 1) * heads_width] = part_ref[...]
    for copy in copies:
        copy.wait()
    weight = weight_ref[...].reshape(quarters * heads_width, width)
    mixed_ref[...] = jnp.dot(all_ref[...], weight, preferred_element_type=F32)
    for row in range(0, hidden_ref.shape[0], STRIP):
        at = slice(row, row + STRIP)
        mixed = hidden_ref[at].astype(F32) + mixed_ref[at]
        normed_ref[at] = normalized(mixed, gain_ref[...], bias_ref[...]).astype(BF16)


def first_norm(place, hidden, own_out, gain, bias, parts, pieces):
    rows, width = hidden.shape
    heads_width = own_out.shape[0]
    layout = tuple(flips for flips, _ in pieces)
    return pl.pallas_call(
        functools.partial(first_norm_kernel, layout),
        out_shape=jax.ShapeDtypeStruct((rows, width), BF16),
        in_specs=[SMEM, VMEM, ANY, VMEM, VMEM] + [VMEM] * len(parts) + [ANY] * len(pieces),
        out_specs=VMEM,
        scratch_shapes=[
            pltpu.VMEM((rows, width), BF16),
            pltpu.VMEM((len(parts), heads_width, width), BF16),
            pltpu.VMEM((rows, width), F32),
            pltpu.SemaphoreType.DMA((1 + sum(len(flips) for flips in layout),)),
        ],
        compiler_params=pltpu.CompilerParams(vmem_limit_bytes=11 * MIB),
        cost_estimate=SHORT,
        name="first_norm",
    )(place, hidden, own_out, gain, bias, *parts, *[value for _, value in pieces])


def gelu(values):
    return 0.5 * values * (1.0 + lax.erf(values * math.sqrt(0.5)))


CHUNK = 512


def feed_chunk(rows, up, down_ref, wide_ref, units_ref):
    wide_ref[...] = jnp.dot(rows, up, preferred_element_type=F32)
    for row in range(0, rows.shape[0], STRIP):
        strip = slice(row, row + STRIP)
        units_ref[strip] = gelu(wide_ref[strip]).astype(BF16)
    return jnp.dot(units_ref[...], down_ref[...], preferred_element_type=F32)


def far_copies(tok, held_ref, core_ref, up_ref, down_ref, sems):
    block = 128
    copies = []
    for side, piece in enumerate((held_ref, core_ref)):
        for index in range(4):
            at = pl.ds(pl.multiple_of((tok ^ (2 * index + side)) * block, block), block)
            for part, target in enumerate((up_ref, down_ref)):
                source = piece.at[pl.ds((2 * index + part) * block, block)]
                copies.append(pltpu.make_async_copy(source, target.at[at], sems.at[len(copies)]))
    return copies


def feed_near_kernel(rows_ref, up_ref, down_ref, sum_ref, wide_ref, units_ref):
    rows = rows_ref[...]
    for index in range(up_ref.shape[1] // CHUNK):
        at = slice(index * CHUNK, (index + 1) * CHUNK)
        product = feed_chunk(rows, up_ref[:, at], down_ref.at[at], wide_ref.at[index % 2], units_ref.at[index % 2])
        if index == 0:
            sum_ref[...] = product
        else:
            sum_ref[...] += product


def feed_far_kernel(
    place_ref, rows_ref, near_ref, held_ref, core_ref, sum_ref, up_ref, down_ref, wide_ref, units_ref, total_ref, sems
):
    copies = far_copies(place_ref[0], held_ref, core_ref, up_ref, down_ref, sems)
    for copy in copies:
        copy.start()
    rows = rows_ref[...]
    total_ref[...] = near_ref[...]
    for copy in copies:
        copy.wait()
    for index in range(up_ref.shape[1] // CHUNK):
        at = slice(index * CHUNK, (index + 1) * CHUNK)
        slot = index % 2
        total_ref[...] += feed_chunk(rows, up_ref[:, at], down_ref.at[at], wide_ref.at[slot], units_ref.at[slot])
    sum_ref[...] = total_ref[...].astype(sum_ref.dtype)


def feed_kernel(
    place_ref, rows_ref, up_near_ref, down_near_ref, held_ref, core_ref, sum_ref, up_ref, down_ref, wide_ref, units_ref, sems
):
    copies = far_copies(place_ref[0], held_ref, core_ref, up_ref, down_ref, sems)
    for copy in copies:
        copy.start()
    feed_near_kernel(rows_ref, up_near_ref, down_near_ref, sum_ref, wide_ref, units_ref)
    rows = rows_ref[...]
    for copy in copies:
        copy.wait()
    for index in range(up_ref.shape[1] // CHUNK):
        at = slice(index * CHUNK, (index + 1) * CHUNK)
        slot = index % 2
        sum_ref[...] += feed_chunk(rows, up_ref[:, at], down_ref.at[at], wide_ref.at[slot], units_ref.at[slot])


def feed_scratch(count):
    return [pltpu.VMEM((2, count, CHUNK), F32), pltpu.VMEM((2, count, CHUNK), BF16)]


def feed_near(rows, up_weight, down_weight):
    return pl.pallas_call(
        feed_near_kernel,
        out_shape=jax.ShapeDtypeStruct(rows.shape, F32),
        in_specs=[VMEM] * 3,
        out_specs=VMEM,
        scratch_shapes=feed_scratch(rows.shape[0]),
        compiler_params=pltpu.CompilerParams(vmem_limit_bytes=14 * MIB),
        cost_estimate=SHORT,
        name="feed_near",
    )(rows, up_weight, down_weight)


def feed_far(place, rows, near, pieces):
    count, width = rows.shape
    units = pieces[0].shape[0]
    return pl.pallas_call(
        feed_far_kernel,
        out_shape=jax.ShapeDtypeStruct((count, width), BF16),
        in_specs=[SMEM] + [VMEM] * 2 + [ANY] * 2,
        out_specs=VMEM,
        scratch_shapes=[pltpu.VMEM((width, units), BF16), pltpu.VMEM((units, width), BF16)]
        + feed_scratch(count)
        + [pltpu.VMEM((count, width), F32), pltpu.SemaphoreType.DMA((16,))],
        compiler_params=pltpu.CompilerParams(vmem_limit_bytes=14 * MIB),
        cost_estimate=SHORT,
        name="feed_far",
    )(place, rows, near, *pieces)


def feed(place, rows, up_weight, down_weight, pieces):
    count, width = rows.shape
    units = up_weight.shape[1]
    return pl.pallas_call(
        feed_kernel,
        out_shape=jax.ShapeDtypeStruct((count, width), F32),
        in_specs=[SMEM] + [VMEM] * 3 + [ANY] * 2,
        out_specs=VMEM,
        scratch_shapes=[pltpu.VMEM((width, units), BF16), pltpu.VMEM((units, width), BF16)]
        + feed_scratch(count)
        + [pltpu.SemaphoreType.DMA((16,))],
        compiler_params=pltpu.CompilerParams(vmem_limit_bytes=18 * MIB),
        cost_estimate=SHORT,
        name="feed_own",
    )(place, rows, up_weight, down_weight, *pieces)


def finish_kernel(normed_ref, near_ref, far_ref, gain_ref, bias_ref, out_ref):
    for row in range(0, normed_ref.shape[0], STRIP):
        at = slice(row, row + STRIP)
        mixed = normed_ref[at].astype(F32) + near_ref[at] + far_ref[at].astype(F32)
        out_ref[at] = normalized(mixed, gain_ref[...], bias_ref[...]).astype(out_ref.dtype)


def finish(normed, near, far, gain, bias):
    return pl.pallas_call(
        finish_kernel,
        out_shape=jax.ShapeDtypeStruct(normed.shape, BF16),
        in_specs=[VMEM] * 5,
        out_specs=VMEM,
        compiler_params=pltpu.CompilerParams(vmem_limit_bytes=6 * MIB),
        name="finish",
    )(normed, near, far, gain, bias)


def decode_kernel(slot_ref, filled_ref, query_ref, cache_ref, out_ref, high_ref, total_ref, sum_ref):
    step = pl.program_id(0)

    @pl.when(step == 0)
    def _():
        high_ref[...] = jnp.full(high_ref.shape, NEG_FILL, F32)
        total_ref[...] = jnp.zeros_like(total_ref)
        sum_ref[...] = jnp.zeros_like(sum_ref)

    row = slot_ref[step]
    filled = filled_ref[step]
    width = query_ref.shape[1]
    head = lax.broadcasted_iota(jnp.int32, (H, width), 0)
    inside = head == lax.broadcasted_iota(jnp.int32, (H, width), 1) // HD
    query = jnp.where(inside, query_ref[pl.ds(row, 1), :], 0.0).astype(BF16)
    scores = lax.dot_general(query, cache_ref[0, 0, 0], (((1,), (1,)), ((), ())), preferred_element_type=F32)
    live = lax.broadcasted_iota(jnp.int32, scores.shape, 1) < filled
    scores = jnp.where(live, scores * (1.0 / math.sqrt(HD)), NEG_FILL)
    high = jnp.max(scores, axis=1, keepdims=True)
    weights = jnp.where(live, jnp.exp(scores - high), 0.0)
    total = jnp.sum(weights, axis=1, keepdims=True)
    summed = jnp.dot(weights.astype(BF16), cache_ref[1, 0, 0], preferred_element_type=F32)
    along = lambda column: jnp.sum(jnp.where(inside, column, 0.0), axis=0, keepdims=True)
    high, total, summed = along(high), along(total), along(summed)
    used = filled > 0
    at = pl.ds(row, 1)
    old = high_ref[at, :]
    new = jnp.where(used, jnp.maximum(old, high), old)
    left = jnp.exp(old - new)
    right = jnp.where(used, jnp.exp(high - new), 0.0)
    high_ref[at, :] = new
    total_ref[at, :] = total_ref[at, :] * left + total * right
    sum_ref[at, :] = sum_ref[at, :] * left + summed * right

    @pl.when(step == pl.num_programs(0) - 1)
    def _():
        out_ref[0] = high_ref[...]
        out_ref[1] = total_ref[...]
        out_ref[2] = sum_ref[...]


def decode(slots, filled, queries, kv_cache):
    requests, width = queries.shape
    pieces = kv_cache.shape[2]
    state = pltpu.VMEM((requests, width), F32)
    return pl.pallas_call(
        decode_kernel,
        grid=(pieces,),
        out_shape=jax.ShapeDtypeStruct((3, requests, width), F32),
        in_specs=[
            SMEM,
            SMEM,
            pl.BlockSpec((requests, width), lambda i: (0, 0)),
            pl.BlockSpec((2, 1, 1, PLEN, width), lambda i: (0, 0, i, 0, 0)),
        ],
        out_specs=pl.BlockSpec((3, requests, width), lambda i: (0, 0, 0)),
        scratch_shapes=[state, state, state],
        compiler_params=pltpu.CompilerParams(vmem_limit_bytes=8 * MIB),
        cost_estimate=SHORT,
        name="decode",
    )(slots, filled, queries, kv_cache)


def decode_partial(queries, own, kv_cache, piece_req, piece_used):
    owners = piece_req[0]
    slots = ((owners // own) ^ lax.axis_index("kv")) * own + owners % own
    return decode(slots, piece_used[0], queries, kv_cache)


def exchanged_partials(partial, own):
    parts = [partial[:, :own]]
    for flip in range(1, lax.axis_size("kv")):
        parts.append(swapped(partial[:, flip * own : (flip + 1) * own], "kv", flip))
    return parts


def merged_partials(parts):
    high = functools.reduce(jnp.maximum, [part[0] for part in parts])
    factors = [jnp.exp(part[0] - high) for part in parts]
    total = sum(part[1] * factor for part, factor in zip(parts, factors))
    summed = sum(part[2] * factor for part, factor in zip(parts, factors))
    return (summed / total).astype(BF16)


def routed_body(
    hidden_in,
    qkv_weight,
    stretch_len,
    out_weight,
    ln1_gain,
    ln1_bias,
    up_weight,
    down_weight,
    ln2_gain,
    ln2_bias,
    dec_query,
    kv_cache,
    piece_req,
    piece_used,
):
    tok = lax.axis_index("tok")
    kv = lax.axis_index("kv")
    toks, kvs = lax.axis_size("tok"), lax.axis_size("kv")
    rows, width = hidden_in.shape
    place = jnp.stack([tok, kv]).astype(jnp.int32)
    eighth = lambda value: lax.dynamic_slice_in_dim(value, tok * (value.shape[0] // toks), value.shape[0] // toks, 0)

    out_part = eighth(out_weight)
    depth = out_part.shape[0]
    small = jnp.concatenate([out_part, dec_query], axis=0)
    others = [swapped(small, "kv", flip) for flip in range(1, kvs)]
    queries = jnp.concatenate([dec_query] + [other[depth:] for other in others], axis=0).astype(F32)
    partial = decode_partial(queries, dec_query.shape[0], kv_cache, piece_req, piece_used)
    out_here = jnp.stack([other[:depth] for other in others])
    out_x, out_y = swapped(out_here, "tok", 2), swapped(out_here, "tok", 4)
    out_all = jnp.stack([out_here, out_x, out_y, swapped(out_y, "tok", 2)])
    out_core = swapped(out_all, "tok", 1)

    met = jnp.sum(out_core[0, 0].astype(F32))
    beside = {1: others, 2: [partial], 3: [met]}
    from_below, from_above = [], []
    rising = falling = hidden_in
    for step in range(1, kvs):
        rising, falling = after(rising, *beside.get(step, ())), after(falling, *beside.get(step, ()))
        links = range(step - 1, kvs - 1)
        rising = lax.ppermute(rising, "kv", [(i, i + 1) for i in links])
        falling = lax.ppermute(falling, "kv", [(kvs - 1 - i, kvs - 2 - i) for i in links])
        from_below.append(rising)
        from_above.append(falling)

    feed_up, feed_down = after((eighth(up_weight), eighth(down_weight)), from_below[1], from_above[1])
    inner_up = lax.ppermute(feed_up, "kv", [(0, 2), (3, 1)])
    inner_down = lax.ppermute(feed_down, "kv", [(0, 2), (3, 1)])
    feed_part = after(jnp.concatenate([feed_up, feed_down], axis=0), rising, falling, inner_up, inner_down)
    feed_outer = lax.ppermute(feed_part, "kv", [(1, 3), (2, 0)])
    feed_inner = jnp.concatenate([inner_up, inner_down], axis=0)

    order = jnp.arange(stretch_len.shape[0])
    ends = jnp.sum(jnp.where(order[:, None] <= order[None, :], stretch_len[:, None], 0), axis=0, dtype=jnp.int32)
    starts = (ends - stretch_len)[None, :]
    ends = ends[None, :]

    shards = [hidden_in] + from_below + from_above
    query, keyval, top, bottom = project(place, jnp.transpose(qkv_weight, (1, 0, 2)), shards)
    before = lax.ppermute(bottom, "tok", [(i, i + 1) for i in range(toks - 1)])
    behind = lax.ppermute(top, "tok", [(i + 1, i) for i in range(toks - 1)])
    window = (place, starts, ends, query, before, keyval, behind, rows)
    parts = [None] * kvs
    parts[3], parts[2] = attend_blocks(*window, (3, 2), "attend_far")
    window = (place, starts, ends, after(query, parts[3]), before, keyval, behind, rows)
    parts[3], parts[2] = swapped(parts[3], "kv", 3), swapped(parts[2], "kv", 2)
    parts[1], parts[0] = attend_blocks(*window, (1, 0), "attend_near")
    inner = (kv == 1) | (kv == 2)
    feed_here = jnp.where(inner, feed_inner, after(feed_outer, *parts[2:], parts[0]))
    parts[1] = swapped(parts[1], "kv", 1)
    feed_x, feed_y = swapped(feed_here, "tok", 2), swapped(feed_here, "tok", 4)
    out_pieces = [((0, 2, 4, 6), out_all), ((1, 3, 5, 7), out_core)]
    normed = first_norm(place, hidden_in, out_weight, ln1_gain[None, :], ln1_bias[None, :], parts, out_pieces)

    partner = swapped(normed, "kv", 1)
    half = feed_here.shape[0] // 2
    far_up = swapped(after(feed_y, normed)[:half], "tok", 2)
    far_down = swapped(after(feed_x, normed)[half:], "tok", 4)
    held = jnp.concatenate([feed_here, feed_x, feed_y, far_up, far_down], axis=0)
    near_away = feed_near(partner, up_weight, down_weight)
    feed_pieces = (held, swapped(after(held, partner), "tok", 1))
    away = feed_far(place, partner, near_away, feed_pieces)
    arrived = swapped(away, "kv", 1)
    dec_parts = exchanged_partials(after(partial, away), dec_query.shape[0])
    mine = feed(place, after(normed, away), up_weight, down_weight, feed_pieces)
    prefill_out = finish(normed, mine, arrived, ln2_gain[None, :], ln2_bias[None, :])

    return prefill_out, merged_partials(after(tuple(dec_parts), mine))


def extended(value, sides, width):
    for axis, dim in sides:
        count, length = (lax.axis_size(axis), value.shape[dim])
        up = [(i, (i + 1) % count) for i in range(count - 1)]
        down = [(j, i) for i, j in up]
        last = lax.slice_in_dim(value, length - width, length, axis=dim)
        leading = lax.slice_in_dim(value, 0, width, axis=dim)
        before = lax.ppermute(last, axis, up)
        after = lax.ppermute(leading, axis, down)
        value = jnp.concatenate([before, value, after], axis=dim)
    return value


def merged(value, axis, join):
    pieces = jax.tree.map(lambda part: lax.all_gather(part, axis), value)
    head = jax.tree.map(lambda part: part[0], pieces)
    tail = jax.tree.map(lambda part: part[1:], pieces)
    subtotal, _ = lax.scan(lambda subtotal, section: (join(subtotal, section), None), head, tail)
    return subtotal


def segment_ids(row_ids, stretch_len):
    stretch_ends = jnp.cumsum(stretch_len)
    return jnp.sum((row_ids[:, None] >= stretch_ends[None, :]).astype(jnp.int32), axis=1)


def layer_norm(values, gain, bias):
    center = values - jnp.mean(values, axis=1, keepdims=True)
    spread = jnp.mean(center * center, axis=1, keepdims=True)
    return center * lax.rsqrt(spread + LN_EPS) * gain + bias


def merge_partials(earlier, later):
    highest = jnp.maximum(earlier[0], later[0])
    left_factor = jnp.exp(earlier[0] - highest)
    right_factor = jnp.exp(later[0] - highest)
    totals = earlier[1] * left_factor + later[1] * right_factor
    weighted = earlier[2] * left_factor[..., None] + later[2] * right_factor[..., None]
    return (highest, totals, weighted)


def row_folder(source, shard_rows):
    return jnp.dot(source, shard_rows, preferred_element_type=jnp.float32)


def general_body(
    hidden_in,
    qkv_weight,
    stretch_len,
    out_weight,
    ln1_gain,
    ln1_bias,
    up_weight,
    down_weight,
    ln2_gain,
    ln2_bias,
    dec_query,
    kv_cache,
    piece_req,
    piece_used,
):
    inv_scale = 1.0 / math.sqrt(HD)
    reach = WIN // 2
    local_width = qkv_weight.shape[2]
    head_count = local_width // HD
    flat_weight = qkv_weight.reshape(qkv_weight.shape[0], 3 * local_width)
    qkv_rows = jnp.dot(
        lax.all_gather(hidden_in, "kv", axis=0, tiled=True),
        flat_weight,
        preferred_element_type=jnp.float32,
    ).astype(jnp.bfloat16)
    row_count = qkv_rows.shape[0]
    query_rows = qkv_rows[:, :local_width]
    keyval_rows = qkv_rows[:, local_width:]
    padded = extended(keyval_rows, (("tok", 0),), reach)
    first_row = lax.axis_index("tok") * row_count
    total_rows = row_count * lax.axis_size("tok")
    qblock = min(512, row_count)
    span = qblock + 2 * reach
    block_count = row_count // qblock

    def attend(block_index):
        start = block_index * qblock
        query_ids = first_row + start + jnp.arange(qblock, dtype=jnp.int32)
        key_ids = first_row + start - reach + jnp.arange(span, dtype=jnp.int32)
        query_seg = segment_ids(query_ids, stretch_len)
        inside = (key_ids >= 0) & (key_ids < total_rows)
        key_seg = jnp.where(inside, segment_ids(key_ids, stretch_len), -1)
        allowed = (key_seg[None, :] == query_seg[:, None]) & (
            jnp.abs(key_ids[None, :] - query_ids[:, None]) <= reach
        )
        queries = lax.dynamic_slice_in_dim(query_rows, start, qblock, 0).reshape(
            qblock, head_count, HD
        )
        both = lax.dynamic_slice_in_dim(padded, start, span, 0)
        key_rows = both[:, :local_width].reshape(span, head_count, HD)
        value_rows = both[:, local_width:].reshape(span, head_count, HD)
        scores = (
            jnp.einsum("ihd,jhd->hij", queries, key_rows, preferred_element_type=jnp.float32)
            * inv_scale
        )
        scores = jnp.where(allowed[None], scores, NEG_FILL)
        row_max = jnp.max(scores, axis=2, keepdims=True)
        weights = jnp.where(allowed[None], jnp.exp(scores - row_max), 0.0)
        totals = jnp.sum(weights, axis=2)
        summed = jnp.einsum(
            "hij,jhd->ihd",
            weights.astype(jnp.bfloat16),
            value_rows,
            preferred_element_type=jnp.float32,
        )
        return (
            (summed / jnp.transpose(totals)[:, :, None])
            .astype(jnp.bfloat16)
            .reshape(qblock, local_width)
        )

    attention = lax.map(attend, jnp.arange(block_count, dtype=jnp.int32)).reshape(
        row_count, local_width
    )
    token_major = lax.all_to_all(attention, "kv", split_axis=0, concat_axis=1, tiled=True)
    projected = row_folder(token_major, lax.all_gather(out_weight, "kv", axis=0, tiled=True))
    normed = layer_norm(hidden_in.astype(jnp.float32) + projected, ln1_gain, ln1_bias).astype(
        jnp.bfloat16
    )
    units = jax.nn.gelu(
        jnp.dot(
            lax.all_gather(normed, "kv", axis=0, tiled=True),
            up_weight,
            preferred_element_type=jnp.float32,
        ),
        approximate=False,
    ).astype(jnp.bfloat16)
    ffn = lax.psum_scatter(
        jnp.dot(units, down_weight, preferred_element_type=jnp.float32).astype(jnp.bfloat16),
        "kv",
        scatter_dimension=0,
        tiled=True,
    ).astype(jnp.float32)
    prefill_out = layer_norm(normed.astype(jnp.float32) + ffn, ln2_gain, ln2_bias).astype(
        jnp.bfloat16
    )
    group_queries = lax.all_gather(dec_query, "kv", axis=0, tiled=True)
    request_count = group_queries.shape[0]
    owners = piece_req[0]
    filled = piece_used[0]
    slot_count = owners.shape[0]
    request_ids = jnp.arange(request_count, dtype=jnp.int32)
    selector = (owners[:, None] == request_ids[None, :]).astype(jnp.bfloat16)
    chosen = jnp.dot(selector, group_queries, preferred_element_type=jnp.float32).astype(
        jnp.bfloat16
    )
    chosen = chosen.reshape(slot_count, H, HD)
    cache_keys = kv_cache[0, 0].reshape(slot_count, PLEN, H, HD)
    cache_values = kv_cache[1, 0].reshape(slot_count, PLEN, H, HD)
    piece_scores = (
        jnp.einsum("phd,pthd->pht", chosen, cache_keys, preferred_element_type=jnp.float32)
        * inv_scale
    )
    active = jnp.arange(PLEN, dtype=jnp.int32)[None, :] < filled[:, None]
    piece_scores = jnp.where(active[:, None, :], piece_scores, NEG_FILL)
    piece_max = jnp.max(piece_scores, axis=2)
    piece_weights = jnp.where(
        active[:, None, :], jnp.exp(piece_scores - piece_max[:, :, None]), 0.0
    )
    piece_totals = jnp.sum(piece_weights, axis=2)
    partial_value = jnp.einsum(
        "pht,pthd->phd",
        piece_weights.astype(jnp.bfloat16),
        cache_values,
        preferred_element_type=jnp.float32,
    )
    member = (owners[None, :] == request_ids[:, None]) & (filled[None, :] > 0)
    highest = jnp.max(jnp.where(member[:, :, None], piece_max[None], NEG_FILL), axis=1)
    factor = jnp.where(member[:, :, None], jnp.exp(piece_max[None] - highest[:, None, :]), 0.0)
    denom = jnp.sum(factor * piece_totals[None], axis=1)
    weighted = jnp.einsum("rph,phd->rhd", factor, partial_value)
    own_requests = dec_query.shape[0]
    joined = merged((highest, denom, weighted), "kv", merge_partials)
    begin = lax.axis_index("kv") * own_requests
    final_denom = lax.dynamic_slice_in_dim(joined[1], begin, own_requests, 0)
    final_weighted = lax.dynamic_slice_in_dim(joined[2], begin, own_requests, 0)
    dec_out = (
        (final_weighted / final_denom[:, :, None])
        .astype(jnp.bfloat16)
        .reshape(own_requests, H * HD)
    )
    return (prefill_out, dec_out)


def solution(mesh):
    placed = (
        P(("tok", "kv"), None),
        P(None, None, "kv"),
        P(),
        P("kv", None),
        P(),
        P(),
        P(None, "kv"),
        P("kv", None),
        P(),
        P(),
        P(("tok", "kv"), None),
        P(None, "tok", "kv", None, None),
        P("tok", "kv"),
        P("tok", "kv"),
    )
    routed = mesh.shape["tok"] == 8 and mesh.shape["kv"] == 4
    return jax.shard_map(
        routed_body if routed else general_body,
        mesh=mesh,
        in_specs=placed,
        out_specs=(P(("tok", "kv"), None), P(("tok", "kv"), None)),
        check_vma=False,
    )
```

```python
import functools
import math

import jax
import jax.numpy as jnp
from jax import lax
from jax.experimental import pallas as pl
from jax.experimental.pallas import tpu as pltpu
from jax.sharding import PartitionSpec as P

H = 16
HD = 64
WIN = 512
PLEN = 128


NEG_FILL = -1e30
LN_EPS = 1e-05
BF16 = jnp.bfloat16
F32 = jnp.float32
STRIP = 32
MIB = 1024 * 1024
ANY = pl.BlockSpec(memory_space=pl.ANY)
VMEM = pl.BlockSpec(memory_space=pltpu.VMEM)
SMEM = pl.BlockSpec(memory_space=pltpu.SMEM)
SHORT = pl.CostEstimate(flops=1, bytes_accessed=1, transcendentals=0)


def swapped(value, axis, flip):
    count = lax.axis_size(axis)
    return lax.ppermute(value, axis, [(i, i ^ flip) for i in range(count)])


def over_edges(value, axis, first):
    count = lax.axis_size(axis)
    edges = [(i, i + 1) for i in range(first, count - 1, 2)]
    return lax.ppermute(value, axis, edges + [(j, i) for i, j in edges])


def chain(value):
    outward = [(1, 0), (2, 3)]
    a1, b1 = over_edges(value, "kv", 0), over_edges(value, "kv", 1)
    a2, b2 = lax.ppermute(b1, "kv", outward), over_edges(a1, "kv", 1)
    a3 = lax.ppermute(b2, "kv", outward)
    return a1, a2, a3, b1, b2


def after(value, *earlier):
    return lax.optimization_barrier((value,) + earlier)[0]


def normalized(values, gain, bias):
    center = values - jnp.mean(values, axis=1, keepdims=True)
    spread = jnp.mean(center * center, axis=1, keepdims=True)
    return center * lax.rsqrt(spread + LN_EPS) * gain + bias


def project_kernel(place_ref, weight_ref, *refs):
    shards, (query_ref, keyval_ref, even_ref, odd_ref, riders_ref, rows_ref, sems, rider_sems) = refs[:-8], refs[-8:]
    own, a1, a2, a3, b1, b2 = shards
    tok, kv = place_ref[0], place_ref[1]
    count, depth = even_ref.shape[0], riders_ref.shape[1]
    blocks = rows_ref.shape[0] // count
    width = weight_ref.shape[2]
    inner = (kv == 1) | (kv == 2)
    outer = jnp.logical_not(inner)
    copies = []
    for source, flip, needed in ((own, 0, kv >= 0), (a1, 1, kv >= 0), (a2, 2, outer), (b2, 2, inner), (a3, 3, outer), (b1, 3, inner)):
        at = pl.ds(pl.multiple_of((kv ^ flip) * count, count), count)
        copies.append((needed, pltpu.make_async_copy(source.at[0:count], rows_ref.at[at], sems.at[len(copies)])))
        if flip:
            rider = source.at[count : count + depth]
            target = riders_ref.at[flip - 1]
            copies.append((needed, pltpu.make_async_copy(rider, target, rider_sems.at[len(copies)])))
    for needed, copy in copies:
        pl.when(needed)(copy.start)
    for needed, copy in copies:
        pl.when(needed)(copy.wait)
    rows = rows_ref[...]
    query = jnp.dot(rows, weight_ref[0], preferred_element_type=F32) * (1.0 / math.sqrt(HD))
    query_ref[...] = query.astype(BF16)
    for part in range(2):
        at = slice(part * width, (part + 1) * width)
        keyval_ref[:, at] = jnp.dot(rows, weight_ref[part + 1], preferred_element_type=F32).astype(BF16)
    top, bottom = slice(0, count), slice((blocks - 1) * count, blocks * count)

    @pl.when(tok % 2 == 0)
    def _():
        even_ref[...] = keyval_ref[bottom]
        odd_ref[...] = keyval_ref[top]

    @pl.when(tok % 2 == 1)
    def _():
        even_ref[...] = keyval_ref[top]
        odd_ref[...] = keyval_ref[bottom]


def project(place, weight, shards, blocks, depth):
    rows, width = shards[0].shape
    heads_width = weight.shape[2]
    edge = jax.ShapeDtypeStruct((rows, 2 * heads_width), BF16)
    return pl.pallas_call(
        project_kernel,
        out_shape=(
            jax.ShapeDtypeStruct((blocks * rows, heads_width), BF16),
            jax.ShapeDtypeStruct((blocks * rows, 2 * heads_width), BF16),
            edge,
            edge,
            jax.ShapeDtypeStruct((blocks - 1, depth, width), BF16),
        ),
        in_specs=[SMEM, VMEM] + [ANY] * len(shards),
        out_specs=(VMEM,) * 5,
        scratch_shapes=[
            pltpu.VMEM((blocks * rows, width), BF16),
            pltpu.SemaphoreType.DMA((2 * len(shards),)),
            pltpu.SemaphoreType.DMA((2 * len(shards),)),
        ],
        compiler_params=pltpu.CompilerParams(vmem_limit_bytes=14 * MIB),
        cost_estimate=SHORT,
        name="project",
    )(place, weight, *shards)


def window_bias(first, count, starts, ends):
    reach = WIN // 2
    query = first + lax.broadcasted_iota(jnp.int32, (count, 1), 0)
    low = jnp.max(jnp.where(starts <= query, starts, 0), axis=1, keepdims=True)
    high = jnp.min(jnp.where(ends > query, ends, 1 << 30), axis=1, keepdims=True)
    low = jnp.maximum(low, query - reach)
    high = jnp.minimum(high, query + reach + 1)
    key = first - count + lax.broadcasted_iota(jnp.int32, (count, 3 * count), 1)
    return jnp.where((key >= low) & (key < high), 0.0, NEG_FILL)


def attend(query, keyval_ref, bias_ref, scores_ref, weights_ref, out_ref):
    count, width = query.shape
    lane = lax.broadcasted_iota(jnp.int32, (count, 2 * HD), 1)
    for start in range(0, width, 2 * HD):
        values = keyval_ref[:, width + start : width + start + 2 * HD]
        halves = []
        for side in range(2):
            head = start // HD + side
            inside = (lane < HD) if side == 0 else (lane >= HD)
            only = jnp.where(inside, query[:, start : start + 2 * HD], jnp.zeros((), BF16))
            scores_ref[head] = lax.dot_general(
                only, keyval_ref[:, start : start + 2 * HD], (((1,), (1,)), ((), ())), preferred_element_type=F32
            )
            totals = []
            for row in range(0, count, STRIP):
                at = slice(row, row + STRIP)
                scores = scores_ref[head, at] + bias_ref[at]
                weights = jnp.exp(scores - jnp.max(scores, axis=1, keepdims=True))
                totals.append(jnp.sum(weights, axis=1, keepdims=True))
                weights_ref[head, at] = weights.astype(BF16)
            summed = jnp.dot(weights_ref[head], values, preferred_element_type=F32)
            halves.append(summed / jnp.concatenate(totals, axis=0))
        out_ref[:, start : start + 2 * HD] = jnp.where(lane < HD, halves[0], halves[1]).astype(BF16)


def attend_kernel(flips, place_ref, starts_ref, ends_ref, query_ref, keyval_ref, even_ref, odd_ref, *refs):
    outs = refs[: len(flips)]
    window_ref, bias_ref, scores_ref, weights_ref, sems = refs[len(flips) :]
    tok, kv = place_ref[0], place_ref[1]
    count = outs[0].shape[0]
    blocks = query_ref.shape[0] // count
    copies = []
    for index, flip in enumerate(flips):
        block = kv ^ flip
        for part in range(3):
            target = window_ref.at[index, part * count : (part + 1) * count]
            sem = sems.at[index, part]
            at = block + part - 1
            inner = (at >= 0) & (at < blocks)
            safe = jnp.where(inner, at, 0)
            source = keyval_ref.at[pl.ds(pl.multiple_of(safe * count, count), count)]
            copies.append((index, inner, pltpu.make_async_copy(source, target, sem)))
            for first_edge, outside in ((tok % 2 == 1, at < 0), (tok % 2 == 0, at >= blocks)):
                if part != 1:
                    copies.append((index, outside & first_edge, pltpu.make_async_copy(even_ref, target, sem)))
                    other = jnp.logical_not(first_edge)
                    copies.append((index, outside & other, pltpu.make_async_copy(odd_ref, target, sem)))
    for _, needed, copy in copies:
        pl.when(needed)(copy.start)
    for index, flip in enumerate(flips):
        block = kv ^ flip
        first = (tok * blocks + block) * count
        bias_ref[...] = window_bias(first, count, starts_ref[...], ends_ref[...])
        for owner, needed, copy in copies:
            if owner == index:
                pl.when(needed)(copy.wait)
        query = query_ref[pl.ds(pl.multiple_of(block * count, count), count)]
        attend(query, window_ref.at[index], bias_ref, scores_ref, weights_ref, outs[index])


def attend_blocks(place, starts, ends, query, keyval, even, odd, rows, flips, name):
    heads_width = query.shape[1]
    return pl.pallas_call(
        functools.partial(attend_kernel, flips),
        out_shape=tuple(jax.ShapeDtypeStruct((rows, heads_width), BF16) for _ in flips),
        in_specs=[SMEM, VMEM, VMEM, VMEM, ANY, ANY, ANY],
        out_specs=(VMEM,) * len(flips),
        scratch_shapes=[
            pltpu.VMEM((len(flips), 3 * rows, 2 * heads_width), BF16),
            pltpu.VMEM((rows, 3 * rows), F32),
            pltpu.VMEM((heads_width // HD, rows, 3 * rows), F32),
            pltpu.VMEM((heads_width // HD, rows, 3 * rows), BF16),
            pltpu.SemaphoreType.DMA((len(flips), 3)),
        ],
        compiler_params=pltpu.CompilerParams(vmem_limit_bytes=14 * MIB),
        cost_estimate=SHORT,
        name=name,
    )(place, starts, ends, query, keyval, even, odd)


def first_norm_kernel(layout, place_ref, hidden_ref, own_out_ref, gain_ref, bias_ref, *refs):
    parts, pieces = refs[: -5 - len(layout)], refs[-5 - len(layout) : -5]
    normed_ref, all_ref, weight_ref, mixed_ref, sems = refs[-5:]
    tok = place_ref[0]
    quarters, heads_width, width = weight_ref.shape
    copies = [pltpu.make_async_copy(own_out_ref, weight_ref.at[0], sems.at[0])]
    for flips, piece in zip(layout, pieces):
        for index, flip in enumerate(flips):
            depth = piece.shape[2]
            at = pl.multiple_of((tok ^ flip) * depth, depth)
            target = weight_ref.at[1:quarters, pl.ds(at, depth)]
            copies.append(pltpu.make_async_copy(piece.at[index], target, sems.at[len(copies)]))
    for copy in copies:
        copy.start()
    for flip, part_ref in enumerate(parts):
        all_ref[:, flip * heads_width : (flip + 1) * heads_width] = part_ref[...]
    for copy in copies:
        copy.wait()
    weight = weight_ref[...].reshape(quarters * heads_width, width)
    mixed_ref[...] = jnp.dot(all_ref[...], weight, preferred_element_type=F32)
    for row in range(0, hidden_ref.shape[0], STRIP):
        at = slice(row, row + STRIP)
        mixed = hidden_ref[at].astype(F32) + mixed_ref[at]
        normed_ref[at] = normalized(mixed, gain_ref[...], bias_ref[...]).astype(BF16)


def first_norm(place, hidden, own_out, gain, bias, parts, pieces):
    rows, width = hidden.shape
    heads_width = own_out.shape[0]
    layout = tuple(flips for flips, _ in pieces)
    return pl.pallas_call(
        functools.partial(first_norm_kernel, layout),
        out_shape=jax.ShapeDtypeStruct((rows, width), BF16),
        in_specs=[SMEM, VMEM, ANY, VMEM, VMEM] + [VMEM] * len(parts) + [ANY] * len(pieces),
        out_specs=VMEM,
        scratch_shapes=[
            pltpu.VMEM((rows, width), BF16),
            pltpu.VMEM((len(parts), heads_width, width), BF16),
            pltpu.VMEM((rows, width), F32),
            pltpu.SemaphoreType.DMA((1 + sum(len(flips) for flips in layout),)),
        ],
        compiler_params=pltpu.CompilerParams(vmem_limit_bytes=11 * MIB),
        cost_estimate=SHORT,
        name="first_norm",
    )(place, hidden, own_out, gain, bias, *parts, *[value for _, value in pieces])


def gelu(values):
    return 0.5 * values * (1.0 + lax.erf(values * math.sqrt(0.5)))


CHUNK = 512


def feed_chunk(rows, up, down_ref, wide_ref, units_ref):
    wide_ref[...] = jnp.dot(rows, up, preferred_element_type=F32)
    for row in range(0, rows.shape[0], STRIP):
        strip = slice(row, row + STRIP)
        units_ref[strip] = gelu(wide_ref[strip]).astype(BF16)
    return jnp.dot(units_ref[...], down_ref[...], preferred_element_type=F32)


def far_copies(tok, held_ref, core_ref, up_ref, down_ref, sems):
    block = 128
    copies = []
    for side, piece in enumerate((held_ref, core_ref)):
        for index in range(4):
            at = pl.ds(pl.multiple_of((tok ^ (2 * index + side)) * block, block), block)
            for part, target in enumerate((up_ref, down_ref)):
                source = piece.at[pl.ds((2 * index + part) * block, block)]
                copies.append(pltpu.make_async_copy(source, target.at[at], sems.at[len(copies)]))
    return copies


def feed_near_kernel(rows_ref, up_ref, down_ref, sum_ref, wide_ref, units_ref):
    rows = rows_ref[...]
    for index in range(up_ref.shape[1] // CHUNK):
        at = slice(index * CHUNK, (index + 1) * CHUNK)
        product = feed_chunk(rows, up_ref[:, at], down_ref.at[at], wide_ref.at[index % 2], units_ref.at[index % 2])
        if index == 0:
            sum_ref[...] = product
        else:
            sum_ref[...] += product


def feed_far_kernel(
    place_ref, rows_ref, near_ref, held_ref, core_ref, sum_ref, up_ref, down_ref, wide_ref, units_ref, total_ref, sems
):
    copies = far_copies(place_ref[0], held_ref, core_ref, up_ref, down_ref, sems)
    for copy in copies:
        copy.start()
    rows = rows_ref[...]
    total_ref[...] = near_ref[...]
    for copy in copies:
        copy.wait()
    for index in range(up_ref.shape[1] // CHUNK):
        at = slice(index * CHUNK, (index + 1) * CHUNK)
        slot = index % 2
        total_ref[...] += feed_chunk(rows, up_ref[:, at], down_ref.at[at], wide_ref.at[slot], units_ref.at[slot])
    sum_ref[...] = total_ref[...].astype(sum_ref.dtype)


def feed_kernel(
    place_ref, rows_ref, up_near_ref, down_near_ref, held_ref, core_ref, sum_ref, up_ref, down_ref, wide_ref, units_ref, sems
):
    copies = far_copies(place_ref[0], held_ref, core_ref, up_ref, down_ref, sems)
    for copy in copies:
        copy.start()
    feed_near_kernel(rows_ref, up_near_ref, down_near_ref, sum_ref, wide_ref, units_ref)
    rows = rows_ref[...]
    for copy in copies:
        copy.wait()
    for index in range(up_ref.shape[1] // CHUNK):
        at = slice(index * CHUNK, (index + 1) * CHUNK)
        slot = index % 2
        sum_ref[...] += feed_chunk(rows, up_ref[:, at], down_ref.at[at], wide_ref.at[slot], units_ref.at[slot])


def feed_scratch(count):
    return [pltpu.VMEM((2, count, CHUNK), F32), pltpu.VMEM((2, count, CHUNK), BF16)]


def feed_near(rows, up_weight, down_weight):
    return pl.pallas_call(
        feed_near_kernel,
        out_shape=jax.ShapeDtypeStruct(rows.shape, F32),
        in_specs=[VMEM] * 3,
        out_specs=VMEM,
        scratch_shapes=feed_scratch(rows.shape[0]),
        compiler_params=pltpu.CompilerParams(vmem_limit_bytes=14 * MIB),
        cost_estimate=SHORT,
        name="feed_near",
    )(rows, up_weight, down_weight)


def feed_far(place, rows, near, pieces):
    count, width = rows.shape
    units = pieces[0].shape[0]
    return pl.pallas_call(
        feed_far_kernel,
        out_shape=jax.ShapeDtypeStruct((count, width), BF16),
        in_specs=[SMEM] + [VMEM] * 2 + [ANY] * 2,
        out_specs=VMEM,
        scratch_shapes=[pltpu.VMEM((width, units), BF16), pltpu.VMEM((units, width), BF16)]
        + feed_scratch(count)
        + [pltpu.VMEM((count, width), F32), pltpu.SemaphoreType.DMA((16,))],
        compiler_params=pltpu.CompilerParams(vmem_limit_bytes=14 * MIB),
        cost_estimate=SHORT,
        name="feed_far",
    )(place, rows, near, *pieces)


def feed(place, rows, up_weight, down_weight, pieces):
    count, width = rows.shape
    units = up_weight.shape[1]
    return pl.pallas_call(
        feed_kernel,
        out_shape=jax.ShapeDtypeStruct((count, width), F32),
        in_specs=[SMEM] + [VMEM] * 3 + [ANY] * 2,
        out_specs=VMEM,
        scratch_shapes=[pltpu.VMEM((width, units), BF16), pltpu.VMEM((units, width), BF16)]
        + feed_scratch(count)
        + [pltpu.SemaphoreType.DMA((16,))],
        compiler_params=pltpu.CompilerParams(vmem_limit_bytes=18 * MIB),
        cost_estimate=SHORT,
        name="feed_own",
    )(place, rows, up_weight, down_weight, *pieces)


def finish_kernel(normed_ref, near_ref, far_ref, gain_ref, bias_ref, out_ref):
    for row in range(0, normed_ref.shape[0], STRIP):
        at = slice(row, row + STRIP)
        mixed = normed_ref[at].astype(F32) + near_ref[at] + far_ref[at].astype(F32)
        out_ref[at] = normalized(mixed, gain_ref[...], bias_ref[...]).astype(out_ref.dtype)


def finish(normed, near, far, gain, bias):
    return pl.pallas_call(
        finish_kernel,
        out_shape=jax.ShapeDtypeStruct(normed.shape, BF16),
        in_specs=[VMEM] * 5,
        out_specs=VMEM,
        compiler_params=pltpu.CompilerParams(vmem_limit_bytes=6 * MIB),
        name="finish",
    )(normed, near, far, gain, bias)


def decode_kernel(slot_ref, filled_ref, query_ref, cache_ref, out_ref, high_ref, total_ref, sum_ref):
    step = pl.program_id(0)

    @pl.when(step == 0)
    def _():
        high_ref[...] = jnp.full(high_ref.shape, NEG_FILL, F32)
        total_ref[...] = jnp.zeros_like(total_ref)
        sum_ref[...] = jnp.zeros_like(sum_ref)

    row = slot_ref[step]
    filled = filled_ref[step]
    width = query_ref.shape[1]
    head = lax.broadcasted_iota(jnp.int32, (H, width), 0)
    inside = head == lax.broadcasted_iota(jnp.int32, (H, width), 1) // HD
    query = jnp.where(inside, query_ref[pl.ds(row, 1), :], 0.0).astype(BF16)
    scores = lax.dot_general(query, cache_ref[0, 0, 0], (((1,), (1,)), ((), ())), preferred_element_type=F32)
    live = lax.broadcasted_iota(jnp.int32, scores.shape, 1) < filled
    scores = jnp.where(live, scores * (1.0 / math.sqrt(HD)), NEG_FILL)
    high = jnp.max(scores, axis=1, keepdims=True)
    weights = jnp.where(live, jnp.exp(scores - high), 0.0)
    total = jnp.sum(weights, axis=1, keepdims=True)
    summed = jnp.dot(weights.astype(BF16), cache_ref[1, 0, 0], preferred_element_type=F32)
    along = lambda column: jnp.sum(jnp.where(inside, column, 0.0), axis=0, keepdims=True)
    high, total, summed = along(high), along(total), along(summed)
    used = filled > 0
    at = pl.ds(row, 1)
    old = high_ref[at, :]
    new = jnp.where(used, jnp.maximum(old, high), old)
    left = jnp.exp(old - new)
    right = jnp.where(used, jnp.exp(high - new), 0.0)
    high_ref[at, :] = new
    total_ref[at, :] = total_ref[at, :] * left + total * right
    sum_ref[at, :] = sum_ref[at, :] * left + summed * right

    @pl.when(step == pl.num_programs(0) - 1)
    def _():
        out_ref[0] = high_ref[...]
        out_ref[1] = total_ref[...]
        out_ref[2] = sum_ref[...]


def decode(slots, filled, queries, kv_cache):
    requests, width = queries.shape
    pieces = kv_cache.shape[2]
    state = pltpu.VMEM((requests, width), F32)
    return pl.pallas_call(
        decode_kernel,
        grid=(pieces,),
        out_shape=jax.ShapeDtypeStruct((3, requests, width), F32),
        in_specs=[
            SMEM,
            SMEM,
            pl.BlockSpec((requests, width), lambda i: (0, 0)),
            pl.BlockSpec((2, 1, 1, PLEN, width), lambda i: (0, 0, i, 0, 0)),
        ],
        out_specs=pl.BlockSpec((3, requests, width), lambda i: (0, 0, 0)),
        scratch_shapes=[state, state, state],
        compiler_params=pltpu.CompilerParams(vmem_limit_bytes=8 * MIB),
        cost_estimate=SHORT,
        name="decode",
    )(slots, filled, queries, kv_cache)


def decode_partial(queries, own, kv_cache, piece_req, piece_used):
    owners = piece_req[0]
    slots = ((owners // own) ^ lax.axis_index("kv")) * own + owners % own
    return decode(slots, piece_used[0], queries, kv_cache)


def exchanged_partials(partial, own):
    parts = [partial[:, :own]]
    for flip in range(1, lax.axis_size("kv")):
        parts.append(swapped(partial[:, flip * own : (flip + 1) * own], "kv", flip))
    return parts


def merged_partials(parts):
    high = functools.reduce(jnp.maximum, [part[0] for part in parts])
    factors = [jnp.exp(part[0] - high) for part in parts]
    total = sum(part[1] * factor for part, factor in zip(parts, factors))
    summed = sum(part[2] * factor for part, factor in zip(parts, factors))
    return (summed / total).astype(BF16)


def routed_body(
    hidden_in,
    qkv_weight,
    stretch_len,
    out_weight,
    ln1_gain,
    ln1_bias,
    up_weight,
    down_weight,
    ln2_gain,
    ln2_bias,
    dec_query,
    kv_cache,
    piece_req,
    piece_used,
):
    tok = lax.axis_index("tok")
    kv = lax.axis_index("kv")
    toks, kvs = lax.axis_size("tok"), lax.axis_size("kv")
    rows, width = hidden_in.shape
    place = jnp.stack([tok, kv]).astype(jnp.int32)
    eighth = lambda value: lax.dynamic_slice_in_dim(value, tok * (value.shape[0] // toks), value.shape[0] // toks, 0)

    out_part = eighth(out_weight)
    depth = out_part.shape[0]
    shards = chain(jnp.concatenate([hidden_in, out_part, dec_query], axis=0))
    a1, a2, a3, b1, b2 = shards
    inner = (kv == 1) | (kv == 2)

    feed_up, feed_down = after((eighth(up_weight), eighth(down_weight)), a2, b2)
    inner_up = lax.ppermute(feed_up, "kv", [(0, 2), (3, 1)])
    inner_down = lax.ppermute(feed_down, "kv", [(0, 2), (3, 1)])
    feed_part = after(jnp.concatenate([feed_up, feed_down], axis=0), a3, inner_up, inner_down)
    feed_outer = lax.ppermute(feed_part, "kv", [(1, 3), (2, 0)])
    feed_inner = jnp.concatenate([inner_up, inner_down], axis=0)

    order = jnp.arange(stretch_len.shape[0])
    ends = jnp.sum(jnp.where(order[:, None] <= order[None, :], stretch_len[:, None], 0), axis=0, dtype=jnp.int32)
    starts = (ends - stretch_len)[None, :]
    ends = ends[None, :]

    weight = jnp.transpose(qkv_weight, (1, 0, 2))
    query, keyval, even, odd, out_here = project(place, weight, (hidden_in,) + shards, kvs, depth)
    even, odd = over_edges(even, "tok", 0), over_edges(odd, "tok", 1)
    window = (place, starts, ends, query, keyval, even, odd, rows)
    parts = [None] * kvs
    parts[3], parts[2] = attend_blocks(*window, (3, 2), "attend_far")
    out_here = after(out_here, parts[3])
    out_all = [out_here] + [swapped(out_here, "tok", flip) for flip in (2, 4, 6)]
    window = (place, starts, ends, after(query, parts[3]), keyval, even, odd, rows)
    parts[3], parts[2] = swapped(parts[3], "kv", 3), swapped(parts[2], "kv", 2)
    parts[1], parts[0] = attend_blocks(*window, (1, 0), "attend_near")
    out_all = after(jnp.stack(out_all), parts[0])
    out_core = swapped(out_all, "tok", 1)
    feed_here = jnp.where(inner, feed_inner, after(feed_outer, *parts[2:], parts[0]))
    parts[1] = swapped(parts[1], "kv", 1)
    feed_x, feed_y = swapped(feed_here, "tok", 2), swapped(feed_here, "tok", 4)
    out_pieces = [((0, 2, 4, 6), out_all), ((1, 3, 5, 7), out_core)]
    normed = first_norm(place, hidden_in, out_weight, ln1_gain[None, :], ln1_bias[None, :], parts, out_pieces)

    partner = swapped(normed, "kv", 1)
    half = feed_here.shape[0] // 2
    far_up = swapped(after(feed_y, normed)[:half], "tok", 2)
    far_down = swapped(after(feed_x, normed)[half:], "tok", 4)
    ends_of = lambda outer_one, inner_one: jnp.where(inner, inner_one[rows + depth :], outer_one[rows + depth :])
    queries = [dec_query, a1[rows + depth :], ends_of(a2, b2), ends_of(a3, b1)]
    queries = after(jnp.concatenate(queries, axis=0).astype(F32), normed)
    partial = decode_partial(queries, dec_query.shape[0], kv_cache, piece_req, piece_used)
    held = jnp.concatenate([feed_here, feed_x, feed_y, after(far_up, partial), far_down], axis=0)
    near_away = feed_near(partner, up_weight, down_weight)
    feed_pieces = (held, swapped(after(held, partner), "tok", 1))
    away = feed_far(place, partner, near_away, feed_pieces)
    arrived = swapped(away, "kv", 1)
    dec_parts = exchanged_partials(after(partial, away), dec_query.shape[0])
    mine = feed(place, after(normed, away), up_weight, down_weight, feed_pieces)
    prefill_out = finish(normed, mine, arrived, ln2_gain[None, :], ln2_bias[None, :])

    return prefill_out, merged_partials(after(tuple(dec_parts), mine))


def extended(value, sides, width):
    for axis, dim in sides:
        count, length = (lax.axis_size(axis), value.shape[dim])
        up = [(i, (i + 1) % count) for i in range(count - 1)]
        down = [(j, i) for i, j in up]
        last = lax.slice_in_dim(value, length - width, length, axis=dim)
        leading = lax.slice_in_dim(value, 0, width, axis=dim)
        before = lax.ppermute(last, axis, up)
        after = lax.ppermute(leading, axis, down)
        value = jnp.concatenate([before, value, after], axis=dim)
    return value


def merged(value, axis, join):
    pieces = jax.tree.map(lambda part: lax.all_gather(part, axis), value)
    head = jax.tree.map(lambda part: part[0], pieces)
    tail = jax.tree.map(lambda part: part[1:], pieces)
    subtotal, _ = lax.scan(lambda subtotal, section: (join(subtotal, section), None), head, tail)
    return subtotal


def segment_ids(row_ids, stretch_len):
    stretch_ends = jnp.cumsum(stretch_len)
    return jnp.sum((row_ids[:, None] >= stretch_ends[None, :]).astype(jnp.int32), axis=1)


def layer_norm(values, gain, bias):
    center = values - jnp.mean(values, axis=1, keepdims=True)
    spread = jnp.mean(center * center, axis=1, keepdims=True)
    return center * lax.rsqrt(spread + LN_EPS) * gain + bias


def merge_partials(earlier, later):
    highest = jnp.maximum(earlier[0], later[0])
    left_factor = jnp.exp(earlier[0] - highest)
    right_factor = jnp.exp(later[0] - highest)
    totals = earlier[1] * left_factor + later[1] * right_factor
    weighted = earlier[2] * left_factor[..., None] + later[2] * right_factor[..., None]
    return (highest, totals, weighted)


def row_folder(source, shard_rows):
    return jnp.dot(source, shard_rows, preferred_element_type=jnp.float32)


def general_body(
    hidden_in,
    qkv_weight,
    stretch_len,
    out_weight,
    ln1_gain,
    ln1_bias,
    up_weight,
    down_weight,
    ln2_gain,
    ln2_bias,
    dec_query,
    kv_cache,
    piece_req,
    piece_used,
):
    inv_scale = 1.0 / math.sqrt(HD)
    reach = WIN // 2
    local_width = qkv_weight.shape[2]
    head_count = local_width // HD
    flat_weight = qkv_weight.reshape(qkv_weight.shape[0], 3 * local_width)
    qkv_rows = jnp.dot(
        lax.all_gather(hidden_in, "kv", axis=0, tiled=True),
        flat_weight,
        preferred_element_type=jnp.float32,
    ).astype(jnp.bfloat16)
    row_count = qkv_rows.shape[0]
    query_rows = qkv_rows[:, :local_width]
    keyval_rows = qkv_rows[:, local_width:]
    padded = extended(keyval_rows, (("tok", 0),), reach)
    first_row = lax.axis_index("tok") * row_count
    total_rows = row_count * lax.axis_size("tok")
    qblock = min(512, row_count)
    span = qblock + 2 * reach
    block_count = row_count // qblock

    def attend(block_index):
        start = block_index * qblock
        query_ids = first_row + start + jnp.arange(qblock, dtype=jnp.int32)
        key_ids = first_row + start - reach + jnp.arange(span, dtype=jnp.int32)
        query_seg = segment_ids(query_ids, stretch_len)
        inside = (key_ids >= 0) & (key_ids < total_rows)
        key_seg = jnp.where(inside, segment_ids(key_ids, stretch_len), -1)
        allowed = (key_seg[None, :] == query_seg[:, None]) & (
            jnp.abs(key_ids[None, :] - query_ids[:, None]) <= reach
        )
        queries = lax.dynamic_slice_in_dim(query_rows, start, qblock, 0).reshape(
            qblock, head_count, HD
        )
        both = lax.dynamic_slice_in_dim(padded, start, span, 0)
        key_rows = both[:, :local_width].reshape(span, head_count, HD)
        value_rows = both[:, local_width:].reshape(span, head_count, HD)
        scores = (
            jnp.einsum("ihd,jhd->hij", queries, key_rows, preferred_element_type=jnp.float32)
            * inv_scale
        )
        scores = jnp.where(allowed[None], scores, NEG_FILL)
        row_max = jnp.max(scores, axis=2, keepdims=True)
        weights = jnp.where(allowed[None], jnp.exp(scores - row_max), 0.0)
        totals = jnp.sum(weights, axis=2)
        summed = jnp.einsum(
            "hij,jhd->ihd",
            weights.astype(jnp.bfloat16),
            value_rows,
            preferred_element_type=jnp.float32,
        )
        return (
            (summed / jnp.transpose(totals)[:, :, None])
            .astype(jnp.bfloat16)
            .reshape(qblock, local_width)
        )

    attention = lax.map(attend, jnp.arange(block_count, dtype=jnp.int32)).reshape(
        row_count, local_width
    )
    token_major = lax.all_to_all(attention, "kv", split_axis=0, concat_axis=1, tiled=True)
    projected = row_folder(token_major, lax.all_gather(out_weight, "kv", axis=0, tiled=True))
    normed = layer_norm(hidden_in.astype(jnp.float32) + projected, ln1_gain, ln1_bias).astype(
        jnp.bfloat16
    )
    units = jax.nn.gelu(
        jnp.dot(
            lax.all_gather(normed, "kv", axis=0, tiled=True),
            up_weight,
            preferred_element_type=jnp.float32,
        ),
        approximate=False,
    ).astype(jnp.bfloat16)
    ffn = lax.psum_scatter(
        jnp.dot(units, down_weight, preferred_element_type=jnp.float32).astype(jnp.bfloat16),
        "kv",
        scatter_dimension=0,
        tiled=True,
    ).astype(jnp.float32)
    prefill_out = layer_norm(normed.astype(jnp.float32) + ffn, ln2_gain, ln2_bias).astype(
        jnp.bfloat16
    )
    group_queries = lax.all_gather(dec_query, "kv", axis=0, tiled=True)
    request_count = group_queries.shape[0]
    owners = piece_req[0]
    filled = piece_used[0]
    slot_count = owners.shape[0]
    request_ids = jnp.arange(request_count, dtype=jnp.int32)
    selector = (owners[:, None] == request_ids[None, :]).astype(jnp.bfloat16)
    chosen = jnp.dot(selector, group_queries, preferred_element_type=jnp.float32).astype(
        jnp.bfloat16
    )
    chosen = chosen.reshape(slot_count, H, HD)
    cache_keys = kv_cache[0, 0].reshape(slot_count, PLEN, H, HD)
    cache_values = kv_cache[1, 0].reshape(slot_count, PLEN, H, HD)
    piece_scores = (
        jnp.einsum("phd,pthd->pht", chosen, cache_keys, preferred_element_type=jnp.float32)
        * inv_scale
    )
    active = jnp.arange(PLEN, dtype=jnp.int32)[None, :] < filled[:, None]
    piece_scores = jnp.where(active[:, None, :], piece_scores, NEG_FILL)
    piece_max = jnp.max(piece_scores, axis=2)
    piece_weights = jnp.where(
        active[:, None, :], jnp.exp(piece_scores - piece_max[:, :, None]), 0.0
    )
    piece_totals = jnp.sum(piece_weights, axis=2)
    partial_value = jnp.einsum(
        "pht,pthd->phd",
        piece_weights.astype(jnp.bfloat16),
        cache_values,
        preferred_element_type=jnp.float32,
    )
    member = (owners[None, :] == request_ids[:, None]) & (filled[None, :] > 0)
    highest = jnp.max(jnp.where(member[:, :, None], piece_max[None], NEG_FILL), axis=1)
    factor = jnp.where(member[:, :, None], jnp.exp(piece_max[None] - highest[:, None, :]), 0.0)
    denom = jnp.sum(factor * piece_totals[None], axis=1)
    weighted = jnp.einsum("rph,phd->rhd", factor, partial_value)
    own_requests = dec_query.shape[0]
    joined = merged((highest, denom, weighted), "kv", merge_partials)
    begin = lax.axis_index("kv") * own_requests
    final_denom = lax.dynamic_slice_in_dim(joined[1], begin, own_requests, 0)
    final_weighted = lax.dynamic_slice_in_dim(joined[2], begin, own_requests, 0)
    dec_out = (
        (final_weighted / final_denom[:, :, None])
        .astype(jnp.bfloat16)
        .reshape(own_requests, H * HD)
    )
    return (prefill_out, dec_out)


def solution(mesh):
    placed = (
        P(("tok", "kv"), None),
        P(None, None, "kv"),
        P(),
        P("kv", None),
        P(),
        P(),
        P(None, "kv"),
        P("kv", None),
        P(),
        P(),
        P(("tok", "kv"), None),
        P(None, "tok", "kv", None, None),
        P("tok", "kv"),
        P("tok", "kv"),
    )
    routed = mesh.shape["tok"] == 8 and mesh.shape["kv"] == 4
    return jax.shard_map(
        routed_body if routed else general_body,
        mesh=mesh,
        in_specs=placed,
        out_specs=(P(("tok", "kv"), None), P(("tok", "kv"), None)),
        check_vma=False,
    )
```

```python
import functools
import math

import jax
import jax.numpy as jnp
from jax import lax
from jax.experimental import pallas as pl
from jax.experimental.pallas import tpu as pltpu
from jax.sharding import PartitionSpec as P

H = 16
HD = 64
WIN = 512
PLEN = 128


NEG_FILL = -1e30
LN_EPS = 1e-05
BF16 = jnp.bfloat16
F32 = jnp.float32
STRIP = 32
MIB = 1024 * 1024
ANY = pl.BlockSpec(memory_space=pl.ANY)
VMEM = pl.BlockSpec(memory_space=pltpu.VMEM)
SMEM = pl.BlockSpec(memory_space=pltpu.SMEM)
SHORT = pl.CostEstimate(flops=1, bytes_accessed=1, transcendentals=0)


def swapped(value, axis, flip):
    count = lax.axis_size(axis)
    return lax.ppermute(value, axis, [(i, i ^ flip) for i in range(count)])


def over_edges(value, axis, first):
    count = lax.axis_size(axis)
    edges = [(i, i + 1) for i in range(first, count - 1, 2)]
    return lax.ppermute(value, axis, edges + [(j, i) for i, j in edges])


def after(value, *earlier):
    return lax.optimization_barrier((value,) + earlier)[0]


def normalized(values, gain, bias):
    center = values - jnp.mean(values, axis=1, keepdims=True)
    spread = jnp.mean(center * center, axis=1, keepdims=True)
    return center * lax.rsqrt(spread + LN_EPS) * gain + bias


def shard_copies(kv, shards, rows_ref, sems, first, step):
    own, a1, a2, a3, b1, b2 = shards
    count = own.shape[0]
    inner = (kv == 1) | (kv == 2)
    outer = jnp.logical_not(inner)
    always = kv >= 0
    sources = ((own, 0, always), (a1, 1, always), (a2, 2, outer), (b2, 2, inner), (a3, 3, outer), (b1, 3, inner))
    copies = []
    for index, (source, flip, held) in enumerate(sources):
        for slot in range(rows_ref.shape[0] // count):
            needed = held & ((kv ^ flip) == first + slot * step)
            target = rows_ref.at[slot * count : (slot + 1) * count]
            copies.append((needed, pltpu.make_async_copy(source, target, sems.at[index])))
    for needed, copy in copies:
        pl.when(needed)(copy.start)
    for needed, copy in copies:
        pl.when(needed)(copy.wait)


def keys_values(rows, weight_ref, keyval_ref):
    width = weight_ref.shape[2]
    for part in range(2):
        at = slice(part * width, (part + 1) * width)
        keyval_ref[:, at] = jnp.dot(rows, weight_ref[part + 1], preferred_element_type=F32).astype(BF16)


def project_edges_kernel(place_ref, weight_ref, *refs):
    shards, (keyval_ref, even_ref, odd_ref, rows_ref, sems) = refs[:-5], refs[-5:]
    tok, kv = place_ref[0], place_ref[1]
    count = even_ref.shape[0]
    shard_copies(kv, shards, rows_ref, sems, 0, 3)
    keys_values(rows_ref[...], weight_ref, keyval_ref)

    @pl.when(tok % 2 == 0)
    def _():
        even_ref[...] = keyval_ref[count:]
        odd_ref[...] = keyval_ref[:count]

    @pl.when(tok % 2 == 1)
    def _():
        even_ref[...] = keyval_ref[:count]
        odd_ref[...] = keyval_ref[count:]


def project_rest_kernel(place_ref, weight_ref, *refs):
    shards, (query_ref, keyval_ref, rows_ref, sems) = refs[:-4], refs[-4:]
    count = shards[0].shape[0]
    shard_copies(place_ref[1], shards, rows_ref, sems, 0, 1)
    keys_values(rows_ref[count:-count], weight_ref, keyval_ref)
    query = jnp.dot(rows_ref[...], weight_ref[0], preferred_element_type=F32) * (1.0 / math.sqrt(HD))
    query_ref[...] = query.astype(BF16)


def project(place, weight, shards, blocks, edges):
    rows, width = shards[0].shape
    heads_width = weight.shape[2]
    shape = lambda count, columns: jax.ShapeDtypeStruct((count * rows, columns), BF16)
    keyval = shape(2, 2 * heads_width)
    if edges:
        outs = (keyval, shape(1, 2 * heads_width), shape(1, 2 * heads_width))
    else:
        outs = (shape(blocks, heads_width), keyval)
    return pl.pallas_call(
        project_edges_kernel if edges else project_rest_kernel,
        out_shape=outs,
        in_specs=[SMEM, VMEM] + [ANY] * len(shards),
        out_specs=(VMEM,) * len(outs),
        scratch_shapes=[
            pltpu.VMEM((2 * rows if edges else blocks * rows, width), BF16),
            pltpu.SemaphoreType.DMA((len(shards),)),
        ],
        compiler_params=pltpu.CompilerParams(vmem_limit_bytes=12 * MIB),
        cost_estimate=SHORT,
        name="project_edges" if edges else "project_rest",
    )(place, weight, *shards)


def window_bias(first, count, starts, ends):
    reach = WIN // 2
    query = first + lax.broadcasted_iota(jnp.int32, (count, 1), 0)
    low = jnp.max(jnp.where(starts <= query, starts, 0), axis=1, keepdims=True)
    high = jnp.min(jnp.where(ends > query, ends, 1 << 30), axis=1, keepdims=True)
    low = jnp.maximum(low, query - reach)
    high = jnp.minimum(high, query + reach + 1)
    key = first - count + lax.broadcasted_iota(jnp.int32, (count, 3 * count), 1)
    return jnp.where((key >= low) & (key < high), 0.0, NEG_FILL)


def attend(query, keyval_ref, bias_ref, scores_ref, weights_ref, out_ref):
    count, width = query.shape
    lane = lax.broadcasted_iota(jnp.int32, (count, 2 * HD), 1)
    for start in range(0, width, 2 * HD):
        values = keyval_ref[:, width + start : width + start + 2 * HD]
        halves = []
        for side in range(2):
            head = start // HD + side
            inside = (lane < HD) if side == 0 else (lane >= HD)
            only = jnp.where(inside, query[:, start : start + 2 * HD], jnp.zeros((), BF16))
            scores_ref[head] = lax.dot_general(
                only, keyval_ref[:, start : start + 2 * HD], (((1,), (1,)), ((), ())), preferred_element_type=F32
            )
            totals = []
            for row in range(0, count, STRIP):
                at = slice(row, row + STRIP)
                scores = scores_ref[head, at] + bias_ref[at]
                weights = jnp.exp(scores - jnp.max(scores, axis=1, keepdims=True))
                totals.append(jnp.sum(weights, axis=1, keepdims=True))
                weights_ref[head, at] = weights.astype(BF16)
            summed = jnp.dot(weights_ref[head], values, preferred_element_type=F32)
            halves.append(summed / jnp.concatenate(totals, axis=0))
        out_ref[:, start : start + 2 * HD] = jnp.where(lane < HD, halves[0], halves[1]).astype(BF16)


def attend_kernel(flips, place_ref, starts_ref, ends_ref, query_ref, middle_ref, edges_ref, even_ref, odd_ref, *refs):
    outs = refs[: len(flips)]
    window_ref, bias_ref, scores_ref, weights_ref, sems = refs[len(flips) :]
    tok, kv = place_ref[0], place_ref[1]
    count = outs[0].shape[0]
    blocks = query_ref.shape[0] // count
    copies = []
    for index, flip in enumerate(flips):
        block = kv ^ flip
        for part in range(3):
            target = window_ref.at[index, part * count : (part + 1) * count]
            sem = sems.at[index, part]
            at = block + part - 1
            middle = (at > 0) & (at < blocks - 1)
            start = jnp.where(middle, at - 1, 0)
            source = middle_ref.at[pl.ds(pl.multiple_of(start * count, count), count)]
            copies.append((index, middle, pltpu.make_async_copy(source, target, sem)))
            for slot, edge in enumerate((0, blocks - 1)):
                source = edges_ref.at[slot * count : (slot + 1) * count]
                copies.append((index, at == edge, pltpu.make_async_copy(source, target, sem)))
            for first_edge, outside in ((tok % 2 == 1, at < 0), (tok % 2 == 0, at >= blocks)):
                if part != 1:
                    copies.append((index, outside & first_edge, pltpu.make_async_copy(even_ref, target, sem)))
                    other = jnp.logical_not(first_edge)
                    copies.append((index, outside & other, pltpu.make_async_copy(odd_ref, target, sem)))
    for _, needed, copy in copies:
        pl.when(needed)(copy.start)
    for index, flip in enumerate(flips):
        block = kv ^ flip
        first = (tok * blocks + block) * count
        bias_ref[...] = window_bias(first, count, starts_ref[...], ends_ref[...])
        for owner, needed, copy in copies:
            if owner == index:
                pl.when(needed)(copy.wait)
        query = query_ref[pl.ds(pl.multiple_of(block * count, count), count)]
        attend(query, window_ref.at[index], bias_ref, scores_ref, weights_ref, outs[index])


def attend_blocks(place, starts, ends, query, middle, edges, even, odd, rows, flips, name):
    heads_width = query.shape[1]
    return pl.pallas_call(
        functools.partial(attend_kernel, flips),
        out_shape=tuple(jax.ShapeDtypeStruct((rows, heads_width), BF16) for _ in flips),
        in_specs=[SMEM, VMEM, VMEM, VMEM, ANY, ANY, ANY, ANY],
        out_specs=(VMEM,) * len(flips),
        scratch_shapes=[
            pltpu.VMEM((len(flips), 3 * rows, 2 * heads_width), BF16),
            pltpu.VMEM((rows, 3 * rows), F32),
            pltpu.VMEM((heads_width // HD, rows, 3 * rows), F32),
            pltpu.VMEM((heads_width // HD, rows, 3 * rows), BF16),
            pltpu.SemaphoreType.DMA((len(flips), 3)),
        ],
        compiler_params=pltpu.CompilerParams(vmem_limit_bytes=14 * MIB),
        cost_estimate=SHORT,
        name=name,
    )(place, starts, ends, query, middle, edges, even, odd)


def first_norm_kernel(layout, place_ref, hidden_ref, own_out_ref, gain_ref, bias_ref, *refs):
    parts, pieces = refs[: -5 - len(layout)], refs[-5 - len(layout) : -5]
    normed_ref, all_ref, weight_ref, mixed_ref, sems = refs[-5:]
    tok = place_ref[0]
    quarters, heads_width, width = weight_ref.shape
    copies = [pltpu.make_async_copy(own_out_ref, weight_ref.at[0], sems.at[0])]
    for flips, piece in zip(layout, pieces):
        for index, flip in enumerate(flips):
            depth = piece.shape[2]
            at = pl.multiple_of((tok ^ flip) * depth, depth)
            target = weight_ref.at[1:quarters, pl.ds(at, depth)]
            copies.append(pltpu.make_async_copy(piece.at[index], target, sems.at[len(copies)]))
    for copy in copies:
        copy.start()
    for flip, part_ref in enumerate(parts):
        all_ref[:, flip * heads_width : (flip + 1) * heads_width] = part_ref[...]
    for copy in copies:
        copy.wait()
    weight = weight_ref[...].reshape(quarters * heads_width, width)
    mixed_ref[...] = jnp.dot(all_ref[...], weight, preferred_element_type=F32)
    for row in range(0, hidden_ref.shape[0], STRIP):
        at = slice(row, row + STRIP)
        mixed = hidden_ref[at].astype(F32) + mixed_ref[at]
        normed_ref[at] = normalized(mixed, gain_ref[...], bias_ref[...]).astype(BF16)


def first_norm(place, hidden, own_out, gain, bias, parts, pieces):
    rows, width = hidden.shape
    heads_width = own_out.shape[0]
    layout = tuple(flips for flips, _ in pieces)
    return pl.pallas_call(
        functools.partial(first_norm_kernel, layout),
        out_shape=jax.ShapeDtypeStruct((rows, width), BF16),
        in_specs=[SMEM, VMEM, ANY, VMEM, VMEM] + [VMEM] * len(parts) + [ANY] * len(pieces),
        out_specs=VMEM,
        scratch_shapes=[
            pltpu.VMEM((rows, width), BF16),
            pltpu.VMEM((len(parts), heads_width, width), BF16),
            pltpu.VMEM((rows, width), F32),
            pltpu.SemaphoreType.DMA((1 + sum(len(flips) for flips in layout),)),
        ],
        compiler_params=pltpu.CompilerParams(vmem_limit_bytes=11 * MIB),
        cost_estimate=SHORT,
        name="first_norm",
    )(place, hidden, own_out, gain, bias, *parts, *[value for _, value in pieces])


def gelu(values):
    return 0.5 * values * (1.0 + lax.erf(values * math.sqrt(0.5)))


CHUNK = 512


def feed_chunk(rows, up, down_ref, wide_ref, units_ref):
    wide_ref[...] = jnp.dot(rows, up, preferred_element_type=F32)
    for row in range(0, rows.shape[0], STRIP):
        strip = slice(row, row + STRIP)
        units_ref[strip] = gelu(wide_ref[strip]).astype(BF16)
    return jnp.dot(units_ref[...], down_ref[...], preferred_element_type=F32)


def far_copies(tok, held_ref, core_ref, up_ref, down_ref, sems):
    block = 128
    copies = []
    for side, piece in enumerate((held_ref, core_ref)):
        for index in range(4):
            at = pl.ds(pl.multiple_of((tok ^ (2 * index + side)) * block, block), block)
            for part, target in enumerate((up_ref, down_ref)):
                source = piece.at[pl.ds((2 * index + part) * block, block)]
                copies.append(pltpu.make_async_copy(source, target.at[at], sems.at[len(copies)]))
    return copies


def feed_near_kernel(rows_ref, up_ref, down_ref, sum_ref, wide_ref, units_ref):
    rows = rows_ref[...]
    for index in range(up_ref.shape[1] // CHUNK):
        at = slice(index * CHUNK, (index + 1) * CHUNK)
        product = feed_chunk(rows, up_ref[:, at], down_ref.at[at], wide_ref.at[index % 2], units_ref.at[index % 2])
        if index == 0:
            sum_ref[...] = product
        else:
            sum_ref[...] += product


def feed_far_kernel(
    place_ref, rows_ref, near_ref, held_ref, core_ref, sum_ref, up_ref, down_ref, wide_ref, units_ref, total_ref, sems
):
    copies = far_copies(place_ref[0], held_ref, core_ref, up_ref, down_ref, sems)
    for copy in copies:
        copy.start()
    rows = rows_ref[...]
    total_ref[...] = near_ref[...]
    for copy in copies:
        copy.wait()
    for index in range(up_ref.shape[1] // CHUNK):
        at = slice(index * CHUNK, (index + 1) * CHUNK)
        slot = index % 2
        total_ref[...] += feed_chunk(rows, up_ref[:, at], down_ref.at[at], wide_ref.at[slot], units_ref.at[slot])
    sum_ref[...] = total_ref[...].astype(sum_ref.dtype)


def feed_kernel(
    place_ref, rows_ref, up_near_ref, down_near_ref, held_ref, core_ref, sum_ref, up_ref, down_ref, wide_ref, units_ref, sems
):
    copies = far_copies(place_ref[0], held_ref, core_ref, up_ref, down_ref, sems)
    for copy in copies:
        copy.start()
    feed_near_kernel(rows_ref, up_near_ref, down_near_ref, sum_ref, wide_ref, units_ref)
    rows = rows_ref[...]
    for copy in copies:
        copy.wait()
    for index in range(up_ref.shape[1] // CHUNK):
        at = slice(index * CHUNK, (index + 1) * CHUNK)
        slot = index % 2
        sum_ref[...] += feed_chunk(rows, up_ref[:, at], down_ref.at[at], wide_ref.at[slot], units_ref.at[slot])


def feed_scratch(count):
    return [pltpu.VMEM((2, count, CHUNK), F32), pltpu.VMEM((2, count, CHUNK), BF16)]


def feed_near(rows, up_weight, down_weight):
    return pl.pallas_call(
        feed_near_kernel,
        out_shape=jax.ShapeDtypeStruct(rows.shape, F32),
        in_specs=[VMEM] * 3,
        out_specs=VMEM,
        scratch_shapes=feed_scratch(rows.shape[0]),
        compiler_params=pltpu.CompilerParams(vmem_limit_bytes=14 * MIB),
        cost_estimate=SHORT,
        name="feed_near",
    )(rows, up_weight, down_weight)


def feed_far(place, rows, near, pieces):
    count, width = rows.shape
    units = pieces[0].shape[0]
    return pl.pallas_call(
        feed_far_kernel,
        out_shape=jax.ShapeDtypeStruct((count, width), BF16),
        in_specs=[SMEM] + [VMEM] * 2 + [ANY] * 2,
        out_specs=VMEM,
        scratch_shapes=[pltpu.VMEM((width, units), BF16), pltpu.VMEM((units, width), BF16)]
        + feed_scratch(count)
        + [pltpu.VMEM((count, width), F32), pltpu.SemaphoreType.DMA((16,))],
        compiler_params=pltpu.CompilerParams(vmem_limit_bytes=14 * MIB),
        cost_estimate=SHORT,
        name="feed_far",
    )(place, rows, near, *pieces)


def feed(place, rows, up_weight, down_weight, pieces):
    count, width = rows.shape
    units = up_weight.shape[1]
    return pl.pallas_call(
        feed_kernel,
        out_shape=jax.ShapeDtypeStruct((count, width), F32),
        in_specs=[SMEM] + [VMEM] * 3 + [ANY] * 2,
        out_specs=VMEM,
        scratch_shapes=[pltpu.VMEM((width, units), BF16), pltpu.VMEM((units, width), BF16)]
        + feed_scratch(count)
        + [pltpu.SemaphoreType.DMA((16,))],
        compiler_params=pltpu.CompilerParams(vmem_limit_bytes=18 * MIB),
        cost_estimate=SHORT,
        name="feed_own",
    )(place, rows, up_weight, down_weight, *pieces)


def finish_kernel(normed_ref, near_ref, far_ref, gain_ref, bias_ref, out_ref):
    for row in range(0, normed_ref.shape[0], STRIP):
        at = slice(row, row + STRIP)
        mixed = normed_ref[at].astype(F32) + near_ref[at] + far_ref[at].astype(F32)
        out_ref[at] = normalized(mixed, gain_ref[...], bias_ref[...]).astype(out_ref.dtype)


def finish(normed, near, far, gain, bias):
    return pl.pallas_call(
        finish_kernel,
        out_shape=jax.ShapeDtypeStruct(normed.shape, BF16),
        in_specs=[VMEM] * 5,
        out_specs=VMEM,
        compiler_params=pltpu.CompilerParams(vmem_limit_bytes=6 * MIB),
        name="finish",
    )(normed, near, far, gain, bias)


def decode_kernel(slot_ref, filled_ref, query_ref, cache_ref, out_ref, high_ref, total_ref, sum_ref):
    step = pl.program_id(0)

    @pl.when(step == 0)
    def _():
        high_ref[...] = jnp.full(high_ref.shape, NEG_FILL, F32)
        total_ref[...] = jnp.zeros_like(total_ref)
        sum_ref[...] = jnp.zeros_like(sum_ref)

    row = slot_ref[step]
    filled = filled_ref[step]
    width = query_ref.shape[1]
    head = lax.broadcasted_iota(jnp.int32, (H, width), 0)
    inside = head == lax.broadcasted_iota(jnp.int32, (H, width), 1) // HD
    query = jnp.where(inside, query_ref[pl.ds(row, 1), :], 0.0).astype(BF16)
    scores = lax.dot_general(query, cache_ref[0, 0, 0], (((1,), (1,)), ((), ())), preferred_element_type=F32)
    live = lax.broadcasted_iota(jnp.int32, scores.shape, 1) < filled
    scores = jnp.where(live, scores * (1.0 / math.sqrt(HD)), NEG_FILL)
    high = jnp.max(scores, axis=1, keepdims=True)
    weights = jnp.where(live, jnp.exp(scores - high), 0.0)
    total = jnp.sum(weights, axis=1, keepdims=True)
    summed = jnp.dot(weights.astype(BF16), cache_ref[1, 0, 0], preferred_element_type=F32)
    along = lambda column: jnp.sum(jnp.where(inside, column, 0.0), axis=0, keepdims=True)
    high, total, summed = along(high), along(total), along(summed)
    used = filled > 0
    at = pl.ds(row, 1)
    old = high_ref[at, :]
    new = jnp.where(used, jnp.maximum(old, high), old)
    left = jnp.exp(old - new)
    right = jnp.where(used, jnp.exp(high - new), 0.0)
    high_ref[at, :] = new
    total_ref[at, :] = total_ref[at, :] * left + total * right
    sum_ref[at, :] = sum_ref[at, :] * left + summed * right

    @pl.when(step == pl.num_programs(0) - 1)
    def _():
        out_ref[0] = high_ref[...]
        out_ref[1] = total_ref[...]
        out_ref[2] = sum_ref[...]


def decode(slots, filled, queries, kv_cache):
    requests, width = queries.shape
    pieces = kv_cache.shape[2]
    state = pltpu.VMEM((requests, width), F32)
    return pl.pallas_call(
        decode_kernel,
        grid=(pieces,),
        out_shape=jax.ShapeDtypeStruct((3, requests, width), F32),
        in_specs=[
            SMEM,
            SMEM,
            pl.BlockSpec((requests, width), lambda i: (0, 0)),
            pl.BlockSpec((2, 1, 1, PLEN, width), lambda i: (0, 0, i, 0, 0)),
        ],
        out_specs=pl.BlockSpec((3, requests, width), lambda i: (0, 0, 0)),
        scratch_shapes=[state, state, state],
        compiler_params=pltpu.CompilerParams(vmem_limit_bytes=8 * MIB),
        cost_estimate=SHORT,
        name="decode",
    )(slots, filled, queries, kv_cache)


def decode_partial(queries, own, kv_cache, piece_req, piece_used):
    owners = piece_req[0]
    slots = ((owners // own) ^ lax.axis_index("kv")) * own + owners % own
    return decode(slots, piece_used[0], queries, kv_cache)


def exchanged_partials(partial, own):
    parts = [partial[:, :own]]
    for flip in range(1, lax.axis_size("kv")):
        parts.append(swapped(partial[:, flip * own : (flip + 1) * own], "kv", flip))
    return parts


def merged_partials(parts):
    high = functools.reduce(jnp.maximum, [part[0] for part in parts])
    factors = [jnp.exp(part[0] - high) for part in parts]
    total = sum(part[1] * factor for part, factor in zip(parts, factors))
    summed = sum(part[2] * factor for part, factor in zip(parts, factors))
    return (summed / total).astype(BF16)


def routed_body(
    hidden_in,
    qkv_weight,
    stretch_len,
    out_weight,
    ln1_gain,
    ln1_bias,
    up_weight,
    down_weight,
    ln2_gain,
    ln2_bias,
    dec_query,
    kv_cache,
    piece_req,
    piece_used,
):
    tok = lax.axis_index("tok")
    kv = lax.axis_index("kv")
    toks, kvs = lax.axis_size("tok"), lax.axis_size("kv")
    rows, width = hidden_in.shape
    place = jnp.stack([tok, kv]).astype(jnp.int32)
    eighth = lambda value: lax.dynamic_slice_in_dim(value, tok * (value.shape[0] // toks), value.shape[0] // toks, 0)

    outward = [(1, 0), (2, 3)]
    a1, b1 = over_edges(hidden_in, "kv", 0), over_edges(hidden_in, "kv", 1)
    out_part = eighth(out_weight)
    depth = out_part.shape[0]
    small = jnp.concatenate([out_part, dec_query], axis=0)
    others = [swapped(small, "kv", flip) for flip in range(1, kvs)]
    a2, b2 = lax.ppermute(b1, "kv", outward), over_edges(a1, "kv", 1)
    queries = jnp.concatenate([dec_query] + [other[depth:] for other in others], axis=0).astype(F32)
    partial = decode_partial(queries, dec_query.shape[0], kv_cache, piece_req, piece_used)
    out_here = jnp.stack([other[:depth] for other in others])
    out_x, out_y = swapped(out_here, "tok", 2), swapped(out_here, "tok", 4)
    out_all = jnp.stack([out_here, out_x, out_y, swapped(out_y, "tok", 2)])
    out_core = swapped(out_all, "tok", 1)
    a3 = lax.ppermute(after(b2, partial), "kv", outward)
    shards = (after(hidden_in, out_x, out_y), a1, a2, a3, b1, b2)
    inner = (kv == 1) | (kv == 2)

    feed_up, feed_down = after((eighth(up_weight), eighth(down_weight)), a2, b2)
    inner_up = lax.ppermute(feed_up, "kv", [(0, 2), (3, 1)])
    inner_down = lax.ppermute(feed_down, "kv", [(0, 2), (3, 1)])
    feed_part = after(jnp.concatenate([feed_up, feed_down], axis=0), a3, inner_up, inner_down)
    feed_outer = lax.ppermute(feed_part, "kv", [(1, 3), (2, 0)])
    feed_inner = jnp.concatenate([inner_up, inner_down], axis=0)

    order = jnp.arange(stretch_len.shape[0])
    ends = jnp.sum(jnp.where(order[:, None] <= order[None, :], stretch_len[:, None], 0), axis=0, dtype=jnp.int32)
    starts = (ends - stretch_len)[None, :]
    ends = ends[None, :]

    weight = jnp.transpose(qkv_weight, (1, 0, 2))
    edges, even, odd = project(place, weight, shards, kvs, True)
    even, odd = over_edges(even, "tok", 0), over_edges(odd, "tok", 1)
    query, middle = project(place, weight, (after(hidden_in, edges),) + shards[1:], kvs, False)
    window = (middle, edges, even, odd, rows)
    parts = [None] * kvs
    parts[3], parts[2] = attend_blocks(place, starts, ends, query, *window, (3, 2), "attend_far")
    query = after(query, parts[3])
    parts[3], parts[2] = swapped(parts[3], "kv", 3), swapped(parts[2], "kv", 2)
    parts[1], parts[0] = attend_blocks(place, starts, ends, query, *window, (1, 0), "attend_near")
    feed_here = jnp.where(inner, feed_inner, after(feed_outer, *parts[2:], parts[0]))
    parts[1] = swapped(parts[1], "kv", 1)
    feed_x, feed_y = swapped(feed_here, "tok", 2), swapped(feed_here, "tok", 4)
    out_pieces = [((0, 2, 4, 6), out_all), ((1, 3, 5, 7), out_core)]
    normed = first_norm(place, hidden_in, out_weight, ln1_gain[None, :], ln1_bias[None, :], parts, out_pieces)

    partner = swapped(normed, "kv", 1)
    half = feed_here.shape[0] // 2
    far_up = swapped(after(feed_y, normed)[:half], "tok", 2)
    far_down = swapped(after(feed_x, normed)[half:], "tok", 4)
    held = jnp.concatenate([feed_here, feed_x, feed_y, far_up, far_down], axis=0)
    near_away = feed_near(partner, up_weight, down_weight)
    feed_pieces = (held, swapped(after(held, partner), "tok", 1))
    away = feed_far(place, partner, near_away, feed_pieces)
    arrived = swapped(away, "kv", 1)
    dec_parts = exchanged_partials(after(partial, away), dec_query.shape[0])
    mine = feed(place, after(normed, away), up_weight, down_weight, feed_pieces)
    prefill_out = finish(normed, mine, arrived, ln2_gain[None, :], ln2_bias[None, :])

    return prefill_out, merged_partials(after(tuple(dec_parts), mine))


def extended(value, sides, width):
    for axis, dim in sides:
        count, length = (lax.axis_size(axis), value.shape[dim])
        up = [(i, (i + 1) % count) for i in range(count - 1)]
        down = [(j, i) for i, j in up]
        last = lax.slice_in_dim(value, length - width, length, axis=dim)
        leading = lax.slice_in_dim(value, 0, width, axis=dim)
        before = lax.ppermute(last, axis, up)
        after = lax.ppermute(leading, axis, down)
        value = jnp.concatenate([before, value, after], axis=dim)
    return value


def merged(value, axis, join):
    pieces = jax.tree.map(lambda part: lax.all_gather(part, axis), value)
    head = jax.tree.map(lambda part: part[0], pieces)
    tail = jax.tree.map(lambda part: part[1:], pieces)
    subtotal, _ = lax.scan(lambda subtotal, section: (join(subtotal, section), None), head, tail)
    return subtotal


def segment_ids(row_ids, stretch_len):
    stretch_ends = jnp.cumsum(stretch_len)
    return jnp.sum((row_ids[:, None] >= stretch_ends[None, :]).astype(jnp.int32), axis=1)


def layer_norm(values, gain, bias):
    center = values - jnp.mean(values, axis=1, keepdims=True)
    spread = jnp.mean(center * center, axis=1, keepdims=True)
    return center * lax.rsqrt(spread + LN_EPS) * gain + bias


def merge_partials(earlier, later):
    highest = jnp.maximum(earlier[0], later[0])
    left_factor = jnp.exp(earlier[0] - highest)
    right_factor = jnp.exp(later[0] - highest)
    totals = earlier[1] * left_factor + later[1] * right_factor
    weighted = earlier[2] * left_factor[..., None] + later[2] * right_factor[..., None]
    return (highest, totals, weighted)


def row_folder(source, shard_rows):
    return jnp.dot(source, shard_rows, preferred_element_type=jnp.float32)


def general_body(
    hidden_in,
    qkv_weight,
    stretch_len,
    out_weight,
    ln1_gain,
    ln1_bias,
    up_weight,
    down_weight,
    ln2_gain,
    ln2_bias,
    dec_query,
    kv_cache,
    piece_req,
    piece_used,
):
    inv_scale = 1.0 / math.sqrt(HD)
    reach = WIN // 2
    local_width = qkv_weight.shape[2]
    head_count = local_width // HD
    flat_weight = qkv_weight.reshape(qkv_weight.shape[0], 3 * local_width)
    qkv_rows = jnp.dot(
        lax.all_gather(hidden_in, "kv", axis=0, tiled=True),
        flat_weight,
        preferred_element_type=jnp.float32,
    ).astype(jnp.bfloat16)
    row_count = qkv_rows.shape[0]
    query_rows = qkv_rows[:, :local_width]
    keyval_rows = qkv_rows[:, local_width:]
    padded = extended(keyval_rows, (("tok", 0),), reach)
    first_row = lax.axis_index("tok") * row_count
    total_rows = row_count * lax.axis_size("tok")
    qblock = min(512, row_count)
    span = qblock + 2 * reach
    block_count = row_count // qblock

    def attend(block_index):
        start = block_index * qblock
        query_ids = first_row + start + jnp.arange(qblock, dtype=jnp.int32)
        key_ids = first_row + start - reach + jnp.arange(span, dtype=jnp.int32)
        query_seg = segment_ids(query_ids, stretch_len)
        inside = (key_ids >= 0) & (key_ids < total_rows)
        key_seg = jnp.where(inside, segment_ids(key_ids, stretch_len), -1)
        allowed = (key_seg[None, :] == query_seg[:, None]) & (
            jnp.abs(key_ids[None, :] - query_ids[:, None]) <= reach
        )
        queries = lax.dynamic_slice_in_dim(query_rows, start, qblock, 0).reshape(
            qblock, head_count, HD
        )
        both = lax.dynamic_slice_in_dim(padded, start, span, 0)
        key_rows = both[:, :local_width].reshape(span, head_count, HD)
        value_rows = both[:, local_width:].reshape(span, head_count, HD)
        scores = (
            jnp.einsum("ihd,jhd->hij", queries, key_rows, preferred_element_type=jnp.float32)
            * inv_scale
        )
        scores = jnp.where(allowed[None], scores, NEG_FILL)
        row_max = jnp.max(scores, axis=2, keepdims=True)
        weights = jnp.where(allowed[None], jnp.exp(scores - row_max), 0.0)
        totals = jnp.sum(weights, axis=2)
        summed = jnp.einsum(
            "hij,jhd->ihd",
            weights.astype(jnp.bfloat16),
            value_rows,
            preferred_element_type=jnp.float32,
        )
        return (
            (summed / jnp.transpose(totals)[:, :, None])
            .astype(jnp.bfloat16)
            .reshape(qblock, local_width)
        )

    attention = lax.map(attend, jnp.arange(block_count, dtype=jnp.int32)).reshape(
        row_count, local_width
    )
    token_major = lax.all_to_all(attention, "kv", split_axis=0, concat_axis=1, tiled=True)
    projected = row_folder(token_major, lax.all_gather(out_weight, "kv", axis=0, tiled=True))
    normed = layer_norm(hidden_in.astype(jnp.float32) + projected, ln1_gain, ln1_bias).astype(
        jnp.bfloat16
    )
    units = jax.nn.gelu(
        jnp.dot(
            lax.all_gather(normed, "kv", axis=0, tiled=True),
            up_weight,
            preferred_element_type=jnp.float32,
        ),
        approximate=False,
    ).astype(jnp.bfloat16)
    ffn = lax.psum_scatter(
        jnp.dot(units, down_weight, preferred_element_type=jnp.float32).astype(jnp.bfloat16),
        "kv",
        scatter_dimension=0,
        tiled=True,
    ).astype(jnp.float32)
    prefill_out = layer_norm(normed.astype(jnp.float32) + ffn, ln2_gain, ln2_bias).astype(
        jnp.bfloat16
    )
    group_queries = lax.all_gather(dec_query, "kv", axis=0, tiled=True)
    request_count = group_queries.shape[0]
    owners = piece_req[0]
    filled = piece_used[0]
    slot_count = owners.shape[0]
    request_ids = jnp.arange(request_count, dtype=jnp.int32)
    selector = (owners[:, None] == request_ids[None, :]).astype(jnp.bfloat16)
    chosen = jnp.dot(selector, group_queries, preferred_element_type=jnp.float32).astype(
        jnp.bfloat16
    )
    chosen = chosen.reshape(slot_count, H, HD)
    cache_keys = kv_cache[0, 0].reshape(slot_count, PLEN, H, HD)
    cache_values = kv_cache[1, 0].reshape(slot_count, PLEN, H, HD)
    piece_scores = (
        jnp.einsum("phd,pthd->pht", chosen, cache_keys, preferred_element_type=jnp.float32)
        * inv_scale
    )
    active = jnp.arange(PLEN, dtype=jnp.int32)[None, :] < filled[:, None]
    piece_scores = jnp.where(active[:, None, :], piece_scores, NEG_FILL)
    piece_max = jnp.max(piece_scores, axis=2)
    piece_weights = jnp.where(
        active[:, None, :], jnp.exp(piece_scores - piece_max[:, :, None]), 0.0
    )
    piece_totals = jnp.sum(piece_weights, axis=2)
    partial_value = jnp.einsum(
        "pht,pthd->phd",
        piece_weights.astype(jnp.bfloat16),
        cache_values,
        preferred_element_type=jnp.float32,
    )
    member = (owners[None, :] == request_ids[:, None]) & (filled[None, :] > 0)
    highest = jnp.max(jnp.where(member[:, :, None], piece_max[None], NEG_FILL), axis=1)
    factor = jnp.where(member[:, :, None], jnp.exp(piece_max[None] - highest[:, None, :]), 0.0)
    denom = jnp.sum(factor * piece_totals[None], axis=1)
    weighted = jnp.einsum("rph,phd->rhd", factor, partial_value)
    own_requests = dec_query.shape[0]
    joined = merged((highest, denom, weighted), "kv", merge_partials)
    begin = lax.axis_index("kv") * own_requests
    final_denom = lax.dynamic_slice_in_dim(joined[1], begin, own_requests, 0)
    final_weighted = lax.dynamic_slice_in_dim(joined[2], begin, own_requests, 0)
    dec_out = (
        (final_weighted / final_denom[:, :, None])
        .astype(jnp.bfloat16)
        .reshape(own_requests, H * HD)
    )
    return (prefill_out, dec_out)


def solution(mesh):
    placed = (
        P(("tok", "kv"), None),
        P(None, None, "kv"),
        P(),
        P("kv", None),
        P(),
        P(),
        P(None, "kv"),
        P("kv", None),
        P(),
        P(),
        P(("tok", "kv"), None),
        P(None, "tok", "kv", None, None),
        P("tok", "kv"),
        P("tok", "kv"),
    )
    routed = mesh.shape["tok"] == 8 and mesh.shape["kv"] == 4
    return jax.shard_map(
        routed_body if routed else general_body,
        mesh=mesh,
        in_specs=placed,
        out_specs=(P(("tok", "kv"), None), P(("tok", "kv"), None)),
        check_vma=False,
    )
```

```python
import functools
import math

import jax
import jax.numpy as jnp
from jax import lax
from jax.experimental import pallas as pl
from jax.experimental.pallas import tpu as pltpu
from jax.sharding import PartitionSpec as P

H = 16
HD = 64
WIN = 512
PLEN = 128


NEG_FILL = -1e30
LN_EPS = 1e-05
BF16 = jnp.bfloat16
F32 = jnp.float32
STRIP = 32
MIB = 1024 * 1024
ANY = pl.BlockSpec(memory_space=pl.ANY)
VMEM = pl.BlockSpec(memory_space=pltpu.VMEM)
SMEM = pl.BlockSpec(memory_space=pltpu.SMEM)
SHORT = pl.CostEstimate(flops=1, bytes_accessed=1, transcendentals=0)


def swapped(value, axis, flip):
    count = lax.axis_size(axis)
    return lax.ppermute(value, axis, [(i, i ^ flip) for i in range(count)])


def over_edges(value, axis, first):
    count = lax.axis_size(axis)
    edges = [(i, i + 1) for i in range(first, count - 1, 2)]
    return lax.ppermute(value, axis, edges + [(j, i) for i, j in edges])


def after(value, *earlier):
    return lax.optimization_barrier((value,) + earlier)[0]


def normalized(values, gain, bias):
    center = values - jnp.mean(values, axis=1, keepdims=True)
    spread = jnp.mean(center * center, axis=1, keepdims=True)
    return center * lax.rsqrt(spread + LN_EPS) * gain + bias


def shard_copies(kv, shards, rows_ref, sems, first, step):
    own, a1, a2, a3, b1, b2 = shards
    count = own.shape[0]
    inner = (kv == 1) | (kv == 2)
    outer = jnp.logical_not(inner)
    always = kv >= 0
    sources = ((own, 0, always), (a1, 1, always), (a2, 2, outer), (b2, 2, inner), (a3, 3, outer), (b1, 3, inner))
    copies = []
    for index, (source, flip, held) in enumerate(sources):
        for slot in range(rows_ref.shape[0] // count):
            needed = held & ((kv ^ flip) == first + slot * step)
            target = rows_ref.at[slot * count : (slot + 1) * count]
            copies.append((needed, pltpu.make_async_copy(source, target, sems.at[index])))
    for needed, copy in copies:
        pl.when(needed)(copy.start)
    for needed, copy in copies:
        pl.when(needed)(copy.wait)


def keys_values(rows, weight_ref, keyval_ref):
    width = weight_ref.shape[2]
    for part in range(2):
        at = slice(part * width, (part + 1) * width)
        keyval_ref[:, at] = jnp.dot(rows, weight_ref[part + 1], preferred_element_type=F32).astype(BF16)


def project_edges_kernel(place_ref, weight_ref, *refs):
    shards, (keyval_ref, even_ref, odd_ref, rows_ref, sems) = refs[:-5], refs[-5:]
    tok, kv = place_ref[0], place_ref[1]
    count = even_ref.shape[0]
    shard_copies(kv, shards, rows_ref, sems, 0, 3)
    keys_values(rows_ref[...], weight_ref, keyval_ref)

    @pl.when(tok % 2 == 0)
    def _():
        even_ref[...] = keyval_ref[count:]
        odd_ref[...] = keyval_ref[:count]

    @pl.when(tok % 2 == 1)
    def _():
        even_ref[...] = keyval_ref[:count]
        odd_ref[...] = keyval_ref[count:]


def project_rest_kernel(place_ref, weight_ref, *refs):
    shards, (query_ref, keyval_ref, rows_ref, sems) = refs[:-4], refs[-4:]
    count = shards[0].shape[0]
    shard_copies(place_ref[1], shards, rows_ref, sems, 0, 1)
    keys_values(rows_ref[count:-count], weight_ref, keyval_ref)
    query = jnp.dot(rows_ref[...], weight_ref[0], preferred_element_type=F32) * (1.0 / math.sqrt(HD))
    query_ref[...] = query.astype(BF16)


def project(place, weight, shards, blocks, edges):
    rows, width = shards[0].shape
    heads_width = weight.shape[2]
    shape = lambda count, columns: jax.ShapeDtypeStruct((count * rows, columns), BF16)
    keyval = shape(2, 2 * heads_width)
    if edges:
        outs = (keyval, shape(1, 2 * heads_width), shape(1, 2 * heads_width))
    else:
        outs = (shape(blocks, heads_width), keyval)
    return pl.pallas_call(
        project_edges_kernel if edges else project_rest_kernel,
        out_shape=outs,
        in_specs=[SMEM, VMEM] + [ANY] * len(shards),
        out_specs=(VMEM,) * len(outs),
        scratch_shapes=[
            pltpu.VMEM((2 * rows if edges else blocks * rows, width), BF16),
            pltpu.SemaphoreType.DMA((len(shards),)),
        ],
        compiler_params=pltpu.CompilerParams(vmem_limit_bytes=12 * MIB),
        cost_estimate=SHORT,
        name="project_edges" if edges else "project_rest",
    )(place, weight, *shards)


def window_bias(first, count, starts, ends):
    reach = WIN // 2
    query = first + lax.broadcasted_iota(jnp.int32, (count, 1), 0)
    low = jnp.max(jnp.where(starts <= query, starts, 0), axis=1, keepdims=True)
    high = jnp.min(jnp.where(ends > query, ends, 1 << 30), axis=1, keepdims=True)
    low = jnp.maximum(low, query - reach)
    high = jnp.minimum(high, query + reach + 1)
    key = first - count + lax.broadcasted_iota(jnp.int32, (count, 3 * count), 1)
    return jnp.where((key >= low) & (key < high), 0.0, NEG_FILL)


def attend(query, keyval_ref, bias_ref, scores_ref, weights_ref, out_ref):
    count, width = query.shape
    lane = lax.broadcasted_iota(jnp.int32, (count, 2 * HD), 1)
    for start in range(0, width, 2 * HD):
        values = keyval_ref[:, width + start : width + start + 2 * HD]
        halves = []
        for side in range(2):
            head = start // HD + side
            inside = (lane < HD) if side == 0 else (lane >= HD)
            only = jnp.where(inside, query[:, start : start + 2 * HD], jnp.zeros((), BF16))
            scores_ref[head] = lax.dot_general(
                only, keyval_ref[:, start : start + 2 * HD], (((1,), (1,)), ((), ())), preferred_element_type=F32
            )
            totals = []
            for row in range(0, count, STRIP):
                at = slice(row, row + STRIP)
                scores = scores_ref[head, at] + bias_ref[at]
                weights = jnp.exp(scores - jnp.max(scores, axis=1, keepdims=True))
                totals.append(jnp.sum(weights, axis=1, keepdims=True))
                weights_ref[head, at] = weights.astype(BF16)
            summed = jnp.dot(weights_ref[head], values, preferred_element_type=F32)
            halves.append(summed / jnp.concatenate(totals, axis=0))
        out_ref[:, start : start + 2 * HD] = jnp.where(lane < HD, halves[0], halves[1]).astype(BF16)


def attend_kernel(flips, place_ref, starts_ref, ends_ref, query_ref, middle_ref, edges_ref, even_ref, odd_ref, *refs):
    out_ref, window_ref, bias_ref, scores_ref, weights_ref, sems = refs
    tok, kv = place_ref[0], place_ref[1]
    count = out_ref.shape[0] // len(flips)
    blocks = query_ref.shape[0] // count
    copies = []
    for index, flip in enumerate(flips):
        block = kv ^ flip
        for part in range(3):
            target = window_ref.at[index, part * count : (part + 1) * count]
            sem = sems.at[index, part]
            at = block + part - 1
            middle = (at > 0) & (at < blocks - 1)
            start = jnp.where(middle, at - 1, 0)
            source = middle_ref.at[pl.ds(pl.multiple_of(start * count, count), count)]
            copies.append((index, middle, pltpu.make_async_copy(source, target, sem)))
            for slot, edge in enumerate((0, blocks - 1)):
                source = edges_ref.at[slot * count : (slot + 1) * count]
                copies.append((index, at == edge, pltpu.make_async_copy(source, target, sem)))
            for first_edge, outside in ((tok % 2 == 1, at < 0), (tok % 2 == 0, at >= blocks)):
                if part != 1:
                    copies.append((index, outside & first_edge, pltpu.make_async_copy(even_ref, target, sem)))
                    other = jnp.logical_not(first_edge)
                    copies.append((index, outside & other, pltpu.make_async_copy(odd_ref, target, sem)))
    for _, needed, copy in copies:
        pl.when(needed)(copy.start)
    for index, flip in enumerate(flips):
        block = kv ^ flip
        first = (tok * blocks + block) * count
        bias_ref[...] = window_bias(first, count, starts_ref[...], ends_ref[...])
        for owner, needed, copy in copies:
            if owner == index:
                pl.when(needed)(copy.wait)
        query = query_ref[pl.ds(pl.multiple_of(block * count, count), count)]
        out = out_ref.at[index * count : (index + 1) * count]
        attend(query, window_ref.at[index], bias_ref, scores_ref, weights_ref, out)


def attend_blocks(place, starts, ends, query, middle, edges, even, odd, rows, flips, name):
    heads_width = query.shape[1]
    return pl.pallas_call(
        functools.partial(attend_kernel, flips),
        out_shape=jax.ShapeDtypeStruct((len(flips) * rows, heads_width), BF16),
        in_specs=[SMEM, VMEM, VMEM, VMEM, ANY, ANY, ANY, ANY],
        out_specs=VMEM,
        scratch_shapes=[
            pltpu.VMEM((len(flips), 3 * rows, 2 * heads_width), BF16),
            pltpu.VMEM((rows, 3 * rows), F32),
            pltpu.VMEM((heads_width // HD, rows, 3 * rows), F32),
            pltpu.VMEM((heads_width // HD, rows, 3 * rows), BF16),
            pltpu.SemaphoreType.DMA((len(flips), 3)),
        ],
        compiler_params=pltpu.CompilerParams(vmem_limit_bytes=14 * MIB),
        cost_estimate=SHORT,
        name=name,
    )(place, starts, ends, query, middle, edges, even, odd)


def first_norm_kernel(layout, place_ref, own_ref, partner_ref, own_out_ref, gain_ref, bias_ref, *refs):
    parts, pieces = refs[:4], refs[4 : 4 + len(layout)]
    normed_ref, away_ref, all_ref, weight_ref, mixed_ref, sems = refs[4 + len(layout) :]
    tok = place_ref[0]
    quarters, heads_width, width = weight_ref.shape
    count = own_ref.shape[0]
    copies = [pltpu.make_async_copy(own_out_ref, weight_ref.at[0], sems.at[0])]
    for flips, piece in zip(layout, pieces):
        for index, flip in enumerate(flips):
            depth = piece.shape[2]
            at = pl.multiple_of((tok ^ flip) * depth, depth)
            target = weight_ref.at[1:quarters, pl.ds(at, depth)]
            copies.append(pltpu.make_async_copy(piece.at[index], target, sems.at[len(copies)]))
    for copy in copies:
        copy.start()
    for flip, part_ref in enumerate(parts):
        columns = slice(flip * heads_width, (flip + 1) * heads_width)
        for half in range(2):
            turned = half ^ (flip % 2)
            all_ref[half * count : (half + 1) * count, columns] = part_ref[turned * count : (turned + 1) * count]
    for copy in copies:
        copy.wait()
    weight = weight_ref[...].reshape(quarters * heads_width, width)
    mixed_ref[...] = jnp.dot(all_ref[...], weight, preferred_element_type=F32)
    for half, (hidden_ref, result_ref) in enumerate(((own_ref, normed_ref), (partner_ref, away_ref))):
        for row in range(0, count, STRIP):
            at = slice(row, row + STRIP)
            mixed = hidden_ref[at].astype(F32) + mixed_ref[half * count + row : half * count + row + STRIP]
            result_ref[at] = normalized(mixed, gain_ref[...], bias_ref[...]).astype(BF16)


def first_norm(place, own, partner, own_out, gain, bias, parts, pieces):
    rows, width = own.shape
    heads_width = own_out.shape[0]
    layout = tuple(flips for flips, _ in pieces)
    return pl.pallas_call(
        functools.partial(first_norm_kernel, layout),
        out_shape=(jax.ShapeDtypeStruct((rows, width), BF16),) * 2,
        in_specs=[SMEM, VMEM, VMEM, ANY, VMEM, VMEM] + [VMEM] * len(parts) + [ANY] * len(pieces),
        out_specs=(VMEM,) * 2,
        scratch_shapes=[
            pltpu.VMEM((2 * rows, width), BF16),
            pltpu.VMEM((len(parts), heads_width, width), BF16),
            pltpu.VMEM((2 * rows, width), F32),
            pltpu.SemaphoreType.DMA((1 + sum(len(flips) for flips in layout),)),
        ],
        compiler_params=pltpu.CompilerParams(vmem_limit_bytes=14 * MIB),
        cost_estimate=SHORT,
        name="first_norm",
    )(place, own, partner, own_out, gain, bias, *parts, *[value for _, value in pieces])


def gelu(values):
    return 0.5 * values * (1.0 + lax.erf(values * math.sqrt(0.5)))


CHUNK = 512


def feed_chunk(rows, up, down_ref, wide_ref, units_ref):
    wide_ref[...] = jnp.dot(rows, up, preferred_element_type=F32)
    for row in range(0, rows.shape[0], STRIP):
        strip = slice(row, row + STRIP)
        units_ref[strip] = gelu(wide_ref[strip]).astype(BF16)
    return jnp.dot(units_ref[...], down_ref[...], preferred_element_type=F32)


def far_copies(tok, held_ref, core_ref, up_ref, down_ref, sems):
    block = 128
    copies = []
    for side, piece in enumerate((held_ref, core_ref)):
        for index in range(4):
            at = pl.ds(pl.multiple_of((tok ^ (2 * index + side)) * block, block), block)
            for part, target in enumerate((up_ref, down_ref)):
                source = piece.at[pl.ds((2 * index + part) * block, block)]
                copies.append(pltpu.make_async_copy(source, target.at[at], sems.at[len(copies)]))
    return copies


def feed_kernel(place_ref, rows_ref, up_near_ref, down_near_ref, held_ref, core_ref, *refs):
    sum_ref, up_ref, down_ref, wide_ref, units_ref, total_ref, sems = refs
    copies = far_copies(place_ref[0], held_ref, core_ref, up_ref, down_ref, sems)
    for copy in copies:
        copy.start()
    rows = rows_ref[...]
    chunks = up_ref.shape[1] // CHUNK
    for index in range(2 * chunks):
        if index == chunks:
            for copy in copies:
                copy.wait()
        up, down = (up_near_ref, down_near_ref) if index < chunks else (up_ref, down_ref)
        at = slice(index % chunks * CHUNK, (index % chunks + 1) * CHUNK)
        product = feed_chunk(rows, up[:, at], down.at[at], wide_ref.at[index % 2], units_ref.at[index % 2])
        if index == 0:
            total_ref[...] = product
        elif index < 2 * chunks - 1:
            total_ref[...] += product
        else:
            sum_ref[...] = (total_ref[...] + product).astype(sum_ref.dtype)


def feed(place, rows, up_weight, down_weight, pieces, dtype, name):
    count, width = rows.shape
    units = up_weight.shape[1]
    return pl.pallas_call(
        feed_kernel,
        out_shape=jax.ShapeDtypeStruct((count, width), dtype),
        in_specs=[SMEM] + [VMEM] * 3 + [ANY] * 2,
        out_specs=VMEM,
        scratch_shapes=[
            pltpu.VMEM((width, units), BF16),
            pltpu.VMEM((units, width), BF16),
            pltpu.VMEM((2, count, CHUNK), F32),
            pltpu.VMEM((2, count, CHUNK), BF16),
            pltpu.VMEM((count, width), F32),
            pltpu.SemaphoreType.DMA((16,)),
        ],
        compiler_params=pltpu.CompilerParams(vmem_limit_bytes=18 * MIB),
        cost_estimate=SHORT,
        name=name,
    )(place, rows, up_weight, down_weight, *pieces)


def finish_kernel(normed_ref, near_ref, far_ref, gain_ref, bias_ref, out_ref):
    for row in range(0, normed_ref.shape[0], STRIP):
        at = slice(row, row + STRIP)
        mixed = normed_ref[at].astype(F32) + near_ref[at] + far_ref[at].astype(F32)
        out_ref[at] = normalized(mixed, gain_ref[...], bias_ref[...]).astype(out_ref.dtype)


def finish(normed, near, far, gain, bias):
    return pl.pallas_call(
        finish_kernel,
        out_shape=jax.ShapeDtypeStruct(normed.shape, BF16),
        in_specs=[VMEM] * 5,
        out_specs=VMEM,
        compiler_params=pltpu.CompilerParams(vmem_limit_bytes=6 * MIB),
        name="finish",
    )(normed, near, far, gain, bias)


def decode_kernel(slot_ref, filled_ref, query_ref, cache_ref, out_ref, high_ref, total_ref, sum_ref):
    step = pl.program_id(0)

    @pl.when(step == 0)
    def _():
        high_ref[...] = jnp.full(high_ref.shape, NEG_FILL, F32)
        total_ref[...] = jnp.zeros_like(total_ref)
        sum_ref[...] = jnp.zeros_like(sum_ref)

    row = slot_ref[step]
    filled = filled_ref[step]
    width = query_ref.shape[1]
    head = lax.broadcasted_iota(jnp.int32, (H, width), 0)
    inside = head == lax.broadcasted_iota(jnp.int32, (H, width), 1) // HD
    query = jnp.where(inside, query_ref[pl.ds(row, 1), :], 0.0).astype(BF16)
    scores = lax.dot_general(query, cache_ref[0, 0, 0], (((1,), (1,)), ((), ())), preferred_element_type=F32)
    live = lax.broadcasted_iota(jnp.int32, scores.shape, 1) < filled
    scores = jnp.where(live, scores * (1.0 / math.sqrt(HD)), NEG_FILL)
    high = jnp.max(scores, axis=1, keepdims=True)
    weights = jnp.where(live, jnp.exp(scores - high), 0.0)
    total = jnp.sum(weights, axis=1, keepdims=True)
    summed = jnp.dot(weights.astype(BF16), cache_ref[1, 0, 0], preferred_element_type=F32)
    along = lambda column: jnp.sum(jnp.where(inside, column, 0.0), axis=0, keepdims=True)
    high, total, summed = along(high), along(total), along(summed)
    used = filled > 0
    at = pl.ds(row, 1)
    old = high_ref[at, :]
    new = jnp.where(used, jnp.maximum(old, high), old)
    left = jnp.exp(old - new)
    right = jnp.where(used, jnp.exp(high - new), 0.0)
    high_ref[at, :] = new
    total_ref[at, :] = total_ref[at, :] * left + total * right
    sum_ref[at, :] = sum_ref[at, :] * left + summed * right

    @pl.when(step == pl.num_programs(0) - 1)
    def _():
        out_ref[0] = high_ref[...]
        out_ref[1] = total_ref[...]
        out_ref[2] = sum_ref[...]


def decode(slots, filled, queries, kv_cache):
    requests, width = queries.shape
    pieces = kv_cache.shape[2]
    state = pltpu.VMEM((requests, width), F32)
    return pl.pallas_call(
        decode_kernel,
        grid=(pieces,),
        out_shape=jax.ShapeDtypeStruct((3, requests, width), F32),
        in_specs=[
            SMEM,
            SMEM,
            pl.BlockSpec((requests, width), lambda i: (0, 0)),
            pl.BlockSpec((2, 1, 1, PLEN, width), lambda i: (0, 0, i, 0, 0)),
        ],
        out_specs=pl.BlockSpec((3, requests, width), lambda i: (0, 0, 0)),
        scratch_shapes=[state, state, state],
        compiler_params=pltpu.CompilerParams(vmem_limit_bytes=8 * MIB),
        cost_estimate=SHORT,
        name="decode",
    )(slots, filled, queries, kv_cache)


def decode_partial(queries, own, kv_cache, piece_req, piece_used):
    owners = piece_req[0]
    slots = ((owners // own) ^ lax.axis_index("kv")) * own + owners % own
    return decode(slots, piece_used[0], queries, kv_cache)


def exchanged_partials(partial, own):
    parts = [partial[:, :own]]
    for flip in range(1, lax.axis_size("kv")):
        parts.append(swapped(partial[:, flip * own : (flip + 1) * own], "kv", flip))
    return parts


def merged_partials(parts):
    high = functools.reduce(jnp.maximum, [part[0] for part in parts])
    factors = [jnp.exp(part[0] - high) for part in parts]
    total = sum(part[1] * factor for part, factor in zip(parts, factors))
    summed = sum(part[2] * factor for part, factor in zip(parts, factors))
    return (summed / total).astype(BF16)


def routed_body(
    hidden_in,
    qkv_weight,
    stretch_len,
    out_weight,
    ln1_gain,
    ln1_bias,
    up_weight,
    down_weight,
    ln2_gain,
    ln2_bias,
    dec_query,
    kv_cache,
    piece_req,
    piece_used,
):
    tok = lax.axis_index("tok")
    kv = lax.axis_index("kv")
    toks, kvs = lax.axis_size("tok"), lax.axis_size("kv")
    rows, width = hidden_in.shape
    place = jnp.stack([tok, kv]).astype(jnp.int32)
    eighth = lambda value: lax.dynamic_slice_in_dim(value, tok * (value.shape[0] // toks), value.shape[0] // toks, 0)

    outward = [(1, 0), (2, 3)]
    a1, b1 = over_edges(hidden_in, "kv", 0), over_edges(hidden_in, "kv", 1)
    out_part = eighth(out_weight)
    depth = out_part.shape[0]
    small = jnp.concatenate([out_part, dec_query], axis=0)
    others = [swapped(small, "kv", flip) for flip in range(1, kvs)]
    a2, b2 = lax.ppermute(b1, "kv", outward), over_edges(a1, "kv", 1)
    queries = jnp.concatenate([dec_query] + [other[depth:] for other in others], axis=0).astype(F32)
    partial = decode_partial(queries, dec_query.shape[0], kv_cache, piece_req, piece_used)
    out_here = jnp.stack([other[:depth] for other in others])
    out_x, out_y = swapped(out_here, "tok", 2), swapped(out_here, "tok", 4)
    a3 = lax.ppermute(after(b2, partial), "kv", outward)
    out_far = swapped(out_here, "tok", 6)
    shards = (after(hidden_in, out_x, out_y, out_far), a1, a2, a3, b1, b2)
    inner = (kv == 1) | (kv == 2)

    feed_part = jnp.concatenate([eighth(up_weight), eighth(down_weight)], axis=0)
    feed_inner = lax.ppermute(after(feed_part, a2, b2), "kv", [(0, 2), (3, 1)])
    feed_outer = lax.ppermute(after(feed_part, a3, feed_inner), "kv", [(1, 3), (2, 0)])

    order = jnp.arange(stretch_len.shape[0])
    ends = jnp.sum(jnp.where(order[:, None] <= order[None, :], stretch_len[:, None], 0), axis=0, dtype=jnp.int32)
    starts = (ends - stretch_len)[None, :]
    ends = ends[None, :]

    weight = jnp.transpose(qkv_weight, (1, 0, 2))
    edges, even, odd = project(place, weight, shards, kvs, True)
    even, odd = over_edges(even, "tok", 0), over_edges(odd, "tok", 1)
    query, middle = project(place, weight, (after(hidden_in, edges),) + shards[1:], kvs, False)
    window = (middle, edges, even, odd, rows)
    far = attend_blocks(place, starts, ends, query, *window, (2, 3), "attend_far")
    far_heads = swapped(far, "kv", 2)
    feed_here = jnp.where(inner, feed_inner, after(feed_outer, far))
    feed_x, feed_y = swapped(feed_here, "tok", 2), swapped(feed_here, "tok", 4)
    near = attend_blocks(place, starts, ends, after(query, feed_here), *window, (0, 1), "attend_near")
    partner_heads, passed_heads = swapped(near, "kv", 1), swapped(far_heads, "kv", 1)
    parts = (near, partner_heads, far_heads, passed_heads)

    out_all = jnp.stack([out_here, out_x, out_y, out_far])
    out_pieces = [((0, 2, 4, 6), out_all), ((1, 3, 5, 7), swapped(after(out_all, near, far_heads), "tok", 1))]
    half = feed_here.shape[0] // 2
    far_up = swapped(after(feed_y, far_heads, partner_heads)[:half], "tok", 2)
    far_down = swapped(after(feed_x, far_heads, partner_heads)[half:], "tok", 4)
    held = jnp.concatenate([feed_here, feed_x, feed_y, far_up, far_down], axis=0)
    feed_pieces = (held, swapped(after(held, passed_heads), "tok", 1))

    gain, bias = ln1_gain[None, :], ln1_bias[None, :]
    normed, partner = first_norm(place, hidden_in, a1, out_weight, gain, bias, parts, out_pieces)
    away = feed(place, partner, up_weight, down_weight, feed_pieces, BF16, "feed_partner")
    arrived = swapped(away, "kv", 1)
    dec_parts = exchanged_partials(after(partial, away), dec_query.shape[0])
    mine = feed(place, after(normed, away), up_weight, down_weight, feed_pieces, F32, "feed_own")
    prefill_out = finish(normed, mine, arrived, ln2_gain[None, :], ln2_bias[None, :])

    return prefill_out, merged_partials(after(tuple(dec_parts), mine))


def extended(value, sides, width):
    for axis, dim in sides:
        count, length = (lax.axis_size(axis), value.shape[dim])
        up = [(i, (i + 1) % count) for i in range(count - 1)]
        down = [(j, i) for i, j in up]
        last = lax.slice_in_dim(value, length - width, length, axis=dim)
        leading = lax.slice_in_dim(value, 0, width, axis=dim)
        before = lax.ppermute(last, axis, up)
        after = lax.ppermute(leading, axis, down)
        value = jnp.concatenate([before, value, after], axis=dim)
    return value


def merged(value, axis, join):
    pieces = jax.tree.map(lambda part: lax.all_gather(part, axis), value)
    head = jax.tree.map(lambda part: part[0], pieces)
    tail = jax.tree.map(lambda part: part[1:], pieces)
    subtotal, _ = lax.scan(lambda subtotal, section: (join(subtotal, section), None), head, tail)
    return subtotal


def segment_ids(row_ids, stretch_len):
    stretch_ends = jnp.cumsum(stretch_len)
    return jnp.sum((row_ids[:, None] >= stretch_ends[None, :]).astype(jnp.int32), axis=1)


def layer_norm(values, gain, bias):
    center = values - jnp.mean(values, axis=1, keepdims=True)
    spread = jnp.mean(center * center, axis=1, keepdims=True)
    return center * lax.rsqrt(spread + LN_EPS) * gain + bias


def merge_partials(earlier, later):
    highest = jnp.maximum(earlier[0], later[0])
    left_factor = jnp.exp(earlier[0] - highest)
    right_factor = jnp.exp(later[0] - highest)
    totals = earlier[1] * left_factor + later[1] * right_factor
    weighted = earlier[2] * left_factor[..., None] + later[2] * right_factor[..., None]
    return (highest, totals, weighted)


def row_folder(source, shard_rows):
    return jnp.dot(source, shard_rows, preferred_element_type=jnp.float32)


def general_body(
    hidden_in,
    qkv_weight,
    stretch_len,
    out_weight,
    ln1_gain,
    ln1_bias,
    up_weight,
    down_weight,
    ln2_gain,
    ln2_bias,
    dec_query,
    kv_cache,
    piece_req,
    piece_used,
):
    inv_scale = 1.0 / math.sqrt(HD)
    reach = WIN // 2
    local_width = qkv_weight.shape[2]
    head_count = local_width // HD
    flat_weight = qkv_weight.reshape(qkv_weight.shape[0], 3 * local_width)
    qkv_rows = jnp.dot(
        lax.all_gather(hidden_in, "kv", axis=0, tiled=True),
        flat_weight,
        preferred_element_type=jnp.float32,
    ).astype(jnp.bfloat16)
    row_count = qkv_rows.shape[0]
    query_rows = qkv_rows[:, :local_width]
    keyval_rows = qkv_rows[:, local_width:]
    padded = extended(keyval_rows, (("tok", 0),), reach)
    first_row = lax.axis_index("tok") * row_count
    total_rows = row_count * lax.axis_size("tok")
    qblock = min(512, row_count)
    span = qblock + 2 * reach
    block_count = row_count // qblock

    def attend(block_index):
        start = block_index * qblock
        query_ids = first_row + start + jnp.arange(qblock, dtype=jnp.int32)
        key_ids = first_row + start - reach + jnp.arange(span, dtype=jnp.int32)
        query_seg = segment_ids(query_ids, stretch_len)
        inside = (key_ids >= 0) & (key_ids < total_rows)
        key_seg = jnp.where(inside, segment_ids(key_ids, stretch_len), -1)
        allowed = (key_seg[None, :] == query_seg[:, None]) & (
            jnp.abs(key_ids[None, :] - query_ids[:, None]) <= reach
        )
        queries = lax.dynamic_slice_in_dim(query_rows, start, qblock, 0).reshape(
            qblock, head_count, HD
        )
        both = lax.dynamic_slice_in_dim(padded, start, span, 0)
        key_rows = both[:, :local_width].reshape(span, head_count, HD)
        value_rows = both[:, local_width:].reshape(span, head_count, HD)
        scores = (
            jnp.einsum("ihd,jhd->hij", queries, key_rows, preferred_element_type=jnp.float32)
            * inv_scale
        )
        scores = jnp.where(allowed[None], scores, NEG_FILL)
        row_max = jnp.max(scores, axis=2, keepdims=True)
        weights = jnp.where(allowed[None], jnp.exp(scores - row_max), 0.0)
        totals = jnp.sum(weights, axis=2)
        summed = jnp.einsum(
            "hij,jhd->ihd",
            weights.astype(jnp.bfloat16),
            value_rows,
            preferred_element_type=jnp.float32,
        )
        return (
            (summed / jnp.transpose(totals)[:, :, None])
            .astype(jnp.bfloat16)
            .reshape(qblock, local_width)
        )

    attention = lax.map(attend, jnp.arange(block_count, dtype=jnp.int32)).reshape(
        row_count, local_width
    )
    token_major = lax.all_to_all(attention, "kv", split_axis=0, concat_axis=1, tiled=True)
    projected = row_folder(token_major, lax.all_gather(out_weight, "kv", axis=0, tiled=True))
    normed = layer_norm(hidden_in.astype(jnp.float32) + projected, ln1_gain, ln1_bias).astype(
        jnp.bfloat16
    )
    units = jax.nn.gelu(
        jnp.dot(
            lax.all_gather(normed, "kv", axis=0, tiled=True),
            up_weight,
            preferred_element_type=jnp.float32,
        ),
        approximate=False,
    ).astype(jnp.bfloat16)
    ffn = lax.psum_scatter(
        jnp.dot(units, down_weight, preferred_element_type=jnp.float32).astype(jnp.bfloat16),
        "kv",
        scatter_dimension=0,
        tiled=True,
    ).astype(jnp.float32)
    prefill_out = layer_norm(normed.astype(jnp.float32) + ffn, ln2_gain, ln2_bias).astype(
        jnp.bfloat16
    )
    group_queries = lax.all_gather(dec_query, "kv", axis=0, tiled=True)
    request_count = group_queries.shape[0]
    owners = piece_req[0]
    filled = piece_used[0]
    slot_count = owners.shape[0]
    request_ids = jnp.arange(request_count, dtype=jnp.int32)
    selector = (owners[:, None] == request_ids[None, :]).astype(jnp.bfloat16)
    chosen = jnp.dot(selector, group_queries, preferred_element_type=jnp.float32).astype(
        jnp.bfloat16
    )
    chosen = chosen.reshape(slot_count, H, HD)
    cache_keys = kv_cache[0, 0].reshape(slot_count, PLEN, H, HD)
    cache_values = kv_cache[1, 0].reshape(slot_count, PLEN, H, HD)
    piece_scores = (
        jnp.einsum("phd,pthd->pht", chosen, cache_keys, preferred_element_type=jnp.float32)
        * inv_scale
    )
    active = jnp.arange(PLEN, dtype=jnp.int32)[None, :] < filled[:, None]
    piece_scores = jnp.where(active[:, None, :], piece_scores, NEG_FILL)
    piece_max = jnp.max(piece_scores, axis=2)
    piece_weights = jnp.where(
        active[:, None, :], jnp.exp(piece_scores - piece_max[:, :, None]), 0.0
    )
    piece_totals = jnp.sum(piece_weights, axis=2)
    partial_value = jnp.einsum(
        "pht,pthd->phd",
        piece_weights.astype(jnp.bfloat16),
        cache_values,
        preferred_element_type=jnp.float32,
    )
    member = (owners[None, :] == request_ids[:, None]) & (filled[None, :] > 0)
    highest = jnp.max(jnp.where(member[:, :, None], piece_max[None], NEG_FILL), axis=1)
    factor = jnp.where(member[:, :, None], jnp.exp(piece_max[None] - highest[:, None, :]), 0.0)
    denom = jnp.sum(factor * piece_totals[None], axis=1)
    weighted = jnp.einsum("rph,phd->rhd", factor, partial_value)
    own_requests = dec_query.shape[0]
    joined = merged((highest, denom, weighted), "kv", merge_partials)
    begin = lax.axis_index("kv") * own_requests
    final_denom = lax.dynamic_slice_in_dim(joined[1], begin, own_requests, 0)
    final_weighted = lax.dynamic_slice_in_dim(joined[2], begin, own_requests, 0)
    dec_out = (
        (final_weighted / final_denom[:, :, None])
        .astype(jnp.bfloat16)
        .reshape(own_requests, H * HD)
    )
    return (prefill_out, dec_out)


def solution(mesh):
    placed = (
        P(("tok", "kv"), None),
        P(None, None, "kv"),
        P(),
        P("kv", None),
        P(),
        P(),
        P(None, "kv"),
        P("kv", None),
        P(),
        P(),
        P(("tok", "kv"), None),
        P(None, "tok", "kv", None, None),
        P("tok", "kv"),
        P("tok", "kv"),
    )
    routed = mesh.shape["tok"] == 8 and mesh.shape["kv"] == 4
    return jax.shard_map(
        routed_body if routed else general_body,
        mesh=mesh,
        in_specs=placed,
        out_specs=(P(("tok", "kv"), None), P(("tok", "kv"), None)),
        check_vma=False,
    )
```

```python
import functools
import math

import jax
import jax.numpy as jnp
from jax import lax
from jax.experimental import pallas as pl
from jax.experimental.pallas import tpu as pltpu
from jax.sharding import PartitionSpec as P

H = 16
HD = 64
WIN = 512
PLEN = 128


NEG_FILL = -1e30
LN_EPS = 1e-05
BF16 = jnp.bfloat16
F32 = jnp.float32
STRIP = 32
MIB = 1024 * 1024
ANY = pl.BlockSpec(memory_space=pl.ANY)
VMEM = pl.BlockSpec(memory_space=pltpu.VMEM)
SMEM = pl.BlockSpec(memory_space=pltpu.SMEM)
SHORT = pl.CostEstimate(flops=1, bytes_accessed=1, transcendentals=0)


def swapped(value, axis, flip):
    count = lax.axis_size(axis)
    return lax.ppermute(value, axis, [(i, i ^ flip) for i in range(count)])


def over_edges(value, axis, first):
    count = lax.axis_size(axis)
    edges = [(i, i + 1) for i in range(first, count - 1, 2)]
    return lax.ppermute(value, axis, edges + [(j, i) for i, j in edges])


def after(value, *earlier):
    return lax.optimization_barrier((value,) + earlier)[0]


def normalized(values, gain, bias):
    center = values - jnp.mean(values, axis=1, keepdims=True)
    spread = jnp.mean(center * center, axis=1, keepdims=True)
    return center * lax.rsqrt(spread + LN_EPS) * gain + bias


def project_early_kernel(place_ref, weight_ref, own, a1, a2, b1, b2, query_ref, keyval_ref, rows_ref, sems):
    kv = place_ref[1]
    count = own.shape[0]
    inner = (kv == 1) | (kv == 2)
    outer = jnp.logical_not(inner)
    copies = []
    for source, flip, needed in ((own, 0, None), (a1, 1, None), (a2, 2, outer), (b2, 2, inner), (b1, 3, inner)):
        at = pl.ds(pl.multiple_of((kv ^ flip) * count, count), count)
        copies.append((needed, pltpu.make_async_copy(source, rows_ref.at[at], sems.at[len(copies)])))
    for needed, copy in copies:
        copy.start() if needed is None else pl.when(needed)(copy.start)
    for needed, copy in copies:
        copy.wait() if needed is None else pl.when(needed)(copy.wait)
    project_rows(rows_ref[...], weight_ref, query_ref, keyval_ref)


def project_rows(rows, weight_ref, query_ref, keyval_ref):
    width = weight_ref.shape[2]
    query = jnp.dot(rows, weight_ref[0], preferred_element_type=F32) * (1.0 / math.sqrt(HD))
    query_ref[...] = query.astype(BF16)
    for part in range(2):
        at = slice(part * width, (part + 1) * width)
        keyval_ref[:, at] = jnp.dot(rows, weight_ref[part + 1], preferred_element_type=F32).astype(BF16)


def project_last_kernel(place_ref, weight_ref, keyval_ref, a3_ref, query_ref, last_ref, even_ref, odd_ref):
    tok, kv = place_ref[0], place_ref[1]
    count = a3_ref.shape[0]
    project_rows(a3_ref[...], weight_ref, query_ref, last_ref)
    last = last_ref[...]
    blocks = keyval_ref.shape[0] // count
    top = jnp.where(kv == blocks - 1, last, keyval_ref[:count])
    bottom = jnp.where(kv == 0, last, keyval_ref[(blocks - 1) * count :])
    even_tok = tok % 2 == 0
    even_ref[...] = jnp.where(even_tok, bottom, top)
    odd_ref[...] = jnp.where(even_tok, top, bottom)


def project_early(place, weight, blocks, shards):
    rows, width = shards[0].shape
    heads_width = weight.shape[2]
    return pl.pallas_call(
        project_early_kernel,
        out_shape=(
            jax.ShapeDtypeStruct((blocks * rows, heads_width), BF16),
            jax.ShapeDtypeStruct((blocks * rows, 2 * heads_width), BF16),
        ),
        in_specs=[SMEM, VMEM] + [ANY] * len(shards),
        out_specs=(VMEM,) * 2,
        scratch_shapes=[pltpu.VMEM((blocks * rows, width), BF16), pltpu.SemaphoreType.DMA((len(shards),))],
        compiler_params=pltpu.CompilerParams(vmem_limit_bytes=12 * MIB),
        cost_estimate=SHORT,
        name="project_early",
    )(place, weight, *shards)


def project_last(place, weight, keyval, a3):
    rows = a3.shape[0]
    heads_width = weight.shape[2]
    keyvals = jax.ShapeDtypeStruct((rows, 2 * heads_width), BF16)
    return pl.pallas_call(
        project_last_kernel,
        out_shape=(jax.ShapeDtypeStruct((rows, heads_width), BF16), keyvals, keyvals, keyvals),
        in_specs=[SMEM] + [VMEM] * 3,
        out_specs=(VMEM,) * 4,
        compiler_params=pltpu.CompilerParams(vmem_limit_bytes=8 * MIB),
        cost_estimate=SHORT,
        name="project_last",
    )(place, weight, keyval, a3)


def window_bias(first, count, starts, ends):
    reach = WIN // 2
    query = first + lax.broadcasted_iota(jnp.int32, (count, 1), 0)
    low = jnp.max(jnp.where(starts <= query, starts, 0), axis=1, keepdims=True)
    high = jnp.min(jnp.where(ends > query, ends, 1 << 30), axis=1, keepdims=True)
    low = jnp.maximum(low, query - reach)
    high = jnp.minimum(high, query + reach + 1)
    key = first - count + lax.broadcasted_iota(jnp.int32, (count, 3 * count), 1)
    return jnp.where((key >= low) & (key < high), 0.0, NEG_FILL)


def attend(query, keyval_ref, bias_ref, scores_ref, weights_ref, out_ref):
    count, width = query.shape
    lane = lax.broadcasted_iota(jnp.int32, (count, 2 * HD), 1)
    for start in range(0, width, 2 * HD):
        values = keyval_ref[:, width + start : width + start + 2 * HD]
        halves = []
        for side in range(2):
            head = start // HD + side
            inside = (lane < HD) if side == 0 else (lane >= HD)
            only = jnp.where(inside, query[:, start : start + 2 * HD], jnp.zeros((), BF16))
            scores_ref[head] = lax.dot_general(
                only, keyval_ref[:, start : start + 2 * HD], (((1,), (1,)), ((), ())), preferred_element_type=F32
            )
            totals = []
            for row in range(0, count, STRIP):
                at = slice(row, row + STRIP)
                scores = scores_ref[head, at] + bias_ref[at]
                weights = jnp.exp(scores - jnp.max(scores, axis=1, keepdims=True))
                totals.append(jnp.sum(weights, axis=1, keepdims=True))
                weights_ref[head, at] = weights.astype(BF16)
            summed = jnp.dot(weights_ref[head], values, preferred_element_type=F32)
            halves.append(summed / jnp.concatenate(totals, axis=0))
        out_ref[:, start : start + 2 * HD] = jnp.where(lane < HD, halves[0], halves[1]).astype(BF16)


def attend_kernel(flips, has_last, has_halo, joins, place_ref, starts_ref, ends_ref, query_ref, keyval_ref, *refs):
    refs = list(refs)
    last_query_ref, last_ref = (refs.pop(0), refs.pop(0)) if has_last else (None, None)
    even_ref, odd_ref = (refs.pop(0), refs.pop(0)) if has_halo else (None, None)
    earlier_ref = refs.pop(0) if joins else None
    out_ref, window_ref, bias_ref, scores_ref, weights_ref, sems = refs
    tok, kv = place_ref[0], place_ref[1]
    count = bias_ref.shape[0]
    blocks = query_ref.shape[0] // count
    inner = (kv == 1) | (kv == 2)
    block = kv ^ jnp.where(inner, flips[1], flips[0])
    missing = jnp.where(inner, -1, kv ^ 3)
    copies = []
    for part in range(3):
        target = window_ref.at[part * count : (part + 1) * count]
        sem = sems.at[part]
        at = block + part - 1
        held = (at >= 0) & (at < blocks) & (at != missing)
        source = keyval_ref.at[pl.ds(pl.multiple_of(jnp.where(held, at, 0) * count, count), count)]
        copies.append((held, pltpu.make_async_copy(source, target, sem)))
        if has_last:
            copies.append((at == missing, pltpu.make_async_copy(last_ref, target, sem)))
        if has_halo and part != 1:
            outside = at < 0 if part == 0 else at >= blocks
            over_even = tok % 2 == (1 if part == 0 else 0)
            copies.append((outside & over_even, pltpu.make_async_copy(even_ref, target, sem)))
            copies.append((outside & jnp.logical_not(over_even), pltpu.make_async_copy(odd_ref, target, sem)))
    for needed, copy in copies:
        pl.when(needed)(copy.start)
    first = (tok * blocks + block) * count
    bias_ref[...] = window_bias(first, count, starts_ref[...], ends_ref[...])
    query = query_ref[pl.ds(pl.multiple_of(block * count, count), count)]
    if has_last:
        query = jnp.where(block == missing, last_query_ref[...], query)
    for needed, copy in copies:
        pl.when(needed)(copy.wait)
    if joins:
        half = jnp.where(inner, flips[1] % 2, flips[0] % 2)
        out_ref[pl.ds(pl.multiple_of((1 - half) * count, count), count)] = earlier_ref[...]
        out_ref = out_ref.at[pl.ds(pl.multiple_of(half * count, count), count)]
    attend(query, window_ref, bias_ref, scores_ref, weights_ref, out_ref)


def attend_block(place, starts, ends, query, keyval, flips, name, last=(), halo=(), earlier=()):
    rows = query.shape[0] // lax.axis_size("kv")
    heads_width = query.shape[1]
    return pl.pallas_call(
        functools.partial(attend_kernel, flips, bool(last), bool(halo), bool(earlier)),
        out_shape=jax.ShapeDtypeStruct(((1 + len(earlier)) * rows, heads_width), BF16),
        in_specs=[SMEM, VMEM, VMEM, VMEM, ANY] + [VMEM, ANY][: len(last)] + [ANY] * len(halo) + [VMEM] * len(earlier),
        out_specs=VMEM,
        scratch_shapes=[
            pltpu.VMEM((3 * rows, 2 * heads_width), BF16),
            pltpu.VMEM((rows, 3 * rows), F32),
            pltpu.VMEM((heads_width // HD, rows, 3 * rows), F32),
            pltpu.VMEM((heads_width // HD, rows, 3 * rows), BF16),
            pltpu.SemaphoreType.DMA((3,)),
        ],
        compiler_params=pltpu.CompilerParams(vmem_limit_bytes=12 * MIB),
        cost_estimate=SHORT,
        name=name,
    )(place, starts, ends, query, keyval, *last, *halo, *earlier)


def first_norm_kernel(layout, place_ref, own_ref, partner_ref, own_out_ref, gain_ref, bias_ref, *refs):
    parts, pieces = refs[:4], refs[4 : 4 + len(layout)]
    normed_ref, away_ref, all_ref, weight_ref, mixed_ref, sems = refs[4 + len(layout) :]
    tok = place_ref[0]
    quarters, heads_width, width = weight_ref.shape
    count = own_ref.shape[0]
    copies = [pltpu.make_async_copy(own_out_ref, weight_ref.at[0], sems.at[0])]
    for flips, piece in zip(layout, pieces):
        for index, flip in enumerate(flips):
            depth = piece.shape[2]
            at = pl.multiple_of((tok ^ flip) * depth, depth)
            target = weight_ref.at[1:quarters, pl.ds(at, depth)]
            copies.append(pltpu.make_async_copy(piece.at[index], target, sems.at[len(copies)]))
    for copy in copies:
        copy.start()
    for flip, part_ref in enumerate(parts):
        columns = slice(flip * heads_width, (flip + 1) * heads_width)
        for half in range(2):
            turned = half ^ (flip % 2)
            all_ref[half * count : (half + 1) * count, columns] = part_ref[turned * count : (turned + 1) * count]
    for copy in copies:
        copy.wait()
    weight = weight_ref[...].reshape(quarters * heads_width, width)
    mixed_ref[...] = jnp.dot(all_ref[...], weight, preferred_element_type=F32)
    for half, (hidden_ref, result_ref) in enumerate(((own_ref, normed_ref), (partner_ref, away_ref))):
        for row in range(0, count, STRIP):
            at = slice(row, row + STRIP)
            mixed = hidden_ref[at].astype(F32) + mixed_ref[half * count + row : half * count + row + STRIP]
            result_ref[at] = normalized(mixed, gain_ref[...], bias_ref[...]).astype(BF16)


def first_norm(place, own, partner, own_out, gain, bias, parts, pieces):
    rows, width = own.shape
    heads_width = own_out.shape[0]
    layout = tuple(flips for flips, _ in pieces)
    return pl.pallas_call(
        functools.partial(first_norm_kernel, layout),
        out_shape=(jax.ShapeDtypeStruct((rows, width), BF16),) * 2,
        in_specs=[SMEM, VMEM, VMEM, ANY, VMEM, VMEM] + [VMEM] * len(parts) + [ANY] * len(pieces),
        out_specs=(VMEM,) * 2,
        scratch_shapes=[
            pltpu.VMEM((2 * rows, width), BF16),
            pltpu.VMEM((len(parts), heads_width, width), BF16),
            pltpu.VMEM((2 * rows, width), F32),
            pltpu.SemaphoreType.DMA((1 + sum(len(flips) for flips in layout),)),
        ],
        compiler_params=pltpu.CompilerParams(vmem_limit_bytes=14 * MIB),
        cost_estimate=SHORT,
        name="first_norm",
    )(place, own, partner, own_out, gain, bias, *parts, *[value for _, value in pieces])


def gelu(values):
    return 0.5 * values * (1.0 + lax.erf(values * math.sqrt(0.5)))


CHUNK = 512


def feed_chunk(rows, up, down_ref, wide_ref, units_ref):
    wide_ref[...] = jnp.dot(rows, up, preferred_element_type=F32)
    for row in range(0, rows.shape[0], STRIP):
        strip = slice(row, row + STRIP)
        units_ref[strip] = gelu(wide_ref[strip]).astype(BF16)
    return jnp.dot(units_ref[...], down_ref[...], preferred_element_type=F32)


def far_copies(tok, held_ref, core_ref, up_ref, down_ref, sems):
    block = 128
    copies = []
    for side, piece in enumerate((held_ref, core_ref)):
        for index in range(4):
            at = pl.ds(pl.multiple_of((tok ^ (2 * index + side)) * block, block), block)
            for part, target in enumerate((up_ref, down_ref)):
                source = piece.at[pl.ds((2 * index + part) * block, block)]
                copies.append(pltpu.make_async_copy(source, target.at[at], sems.at[len(copies)]))
    return copies


def feed_kernel(place_ref, rows_ref, up_near_ref, down_near_ref, held_ref, core_ref, *refs):
    sum_ref, up_ref, down_ref, wide_ref, units_ref, total_ref, sems = refs
    copies = far_copies(place_ref[0], held_ref, core_ref, up_ref, down_ref, sems)
    for copy in copies:
        copy.start()
    rows = rows_ref[...]
    chunks = up_ref.shape[1] // CHUNK
    for index in range(2 * chunks):
        if index == chunks:
            for copy in copies:
                copy.wait()
        up, down = (up_near_ref, down_near_ref) if index < chunks else (up_ref, down_ref)
        at = slice(index % chunks * CHUNK, (index % chunks + 1) * CHUNK)
        product = feed_chunk(rows, up[:, at], down.at[at], wide_ref.at[index % 2], units_ref.at[index % 2])
        if index == 0:
            total_ref[...] = product
        elif index < 2 * chunks - 1:
            total_ref[...] += product
        else:
            sum_ref[...] = (total_ref[...] + product).astype(sum_ref.dtype)


def feed(place, rows, up_weight, down_weight, pieces, dtype, name):
    count, width = rows.shape
    units = up_weight.shape[1]
    return pl.pallas_call(
        feed_kernel,
        out_shape=jax.ShapeDtypeStruct((count, width), dtype),
        in_specs=[SMEM] + [VMEM] * 3 + [ANY] * 2,
        out_specs=VMEM,
        scratch_shapes=[
            pltpu.VMEM((width, units), BF16),
            pltpu.VMEM((units, width), BF16),
            pltpu.VMEM((2, count, CHUNK), F32),
            pltpu.VMEM((2, count, CHUNK), BF16),
            pltpu.VMEM((count, width), F32),
            pltpu.SemaphoreType.DMA((16,)),
        ],
        compiler_params=pltpu.CompilerParams(vmem_limit_bytes=18 * MIB),
        cost_estimate=SHORT,
        name=name,
    )(place, rows, up_weight, down_weight, *pieces)


def finish_kernel(normed_ref, near_ref, far_ref, gain_ref, bias_ref, out_ref):
    for row in range(0, normed_ref.shape[0], STRIP):
        at = slice(row, row + STRIP)
        mixed = normed_ref[at].astype(F32) + near_ref[at] + far_ref[at].astype(F32)
        out_ref[at] = normalized(mixed, gain_ref[...], bias_ref[...]).astype(out_ref.dtype)


def finish(normed, near, far, gain, bias):
    return pl.pallas_call(
        finish_kernel,
        out_shape=jax.ShapeDtypeStruct(normed.shape, BF16),
        in_specs=[VMEM] * 5,
        out_specs=VMEM,
        compiler_params=pltpu.CompilerParams(vmem_limit_bytes=6 * MIB),
        name="finish",
    )(normed, near, far, gain, bias)


def decode_kernel(slot_ref, filled_ref, query_ref, cache_ref, out_ref, high_ref, total_ref, sum_ref):
    step = pl.program_id(0)

    @pl.when(step == 0)
    def _():
        high_ref[...] = jnp.full(high_ref.shape, NEG_FILL, F32)
        total_ref[...] = jnp.zeros_like(total_ref)
        sum_ref[...] = jnp.zeros_like(sum_ref)

    row = slot_ref[step]
    filled = filled_ref[step]
    width = query_ref.shape[1]
    head = lax.broadcasted_iota(jnp.int32, (H, width), 0)
    inside = head == lax.broadcasted_iota(jnp.int32, (H, width), 1) // HD
    query = jnp.where(inside, query_ref[pl.ds(row, 1), :], 0.0).astype(BF16)
    scores = lax.dot_general(query, cache_ref[0, 0, 0], (((1,), (1,)), ((), ())), preferred_element_type=F32)
    live = lax.broadcasted_iota(jnp.int32, scores.shape, 1) < filled
    scores = jnp.where(live, scores * (1.0 / math.sqrt(HD)), NEG_FILL)
    high = jnp.max(scores, axis=1, keepdims=True)
    weights = jnp.where(live, jnp.exp(scores - high), 0.0)
    total = jnp.sum(weights, axis=1, keepdims=True)
    summed = jnp.dot(weights.astype(BF16), cache_ref[1, 0, 0], preferred_element_type=F32)
    along = lambda column: jnp.sum(jnp.where(inside, column, 0.0), axis=0, keepdims=True)
    high, total, summed = along(high), along(total), along(summed)
    used = filled > 0
    at = pl.ds(row, 1)
    old = high_ref[at, :]
    new = jnp.where(used, jnp.maximum(old, high), old)
    left = jnp.exp(old - new)
    right = jnp.where(used, jnp.exp(high - new), 0.0)
    high_ref[at, :] = new
    total_ref[at, :] = total_ref[at, :] * left + total * right
    sum_ref[at, :] = sum_ref[at, :] * left + summed * right

    @pl.when(step == pl.num_programs(0) - 1)
    def _():
        out_ref[0] = high_ref[...]
        out_ref[1] = total_ref[...]
        out_ref[2] = sum_ref[...]


def decode(slots, filled, queries, kv_cache):
    requests, width = queries.shape
    pieces = kv_cache.shape[2]
    state = pltpu.VMEM((requests, width), F32)
    return pl.pallas_call(
        decode_kernel,
        grid=(pieces,),
        out_shape=jax.ShapeDtypeStruct((3, requests, width), F32),
        in_specs=[
            SMEM,
            SMEM,
            pl.BlockSpec((requests, width), lambda i: (0, 0)),
            pl.BlockSpec((2, 1, 1, PLEN, width), lambda i: (0, 0, i, 0, 0)),
        ],
        out_specs=pl.BlockSpec((3, requests, width), lambda i: (0, 0, 0)),
        scratch_shapes=[state, state, state],
        compiler_params=pltpu.CompilerParams(vmem_limit_bytes=8 * MIB),
        cost_estimate=SHORT,
        name="decode",
    )(slots, filled, queries, kv_cache)


def decode_partial(queries, own, kv_cache, piece_req, piece_used):
    owners = piece_req[0]
    slots = ((owners // own) ^ lax.axis_index("kv")) * own + owners % own
    return decode(slots, piece_used[0], queries, kv_cache)


def exchanged_partials(partial, own):
    parts = [partial[:, :own]]
    for flip in range(1, lax.axis_size("kv")):
        parts.append(swapped(partial[:, flip * own : (flip + 1) * own], "kv", flip))
    return parts


def merged_partials(parts):
    high = functools.reduce(jnp.maximum, [part[0] for part in parts])
    factors = [jnp.exp(part[0] - high) for part in parts]
    total = sum(part[1] * factor for part, factor in zip(parts, factors))
    summed = sum(part[2] * factor for part, factor in zip(parts, factors))
    return (summed / total).astype(BF16)


def routed_body(
    hidden_in,
    qkv_weight,
    stretch_len,
    out_weight,
    ln1_gain,
    ln1_bias,
    up_weight,
    down_weight,
    ln2_gain,
    ln2_bias,
    dec_query,
    kv_cache,
    piece_req,
    piece_used,
):
    tok = lax.axis_index("tok")
    kv = lax.axis_index("kv")
    toks, kvs = lax.axis_size("tok"), lax.axis_size("kv")
    rows, width = hidden_in.shape
    place = jnp.stack([tok, kv]).astype(jnp.int32)
    eighth = lambda value: lax.dynamic_slice_in_dim(value, tok * (value.shape[0] // toks), value.shape[0] // toks, 0)

    outward = [(1, 0), (2, 3)]
    a1, b1 = over_edges(hidden_in, "kv", 0), over_edges(hidden_in, "kv", 1)
    out_part = eighth(out_weight)
    depth = out_part.shape[0]
    small = jnp.concatenate([out_part, dec_query], axis=0)
    others = [swapped(small, "kv", flip) for flip in range(1, kvs)]
    a2, b2 = lax.ppermute(b1, "kv", outward), over_edges(a1, "kv", 1)
    queries = jnp.concatenate([dec_query] + [other[depth:] for other in others], axis=0).astype(F32)
    partial = decode_partial(queries, dec_query.shape[0], kv_cache, piece_req, piece_used)
    out_here = jnp.stack([other[:depth] for other in others])
    out_x, out_y = swapped(out_here, "tok", 2), swapped(out_here, "tok", 4)
    a3 = lax.ppermute(after(b2, partial), "kv", outward)
    out_far = swapped(out_here, "tok", 6)
    inner = (kv == 1) | (kv == 2)

    order = jnp.arange(stretch_len.shape[0])
    ends = jnp.sum(jnp.where(order[:, None] <= order[None, :], stretch_len[:, None], 0), axis=0, dtype=jnp.int32)
    starts = (ends - stretch_len)[None, :]
    ends = ends[None, :]

    weight = jnp.transpose(qkv_weight, (1, 0, 2))
    query, keyval = project_early(place, weight, kvs, (hidden_in, a1, a2, b1, b2))
    block = (place, starts, ends, query, keyval)
    one = attend_block(*block, (1, 0), "attend_early")

    feed_part = jnp.concatenate([eighth(up_weight), eighth(down_weight)], axis=0)
    feed_inner = lax.ppermute(after(feed_part, query), "kv", [(0, 2), (3, 1)])
    feed_outer = lax.ppermute(after(feed_part, a3, one, feed_inner), "kv", [(1, 3), (2, 0)])

    *last, even, odd = project_last(place, weight, keyval, after(a3, out_x, out_y, out_far))
    halo = over_edges(even, "tok", 0), over_edges(odd, "tok", 1)
    two = attend_block(*block, (2, 3), "attend_last", last)
    out_all = jnp.stack([out_here, out_x, out_y, out_far])
    out_core = swapped(out_all, "tok", 1)
    far = attend_block(*block, (3, 2), "attend_far", last, halo, (two,))
    far_heads = swapped(far, "kv", 2)
    block = (place, starts, ends, after(query, far, out_core), keyval)
    near = attend_block(*block, (0, 1), "attend_near", last, halo, (one,))
    feed_here = jnp.where(inner, feed_inner, after(feed_outer, near))
    feed_x, feed_y = swapped(feed_here, "tok", 2), swapped(feed_here, "tok", 4)
    partner_heads, passed_heads = swapped(near, "kv", 1), swapped(far_heads, "kv", 1)
    parts = (near, partner_heads, far_heads, passed_heads)

    out_pieces = [((0, 2, 4, 6), out_all), ((1, 3, 5, 7), out_core)]
    half = feed_here.shape[0] // 2
    far_up = swapped(after(feed_y, far_heads, partner_heads)[:half], "tok", 2)
    far_down = swapped(after(feed_x, far_heads, partner_heads)[half:], "tok", 4)
    held = jnp.concatenate([feed_here, feed_x, feed_y, far_up, far_down], axis=0)
    feed_pieces = (held, swapped(after(held, passed_heads), "tok", 1))

    gain, bias = ln1_gain[None, :], ln1_bias[None, :]
    normed, partner = first_norm(place, hidden_in, a1, out_weight, gain, bias, parts, out_pieces)
    away = feed(place, partner, up_weight, down_weight, feed_pieces, BF16, "feed_partner")
    arrived = swapped(away, "kv", 1)
    dec_parts = exchanged_partials(after(partial, away), dec_query.shape[0])
    mine = feed(place, after(normed, away), up_weight, down_weight, feed_pieces, F32, "feed_own")
    prefill_out = finish(normed, mine, arrived, ln2_gain[None, :], ln2_bias[None, :])

    return prefill_out, merged_partials(after(tuple(dec_parts), mine))


def extended(value, sides, width):
    for axis, dim in sides:
        count, length = (lax.axis_size(axis), value.shape[dim])
        up = [(i, (i + 1) % count) for i in range(count - 1)]
        down = [(j, i) for i, j in up]
        last = lax.slice_in_dim(value, length - width, length, axis=dim)
        leading = lax.slice_in_dim(value, 0, width, axis=dim)
        before = lax.ppermute(last, axis, up)
        after = lax.ppermute(leading, axis, down)
        value = jnp.concatenate([before, value, after], axis=dim)
    return value


def merged(value, axis, join):
    pieces = jax.tree.map(lambda part: lax.all_gather(part, axis), value)
    head = jax.tree.map(lambda part: part[0], pieces)
    tail = jax.tree.map(lambda part: part[1:], pieces)
    subtotal, _ = lax.scan(lambda subtotal, section: (join(subtotal, section), None), head, tail)
    return subtotal


def segment_ids(row_ids, stretch_len):
    stretch_ends = jnp.cumsum(stretch_len)
    return jnp.sum((row_ids[:, None] >= stretch_ends[None, :]).astype(jnp.int32), axis=1)


def layer_norm(values, gain, bias):
    center = values - jnp.mean(values, axis=1, keepdims=True)
    spread = jnp.mean(center * center, axis=1, keepdims=True)
    return center * lax.rsqrt(spread + LN_EPS) * gain + bias


def merge_partials(earlier, later):
    highest = jnp.maximum(earlier[0], later[0])
    left_factor = jnp.exp(earlier[0] - highest)
    right_factor = jnp.exp(later[0] - highest)
    totals = earlier[1] * left_factor + later[1] * right_factor
    weighted = earlier[2] * left_factor[..., None] + later[2] * right_factor[..., None]
    return (highest, totals, weighted)


def row_folder(source, shard_rows):
    return jnp.dot(source, shard_rows, preferred_element_type=jnp.float32)


def general_body(
    hidden_in,
    qkv_weight,
    stretch_len,
    out_weight,
    ln1_gain,
    ln1_bias,
    up_weight,
    down_weight,
    ln2_gain,
    ln2_bias,
    dec_query,
    kv_cache,
    piece_req,
    piece_used,
):
    inv_scale = 1.0 / math.sqrt(HD)
    reach = WIN // 2
    local_width = qkv_weight.shape[2]
    head_count = local_width // HD
    flat_weight = qkv_weight.reshape(qkv_weight.shape[0], 3 * local_width)
    qkv_rows = jnp.dot(
        lax.all_gather(hidden_in, "kv", axis=0, tiled=True),
        flat_weight,
        preferred_element_type=jnp.float32,
    ).astype(jnp.bfloat16)
    row_count = qkv_rows.shape[0]
    query_rows = qkv_rows[:, :local_width]
    keyval_rows = qkv_rows[:, local_width:]
    padded = extended(keyval_rows, (("tok", 0),), reach)
    first_row = lax.axis_index("tok") * row_count
    total_rows = row_count * lax.axis_size("tok")
    qblock = min(512, row_count)
    span = qblock + 2 * reach
    block_count = row_count // qblock

    def attend(block_index):
        start = block_index * qblock
        query_ids = first_row + start + jnp.arange(qblock, dtype=jnp.int32)
        key_ids = first_row + start - reach + jnp.arange(span, dtype=jnp.int32)
        query_seg = segment_ids(query_ids, stretch_len)
        inside = (key_ids >= 0) & (key_ids < total_rows)
        key_seg = jnp.where(inside, segment_ids(key_ids, stretch_len), -1)
        allowed = (key_seg[None, :] == query_seg[:, None]) & (
            jnp.abs(key_ids[None, :] - query_ids[:, None]) <= reach
        )
        queries = lax.dynamic_slice_in_dim(query_rows, start, qblock, 0).reshape(
            qblock, head_count, HD
        )
        both = lax.dynamic_slice_in_dim(padded, start, span, 0)
        key_rows = both[:, :local_width].reshape(span, head_count, HD)
        value_rows = both[:, local_width:].reshape(span, head_count, HD)
        scores = (
            jnp.einsum("ihd,jhd->hij", queries, key_rows, preferred_element_type=jnp.float32)
            * inv_scale
        )
        scores = jnp.where(allowed[None], scores, NEG_FILL)
        row_max = jnp.max(scores, axis=2, keepdims=True)
        weights = jnp.where(allowed[None], jnp.exp(scores - row_max), 0.0)
        totals = jnp.sum(weights, axis=2)
        summed = jnp.einsum(
            "hij,jhd->ihd",
            weights.astype(jnp.bfloat16),
            value_rows,
            preferred_element_type=jnp.float32,
        )
        return (
            (summed / jnp.transpose(totals)[:, :, None])
            .astype(jnp.bfloat16)
            .reshape(qblock, local_width)
        )

    attention = lax.map(attend, jnp.arange(block_count, dtype=jnp.int32)).reshape(
        row_count, local_width
    )
    token_major = lax.all_to_all(attention, "kv", split_axis=0, concat_axis=1, tiled=True)
    projected = row_folder(token_major, lax.all_gather(out_weight, "kv", axis=0, tiled=True))
    normed = layer_norm(hidden_in.astype(jnp.float32) + projected, ln1_gain, ln1_bias).astype(
        jnp.bfloat16
    )
    units = jax.nn.gelu(
        jnp.dot(
            lax.all_gather(normed, "kv", axis=0, tiled=True),
            up_weight,
            preferred_element_type=jnp.float32,
        ),
        approximate=False,
    ).astype(jnp.bfloat16)
    ffn = lax.psum_scatter(
        jnp.dot(units, down_weight, preferred_element_type=jnp.float32).astype(jnp.bfloat16),
        "kv",
        scatter_dimension=0,
        tiled=True,
    ).astype(jnp.float32)
    prefill_out = layer_norm(normed.astype(jnp.float32) + ffn, ln2_gain, ln2_bias).astype(
        jnp.bfloat16
    )
    group_queries = lax.all_gather(dec_query, "kv", axis=0, tiled=True)
    request_count = group_queries.shape[0]
    owners = piece_req[0]
    filled = piece_used[0]
    slot_count = owners.shape[0]
    request_ids = jnp.arange(request_count, dtype=jnp.int32)
    selector = (owners[:, None] == request_ids[None, :]).astype(jnp.bfloat16)
    chosen = jnp.dot(selector, group_queries, preferred_element_type=jnp.float32).astype(
        jnp.bfloat16
    )
    chosen = chosen.reshape(slot_count, H, HD)
    cache_keys = kv_cache[0, 0].reshape(slot_count, PLEN, H, HD)
    cache_values = kv_cache[1, 0].reshape(slot_count, PLEN, H, HD)
    piece_scores = (
        jnp.einsum("phd,pthd->pht", chosen, cache_keys, preferred_element_type=jnp.float32)
        * inv_scale
    )
    active = jnp.arange(PLEN, dtype=jnp.int32)[None, :] < filled[:, None]
    piece_scores = jnp.where(active[:, None, :], piece_scores, NEG_FILL)
    piece_max = jnp.max(piece_scores, axis=2)
    piece_weights = jnp.where(
        active[:, None, :], jnp.exp(piece_scores - piece_max[:, :, None]), 0.0
    )
    piece_totals = jnp.sum(piece_weights, axis=2)
    partial_value = jnp.einsum(
        "pht,pthd->phd",
        piece_weights.astype(jnp.bfloat16),
        cache_values,
        preferred_element_type=jnp.float32,
    )
    member = (owners[None, :] == request_ids[:, None]) & (filled[None, :] > 0)
    highest = jnp.max(jnp.where(member[:, :, None], piece_max[None], NEG_FILL), axis=1)
    factor = jnp.where(member[:, :, None], jnp.exp(piece_max[None] - highest[:, None, :]), 0.0)
    denom = jnp.sum(factor * piece_totals[None], axis=1)
    weighted = jnp.einsum("rph,phd->rhd", factor, partial_value)
    own_requests = dec_query.shape[0]
    joined = merged((highest, denom, weighted), "kv", merge_partials)
    begin = lax.axis_index("kv") * own_requests
    final_denom = lax.dynamic_slice_in_dim(joined[1], begin, own_requests, 0)
    final_weighted = lax.dynamic_slice_in_dim(joined[2], begin, own_requests, 0)
    dec_out = (
        (final_weighted / final_denom[:, :, None])
        .astype(jnp.bfloat16)
        .reshape(own_requests, H * HD)
    )
    return (prefill_out, dec_out)


def solution(mesh):
    placed = (
        P(("tok", "kv"), None),
        P(None, None, "kv"),
        P(),
        P("kv", None),
        P(),
        P(),
        P(None, "kv"),
        P("kv", None),
        P(),
        P(),
        P(("tok", "kv"), None),
        P(None, "tok", "kv", None, None),
        P("tok", "kv"),
        P("tok", "kv"),
    )
    routed = mesh.shape["tok"] == 8 and mesh.shape["kv"] == 4
    return jax.shard_map(
        routed_body if routed else general_body,
        mesh=mesh,
        in_specs=placed,
        out_specs=(P(("tok", "kv"), None), P(("tok", "kv"), None)),
        check_vma=False,
    )
```

```python
import functools
import math

import jax
import jax.numpy as jnp
from jax import lax
from jax.experimental import pallas as pl
from jax.experimental.pallas import tpu as pltpu
from jax.sharding import PartitionSpec as P

H = 16
HD = 64
WIN = 512
PLEN = 128


NEG_FILL = -1e30
LN_EPS = 1e-05
BF16 = jnp.bfloat16
F32 = jnp.float32
STRIP = 32
MIB = 1024 * 1024
ANY = pl.BlockSpec(memory_space=pl.ANY)
VMEM = pl.BlockSpec(memory_space=pltpu.VMEM)
SMEM = pl.BlockSpec(memory_space=pltpu.SMEM)
SHORT = pl.CostEstimate(flops=1, bytes_accessed=1, transcendentals=0)


def swapped(value, axis, flip):
    count = lax.axis_size(axis)
    return lax.ppermute(value, axis, [(i, i ^ flip) for i in range(count)])


def over_edges(value, axis, first):
    count = lax.axis_size(axis)
    edges = [(i, i + 1) for i in range(first, count - 1, 2)]
    return lax.ppermute(value, axis, edges + [(j, i) for i, j in edges])


def after(value, *earlier):
    return lax.optimization_barrier((value,) + earlier)[0]


def normalized(values, gain, bias):
    center = values - jnp.mean(values, axis=1, keepdims=True)
    spread = jnp.mean(center * center, axis=1, keepdims=True)
    return center * lax.rsqrt(spread + LN_EPS) * gain + bias


def project_early_kernel(place_ref, weight_ref, own, a1, a2, b1, b2, query_ref, keyval_ref, rows_ref, sems):
    kv = place_ref[1]
    count = own.shape[0]
    inner = (kv == 1) | (kv == 2)
    outer = jnp.logical_not(inner)
    copies = []
    for source, flip, needed in ((own, 0, None), (a1, 1, None), (a2, 2, outer), (b2, 2, inner), (b1, 3, inner)):
        at = pl.ds(pl.multiple_of((kv ^ flip) * count, count), count)
        copies.append((needed, pltpu.make_async_copy(source, rows_ref.at[at], sems.at[len(copies)])))
    for needed, copy in copies:
        copy.start() if needed is None else pl.when(needed)(copy.start)
    for needed, copy in copies:
        copy.wait() if needed is None else pl.when(needed)(copy.wait)
    project_rows(rows_ref[...], weight_ref, query_ref, keyval_ref)


def project_rows(rows, weight_ref, query_ref, keyval_ref):
    width = weight_ref.shape[2]
    query = jnp.dot(rows, weight_ref[0], preferred_element_type=F32) * (1.0 / math.sqrt(HD))
    query_ref[...] = query.astype(BF16)
    for part in range(2):
        at = slice(part * width, (part + 1) * width)
        keyval_ref[:, at] = jnp.dot(rows, weight_ref[part + 1], preferred_element_type=F32).astype(BF16)


def project_last_kernel(place_ref, weight_ref, keyval_ref, a3_ref, query_ref, last_ref, even_ref, odd_ref):
    tok, kv = place_ref[0], place_ref[1]
    count = a3_ref.shape[0]
    project_rows(a3_ref[...], weight_ref, query_ref, last_ref)
    last = last_ref[...]
    blocks = keyval_ref.shape[0] // count
    top = jnp.where(kv == blocks - 1, last, keyval_ref[:count])
    bottom = jnp.where(kv == 0, last, keyval_ref[(blocks - 1) * count :])
    even_tok = tok % 2 == 0
    even_ref[...] = jnp.where(even_tok, bottom, top)
    odd_ref[...] = jnp.where(even_tok, top, bottom)


def project_early(place, weight, blocks, shards):
    rows, width = shards[0].shape
    heads_width = weight.shape[2]
    return pl.pallas_call(
        project_early_kernel,
        out_shape=(
            jax.ShapeDtypeStruct((blocks * rows, heads_width), BF16),
            jax.ShapeDtypeStruct((blocks * rows, 2 * heads_width), BF16),
        ),
        in_specs=[SMEM, VMEM] + [ANY] * len(shards),
        out_specs=(VMEM,) * 2,
        scratch_shapes=[pltpu.VMEM((blocks * rows, width), BF16), pltpu.SemaphoreType.DMA((len(shards),))],
        compiler_params=pltpu.CompilerParams(vmem_limit_bytes=12 * MIB),
        cost_estimate=SHORT,
        name="project_early",
    )(place, weight, *shards)


def project_last(place, weight, keyval, a3):
    rows = a3.shape[0]
    heads_width = weight.shape[2]
    keyvals = jax.ShapeDtypeStruct((rows, 2 * heads_width), BF16)
    return pl.pallas_call(
        project_last_kernel,
        out_shape=(jax.ShapeDtypeStruct((rows, heads_width), BF16), keyvals, keyvals, keyvals),
        in_specs=[SMEM] + [VMEM] * 3,
        out_specs=(VMEM,) * 4,
        compiler_params=pltpu.CompilerParams(vmem_limit_bytes=8 * MIB),
        cost_estimate=SHORT,
        name="project_last",
    )(place, weight, keyval, a3)


def window_bias(first, count, starts, ends):
    reach = WIN // 2
    query = first + lax.broadcasted_iota(jnp.int32, (count, 1), 0)
    low = jnp.max(jnp.where(starts <= query, starts, 0), axis=1, keepdims=True)
    high = jnp.min(jnp.where(ends > query, ends, 1 << 30), axis=1, keepdims=True)
    low = jnp.maximum(low, query - reach)
    high = jnp.minimum(high, query + reach + 1)
    key = first - count + lax.broadcasted_iota(jnp.int32, (count, 3 * count), 1)
    return jnp.where((key >= low) & (key < high), 0.0, NEG_FILL)


def attend(query, keyval_ref, bias_ref, scores_ref, weights_ref, out_ref):
    count, width = query.shape
    lane = lax.broadcasted_iota(jnp.int32, (count, 2 * HD), 1)
    for start in range(0, width, 2 * HD):
        values = keyval_ref[:, width + start : width + start + 2 * HD]
        halves = []
        for side in range(2):
            head = start // HD + side
            inside = (lane < HD) if side == 0 else (lane >= HD)
            only = jnp.where(inside, query[:, start : start + 2 * HD], jnp.zeros((), BF16))
            scores_ref[head] = lax.dot_general(
                only, keyval_ref[:, start : start + 2 * HD], (((1,), (1,)), ((), ())), preferred_element_type=F32
            )
            totals = []
            for row in range(0, count, STRIP):
                at = slice(row, row + STRIP)
                scores = scores_ref[head, at] + bias_ref[at]
                weights = jnp.exp(scores - jnp.max(scores, axis=1, keepdims=True))
                totals.append(jnp.sum(weights, axis=1, keepdims=True))
                weights_ref[head, at] = weights.astype(BF16)
            summed = jnp.dot(weights_ref[head], values, preferred_element_type=F32)
            halves.append(summed / jnp.concatenate(totals, axis=0))
        out_ref[:, start : start + 2 * HD] = jnp.where(lane < HD, halves[0], halves[1]).astype(BF16)


def attend_kernel(flips, has_last, has_halo, joins, place_ref, starts_ref, ends_ref, query_ref, keyval_ref, *refs):
    refs = list(refs)
    last_query_ref, last_ref = (refs.pop(0), refs.pop(0)) if has_last else (None, None)
    even_ref, odd_ref = (refs.pop(0), refs.pop(0)) if has_halo else (None, None)
    earlier_ref = refs.pop(0) if joins else None
    out_ref, window_ref, bias_ref, scores_ref, weights_ref, sems = refs
    tok, kv = place_ref[0], place_ref[1]
    count = bias_ref.shape[0]
    blocks = query_ref.shape[0] // count
    inner = (kv == 1) | (kv == 2)
    block = kv ^ jnp.where(inner, flips[1], flips[0])
    missing = jnp.where(inner, -1, kv ^ 3)
    copies = []
    for part in range(3):
        target = window_ref.at[part * count : (part + 1) * count]
        sem = sems.at[part]
        at = block + part - 1
        held = (at >= 0) & (at < blocks) & (at != missing)
        source = keyval_ref.at[pl.ds(pl.multiple_of(jnp.where(held, at, 0) * count, count), count)]
        copies.append((held, pltpu.make_async_copy(source, target, sem)))
        if has_last:
            copies.append((at == missing, pltpu.make_async_copy(last_ref, target, sem)))
        if has_halo and part != 1:
            outside = at < 0 if part == 0 else at >= blocks
            over_even = tok % 2 == (1 if part == 0 else 0)
            copies.append((outside & over_even, pltpu.make_async_copy(even_ref, target, sem)))
            copies.append((outside & jnp.logical_not(over_even), pltpu.make_async_copy(odd_ref, target, sem)))
    for needed, copy in copies:
        pl.when(needed)(copy.start)
    first = (tok * blocks + block) * count
    bias_ref[...] = window_bias(first, count, starts_ref[...], ends_ref[...])
    query = query_ref[pl.ds(pl.multiple_of(block * count, count), count)]
    if has_last:
        query = jnp.where(block == missing, last_query_ref[...], query)
    for needed, copy in copies:
        pl.when(needed)(copy.wait)
    if joins:
        if out_ref.shape[0] > 2 * count:
            out_ref[2 * count :] = jnp.zeros_like(out_ref[2 * count :])
        half = jnp.where(inner, flips[1] % 2, flips[0] % 2)
        out_ref[pl.ds(pl.multiple_of((1 - half) * count, count), count)] = earlier_ref[...]
        out_ref = out_ref.at[pl.ds(pl.multiple_of(half * count, count), count)]
    attend(query, window_ref, bias_ref, scores_ref, weights_ref, out_ref)


def attend_block(place, starts, ends, query, keyval, flips, name, last=(), halo=(), earlier=(), spare=0):
    rows = query.shape[0] // lax.axis_size("kv")
    heads_width = query.shape[1]
    return pl.pallas_call(
        functools.partial(attend_kernel, flips, bool(last), bool(halo), bool(earlier)),
        out_shape=jax.ShapeDtypeStruct(((1 + len(earlier)) * rows + spare, heads_width), BF16),
        in_specs=[SMEM, VMEM, VMEM, VMEM, ANY] + [VMEM, ANY][: len(last)] + [ANY] * len(halo) + [VMEM] * len(earlier),
        out_specs=VMEM,
        scratch_shapes=[
            pltpu.VMEM((3 * rows, 2 * heads_width), BF16),
            pltpu.VMEM((rows, 3 * rows), F32),
            pltpu.VMEM((heads_width // HD, rows, 3 * rows), F32),
            pltpu.VMEM((heads_width // HD, rows, 3 * rows), BF16),
            pltpu.SemaphoreType.DMA((3,)),
        ],
        compiler_params=pltpu.CompilerParams(vmem_limit_bytes=12 * MIB),
        cost_estimate=SHORT,
        name=name,
    )(place, starts, ends, query, keyval, *last, *halo, *earlier)


def first_norm_kernel(layout, place_ref, own_ref, partner_ref, own_out_ref, gain_ref, bias_ref, *refs):
    parts, pieces = refs[:4], refs[4 : 4 + len(layout)]
    normed_ref, away_ref, all_ref, weight_ref, mixed_ref, sems = refs[4 + len(layout) :]
    tok = place_ref[0]
    quarters, heads_width, width = weight_ref.shape
    count = own_ref.shape[0]
    copies = [pltpu.make_async_copy(own_out_ref, weight_ref.at[0], sems.at[0])]
    for flips, piece in zip(layout, pieces):
        for index, flip in enumerate(flips):
            depth = piece.shape[2]
            at = pl.multiple_of((tok ^ flip) * depth, depth)
            target = weight_ref.at[1:quarters, pl.ds(at, depth)]
            copies.append(pltpu.make_async_copy(piece.at[index], target, sems.at[len(copies)]))
    for copy in copies:
        copy.start()
    for flip, part_ref in enumerate(parts):
        columns = slice(flip * heads_width, (flip + 1) * heads_width)
        for half in range(2):
            turned = half ^ (flip % 2)
            all_ref[half * count : (half + 1) * count, columns] = part_ref[turned * count : (turned + 1) * count]
    for copy in copies:
        copy.wait()
    weight = weight_ref[...].reshape(quarters * heads_width, width)
    mixed_ref[...] = jnp.dot(all_ref[...], weight, preferred_element_type=F32)
    for half, (hidden_ref, result_ref) in enumerate(((own_ref, normed_ref), (partner_ref, away_ref))):
        for row in range(0, count, STRIP):
            at = slice(row, row + STRIP)
            mixed = hidden_ref[at].astype(F32) + mixed_ref[half * count + row : half * count + row + STRIP]
            result_ref[at] = normalized(mixed, gain_ref[...], bias_ref[...]).astype(BF16)


def first_norm(place, own, partner, own_out, gain, bias, parts, pieces):
    rows, width = own.shape
    heads_width = own_out.shape[0]
    layout = tuple(flips for flips, _ in pieces)
    return pl.pallas_call(
        functools.partial(first_norm_kernel, layout),
        out_shape=(jax.ShapeDtypeStruct((rows, width), BF16),) * 2,
        in_specs=[SMEM, VMEM, VMEM, ANY, VMEM, VMEM] + [VMEM] * len(parts) + [ANY] * len(pieces),
        out_specs=(VMEM,) * 2,
        scratch_shapes=[
            pltpu.VMEM((2 * rows, width), BF16),
            pltpu.VMEM((len(parts), heads_width, width), BF16),
            pltpu.VMEM((2 * rows, width), F32),
            pltpu.SemaphoreType.DMA((1 + sum(len(flips) for flips in layout),)),
        ],
        compiler_params=pltpu.CompilerParams(vmem_limit_bytes=14 * MIB),
        cost_estimate=SHORT,
        name="first_norm",
    )(place, own, partner, own_out, gain, bias, *parts, *[value for _, value in pieces])


def gelu(values):
    return 0.5 * values * (1.0 + lax.erf(values * math.sqrt(0.5)))


CHUNK = 512


def feed_chunk(rows, up, down_ref, wide_ref, units_ref):
    wide_ref[...] = jnp.dot(rows, up, preferred_element_type=F32)
    for row in range(0, rows.shape[0], STRIP):
        strip = slice(row, row + STRIP)
        units_ref[strip] = gelu(wide_ref[strip]).astype(BF16)
    return jnp.dot(units_ref[...], down_ref[...], preferred_element_type=F32)


def far_copies(tok, held_ref, core_ref, up_ref, down_ref, sems):
    block = 128
    copies = []
    for side, piece in enumerate((held_ref, core_ref)):
        for index in range(4):
            at = pl.ds(pl.multiple_of((tok ^ (2 * index + side)) * block, block), block)
            for part, target in enumerate((up_ref, down_ref)):
                source = piece.at[pl.ds((2 * index + part) * block, block)]
                copies.append(pltpu.make_async_copy(source, target.at[at], sems.at[len(copies)]))
    return copies


def feed_kernel(place_ref, rows_ref, up_near_ref, down_near_ref, held_ref, core_ref, *refs):
    sum_ref, up_ref, down_ref, wide_ref, units_ref, total_ref, sems = refs
    copies = far_copies(place_ref[0], held_ref, core_ref, up_ref, down_ref, sems)
    for copy in copies:
        copy.start()
    rows = rows_ref[...]
    chunks = up_ref.shape[1] // CHUNK
    for index in range(2 * chunks):
        if index == chunks:
            for copy in copies:
                copy.wait()
        up, down = (up_near_ref, down_near_ref) if index < chunks else (up_ref, down_ref)
        at = slice(index % chunks * CHUNK, (index % chunks + 1) * CHUNK)
        product = feed_chunk(rows, up[:, at], down.at[at], wide_ref.at[index % 2], units_ref.at[index % 2])
        if index == 0:
            total_ref[...] = product
        elif index < 2 * chunks - 1:
            total_ref[...] += product
        else:
            sum_ref[...] = (total_ref[...] + product).astype(sum_ref.dtype)


def feed(place, rows, up_weight, down_weight, pieces, dtype, name):
    count, width = rows.shape
    units = up_weight.shape[1]
    return pl.pallas_call(
        feed_kernel,
        out_shape=jax.ShapeDtypeStruct((count, width), dtype),
        in_specs=[SMEM] + [VMEM] * 3 + [ANY] * 2,
        out_specs=VMEM,
        scratch_shapes=[
            pltpu.VMEM((width, units), BF16),
            pltpu.VMEM((units, width), BF16),
            pltpu.VMEM((2, count, CHUNK), F32),
            pltpu.VMEM((2, count, CHUNK), BF16),
            pltpu.VMEM((count, width), F32),
            pltpu.SemaphoreType.DMA((16,)),
        ],
        compiler_params=pltpu.CompilerParams(vmem_limit_bytes=18 * MIB),
        cost_estimate=SHORT,
        name=name,
    )(place, rows, up_weight, down_weight, *pieces)


def finish_kernel(normed_ref, near_ref, far_ref, gain_ref, bias_ref, out_ref):
    for row in range(0, normed_ref.shape[0], STRIP):
        at = slice(row, row + STRIP)
        mixed = normed_ref[at].astype(F32) + near_ref[at] + far_ref[at].astype(F32)
        out_ref[at] = normalized(mixed, gain_ref[...], bias_ref[...]).astype(out_ref.dtype)


def finish(normed, near, far, gain, bias):
    return pl.pallas_call(
        finish_kernel,
        out_shape=jax.ShapeDtypeStruct(normed.shape, BF16),
        in_specs=[VMEM] * 5,
        out_specs=VMEM,
        compiler_params=pltpu.CompilerParams(vmem_limit_bytes=6 * MIB),
        name="finish",
    )(normed, near, far, gain, bias)


def decode_kernel(slot_ref, filled_ref, query_ref, cache_ref, out_ref, high_ref, total_ref, sum_ref):
    step = pl.program_id(0)

    @pl.when(step == 0)
    def _():
        high_ref[...] = jnp.full(high_ref.shape, NEG_FILL, F32)
        total_ref[...] = jnp.zeros_like(total_ref)
        sum_ref[...] = jnp.zeros_like(sum_ref)

    row = slot_ref[step]
    filled = filled_ref[step]
    width = query_ref.shape[1]
    head = lax.broadcasted_iota(jnp.int32, (H, width), 0)
    inside = head == lax.broadcasted_iota(jnp.int32, (H, width), 1) // HD
    query = jnp.where(inside, query_ref[pl.ds(row, 1), :], 0.0).astype(BF16)
    scores = lax.dot_general(query, cache_ref[0, 0, 0], (((1,), (1,)), ((), ())), preferred_element_type=F32)
    live = lax.broadcasted_iota(jnp.int32, scores.shape, 1) < filled
    scores = jnp.where(live, scores * (1.0 / math.sqrt(HD)), NEG_FILL)
    high = jnp.max(scores, axis=1, keepdims=True)
    weights = jnp.where(live, jnp.exp(scores - high), 0.0)
    total = jnp.sum(weights, axis=1, keepdims=True)
    summed = jnp.dot(weights.astype(BF16), cache_ref[1, 0, 0], preferred_element_type=F32)
    along = lambda column: jnp.sum(jnp.where(inside, column, 0.0), axis=0, keepdims=True)
    high, total, summed = along(high), along(total), along(summed)
    used = filled > 0
    at = pl.ds(row, 1)
    old = high_ref[at, :]
    new = jnp.where(used, jnp.maximum(old, high), old)
    left = jnp.exp(old - new)
    right = jnp.where(used, jnp.exp(high - new), 0.0)
    high_ref[at, :] = new
    total_ref[at, :] = total_ref[at, :] * left + total * right
    sum_ref[at, :] = sum_ref[at, :] * left + summed * right

    @pl.when(step == pl.num_programs(0) - 1)
    def _():
        out_ref[0] = high_ref[...]
        out_ref[1] = total_ref[...]
        out_ref[2] = sum_ref[...]


def decode(slots, filled, queries, kv_cache):
    requests, width = queries.shape
    pieces = kv_cache.shape[2]
    state = pltpu.VMEM((requests, width), F32)
    return pl.pallas_call(
        decode_kernel,
        grid=(pieces,),
        out_shape=jax.ShapeDtypeStruct((3, requests, width), F32),
        in_specs=[
            SMEM,
            SMEM,
            pl.BlockSpec((requests, width), lambda i: (0, 0)),
            pl.BlockSpec((2, 1, 1, PLEN, width), lambda i: (0, 0, i, 0, 0)),
        ],
        out_specs=pl.BlockSpec((3, requests, width), lambda i: (0, 0, 0)),
        scratch_shapes=[state, state, state],
        compiler_params=pltpu.CompilerParams(vmem_limit_bytes=8 * MIB),
        cost_estimate=SHORT,
        name="decode",
    )(slots, filled, queries, kv_cache)


def decode_partial(queries, own, kv_cache, piece_req, piece_used):
    owners = piece_req[0]
    slots = ((owners // own) ^ lax.axis_index("kv")) * own + owners % own
    return decode(slots, piece_used[0], queries, kv_cache)


def exchanged_partials(partial, own):
    parts = [partial[:, :own]]
    for flip in range(1, lax.axis_size("kv")):
        parts.append(swapped(partial[:, flip * own : (flip + 1) * own], "kv", flip))
    return parts


def merged_partials(parts):
    high = functools.reduce(jnp.maximum, [part[0] for part in parts])
    factors = [jnp.exp(part[0] - high) for part in parts]
    total = sum(part[1] * factor for part, factor in zip(parts, factors))
    summed = sum(part[2] * factor for part, factor in zip(parts, factors))
    return (summed / total).astype(BF16)


def routed_body(
    hidden_in,
    qkv_weight,
    stretch_len,
    out_weight,
    ln1_gain,
    ln1_bias,
    up_weight,
    down_weight,
    ln2_gain,
    ln2_bias,
    dec_query,
    kv_cache,
    piece_req,
    piece_used,
):
    tok = lax.axis_index("tok")
    kv = lax.axis_index("kv")
    toks, kvs = lax.axis_size("tok"), lax.axis_size("kv")
    rows, width = hidden_in.shape
    place = jnp.stack([tok, kv]).astype(jnp.int32)
    eighth = lambda value: lax.dynamic_slice_in_dim(value, tok * (value.shape[0] // toks), value.shape[0] // toks, 0)

    outward = [(1, 0), (2, 3)]
    a1, b1 = over_edges(hidden_in, "kv", 0), over_edges(hidden_in, "kv", 1)
    out_part = eighth(out_weight)
    depth = out_part.shape[0]
    small = jnp.concatenate([out_part, dec_query], axis=0)
    others = [swapped(small, "kv", flip) for flip in range(1, kvs)]
    a2, b2 = lax.ppermute(b1, "kv", outward), over_edges(a1, "kv", 1)
    out_here = after(jnp.stack([other[:depth] for other in others]), b2)
    out_x, out_y = swapped(out_here, "tok", 2), swapped(out_here, "tok", 4)
    a3 = lax.ppermute(b2, "kv", outward)
    out_far = swapped(out_y, "tok", 2)
    inner = (kv == 1) | (kv == 2)

    order = jnp.arange(stretch_len.shape[0])
    ends = jnp.sum(jnp.where(order[:, None] <= order[None, :], stretch_len[:, None], 0), axis=0, dtype=jnp.int32)
    starts = (ends - stretch_len)[None, :]
    ends = ends[None, :]

    weight = jnp.transpose(qkv_weight, (1, 0, 2))
    query, keyval = project_early(place, weight, kvs, (hidden_in, a1, a2, b1, b2))
    block = (place, starts, ends, query, keyval)
    one = attend_block(*block, (1, 0), "attend_early")

    feed_up, feed_down = after((eighth(up_weight), eighth(down_weight)), a2, b2)
    inner_up = lax.ppermute(feed_up, "kv", [(0, 2), (3, 1)])
    inner_down = lax.ppermute(feed_down, "kv", [(0, 2), (3, 1)])
    feed_part = jnp.concatenate([feed_up, feed_down], axis=0)
    feed_part = after(feed_part, a3, one, out_x, out_y, inner_up, inner_down)
    feed_outer = lax.ppermute(feed_part, "kv", [(1, 3), (2, 0)])
    feed_inner = jnp.concatenate([inner_up, inner_down], axis=0)

    *last, even, odd = project_last(place, weight, keyval, a3)
    halo = over_edges(even, "tok", 0), over_edges(odd, "tok", 1)
    two = attend_block(*block, (2, 3), "attend_last", last)
    out_all = jnp.stack([out_here, out_x, out_y, out_far])
    out_core = swapped(out_all, "tok", 1)
    feed_here = jnp.where(inner, feed_inner, after(feed_outer, two))
    feed_x, feed_y = swapped(feed_here, "tok", 2), swapped(feed_here, "tok", 4)
    block = (place, starts, ends, after(query, feed_here, out_core), keyval)
    far = attend_block(*block, (3, 2), "attend_far", last, halo, (two,), 16)
    far_heads = swapped(far, "kv", 2)
    block = (place, starts, ends, after(query, far), keyval)
    near = attend_block(*block, (0, 1), "attend_near", last, halo, (one,))
    partner_heads, passed_heads = swapped(near, "kv", 1), swapped(far_heads, "kv", 1)
    parts = (near, partner_heads, far_heads, passed_heads)

    out_pieces = [((0, 2, 4, 6), out_all), ((1, 3, 5, 7), out_core)]
    queries = jnp.concatenate([dec_query] + [other[depth:] for other in others], axis=0)
    queries = after(queries, near).astype(F32)
    partial = decode_partial(queries, dec_query.shape[0], kv_cache, piece_req, piece_used)
    half = feed_here.shape[0] // 2
    far_up = swapped(after(feed_y, far_heads, partner_heads, partial)[:half], "tok", 2)
    far_down = swapped(after(feed_x, far_heads, partner_heads, partial)[half:], "tok", 4)
    held = jnp.concatenate([feed_here, feed_x, feed_y, far_up, far_down], axis=0)
    feed_pieces = (held, swapped(after(held, passed_heads), "tok", 1))

    gain, bias = ln1_gain[None, :], ln1_bias[None, :]
    normed, partner = first_norm(place, hidden_in, a1, out_weight, gain, bias, parts, out_pieces)
    away = feed(place, partner, up_weight, down_weight, feed_pieces, BF16, "feed_partner")
    arrived = swapped(away, "kv", 1)
    dec_parts = exchanged_partials(after(partial, away), dec_query.shape[0])
    mine = feed(place, after(normed, away), up_weight, down_weight, feed_pieces, F32, "feed_own")
    prefill_out = finish(normed, mine, arrived, ln2_gain[None, :], ln2_bias[None, :])

    return prefill_out, merged_partials(after(tuple(dec_parts), mine))


def extended(value, sides, width):
    for axis, dim in sides:
        count, length = (lax.axis_size(axis), value.shape[dim])
        up = [(i, (i + 1) % count) for i in range(count - 1)]
        down = [(j, i) for i, j in up]
        last = lax.slice_in_dim(value, length - width, length, axis=dim)
        leading = lax.slice_in_dim(value, 0, width, axis=dim)
        before = lax.ppermute(last, axis, up)
        after = lax.ppermute(leading, axis, down)
        value = jnp.concatenate([before, value, after], axis=dim)
    return value


def merged(value, axis, join):
    pieces = jax.tree.map(lambda part: lax.all_gather(part, axis), value)
    head = jax.tree.map(lambda part: part[0], pieces)
    tail = jax.tree.map(lambda part: part[1:], pieces)
    subtotal, _ = lax.scan(lambda subtotal, section: (join(subtotal, section), None), head, tail)
    return subtotal


def segment_ids(row_ids, stretch_len):
    stretch_ends = jnp.cumsum(stretch_len)
    return jnp.sum((row_ids[:, None] >= stretch_ends[None, :]).astype(jnp.int32), axis=1)


def layer_norm(values, gain, bias):
    center = values - jnp.mean(values, axis=1, keepdims=True)
    spread = jnp.mean(center * center, axis=1, keepdims=True)
    return center * lax.rsqrt(spread + LN_EPS) * gain + bias


def merge_partials(earlier, later):
    highest = jnp.maximum(earlier[0], later[0])
    left_factor = jnp.exp(earlier[0] - highest)
    right_factor = jnp.exp(later[0] - highest)
    totals = earlier[1] * left_factor + later[1] * right_factor
    weighted = earlier[2] * left_factor[..., None] + later[2] * right_factor[..., None]
    return (highest, totals, weighted)


def row_folder(source, shard_rows):
    return jnp.dot(source, shard_rows, preferred_element_type=jnp.float32)


def general_body(
    hidden_in,
    qkv_weight,
    stretch_len,
    out_weight,
    ln1_gain,
    ln1_bias,
    up_weight,
    down_weight,
    ln2_gain,
    ln2_bias,
    dec_query,
    kv_cache,
    piece_req,
    piece_used,
):
    inv_scale = 1.0 / math.sqrt(HD)
    reach = WIN // 2
    local_width = qkv_weight.shape[2]
    head_count = local_width // HD
    flat_weight = qkv_weight.reshape(qkv_weight.shape[0], 3 * local_width)
    qkv_rows = jnp.dot(
        lax.all_gather(hidden_in, "kv", axis=0, tiled=True),
        flat_weight,
        preferred_element_type=jnp.float32,
    ).astype(jnp.bfloat16)
    row_count = qkv_rows.shape[0]
    query_rows = qkv_rows[:, :local_width]
    keyval_rows = qkv_rows[:, local_width:]
    padded = extended(keyval_rows, (("tok", 0),), reach)
    first_row = lax.axis_index("tok") * row_count
    total_rows = row_count * lax.axis_size("tok")
    qblock = min(512, row_count)
    span = qblock + 2 * reach
    block_count = row_count // qblock

    def attend(block_index):
        start = block_index * qblock
        query_ids = first_row + start + jnp.arange(qblock, dtype=jnp.int32)
        key_ids = first_row + start - reach + jnp.arange(span, dtype=jnp.int32)
        query_seg = segment_ids(query_ids, stretch_len)
        inside = (key_ids >= 0) & (key_ids < total_rows)
        key_seg = jnp.where(inside, segment_ids(key_ids, stretch_len), -1)
        allowed = (key_seg[None, :] == query_seg[:, None]) & (
            jnp.abs(key_ids[None, :] - query_ids[:, None]) <= reach
        )
        queries = lax.dynamic_slice_in_dim(query_rows, start, qblock, 0).reshape(
            qblock, head_count, HD
        )
        both = lax.dynamic_slice_in_dim(padded, start, span, 0)
        key_rows = both[:, :local_width].reshape(span, head_count, HD)
        value_rows = both[:, local_width:].reshape(span, head_count, HD)
        scores = (
            jnp.einsum("ihd,jhd->hij", queries, key_rows, preferred_element_type=jnp.float32)
            * inv_scale
        )
        scores = jnp.where(allowed[None], scores, NEG_FILL)
        row_max = jnp.max(scores, axis=2, keepdims=True)
        weights = jnp.where(allowed[None], jnp.exp(scores - row_max), 0.0)
        totals = jnp.sum(weights, axis=2)
        summed = jnp.einsum(
            "hij,jhd->ihd",
            weights.astype(jnp.bfloat16),
            value_rows,
            preferred_element_type=jnp.float32,
        )
        return (
            (summed / jnp.transpose(totals)[:, :, None])
            .astype(jnp.bfloat16)
            .reshape(qblock, local_width)
        )

    attention = lax.map(attend, jnp.arange(block_count, dtype=jnp.int32)).reshape(
        row_count, local_width
    )
    token_major = lax.all_to_all(attention, "kv", split_axis=0, concat_axis=1, tiled=True)
    projected = row_folder(token_major, lax.all_gather(out_weight, "kv", axis=0, tiled=True))
    normed = layer_norm(hidden_in.astype(jnp.float32) + projected, ln1_gain, ln1_bias).astype(
        jnp.bfloat16
    )
    units = jax.nn.gelu(
        jnp.dot(
            lax.all_gather(normed, "kv", axis=0, tiled=True),
            up_weight,
            preferred_element_type=jnp.float32,
        ),
        approximate=False,
    ).astype(jnp.bfloat16)
    ffn = lax.psum_scatter(
        jnp.dot(units, down_weight, preferred_element_type=jnp.float32).astype(jnp.bfloat16),
        "kv",
        scatter_dimension=0,
        tiled=True,
    ).astype(jnp.float32)
    prefill_out = layer_norm(normed.astype(jnp.float32) + ffn, ln2_gain, ln2_bias).astype(
        jnp.bfloat16
    )
    group_queries = lax.all_gather(dec_query, "kv", axis=0, tiled=True)
    request_count = group_queries.shape[0]
    owners = piece_req[0]
    filled = piece_used[0]
    slot_count = owners.shape[0]
    request_ids = jnp.arange(request_count, dtype=jnp.int32)
    selector = (owners[:, None] == request_ids[None, :]).astype(jnp.bfloat16)
    chosen = jnp.dot(selector, group_queries, preferred_element_type=jnp.float32).astype(
        jnp.bfloat16
    )
    chosen = chosen.reshape(slot_count, H, HD)
    cache_keys = kv_cache[0, 0].reshape(slot_count, PLEN, H, HD)
    cache_values = kv_cache[1, 0].reshape(slot_count, PLEN, H, HD)
    piece_scores = (
        jnp.einsum("phd,pthd->pht", chosen, cache_keys, preferred_element_type=jnp.float32)
        * inv_scale
    )
    active = jnp.arange(PLEN, dtype=jnp.int32)[None, :] < filled[:, None]
    piece_scores = jnp.where(active[:, None, :], piece_scores, NEG_FILL)
    piece_max = jnp.max(piece_scores, axis=2)
    piece_weights = jnp.where(
        active[:, None, :], jnp.exp(piece_scores - piece_max[:, :, None]), 0.0
    )
    piece_totals = jnp.sum(piece_weights, axis=2)
    partial_value = jnp.einsum(
        "pht,pthd->phd",
        piece_weights.astype(jnp.bfloat16),
        cache_values,
        preferred_element_type=jnp.float32,
    )
    member = (owners[None, :] == request_ids[:, None]) & (filled[None, :] > 0)
    highest = jnp.max(jnp.where(member[:, :, None], piece_max[None], NEG_FILL), axis=1)
    factor = jnp.where(member[:, :, None], jnp.exp(piece_max[None] - highest[:, None, :]), 0.0)
    denom = jnp.sum(factor * piece_totals[None], axis=1)
    weighted = jnp.einsum("rph,phd->rhd", factor, partial_value)
    own_requests = dec_query.shape[0]
    joined = merged((highest, denom, weighted), "kv", merge_partials)
    begin = lax.axis_index("kv") * own_requests
    final_denom = lax.dynamic_slice_in_dim(joined[1], begin, own_requests, 0)
    final_weighted = lax.dynamic_slice_in_dim(joined[2], begin, own_requests, 0)
    dec_out = (
        (final_weighted / final_denom[:, :, None])
        .astype(jnp.bfloat16)
        .reshape(own_requests, H * HD)
    )
    return (prefill_out, dec_out)


def solution(mesh):
    placed = (
        P(("tok", "kv"), None),
        P(None, None, "kv"),
        P(),
        P("kv", None),
        P(),
        P(),
        P(None, "kv"),
        P("kv", None),
        P(),
        P(),
        P(("tok", "kv"), None),
        P(None, "tok", "kv", None, None),
        P("tok", "kv"),
        P("tok", "kv"),
    )
    routed = mesh.shape["tok"] == 8 and mesh.shape["kv"] == 4
    return jax.shard_map(
        routed_body if routed else general_body,
        mesh=mesh,
        in_specs=placed,
        out_specs=(P(("tok", "kv"), None), P(("tok", "kv"), None)),
        check_vma=False,
    )
```

```python
import functools
import math

import jax
import jax.numpy as jnp
from jax import lax
from jax.experimental import pallas as pl
from jax.experimental.pallas import tpu as pltpu
from jax.sharding import PartitionSpec as P

H = 16
HD = 64
WIN = 512
PLEN = 128


NEG_FILL = -1e30
LN_EPS = 1e-05
BF16 = jnp.bfloat16
F32 = jnp.float32
STRIP = 32
MIB = 1024 * 1024
ANY = pl.BlockSpec(memory_space=pl.ANY)
VMEM = pl.BlockSpec(memory_space=pltpu.VMEM)
SMEM = pl.BlockSpec(memory_space=pltpu.SMEM)
SHORT = pl.CostEstimate(flops=1, bytes_accessed=1, transcendentals=0)


def swapped(value, axis, flip):
    count = lax.axis_size(axis)
    return lax.ppermute(value, axis, [(i, i ^ flip) for i in range(count)])


def over_edges(value, axis, first):
    count = lax.axis_size(axis)
    edges = [(i, i + 1) for i in range(first, count - 1, 2)]
    return lax.ppermute(value, axis, edges + [(j, i) for i, j in edges])


def after(value, *earlier):
    return lax.optimization_barrier((value,) + earlier)[0]


def normalized(values, gain, bias):
    center = values - jnp.mean(values, axis=1, keepdims=True)
    spread = jnp.mean(center * center, axis=1, keepdims=True)
    return center * lax.rsqrt(spread + LN_EPS) * gain + bias


def project_rows(rows, weight_ref, query_ref, keyval_ref):
    width = weight_ref.shape[2]
    query = jnp.dot(rows, weight_ref[0], preferred_element_type=F32) * (1.0 / math.sqrt(HD))
    query_ref[...] = query.astype(BF16)
    for part in range(2):
        at = slice(part * width, (part + 1) * width)
        keyval_ref[:, at] = jnp.dot(rows, weight_ref[part + 1], preferred_element_type=F32).astype(BF16)


def is_inner(kv):
    return (kv == 1) | (kv == 2)


def project_first_kernel(weight_ref, own_ref, a1_ref, b1_ref, query_ref, keyval_ref, rows_ref):
    count = own_ref.shape[0]
    for index, source in enumerate((own_ref, a1_ref, b1_ref)):
        rows_ref[index * count : (index + 1) * count] = source[...]
    project_rows(rows_ref[...], weight_ref, query_ref, keyval_ref)


def project_second_kernel(place_ref, weight_ref, a2_ref, b2_ref, query_ref, keyval_ref):
    rows = jnp.where(is_inner(place_ref[1]), b2_ref[...], a2_ref[...])
    project_rows(rows, weight_ref, query_ref, keyval_ref)


def project_last_kernel(place_ref, weight_ref, first_ref, second_ref, a3_ref, query_ref, last_ref, even_ref, odd_ref):
    tok, kv = place_ref[0], place_ref[1]
    count = a3_ref.shape[0]
    project_rows(a3_ref[...], weight_ref, query_ref, last_ref)
    inner = is_inner(kv)
    close = jnp.where(inner, first_ref[count : 2 * count], first_ref[:count])
    other = jnp.where(inner, second_ref[...], last_ref[...])
    low, even_tok = kv < 2, tok % 2 == 0
    top, bottom = jnp.where(low, close, other), jnp.where(low, other, close)
    even_ref[...] = jnp.where(even_tok, bottom, top)
    odd_ref[...] = jnp.where(even_tok, top, bottom)


def project_call(kernel, name, rows, width, heads_width, operands, extra=0, scratch=()):
    keyval = lambda count: jax.ShapeDtypeStruct((count, 2 * heads_width), BF16)
    edge = operands[-1].shape[0]
    return pl.pallas_call(
        kernel,
        out_shape=(jax.ShapeDtypeStruct((rows, heads_width), BF16), keyval(rows)) + (keyval(edge),) * extra,
        in_specs=[SMEM if operand.ndim == 1 else VMEM for operand in operands],
        out_specs=(VMEM,) * (2 + extra),
        scratch_shapes=list(scratch),
        compiler_params=pltpu.CompilerParams(vmem_limit_bytes=10 * MIB),
        cost_estimate=SHORT,
        name=name,
    )(*operands)


def window_bias(first, count, starts, ends):
    reach = WIN // 2
    query = first + lax.broadcasted_iota(jnp.int32, (count, 1), 0)
    low = jnp.max(jnp.where(starts <= query, starts, 0), axis=1, keepdims=True)
    high = jnp.min(jnp.where(ends > query, ends, 1 << 30), axis=1, keepdims=True)
    low = jnp.maximum(low, query - reach)
    high = jnp.minimum(high, query + reach + 1)
    key = first - count + lax.broadcasted_iota(jnp.int32, (count, 3 * count), 1)
    return jnp.where((key >= low) & (key < high), 0.0, NEG_FILL)


def attend(query, keyval_ref, bias_ref, scores_ref, weights_ref, out_ref):
    count, width = query.shape
    lane = lax.broadcasted_iota(jnp.int32, (count, 2 * HD), 1)
    for start in range(0, width, 2 * HD):
        values = keyval_ref[:, width + start : width + start + 2 * HD]
        halves = []
        for side in range(2):
            head = start // HD + side
            inside = (lane < HD) if side == 0 else (lane >= HD)
            only = jnp.where(inside, query[:, start : start + 2 * HD], jnp.zeros((), BF16))
            scores_ref[head] = lax.dot_general(
                only, keyval_ref[:, start : start + 2 * HD], (((1,), (1,)), ((), ())), preferred_element_type=F32
            )
            totals = []
            for row in range(0, count, STRIP):
                at = slice(row, row + STRIP)
                scores = scores_ref[head, at] + bias_ref[at]
                weights = jnp.exp(scores - jnp.max(scores, axis=1, keepdims=True))
                totals.append(jnp.sum(weights, axis=1, keepdims=True))
                weights_ref[head, at] = weights.astype(BF16)
            summed = jnp.dot(weights_ref[head], values, preferred_element_type=F32)
            halves.append(summed / jnp.concatenate(totals, axis=0))
        out_ref[:, start : start + 2 * HD] = jnp.where(lane < HD, halves[0], halves[1]).astype(BF16)


def attend_kernel(flips, has_halo, *refs):
    place_ref, starts_ref, ends_ref, query0_ref, keyval0_ref, query1_ref, keyval1_ref, query2_ref, keyval2_ref = refs[:9]
    even_ref, odd_ref = refs[9:11] if has_halo else (None, None)
    out_ref, window_ref, bias_ref, scores_ref, weights_ref, sems = refs[-6:]
    tok, kv = place_ref[0], place_ref[1]
    count = out_ref.shape[0]
    blocks = 4
    inner = is_inner(kv)
    outer = jnp.logical_not(inner)
    block = kv ^ jnp.where(inner, flips[1], flips[0])
    copies = []
    for part in range(3):
        target = window_ref.at[part * count : (part + 1) * count]
        sem = sems.at[part]
        at = block + part - 1
        here = (at >= 0) & (at < blocks)
        flip = at ^ kv
        first = here & ((flip == 0) | (flip == 1) | (inner & (flip == 3)))
        slot = jnp.where(first, jnp.minimum(flip, 2), 0)
        source = keyval0_ref.at[pl.ds(pl.multiple_of(slot * count, count), count)]
        copies.append((first, pltpu.make_async_copy(source, target, sem)))
        copies.append((here & (flip == 2), pltpu.make_async_copy(keyval1_ref, target, sem)))
        copies.append((here & outer & (flip == 3), pltpu.make_async_copy(keyval2_ref, target, sem)))
        if has_halo and part != 1:
            outside = at < 0 if part == 0 else at >= blocks
            over_even = tok % 2 == (1 if part == 0 else 0)
            copies.append((outside & over_even, pltpu.make_async_copy(even_ref, target, sem)))
            copies.append((outside & jnp.logical_not(over_even), pltpu.make_async_copy(odd_ref, target, sem)))
    for needed, copy in copies:
        pl.when(needed)(copy.start)
    bias_ref[...] = window_bias((tok * blocks + block) * count, count, starts_ref[...], ends_ref[...])

    def query_of(flip, is_inner_one):
        if flip == 2:
            return query1_ref[...]
        if flip == 3 and not is_inner_one:
            return query2_ref[...]
        slot = min(flip, 2)
        return query0_ref[slot * count : (slot + 1) * count]

    query = jnp.where(inner, query_of(flips[1], True), query_of(flips[0], False))
    for needed, copy in copies:
        pl.when(needed)(copy.wait)
    attend(query, window_ref, bias_ref, scores_ref, weights_ref, out_ref)


def attend_block(place, starts, ends, projected, flips, name, halo=()):
    rows, heads_width = projected[-2].shape
    return pl.pallas_call(
        functools.partial(attend_kernel, flips, bool(halo)),
        out_shape=jax.ShapeDtypeStruct((rows, heads_width), BF16),
        in_specs=[SMEM, VMEM, VMEM] + [VMEM, ANY] * 3 + [ANY] * len(halo),
        out_specs=VMEM,
        scratch_shapes=[
            pltpu.VMEM((3 * rows, 2 * heads_width), BF16),
            pltpu.VMEM((rows, 3 * rows), F32),
            pltpu.VMEM((heads_width // HD, rows, 3 * rows), F32),
            pltpu.VMEM((heads_width // HD, rows, 3 * rows), BF16),
            pltpu.SemaphoreType.DMA((3,)),
        ],
        compiler_params=pltpu.CompilerParams(vmem_limit_bytes=12 * MIB),
        cost_estimate=SHORT,
        name=name,
    )(place, starts, ends, *projected, *halo)


def first_norm_kernel(layout, place_ref, own_ref, partner_ref, own_out_ref, gain_ref, bias_ref, *refs):
    parts, pieces = refs[:8], refs[8 : 8 + len(layout)]
    normed_ref, away_ref, all_ref, weight_ref, mixed_ref, sems = refs[8 + len(layout) :]
    tok, kv = place_ref[0], place_ref[1]
    quarters, heads_width, width = weight_ref.shape
    count = own_ref.shape[0]
    copies = [pltpu.make_async_copy(own_out_ref, weight_ref.at[0], sems.at[0])]
    for flips, piece in zip(layout, pieces):
        for index, flip in enumerate(flips):
            depth = piece.shape[2]
            at = pl.multiple_of((tok ^ flip) * depth, depth)
            target = weight_ref.at[1:quarters, pl.ds(at, depth)]
            copies.append(pltpu.make_async_copy(piece.at[index], target, sems.at[len(copies)]))
    for copy in copies:
        copy.start()
    early = jnp.where(is_inner(kv), 0, 1)
    for index, part_ref in enumerate(parts):
        flip = index % 4
        half = early if index < 4 else 1 - early
        at = pl.ds(pl.multiple_of(half * count, count), count)
        all_ref[at, flip * heads_width : (flip + 1) * heads_width] = part_ref[...]
    for copy in copies:
        copy.wait()
    weight = weight_ref[...].reshape(quarters * heads_width, width)
    mixed_ref[...] = jnp.dot(all_ref[...], weight, preferred_element_type=F32)
    for half, (hidden_ref, result_ref) in enumerate(((own_ref, normed_ref), (partner_ref, away_ref))):
        for row in range(0, count, STRIP):
            at = slice(row, row + STRIP)
            mixed = hidden_ref[at].astype(F32) + mixed_ref[half * count + row : half * count + row + STRIP]
            result_ref[at] = normalized(mixed, gain_ref[...], bias_ref[...]).astype(BF16)


def first_norm(place, own, partner, own_out, gain, bias, parts, pieces):
    rows, width = own.shape
    heads_width = own_out.shape[0]
    layout = tuple(flips for flips, _ in pieces)
    return pl.pallas_call(
        functools.partial(first_norm_kernel, layout),
        out_shape=(jax.ShapeDtypeStruct((rows, width), BF16),) * 2,
        in_specs=[SMEM, VMEM, VMEM, ANY, VMEM, VMEM] + [VMEM] * len(parts) + [ANY] * len(pieces),
        out_specs=(VMEM,) * 2,
        scratch_shapes=[
            pltpu.VMEM((2 * rows, width), BF16),
            pltpu.VMEM((width // heads_width, heads_width, width), BF16),
            pltpu.VMEM((2 * rows, width), F32),
            pltpu.SemaphoreType.DMA((1 + sum(len(flips) for flips in layout),)),
        ],
        compiler_params=pltpu.CompilerParams(vmem_limit_bytes=14 * MIB),
        cost_estimate=SHORT,
        name="first_norm",
    )(place, own, partner, own_out, gain, bias, *parts, *[value for _, value in pieces])


def gelu(values):
    return 0.5 * values * (1.0 + lax.erf(values * math.sqrt(0.5)))


CHUNK = 512


def feed_chunk(rows, up, down_ref, wide_ref, units_ref):
    wide_ref[...] = jnp.dot(rows, up, preferred_element_type=F32)
    for row in range(0, rows.shape[0], STRIP):
        strip = slice(row, row + STRIP)
        units_ref[strip] = gelu(wide_ref[strip]).astype(BF16)
    return jnp.dot(units_ref[...], down_ref[...], preferred_element_type=F32)


def far_copies(tok, held_ref, core_ref, up_ref, down_ref, sems):
    block = 128
    copies = []
    for side, piece in enumerate((held_ref, core_ref)):
        for index in range(4):
            at = pl.ds(pl.multiple_of((tok ^ (2 * index + side)) * block, block), block)
            for part, target in enumerate((up_ref, down_ref)):
                source = piece.at[pl.ds((2 * index + part) * block, block)]
                copies.append(pltpu.make_async_copy(source, target.at[at], sems.at[len(copies)]))
    return copies


def feed_kernel(place_ref, rows_ref, up_near_ref, down_near_ref, held_ref, core_ref, *refs):
    sum_ref, up_ref, down_ref, wide_ref, units_ref, total_ref, sems = refs
    copies = far_copies(place_ref[0], held_ref, core_ref, up_ref, down_ref, sems)
    for copy in copies:
        copy.start()
    rows = rows_ref[...]
    chunks = up_ref.shape[1] // CHUNK
    for index in range(2 * chunks):
        if index == chunks:
            for copy in copies:
                copy.wait()
        up, down = (up_near_ref, down_near_ref) if index < chunks else (up_ref, down_ref)
        at = slice(index % chunks * CHUNK, (index % chunks + 1) * CHUNK)
        product = feed_chunk(rows, up[:, at], down.at[at], wide_ref.at[index % 2], units_ref.at[index % 2])
        if index == 0:
            total_ref[...] = product
        elif index < 2 * chunks - 1:
            total_ref[...] += product
        else:
            sum_ref[...] = (total_ref[...] + product).astype(sum_ref.dtype)


def feed(place, rows, up_weight, down_weight, pieces, dtype, name):
    count, width = rows.shape
    units = up_weight.shape[1]
    return pl.pallas_call(
        feed_kernel,
        out_shape=jax.ShapeDtypeStruct((count, width), dtype),
        in_specs=[SMEM] + [VMEM] * 3 + [ANY] * 2,
        out_specs=VMEM,
        scratch_shapes=[
            pltpu.VMEM((width, units), BF16),
            pltpu.VMEM((units, width), BF16),
            pltpu.VMEM((2, count, CHUNK), F32),
            pltpu.VMEM((2, count, CHUNK), BF16),
            pltpu.VMEM((count, width), F32),
            pltpu.SemaphoreType.DMA((16,)),
        ],
        compiler_params=pltpu.CompilerParams(vmem_limit_bytes=18 * MIB),
        cost_estimate=SHORT,
        name=name,
    )(place, rows, up_weight, down_weight, *pieces)


def finish_kernel(normed_ref, near_ref, far_ref, gain_ref, bias_ref, out_ref):
    for row in range(0, normed_ref.shape[0], STRIP):
        at = slice(row, row + STRIP)
        mixed = normed_ref[at].astype(F32) + near_ref[at] + far_ref[at].astype(F32)
        out_ref[at] = normalized(mixed, gain_ref[...], bias_ref[...]).astype(out_ref.dtype)


def finish(normed, near, far, gain, bias):
    return pl.pallas_call(
        finish_kernel,
        out_shape=jax.ShapeDtypeStruct(normed.shape, BF16),
        in_specs=[VMEM] * 5,
        out_specs=VMEM,
        compiler_params=pltpu.CompilerParams(vmem_limit_bytes=6 * MIB),
        name="finish",
    )(normed, near, far, gain, bias)


def decode_kernel(slot_ref, filled_ref, query_ref, cache_ref, out_ref, high_ref, total_ref, sum_ref):
    step = pl.program_id(0)

    @pl.when(step == 0)
    def _():
        high_ref[...] = jnp.full(high_ref.shape, NEG_FILL, F32)
        total_ref[...] = jnp.zeros_like(total_ref)
        sum_ref[...] = jnp.zeros_like(sum_ref)

    row = slot_ref[step]
    filled = filled_ref[step]
    width = query_ref.shape[1]
    head = lax.broadcasted_iota(jnp.int32, (H, width), 0)
    inside = head == lax.broadcasted_iota(jnp.int32, (H, width), 1) // HD
    query = jnp.where(inside, query_ref[pl.ds(row, 1), :], 0.0).astype(BF16)
    scores = lax.dot_general(query, cache_ref[0, 0, 0], (((1,), (1,)), ((), ())), preferred_element_type=F32)
    live = lax.broadcasted_iota(jnp.int32, scores.shape, 1) < filled
    scores = jnp.where(live, scores * (1.0 / math.sqrt(HD)), NEG_FILL)
    high = jnp.max(scores, axis=1, keepdims=True)
    weights = jnp.where(live, jnp.exp(scores - high), 0.0)
    total = jnp.sum(weights, axis=1, keepdims=True)
    summed = jnp.dot(weights.astype(BF16), cache_ref[1, 0, 0], preferred_element_type=F32)
    along = lambda column: jnp.sum(jnp.where(inside, column, 0.0), axis=0, keepdims=True)
    high, total, summed = along(high), along(total), along(summed)
    used = filled > 0
    at = pl.ds(row, 1)
    old = high_ref[at, :]
    new = jnp.where(used, jnp.maximum(old, high), old)
    left = jnp.exp(old - new)
    right = jnp.where(used, jnp.exp(high - new), 0.0)
    high_ref[at, :] = new
    total_ref[at, :] = total_ref[at, :] * left + total * right
    sum_ref[at, :] = sum_ref[at, :] * left + summed * right

    @pl.when(step == pl.num_programs(0) - 1)
    def _():
        out_ref[0] = high_ref[...]
        out_ref[1] = total_ref[...]
        out_ref[2] = sum_ref[...]


def decode(slots, filled, queries, kv_cache):
    requests, width = queries.shape
    pieces = kv_cache.shape[2]
    state = pltpu.VMEM((requests, width), F32)
    return pl.pallas_call(
        decode_kernel,
        grid=(pieces,),
        out_shape=jax.ShapeDtypeStruct((3, requests, width), F32),
        in_specs=[
            SMEM,
            SMEM,
            pl.BlockSpec((requests, width), lambda i: (0, 0)),
            pl.BlockSpec((2, 1, 1, PLEN, width), lambda i: (0, 0, i, 0, 0)),
        ],
        out_specs=pl.BlockSpec((3, requests, width), lambda i: (0, 0, 0)),
        scratch_shapes=[state, state, state],
        compiler_params=pltpu.CompilerParams(vmem_limit_bytes=8 * MIB),
        cost_estimate=SHORT,
        name="decode",
    )(slots, filled, queries, kv_cache)


def decode_partial(queries, own, kv_cache, piece_req, piece_used):
    owners = piece_req[0]
    slots = ((owners // own) ^ lax.axis_index("kv")) * own + owners % own
    return decode(slots, piece_used[0], queries, kv_cache)


def exchanged_partials(partial, own):
    parts = [partial[:, :own]]
    for flip in range(1, lax.axis_size("kv")):
        parts.append(swapped(partial[:, flip * own : (flip + 1) * own], "kv", flip))
    return parts


def merged_partials(parts):
    high = functools.reduce(jnp.maximum, [part[0] for part in parts])
    factors = [jnp.exp(part[0] - high) for part in parts]
    total = sum(part[1] * factor for part, factor in zip(parts, factors))
    summed = sum(part[2] * factor for part, factor in zip(parts, factors))
    return (summed / total).astype(BF16)


def routed_body(
    hidden_in,
    qkv_weight,
    stretch_len,
    out_weight,
    ln1_gain,
    ln1_bias,
    up_weight,
    down_weight,
    ln2_gain,
    ln2_bias,
    dec_query,
    kv_cache,
    piece_req,
    piece_used,
):
    tok = lax.axis_index("tok")
    kv = lax.axis_index("kv")
    toks, kvs = lax.axis_size("tok"), lax.axis_size("kv")
    rows, width = hidden_in.shape
    heads_width = out_weight.shape[0]
    place = jnp.stack([tok, kv]).astype(jnp.int32)
    eighth = lambda value: lax.dynamic_slice_in_dim(value, tok * (value.shape[0] // toks), value.shape[0] // toks, 0)

    outward = [(1, 0), (2, 3)]
    a1, b1 = over_edges(hidden_in, "kv", 0), over_edges(hidden_in, "kv", 1)
    out_part = eighth(out_weight)
    depth = out_part.shape[0]
    small = jnp.concatenate([out_part, dec_query], axis=0)
    others = [swapped(small, "kv", flip) for flip in range(1, kvs)]
    a2, b2 = lax.ppermute(b1, "kv", outward), over_edges(a1, "kv", 1)
    out_here = after(jnp.stack([other[:depth] for other in others]), b2)
    out_x, out_y = swapped(out_here, "tok", 2), swapped(out_here, "tok", 4)
    weight = jnp.transpose(qkv_weight, (1, 0, 2))
    sizes = (width, heads_width)
    first = project_call(
        project_first_kernel, "project_first", 3 * rows, *sizes, (weight, hidden_in, a1, b1), 0, [pltpu.VMEM((3 * rows, width), BF16)]
    )
    a3 = lax.ppermute(after(b2, first[0]), "kv", outward)
    second = project_call(project_second_kernel, "project_second", rows, *sizes, (place, weight, a2, b2))
    out_far = swapped(out_y, "tok", 2)
    inner = (kv == 1) | (kv == 2)

    order = jnp.arange(stretch_len.shape[0])
    ends = jnp.sum(jnp.where(order[:, None] <= order[None, :], stretch_len[:, None], 0), axis=0, dtype=jnp.int32)
    starts = (ends - stretch_len)[None, :]
    ends = ends[None, :]

    feed_up, feed_down = after((eighth(up_weight), eighth(down_weight)), a2, b2)
    inner_up = lax.ppermute(feed_up, "kv", [(0, 2), (3, 1)])
    inner_down = lax.ppermute(feed_down, "kv", [(0, 2), (3, 1)])
    feed_part = jnp.concatenate([feed_up, feed_down], axis=0)
    feed_part = after(feed_part, a3, second[0], out_x, out_y, inner_up, inner_down)
    feed_outer = lax.ppermute(feed_part, "kv", [(1, 3), (2, 0)])
    feed_inner = jnp.concatenate([inner_up, inner_down], axis=0)

    *last, even, odd = project_call(
        project_last_kernel, "project_last", rows, *sizes, (place, weight, first[1], second[1], a3), 2
    )
    halo = over_edges(even, "tok", 0), over_edges(odd, "tok", 1)
    projected = (*first, *second, *last)
    two = attend_block(place, starts, ends, projected, (2, 3), "attend_two")
    two_there = swapped(two, "kv", 2)
    out_all = jnp.stack([out_here, out_x, out_y, out_far])
    out_core = swapped(out_all, "tok", 1)
    feed_here = jnp.where(inner, feed_inner, after(feed_outer, two))
    feed_x, feed_y = swapped(feed_here, "tok", 2), swapped(feed_here, "tok", 4)
    far = attend_block(after(place, feed_here, out_core), starts, ends, projected, (3, 2), "attend_far", halo)
    far_there = swapped(far, "kv", 2)
    two_passed = swapped(after(two_there, far), "kv", 1)
    one = attend_block(after(place, far, two_there), starts, ends, projected, (1, 0), "attend_one")
    one_there = swapped(one, "kv", 1)
    near = attend_block(after(place, one), starts, ends, projected, (0, 1), "attend_near", halo)
    near_there, far_passed = swapped(near, "kv", 1), swapped(far_there, "kv", 1)
    parts = (one, one_there, two_there, two_passed, near, near_there, far_there, far_passed)
    out_pieces = [((0, 2, 4, 6), out_all), ((1, 3, 5, 7), out_core)]
    queries = jnp.concatenate([dec_query] + [other[depth:] for other in others], axis=0)
    queries = after(queries, near, two_passed).astype(F32)
    partial = decode_partial(queries, dec_query.shape[0], kv_cache, piece_req, piece_used)
    half = feed_here.shape[0] // 2
    far_up = swapped(after(feed_y, far_there, near_there, partial)[:half], "tok", 2)
    far_down = swapped(after(feed_x, far_there, near_there, partial)[half:], "tok", 4)
    held = jnp.concatenate([feed_here, feed_x, feed_y, far_up, far_down], axis=0)
    feed_pieces = (held, swapped(after(held, far_passed, one_there), "tok", 1))

    gain, bias = ln1_gain[None, :], ln1_bias[None, :]
    normed, partner = first_norm(place, hidden_in, a1, out_weight, gain, bias, parts, out_pieces)
    away = feed(place, partner, up_weight, down_weight, feed_pieces, BF16, "feed_partner")
    arrived = swapped(away, "kv", 1)
    dec_parts = exchanged_partials(after(partial, away), dec_query.shape[0])
    mine = feed(place, after(normed, away), up_weight, down_weight, feed_pieces, F32, "feed_own")
    prefill_out = finish(normed, mine, arrived, ln2_gain[None, :], ln2_bias[None, :])

    return prefill_out, merged_partials(after(tuple(dec_parts), mine))


def extended(value, sides, width):
    for axis, dim in sides:
        count, length = (lax.axis_size(axis), value.shape[dim])
        up = [(i, (i + 1) % count) for i in range(count - 1)]
        down = [(j, i) for i, j in up]
        last = lax.slice_in_dim(value, length - width, length, axis=dim)
        leading = lax.slice_in_dim(value, 0, width, axis=dim)
        before = lax.ppermute(last, axis, up)
        after = lax.ppermute(leading, axis, down)
        value = jnp.concatenate([before, value, after], axis=dim)
    return value


def merged(value, axis, join):
    pieces = jax.tree.map(lambda part: lax.all_gather(part, axis), value)
    head = jax.tree.map(lambda part: part[0], pieces)
    tail = jax.tree.map(lambda part: part[1:], pieces)
    subtotal, _ = lax.scan(lambda subtotal, section: (join(subtotal, section), None), head, tail)
    return subtotal


def segment_ids(row_ids, stretch_len):
    stretch_ends = jnp.cumsum(stretch_len)
    return jnp.sum((row_ids[:, None] >= stretch_ends[None, :]).astype(jnp.int32), axis=1)


def layer_norm(values, gain, bias):
    center = values - jnp.mean(values, axis=1, keepdims=True)
    spread = jnp.mean(center * center, axis=1, keepdims=True)
    return center * lax.rsqrt(spread + LN_EPS) * gain + bias


def merge_partials(earlier, later):
    highest = jnp.maximum(earlier[0], later[0])
    left_factor = jnp.exp(earlier[0] - highest)
    right_factor = jnp.exp(later[0] - highest)
    totals = earlier[1] * left_factor + later[1] * right_factor
    weighted = earlier[2] * left_factor[..., None] + later[2] * right_factor[..., None]
    return (highest, totals, weighted)


def row_folder(source, shard_rows):
    return jnp.dot(source, shard_rows, preferred_element_type=jnp.float32)


def general_body(
    hidden_in,
    qkv_weight,
    stretch_len,
    out_weight,
    ln1_gain,
    ln1_bias,
    up_weight,
    down_weight,
    ln2_gain,
    ln2_bias,
    dec_query,
    kv_cache,
    piece_req,
    piece_used,
):
    inv_scale = 1.0 / math.sqrt(HD)
    reach = WIN // 2
    local_width = qkv_weight.shape[2]
    head_count = local_width // HD
    flat_weight = qkv_weight.reshape(qkv_weight.shape[0], 3 * local_width)
    qkv_rows = jnp.dot(
        lax.all_gather(hidden_in, "kv", axis=0, tiled=True),
        flat_weight,
        preferred_element_type=jnp.float32,
    ).astype(jnp.bfloat16)
    row_count = qkv_rows.shape[0]
    query_rows = qkv_rows[:, :local_width]
    keyval_rows = qkv_rows[:, local_width:]
    padded = extended(keyval_rows, (("tok", 0),), reach)
    first_row = lax.axis_index("tok") * row_count
    total_rows = row_count * lax.axis_size("tok")
    qblock = min(512, row_count)
    span = qblock + 2 * reach
    block_count = row_count // qblock

    def attend(block_index):
        start = block_index * qblock
        query_ids = first_row + start + jnp.arange(qblock, dtype=jnp.int32)
        key_ids = first_row + start - reach + jnp.arange(span, dtype=jnp.int32)
        query_seg = segment_ids(query_ids, stretch_len)
        inside = (key_ids >= 0) & (key_ids < total_rows)
        key_seg = jnp.where(inside, segment_ids(key_ids, stretch_len), -1)
        allowed = (key_seg[None, :] == query_seg[:, None]) & (
            jnp.abs(key_ids[None, :] - query_ids[:, None]) <= reach
        )
        queries = lax.dynamic_slice_in_dim(query_rows, start, qblock, 0).reshape(
            qblock, head_count, HD
        )
        both = lax.dynamic_slice_in_dim(padded, start, span, 0)
        key_rows = both[:, :local_width].reshape(span, head_count, HD)
        value_rows = both[:, local_width:].reshape(span, head_count, HD)
        scores = (
            jnp.einsum("ihd,jhd->hij", queries, key_rows, preferred_element_type=jnp.float32)
            * inv_scale
        )
        scores = jnp.where(allowed[None], scores, NEG_FILL)
        row_max = jnp.max(scores, axis=2, keepdims=True)
        weights = jnp.where(allowed[None], jnp.exp(scores - row_max), 0.0)
        totals = jnp.sum(weights, axis=2)
        summed = jnp.einsum(
            "hij,jhd->ihd",
            weights.astype(jnp.bfloat16),
            value_rows,
            preferred_element_type=jnp.float32,
        )
        return (
            (summed / jnp.transpose(totals)[:, :, None])
            .astype(jnp.bfloat16)
            .reshape(qblock, local_width)
        )

    attention = lax.map(attend, jnp.arange(block_count, dtype=jnp.int32)).reshape(
        row_count, local_width
    )
    token_major = lax.all_to_all(attention, "kv", split_axis=0, concat_axis=1, tiled=True)
    projected = row_folder(token_major, lax.all_gather(out_weight, "kv", axis=0, tiled=True))
    normed = layer_norm(hidden_in.astype(jnp.float32) + projected, ln1_gain, ln1_bias).astype(
        jnp.bfloat16
    )
    units = jax.nn.gelu(
        jnp.dot(
            lax.all_gather(normed, "kv", axis=0, tiled=True),
            up_weight,
            preferred_element_type=jnp.float32,
        ),
        approximate=False,
    ).astype(jnp.bfloat16)
    ffn = lax.psum_scatter(
        jnp.dot(units, down_weight, preferred_element_type=jnp.float32).astype(jnp.bfloat16),
        "kv",
        scatter_dimension=0,
        tiled=True,
    ).astype(jnp.float32)
    prefill_out = layer_norm(normed.astype(jnp.float32) + ffn, ln2_gain, ln2_bias).astype(
        jnp.bfloat16
    )
    group_queries = lax.all_gather(dec_query, "kv", axis=0, tiled=True)
    request_count = group_queries.shape[0]
    owners = piece_req[0]
    filled = piece_used[0]
    slot_count = owners.shape[0]
    request_ids = jnp.arange(request_count, dtype=jnp.int32)
    selector = (owners[:, None] == request_ids[None, :]).astype(jnp.bfloat16)
    chosen = jnp.dot(selector, group_queries, preferred_element_type=jnp.float32).astype(
        jnp.bfloat16
    )
    chosen = chosen.reshape(slot_count, H, HD)
    cache_keys = kv_cache[0, 0].reshape(slot_count, PLEN, H, HD)
    cache_values = kv_cache[1, 0].reshape(slot_count, PLEN, H, HD)
    piece_scores = (
        jnp.einsum("phd,pthd->pht", chosen, cache_keys, preferred_element_type=jnp.float32)
        * inv_scale
    )
    active = jnp.arange(PLEN, dtype=jnp.int32)[None, :] < filled[:, None]
    piece_scores = jnp.where(active[:, None, :], piece_scores, NEG_FILL)
    piece_max = jnp.max(piece_scores, axis=2)
    piece_weights = jnp.where(
        active[:, None, :], jnp.exp(piece_scores - piece_max[:, :, None]), 0.0
    )
    piece_totals = jnp.sum(piece_weights, axis=2)
    partial_value = jnp.einsum(
        "pht,pthd->phd",
        piece_weights.astype(jnp.bfloat16),
        cache_values,
        preferred_element_type=jnp.float32,
    )
    member = (owners[None, :] == request_ids[:, None]) & (filled[None, :] > 0)
    highest = jnp.max(jnp.where(member[:, :, None], piece_max[None], NEG_FILL), axis=1)
    factor = jnp.where(member[:, :, None], jnp.exp(piece_max[None] - highest[:, None, :]), 0.0)
    denom = jnp.sum(factor * piece_totals[None], axis=1)
    weighted = jnp.einsum("rph,phd->rhd", factor, partial_value)
    own_requests = dec_query.shape[0]
    joined = merged((highest, denom, weighted), "kv", merge_partials)
    begin = lax.axis_index("kv") * own_requests
    final_denom = lax.dynamic_slice_in_dim(joined[1], begin, own_requests, 0)
    final_weighted = lax.dynamic_slice_in_dim(joined[2], begin, own_requests, 0)
    dec_out = (
        (final_weighted / final_denom[:, :, None])
        .astype(jnp.bfloat16)
        .reshape(own_requests, H * HD)
    )
    return (prefill_out, dec_out)


def solution(mesh):
    placed = (
        P(("tok", "kv"), None),
        P(None, None, "kv"),
        P(),
        P("kv", None),
        P(),
        P(),
        P(None, "kv"),
        P("kv", None),
        P(),
        P(),
        P(("tok", "kv"), None),
        P(None, "tok", "kv", None, None),
        P("tok", "kv"),
        P("tok", "kv"),
    )
    routed = mesh.shape["tok"] == 8 and mesh.shape["kv"] == 4
    return jax.shard_map(
        routed_body if routed else general_body,
        mesh=mesh,
        in_specs=placed,
        out_specs=(P(("tok", "kv"), None), P(("tok", "kv"), None)),
        check_vma=False,
    )
```

```python
import functools
import math

import jax
import jax.numpy as jnp
from jax import lax
from jax.experimental import pallas as pl
from jax.experimental.pallas import tpu as pltpu
from jax.sharding import PartitionSpec as P

H = 16
HD = 64
WIN = 512
PLEN = 128


NEG_FILL = -1e30
LN_EPS = 1e-05
BF16 = jnp.bfloat16
F32 = jnp.float32
STRIP = 32
MIB = 1024 * 1024
ANY = pl.BlockSpec(memory_space=pl.ANY)
VMEM = pl.BlockSpec(memory_space=pltpu.VMEM)
SMEM = pl.BlockSpec(memory_space=pltpu.SMEM)
SHORT = pl.CostEstimate(flops=1, bytes_accessed=1, transcendentals=0)


def swapped(value, axis, flip):
    count = lax.axis_size(axis)
    return lax.ppermute(value, axis, [(i, i ^ flip) for i in range(count)])


def over_edges(value, axis, first):
    count = lax.axis_size(axis)
    edges = [(i, i + 1) for i in range(first, count - 1, 2)]
    return lax.ppermute(value, axis, edges + [(j, i) for i, j in edges])


def after(value, *earlier):
    return lax.optimization_barrier((value,) + earlier)[0]


def normalized(values, gain, bias):
    center = values - jnp.mean(values, axis=1, keepdims=True)
    spread = jnp.mean(center * center, axis=1, keepdims=True)
    return center * lax.rsqrt(spread + LN_EPS) * gain + bias


def project_rows(rows, weight_ref, query_ref, keyval_ref):
    width = weight_ref.shape[2]
    query = jnp.dot(rows, weight_ref[0], preferred_element_type=F32) * (1.0 / math.sqrt(HD))
    query_ref[...] = query.astype(BF16)
    for part in range(2):
        at = slice(part * width, (part + 1) * width)
        keyval_ref[:, at] = jnp.dot(rows, weight_ref[part + 1], preferred_element_type=F32).astype(BF16)


def is_inner(kv):
    return (kv == 1) | (kv == 2)


def project_first_kernel(weight_ref, own_ref, a1_ref, b1_ref, query_ref, keyval_ref, rows_ref):
    count = own_ref.shape[0]
    for index, source in enumerate((own_ref, a1_ref, b1_ref)):
        rows_ref[index * count : (index + 1) * count] = source[...]
    project_rows(rows_ref[...], weight_ref, query_ref, keyval_ref)


def project_second_kernel(place_ref, weight_ref, a2_ref, b2_ref, query_ref, keyval_ref):
    rows = jnp.where(is_inner(place_ref[1]), b2_ref[...], a2_ref[...])
    project_rows(rows, weight_ref, query_ref, keyval_ref)


def project_last_kernel(place_ref, weight_ref, first_ref, second_ref, a3_ref, query_ref, last_ref, even_ref, odd_ref):
    tok, kv = place_ref[0], place_ref[1]
    count = a3_ref.shape[0]
    project_rows(a3_ref[...], weight_ref, query_ref, last_ref)
    inner = is_inner(kv)
    close = jnp.where(inner, first_ref[count : 2 * count], first_ref[:count])
    other = jnp.where(inner, second_ref[...], last_ref[...])
    low, even_tok = kv < 2, tok % 2 == 0
    top, bottom = jnp.where(low, close, other), jnp.where(low, other, close)
    even_ref[...] = jnp.where(even_tok, bottom, top)
    odd_ref[...] = jnp.where(even_tok, top, bottom)


def project_call(kernel, name, rows, width, heads_width, operands, extra=0, scratch=()):
    keyval = lambda count: jax.ShapeDtypeStruct((count, 2 * heads_width), BF16)
    edge = operands[-1].shape[0]
    return pl.pallas_call(
        kernel,
        out_shape=(jax.ShapeDtypeStruct((rows, heads_width), BF16), keyval(rows)) + (keyval(edge),) * extra,
        in_specs=[SMEM if operand.ndim == 1 else VMEM for operand in operands],
        out_specs=(VMEM,) * (2 + extra),
        scratch_shapes=list(scratch),
        compiler_params=pltpu.CompilerParams(vmem_limit_bytes=10 * MIB),
        cost_estimate=SHORT,
        name=name,
    )(*operands)


def window_bias(first, count, starts, ends):
    reach = WIN // 2
    query = first + lax.broadcasted_iota(jnp.int32, (count, 1), 0)
    low = jnp.max(jnp.where(starts <= query, starts, 0), axis=1, keepdims=True)
    high = jnp.min(jnp.where(ends > query, ends, 1 << 30), axis=1, keepdims=True)
    low = jnp.maximum(low, query - reach)
    high = jnp.minimum(high, query + reach + 1)
    key = first - count + lax.broadcasted_iota(jnp.int32, (count, 3 * count), 1)
    return jnp.where((key >= low) & (key < high), 0.0, NEG_FILL)


def attend(query, keyval_ref, bias_ref, scores_ref, weights_ref, out_ref):
    count, width = query.shape
    lane = lax.broadcasted_iota(jnp.int32, (count, 2 * HD), 1)
    for start in range(0, width, 2 * HD):
        values = keyval_ref[:, width + start : width + start + 2 * HD]
        halves = []
        for side in range(2):
            head = start // HD + side
            inside = (lane < HD) if side == 0 else (lane >= HD)
            only = jnp.where(inside, query[:, start : start + 2 * HD], jnp.zeros((), BF16))
            scores_ref[head] = lax.dot_general(
                only, keyval_ref[:, start : start + 2 * HD], (((1,), (1,)), ((), ())), preferred_element_type=F32
            )
            totals = []
            for row in range(0, count, STRIP):
                at = slice(row, row + STRIP)
                scores = scores_ref[head, at] + bias_ref[at]
                weights = jnp.exp(scores - jnp.max(scores, axis=1, keepdims=True))
                totals.append(jnp.sum(weights, axis=1, keepdims=True))
                weights_ref[head, at] = weights.astype(BF16)
            summed = jnp.dot(weights_ref[head], values, preferred_element_type=F32)
            halves.append(summed / jnp.concatenate(totals, axis=0))
        out_ref[:, start : start + 2 * HD] = jnp.where(lane < HD, halves[0], halves[1]).astype(BF16)


def attend_kernel(flips, has_halo, joins, *refs):
    place_ref, starts_ref, ends_ref, query0_ref, keyval0_ref, query1_ref, keyval1_ref, query2_ref, keyval2_ref = refs[:9]
    even_ref, odd_ref = refs[9:11] if has_halo else (None, None)
    out_ref, window_ref, bias_ref, scores_ref, weights_ref, sems = refs[-6:]
    tok, kv = place_ref[0], place_ref[1]
    count = bias_ref.shape[0]
    blocks = 4
    if joins:
        out_ref[:count] = refs[-7][...]
        out_ref[2 * count :] = jnp.zeros_like(out_ref[2 * count :])
        out_ref = out_ref.at[count : 2 * count]
    inner = is_inner(kv)
    outer = jnp.logical_not(inner)
    block = kv ^ jnp.where(inner, flips[1], flips[0])
    copies = []
    for part in range(3):
        target = window_ref.at[part * count : (part + 1) * count]
        sem = sems.at[part]
        at = block + part - 1
        here = (at >= 0) & (at < blocks)
        flip = at ^ kv
        first = here & ((flip == 0) | (flip == 1) | (inner & (flip == 3)))
        slot = jnp.where(first, jnp.minimum(flip, 2), 0)
        source = keyval0_ref.at[pl.ds(pl.multiple_of(slot * count, count), count)]
        copies.append((first, pltpu.make_async_copy(source, target, sem)))
        copies.append((here & (flip == 2), pltpu.make_async_copy(keyval1_ref, target, sem)))
        copies.append((here & outer & (flip == 3), pltpu.make_async_copy(keyval2_ref, target, sem)))
        if has_halo and part != 1:
            outside = at < 0 if part == 0 else at >= blocks
            over_even = tok % 2 == (1 if part == 0 else 0)
            copies.append((outside & over_even, pltpu.make_async_copy(even_ref, target, sem)))
            copies.append((outside & jnp.logical_not(over_even), pltpu.make_async_copy(odd_ref, target, sem)))
    for needed, copy in copies:
        pl.when(needed)(copy.start)
    bias_ref[...] = window_bias((tok * blocks + block) * count, count, starts_ref[...], ends_ref[...])

    def query_of(flip, is_inner_one):
        if flip == 2:
            return query1_ref[...]
        if flip == 3 and not is_inner_one:
            return query2_ref[...]
        slot = min(flip, 2)
        return query0_ref[slot * count : (slot + 1) * count]

    query = jnp.where(inner, query_of(flips[1], True), query_of(flips[0], False))
    for needed, copy in copies:
        pl.when(needed)(copy.wait)
    attend(query, window_ref, bias_ref, scores_ref, weights_ref, out_ref)


def attend_block(place, starts, ends, projected, flips, name, halo=(), earlier=(), spare=0):
    rows, heads_width = projected[-2].shape
    return pl.pallas_call(
        functools.partial(attend_kernel, flips, bool(halo), bool(earlier)),
        out_shape=jax.ShapeDtypeStruct(((1 + len(earlier)) * rows + spare, heads_width), BF16),
        in_specs=[SMEM, VMEM, VMEM] + [VMEM, ANY] * 3 + [ANY] * len(halo) + [VMEM] * len(earlier),
        out_specs=VMEM,
        scratch_shapes=[
            pltpu.VMEM((3 * rows, 2 * heads_width), BF16),
            pltpu.VMEM((rows, 3 * rows), F32),
            pltpu.VMEM((heads_width // HD, rows, 3 * rows), F32),
            pltpu.VMEM((heads_width // HD, rows, 3 * rows), BF16),
            pltpu.SemaphoreType.DMA((3,)),
        ],
        compiler_params=pltpu.CompilerParams(vmem_limit_bytes=12 * MIB),
        cost_estimate=SHORT,
        name=name,
    )(place, starts, ends, *projected, *halo, *earlier)


def first_norm_kernel(layout, place_ref, own_ref, partner_ref, own_out_ref, gain_ref, bias_ref, *refs):
    parts, pieces = refs[:4], refs[4 : 4 + len(layout)]
    normed_ref, away_ref, all_ref, weight_ref, mixed_ref, sems = refs[4 + len(layout) :]
    tok, kv = place_ref[0], place_ref[1]
    quarters, heads_width, width = weight_ref.shape
    count = own_ref.shape[0]
    copies = [pltpu.make_async_copy(own_out_ref, weight_ref.at[0], sems.at[0])]
    for flips, piece in zip(layout, pieces):
        for index, flip in enumerate(flips):
            depth = piece.shape[2]
            at = pl.multiple_of((tok ^ flip) * depth, depth)
            target = weight_ref.at[1:quarters, pl.ds(at, depth)]
            copies.append(pltpu.make_async_copy(piece.at[index], target, sems.at[len(copies)]))
    for copy in copies:
        copy.start()
    early = jnp.where(is_inner(kv), 0, 1)
    for flip, part_ref in enumerate(parts):
        for half, place in enumerate((early, 1 - early)):
            at = pl.ds(pl.multiple_of(place * count, count), count)
            columns = slice(flip * heads_width, (flip + 1) * heads_width)
            all_ref[at, columns] = part_ref[half * count : (half + 1) * count]
    for copy in copies:
        copy.wait()
    weight = weight_ref[...].reshape(quarters * heads_width, width)
    mixed_ref[...] = jnp.dot(all_ref[...], weight, preferred_element_type=F32)
    for half, (hidden_ref, result_ref) in enumerate(((own_ref, normed_ref), (partner_ref, away_ref))):
        for row in range(0, count, STRIP):
            at = slice(row, row + STRIP)
            mixed = hidden_ref[at].astype(F32) + mixed_ref[half * count + row : half * count + row + STRIP]
            result_ref[at] = normalized(mixed, gain_ref[...], bias_ref[...]).astype(BF16)


def first_norm(place, own, partner, own_out, gain, bias, parts, pieces):
    rows, width = own.shape
    heads_width = own_out.shape[0]
    layout = tuple(flips for flips, _ in pieces)
    return pl.pallas_call(
        functools.partial(first_norm_kernel, layout),
        out_shape=(jax.ShapeDtypeStruct((rows, width), BF16),) * 2,
        in_specs=[SMEM, VMEM, VMEM, ANY, VMEM, VMEM] + [VMEM] * len(parts) + [ANY] * len(pieces),
        out_specs=(VMEM,) * 2,
        scratch_shapes=[
            pltpu.VMEM((2 * rows, width), BF16),
            pltpu.VMEM((width // heads_width, heads_width, width), BF16),
            pltpu.VMEM((2 * rows, width), F32),
            pltpu.SemaphoreType.DMA((1 + sum(len(flips) for flips in layout),)),
        ],
        compiler_params=pltpu.CompilerParams(vmem_limit_bytes=14 * MIB),
        cost_estimate=SHORT,
        name="first_norm",
    )(place, own, partner, own_out, gain, bias, *parts, *[value for _, value in pieces])


def gelu(values):
    return 0.5 * values * (1.0 + lax.erf(values * math.sqrt(0.5)))


CHUNK = 512


def feed_chunk(rows, up, down_ref, wide_ref, units_ref):
    wide_ref[...] = jnp.dot(rows, up, preferred_element_type=F32)
    for row in range(0, rows.shape[0], STRIP):
        strip = slice(row, row + STRIP)
        units_ref[strip] = gelu(wide_ref[strip]).astype(BF16)
    return jnp.dot(units_ref[...], down_ref[...], preferred_element_type=F32)


def far_copies(tok, pieces, up_ref, down_ref, sems):
    block = 128
    copies = []
    for target, sides in ((up_ref, pieces[:2]), (down_ref, pieces[2:])):
        for side, piece in enumerate(sides):
            for index in range(4):
                at = pl.ds(pl.multiple_of((tok ^ (2 * index + side)) * block, block), block)
                source = piece.at[pl.ds(index * block, block)]
                copies.append(pltpu.make_async_copy(source, target.at[at], sems.at[len(copies)]))
    return copies


def feed_kernel(place_ref, rows_ref, up_near_ref, down_near_ref, *refs):
    pieces, (sum_ref, up_ref, down_ref, wide_ref, units_ref, total_ref, sems) = refs[:4], refs[4:]
    copies = far_copies(place_ref[0], pieces, up_ref, down_ref, sems)
    for copy in copies:
        copy.start()
    rows = rows_ref[...]
    chunks = up_ref.shape[1] // CHUNK
    for index in range(2 * chunks):
        if index == chunks:
            for copy in copies:
                copy.wait()
        up, down = (up_near_ref, down_near_ref) if index < chunks else (up_ref, down_ref)
        at = slice(index % chunks * CHUNK, (index % chunks + 1) * CHUNK)
        product = feed_chunk(rows, up[:, at], down.at[at], wide_ref.at[index % 2], units_ref.at[index % 2])
        if index == 0:
            total_ref[...] = product
        elif index < 2 * chunks - 1:
            total_ref[...] += product
        else:
            sum_ref[...] = (total_ref[...] + product).astype(sum_ref.dtype)


def feed(place, rows, up_weight, down_weight, pieces, dtype, name):
    count, width = rows.shape
    units = up_weight.shape[1]
    return pl.pallas_call(
        feed_kernel,
        out_shape=jax.ShapeDtypeStruct((count, width), dtype),
        in_specs=[SMEM] + [VMEM] * 3 + [ANY] * len(pieces),
        out_specs=VMEM,
        scratch_shapes=[
            pltpu.VMEM((width, units), BF16),
            pltpu.VMEM((units, width), BF16),
            pltpu.VMEM((2, count, CHUNK), F32),
            pltpu.VMEM((2, count, CHUNK), BF16),
            pltpu.VMEM((count, width), F32),
            pltpu.SemaphoreType.DMA((16,)),
        ],
        compiler_params=pltpu.CompilerParams(vmem_limit_bytes=18 * MIB),
        cost_estimate=SHORT,
        name=name,
    )(place, rows, up_weight, down_weight, *pieces)


def finish_kernel(normed_ref, near_ref, far_ref, gain_ref, bias_ref, out_ref):
    for row in range(0, normed_ref.shape[0], STRIP):
        at = slice(row, row + STRIP)
        mixed = normed_ref[at].astype(F32) + near_ref[at] + far_ref[at].astype(F32)
        out_ref[at] = normalized(mixed, gain_ref[...], bias_ref[...]).astype(out_ref.dtype)


def finish(normed, near, far, gain, bias):
    return pl.pallas_call(
        finish_kernel,
        out_shape=jax.ShapeDtypeStruct(normed.shape, BF16),
        in_specs=[VMEM] * 5,
        out_specs=VMEM,
        compiler_params=pltpu.CompilerParams(vmem_limit_bytes=6 * MIB),
        name="finish",
    )(normed, near, far, gain, bias)


def decode_kernel(slot_ref, filled_ref, query_ref, cache_ref, out_ref, high_ref, total_ref, sum_ref):
    step = pl.program_id(0)

    @pl.when(step == 0)
    def _():
        high_ref[...] = jnp.full(high_ref.shape, NEG_FILL, F32)
        total_ref[...] = jnp.zeros_like(total_ref)
        sum_ref[...] = jnp.zeros_like(sum_ref)

    row = slot_ref[step]
    filled = filled_ref[step]
    width = query_ref.shape[1]
    head = lax.broadcasted_iota(jnp.int32, (H, width), 0)
    inside = head == lax.broadcasted_iota(jnp.int32, (H, width), 1) // HD
    query = jnp.where(inside, query_ref[pl.ds(row, 1), :], 0.0).astype(BF16)
    scores = lax.dot_general(query, cache_ref[0, 0, 0], (((1,), (1,)), ((), ())), preferred_element_type=F32)
    live = lax.broadcasted_iota(jnp.int32, scores.shape, 1) < filled
    scores = jnp.where(live, scores * (1.0 / math.sqrt(HD)), NEG_FILL)
    high = jnp.max(scores, axis=1, keepdims=True)
    weights = jnp.where(live, jnp.exp(scores - high), 0.0)
    total = jnp.sum(weights, axis=1, keepdims=True)
    summed = jnp.dot(weights.astype(BF16), cache_ref[1, 0, 0], preferred_element_type=F32)
    along = lambda column: jnp.sum(jnp.where(inside, column, 0.0), axis=0, keepdims=True)
    high, total, summed = along(high), along(total), along(summed)
    used = filled > 0
    at = pl.ds(row, 1)
    old = high_ref[at, :]
    new = jnp.where(used, jnp.maximum(old, high), old)
    left = jnp.exp(old - new)
    right = jnp.where(used, jnp.exp(high - new), 0.0)
    high_ref[at, :] = new
    total_ref[at, :] = total_ref[at, :] * left + total * right
    sum_ref[at, :] = sum_ref[at, :] * left + summed * right

    @pl.when(step == pl.num_programs(0) - 1)
    def _():
        out_ref[0] = high_ref[...]
        out_ref[1] = total_ref[...]
        out_ref[2] = sum_ref[...]


def decode(slots, filled, queries, kv_cache):
    requests, width = queries.shape
    pieces = kv_cache.shape[2]
    state = pltpu.VMEM((requests, width), F32)
    return pl.pallas_call(
        decode_kernel,
        grid=(pieces,),
        out_shape=jax.ShapeDtypeStruct((3, requests, width), F32),
        in_specs=[
            SMEM,
            SMEM,
            pl.BlockSpec((requests, width), lambda i: (0, 0)),
            pl.BlockSpec((2, 1, 1, PLEN, width), lambda i: (0, 0, i, 0, 0)),
        ],
        out_specs=pl.BlockSpec((3, requests, width), lambda i: (0, 0, 0)),
        scratch_shapes=[state, state, state],
        compiler_params=pltpu.CompilerParams(vmem_limit_bytes=8 * MIB),
        cost_estimate=SHORT,
        name="decode",
    )(slots, filled, queries, kv_cache)


def decode_partial(queries, own, kv_cache, piece_req, piece_used):
    owners = piece_req[0]
    slots = ((owners // own) ^ lax.axis_index("kv")) * own + owners % own
    return decode(slots, piece_used[0], queries, kv_cache)


def exchanged_partials(partial, own):
    parts = [partial[:, :own]]
    for flip in range(1, lax.axis_size("kv")):
        parts.append(swapped(partial[:, flip * own : (flip + 1) * own], "kv", flip))
    return parts


def merged_partials(parts):
    high = functools.reduce(jnp.maximum, [part[0] for part in parts])
    factors = [jnp.exp(part[0] - high) for part in parts]
    total = sum(part[1] * factor for part, factor in zip(parts, factors))
    summed = sum(part[2] * factor for part, factor in zip(parts, factors))
    return (summed / total).astype(BF16)


def routed_body(
    hidden_in,
    qkv_weight,
    stretch_len,
    out_weight,
    ln1_gain,
    ln1_bias,
    up_weight,
    down_weight,
    ln2_gain,
    ln2_bias,
    dec_query,
    kv_cache,
    piece_req,
    piece_used,
):
    tok = lax.axis_index("tok")
    kv = lax.axis_index("kv")
    toks, kvs = lax.axis_size("tok"), lax.axis_size("kv")
    rows, width = hidden_in.shape
    heads_width = out_weight.shape[0]
    place = jnp.stack([tok, kv]).astype(jnp.int32)
    eighth = lambda value: lax.dynamic_slice_in_dim(value, tok * (value.shape[0] // toks), value.shape[0] // toks, 0)

    outward = [(1, 0), (2, 3)]
    a1, b1 = over_edges(hidden_in, "kv", 0), over_edges(hidden_in, "kv", 1)
    out_part = eighth(out_weight)
    depth = out_part.shape[0]
    small = jnp.concatenate([out_part, dec_query], axis=0)
    others = [swapped(small, "kv", flip) for flip in range(1, kvs)]
    a2, b2 = lax.ppermute(b1, "kv", outward), over_edges(a1, "kv", 1)
    out_here = after(jnp.stack([other[:depth] for other in others]), b2)
    out_x, out_y = swapped(out_here, "tok", 2), swapped(out_here, "tok", 4)
    weight = jnp.transpose(qkv_weight, (1, 0, 2))
    sizes = (width, heads_width)
    first = project_call(
        project_first_kernel, "project_first", 3 * rows, *sizes, (weight, hidden_in, a1, b1), 0, [pltpu.VMEM((3 * rows, width), BF16)]
    )
    a3 = lax.ppermute(after(b2, a2, first[0]), "kv", outward)
    second = project_call(project_second_kernel, "project_second", rows, *sizes, (place, weight, a2, b2))
    out_far = swapped(out_y, "tok", 2)

    order = jnp.arange(stretch_len.shape[0])
    ends = jnp.sum(jnp.where(order[:, None] <= order[None, :], stretch_len[:, None], 0), axis=0, dtype=jnp.int32)
    starts = (ends - stretch_len)[None, :]
    ends = ends[None, :]

    up_here = swapped(after(eighth(up_weight), a3), "kv", 2)
    down_here = swapped(after(eighth(down_weight), a3), "kv", 2)

    *last, even, odd = project_call(
        project_last_kernel, "project_last", rows, *sizes, (place, weight, first[1], second[1], a3), 2
    )
    halo = over_edges(even, "tok", 0), over_edges(odd, "tok", 1)
    projected = (*first, *second, *last)
    two = attend_block(after(place, halo[0]), starts, ends, projected, (2, 3), "attend_two")
    up_late = after(up_here, two)
    up_x, up_y = swapped(up_late, "tok", 2), swapped(up_late, "tok", 4)
    out_all = jnp.stack([out_here, out_x, out_y, out_far])
    out_core = swapped(out_all, "tok", 1)
    queries = jnp.concatenate([dec_query] + [other[depth:] for other in others], axis=0)
    queries = after(queries, two).astype(F32)
    partial = decode_partial(queries, dec_query.shape[0], kv_cache, piece_req, piece_used)
    far = attend_block(after(place, up_late, out_core, partial), starts, ends, projected, (3, 2), "attend_far", halo, (two,), 32)
    far_there = swapped(far, "kv", 2)
    one = attend_block(after(place, far), starts, ends, projected, (1, 0), "attend_one")
    near = attend_block(after(place, one, down_here, up_x, up_y), starts, ends, projected, (0, 1), "attend_near", halo, (one,), 16)
    near_there = swapped(near, "kv", 1)
    down_late = after(down_here, near)
    down_x, down_y = swapped(down_late, "tok", 2), swapped(down_late, "tok", 4)
    far_passed = swapped(far_there, "kv", 1)
    parts = (near, near_there, far_there, far_passed)
    out_pieces = [((0, 2, 4, 6), out_all), ((1, 3, 5, 7), out_core)]
    up_far = swapped(after(up_y, near_there, far_there), "tok", 2)
    down_far = swapped(after(down_x, near_there, far_there), "tok", 4)
    up_held = jnp.concatenate([up_late, up_x, up_y, up_far], axis=0)
    down_held = jnp.concatenate([down_late, down_x, down_y, down_far], axis=0)
    up_core = swapped(after(up_held, near_there), "tok", 1)
    down_core = swapped(after(down_held, far_passed), "tok", 1)
    feed_pieces = (up_held, up_core, down_held, down_core)

    gain, bias = ln1_gain[None, :], ln1_bias[None, :]
    normed, partner = first_norm(place, hidden_in, a1, out_weight, gain, bias, parts, out_pieces)
    away = feed(place, partner, up_weight, down_weight, feed_pieces, BF16, "feed_partner")
    arrived = swapped(away, "kv", 1)
    dec_parts = exchanged_partials(after(partial, away), dec_query.shape[0])
    mine = feed(place, after(normed, away), up_weight, down_weight, feed_pieces, F32, "feed_own")
    prefill_out = finish(normed, mine, arrived, ln2_gain[None, :], ln2_bias[None, :])

    return prefill_out, merged_partials(after(tuple(dec_parts), mine))


def extended(value, sides, width):
    for axis, dim in sides:
        count, length = (lax.axis_size(axis), value.shape[dim])
        up = [(i, (i + 1) % count) for i in range(count - 1)]
        down = [(j, i) for i, j in up]
        last = lax.slice_in_dim(value, length - width, length, axis=dim)
        leading = lax.slice_in_dim(value, 0, width, axis=dim)
        before = lax.ppermute(last, axis, up)
        after = lax.ppermute(leading, axis, down)
        value = jnp.concatenate([before, value, after], axis=dim)
    return value


def merged(value, axis, join):
    pieces = jax.tree.map(lambda part: lax.all_gather(part, axis), value)
    head = jax.tree.map(lambda part: part[0], pieces)
    tail = jax.tree.map(lambda part: part[1:], pieces)
    subtotal, _ = lax.scan(lambda subtotal, section: (join(subtotal, section), None), head, tail)
    return subtotal


def segment_ids(row_ids, stretch_len):
    stretch_ends = jnp.cumsum(stretch_len)
    return jnp.sum((row_ids[:, None] >= stretch_ends[None, :]).astype(jnp.int32), axis=1)


def layer_norm(values, gain, bias):
    center = values - jnp.mean(values, axis=1, keepdims=True)
    spread = jnp.mean(center * center, axis=1, keepdims=True)
    return center * lax.rsqrt(spread + LN_EPS) * gain + bias


def merge_partials(earlier, later):
    highest = jnp.maximum(earlier[0], later[0])
    left_factor = jnp.exp(earlier[0] - highest)
    right_factor = jnp.exp(later[0] - highest)
    totals = earlier[1] * left_factor + later[1] * right_factor
    weighted = earlier[2] * left_factor[..., None] + later[2] * right_factor[..., None]
    return (highest, totals, weighted)


def row_folder(source, shard_rows):
    return jnp.dot(source, shard_rows, preferred_element_type=jnp.float32)


def general_body(
    hidden_in,
    qkv_weight,
    stretch_len,
    out_weight,
    ln1_gain,
    ln1_bias,
    up_weight,
    down_weight,
    ln2_gain,
    ln2_bias,
    dec_query,
    kv_cache,
    piece_req,
    piece_used,
):
    inv_scale = 1.0 / math.sqrt(HD)
    reach = WIN // 2
    local_width = qkv_weight.shape[2]
    head_count = local_width // HD
    flat_weight = qkv_weight.reshape(qkv_weight.shape[0], 3 * local_width)
    qkv_rows = jnp.dot(
        lax.all_gather(hidden_in, "kv", axis=0, tiled=True),
        flat_weight,
        preferred_element_type=jnp.float32,
    ).astype(jnp.bfloat16)
    row_count = qkv_rows.shape[0]
    query_rows = qkv_rows[:, :local_width]
    keyval_rows = qkv_rows[:, local_width:]
    padded = extended(keyval_rows, (("tok", 0),), reach)
    first_row = lax.axis_index("tok") * row_count
    total_rows = row_count * lax.axis_size("tok")
    qblock = min(512, row_count)
    span = qblock + 2 * reach
    block_count = row_count // qblock

    def attend(block_index):
        start = block_index * qblock
        query_ids = first_row + start + jnp.arange(qblock, dtype=jnp.int32)
        key_ids = first_row + start - reach + jnp.arange(span, dtype=jnp.int32)
        query_seg = segment_ids(query_ids, stretch_len)
        inside = (key_ids >= 0) & (key_ids < total_rows)
        key_seg = jnp.where(inside, segment_ids(key_ids, stretch_len), -1)
        allowed = (key_seg[None, :] == query_seg[:, None]) & (
            jnp.abs(key_ids[None, :] - query_ids[:, None]) <= reach
        )
        queries = lax.dynamic_slice_in_dim(query_rows, start, qblock, 0).reshape(
            qblock, head_count, HD
        )
        both = lax.dynamic_slice_in_dim(padded, start, span, 0)
        key_rows = both[:, :local_width].reshape(span, head_count, HD)
        value_rows = both[:, local_width:].reshape(span, head_count, HD)
        scores = (
            jnp.einsum("ihd,jhd->hij", queries, key_rows, preferred_element_type=jnp.float32)
            * inv_scale
        )
        scores = jnp.where(allowed[None], scores, NEG_FILL)
        row_max = jnp.max(scores, axis=2, keepdims=True)
        weights = jnp.where(allowed[None], jnp.exp(scores - row_max), 0.0)
        totals = jnp.sum(weights, axis=2)
        summed = jnp.einsum(
            "hij,jhd->ihd",
            weights.astype(jnp.bfloat16),
            value_rows,
            preferred_element_type=jnp.float32,
        )
        return (
            (summed / jnp.transpose(totals)[:, :, None])
            .astype(jnp.bfloat16)
            .reshape(qblock, local_width)
        )

    attention = lax.map(attend, jnp.arange(block_count, dtype=jnp.int32)).reshape(
        row_count, local_width
    )
    token_major = lax.all_to_all(attention, "kv", split_axis=0, concat_axis=1, tiled=True)
    projected = row_folder(token_major, lax.all_gather(out_weight, "kv", axis=0, tiled=True))
    normed = layer_norm(hidden_in.astype(jnp.float32) + projected, ln1_gain, ln1_bias).astype(
        jnp.bfloat16
    )
    units = jax.nn.gelu(
        jnp.dot(
            lax.all_gather(normed, "kv", axis=0, tiled=True),
            up_weight,
            preferred_element_type=jnp.float32,
        ),
        approximate=False,
    ).astype(jnp.bfloat16)
    ffn = lax.psum_scatter(
        jnp.dot(units, down_weight, preferred_element_type=jnp.float32).astype(jnp.bfloat16),
        "kv",
        scatter_dimension=0,
        tiled=True,
    ).astype(jnp.float32)
    prefill_out = layer_norm(normed.astype(jnp.float32) + ffn, ln2_gain, ln2_bias).astype(
        jnp.bfloat16
    )
    group_queries = lax.all_gather(dec_query, "kv", axis=0, tiled=True)
    request_count = group_queries.shape[0]
    owners = piece_req[0]
    filled = piece_used[0]
    slot_count = owners.shape[0]
    request_ids = jnp.arange(request_count, dtype=jnp.int32)
    selector = (owners[:, None] == request_ids[None, :]).astype(jnp.bfloat16)
    chosen = jnp.dot(selector, group_queries, preferred_element_type=jnp.float32).astype(
        jnp.bfloat16
    )
    chosen = chosen.reshape(slot_count, H, HD)
    cache_keys = kv_cache[0, 0].reshape(slot_count, PLEN, H, HD)
    cache_values = kv_cache[1, 0].reshape(slot_count, PLEN, H, HD)
    piece_scores = (
        jnp.einsum("phd,pthd->pht", chosen, cache_keys, preferred_element_type=jnp.float32)
        * inv_scale
    )
    active = jnp.arange(PLEN, dtype=jnp.int32)[None, :] < filled[:, None]
    piece_scores = jnp.where(active[:, None, :], piece_scores, NEG_FILL)
    piece_max = jnp.max(piece_scores, axis=2)
    piece_weights = jnp.where(
        active[:, None, :], jnp.exp(piece_scores - piece_max[:, :, None]), 0.0
    )
    piece_totals = jnp.sum(piece_weights, axis=2)
    partial_value = jnp.einsum(
        "pht,pthd->phd",
        piece_weights.astype(jnp.bfloat16),
        cache_values,
        preferred_element_type=jnp.float32,
    )
    member = (owners[None, :] == request_ids[:, None]) & (filled[None, :] > 0)
    highest = jnp.max(jnp.where(member[:, :, None], piece_max[None], NEG_FILL), axis=1)
    factor = jnp.where(member[:, :, None], jnp.exp(piece_max[None] - highest[:, None, :]), 0.0)
    denom = jnp.sum(factor * piece_totals[None], axis=1)
    weighted = jnp.einsum("rph,phd->rhd", factor, partial_value)
    own_requests = dec_query.shape[0]
    joined = merged((highest, denom, weighted), "kv", merge_partials)
    begin = lax.axis_index("kv") * own_requests
    final_denom = lax.dynamic_slice_in_dim(joined[1], begin, own_requests, 0)
    final_weighted = lax.dynamic_slice_in_dim(joined[2], begin, own_requests, 0)
    dec_out = (
        (final_weighted / final_denom[:, :, None])
        .astype(jnp.bfloat16)
        .reshape(own_requests, H * HD)
    )
    return (prefill_out, dec_out)


def solution(mesh):
    placed = (
        P(("tok", "kv"), None),
        P(None, None, "kv"),
        P(),
        P("kv", None),
        P(),
        P(),
        P(None, "kv"),
        P("kv", None),
        P(),
        P(),
        P(("tok", "kv"), None),
        P(None, "tok", "kv", None, None),
        P("tok", "kv"),
        P("tok", "kv"),
    )
    routed = mesh.shape["tok"] == 8 and mesh.shape["kv"] == 4
    return jax.shard_map(
        routed_body if routed else general_body,
        mesh=mesh,
        in_specs=placed,
        out_specs=(P(("tok", "kv"), None), P(("tok", "kv"), None)),
        check_vma=False,
    )
```

```python
import functools
import math

import jax
import jax.numpy as jnp
from jax import lax
from jax.experimental import pallas as pl
from jax.experimental.pallas import tpu as pltpu
from jax.sharding import PartitionSpec as P

H = 16
HD = 64
WIN = 512
PLEN = 128


NEG_FILL = -1e30
LN_EPS = 1e-05
BF16 = jnp.bfloat16
F32 = jnp.float32
STRIP = 32
MIB = 1024 * 1024
ANY = pl.BlockSpec(memory_space=pl.ANY)
VMEM = pl.BlockSpec(memory_space=pltpu.VMEM)
SMEM = pl.BlockSpec(memory_space=pltpu.SMEM)
SHORT = pl.CostEstimate(flops=1, bytes_accessed=1, transcendentals=0)


def swapped(value, axis, flip):
    count = lax.axis_size(axis)
    return lax.ppermute(value, axis, [(i, i ^ flip) for i in range(count)])


def over_edges(value, axis, first):
    count = lax.axis_size(axis)
    edges = [(i, i + 1) for i in range(first, count - 1, 2)]
    return lax.ppermute(value, axis, edges + [(j, i) for i, j in edges])


def after(value, *earlier):
    return lax.optimization_barrier((value,) + earlier)[0]


def normalized(values, gain, bias):
    center = values - jnp.mean(values, axis=1, keepdims=True)
    spread = jnp.mean(center * center, axis=1, keepdims=True)
    return center * lax.rsqrt(spread + LN_EPS) * gain + bias


def project_rows(rows, weight_ref, query_ref, keyval_ref):
    width = weight_ref.shape[2]
    query = jnp.dot(rows, weight_ref[0], preferred_element_type=F32) * (1.0 / math.sqrt(HD))
    query_ref[...] = query.astype(BF16)
    for part in range(2):
        at = slice(part * width, (part + 1) * width)
        keyval_ref[:, at] = jnp.dot(rows, weight_ref[part + 1], preferred_element_type=F32).astype(BF16)


def is_inner(kv):
    return (kv == 1) | (kv == 2)


def project_first_kernel(weight_ref, own_ref, a1_ref, b1_ref, query_ref, keyval_ref, rows_ref):
    count = own_ref.shape[0]
    for index, source in enumerate((own_ref, a1_ref, b1_ref)):
        rows_ref[index * count : (index + 1) * count] = source[...]
    project_rows(rows_ref[...], weight_ref, query_ref, keyval_ref)


def project_second_kernel(place_ref, weight_ref, a2_ref, b2_ref, query_ref, keyval_ref):
    rows = jnp.where(is_inner(place_ref[1]), b2_ref[...], a2_ref[...])
    project_rows(rows, weight_ref, query_ref, keyval_ref)


def project_last_kernel(place_ref, weight_ref, first_ref, second_ref, a3_ref, query_ref, last_ref, even_ref, odd_ref):
    tok, kv = place_ref[0], place_ref[1]
    count = a3_ref.shape[0]
    project_rows(a3_ref[...], weight_ref, query_ref, last_ref)
    inner = is_inner(kv)
    close = jnp.where(inner, first_ref[count : 2 * count], first_ref[:count])
    other = jnp.where(inner, second_ref[...], last_ref[...])
    low, even_tok = kv < 2, tok % 2 == 0
    top, bottom = jnp.where(low, close, other), jnp.where(low, other, close)
    even_ref[...] = jnp.where(even_tok, bottom, top)
    odd_ref[...] = jnp.where(even_tok, top, bottom)


def project_call(kernel, name, rows, width, heads_width, operands, extra=0, scratch=()):
    keyval = lambda count: jax.ShapeDtypeStruct((count, 2 * heads_width), BF16)
    edge = operands[-1].shape[0]
    return pl.pallas_call(
        kernel,
        out_shape=(jax.ShapeDtypeStruct((rows, heads_width), BF16), keyval(rows)) + (keyval(edge),) * extra,
        in_specs=[SMEM if operand.ndim == 1 else VMEM for operand in operands],
        out_specs=(VMEM,) * (2 + extra),
        scratch_shapes=list(scratch),
        compiler_params=pltpu.CompilerParams(vmem_limit_bytes=10 * MIB),
        cost_estimate=SHORT,
        name=name,
    )(*operands)


def window_bias(first, count, starts, ends):
    reach = WIN // 2
    query = first + lax.broadcasted_iota(jnp.int32, (count, 1), 0)
    low = jnp.max(jnp.where(starts <= query, starts, 0), axis=1, keepdims=True)
    high = jnp.min(jnp.where(ends > query, ends, 1 << 30), axis=1, keepdims=True)
    low = jnp.maximum(low, query - reach)
    high = jnp.minimum(high, query + reach + 1)
    key = first - count + lax.broadcasted_iota(jnp.int32, (count, 3 * count), 1)
    return jnp.where((key >= low) & (key < high), 0.0, NEG_FILL)


def attend(query, keyval_ref, bias_ref, scores_ref, weights_ref, out_ref):
    count, width = query.shape
    lane = lax.broadcasted_iota(jnp.int32, (count, 2 * HD), 1)
    for start in range(0, width, 2 * HD):
        values = keyval_ref[:, width + start : width + start + 2 * HD]
        halves = []
        for side in range(2):
            head = start // HD + side
            inside = (lane < HD) if side == 0 else (lane >= HD)
            only = jnp.where(inside, query[:, start : start + 2 * HD], jnp.zeros((), BF16))
            scores_ref[head] = lax.dot_general(
                only, keyval_ref[:, start : start + 2 * HD], (((1,), (1,)), ((), ())), preferred_element_type=F32
            )
            totals = []
            for row in range(0, count, STRIP):
                at = slice(row, row + STRIP)
                scores = scores_ref[head, at] + bias_ref[at]
                weights = jnp.exp(scores - jnp.max(scores, axis=1, keepdims=True))
                totals.append(jnp.sum(weights, axis=1, keepdims=True))
                weights_ref[head, at] = weights.astype(BF16)
            summed = jnp.dot(weights_ref[head], values, preferred_element_type=F32)
            halves.append(summed / jnp.concatenate(totals, axis=0))
        out_ref[:, start : start + 2 * HD] = jnp.where(lane < HD, halves[0], halves[1]).astype(BF16)


def attend_kernel(flips, has_halo, *refs):
    place_ref, starts_ref, ends_ref, query0_ref, keyval0_ref, query1_ref, keyval1_ref, query2_ref, keyval2_ref = refs[:9]
    even_ref, odd_ref = refs[9:11] if has_halo else (None, None)
    out_ref, window_ref, bias_ref, scores_ref, weights_ref, sems = refs[-6:]
    tok, kv = place_ref[0], place_ref[1]
    count = bias_ref.shape[0]
    blocks = 4
    if out_ref.shape[0] > count:
        out_ref[count:] = jnp.zeros_like(out_ref[count:])
        out_ref = out_ref.at[:count]
    inner = is_inner(kv)
    outer = jnp.logical_not(inner)
    block = kv ^ jnp.where(inner, flips[1], flips[0])
    copies = []
    for part in range(3):
        target = window_ref.at[part * count : (part + 1) * count]
        sem = sems.at[part]
        at = block + part - 1
        here = (at >= 0) & (at < blocks)
        flip = at ^ kv
        first = here & ((flip == 0) | (flip == 1) | (inner & (flip == 3)))
        slot = jnp.where(first, jnp.minimum(flip, 2), 0)
        source = keyval0_ref.at[pl.ds(pl.multiple_of(slot * count, count), count)]
        copies.append((first, pltpu.make_async_copy(source, target, sem)))
        copies.append((here & (flip == 2), pltpu.make_async_copy(keyval1_ref, target, sem)))
        copies.append((here & outer & (flip == 3), pltpu.make_async_copy(keyval2_ref, target, sem)))
        if has_halo and part != 1:
            outside = at < 0 if part == 0 else at >= blocks
            over_even = tok % 2 == (1 if part == 0 else 0)
            copies.append((outside & over_even, pltpu.make_async_copy(even_ref, target, sem)))
            copies.append((outside & jnp.logical_not(over_even), pltpu.make_async_copy(odd_ref, target, sem)))
    for needed, copy in copies:
        pl.when(needed)(copy.start)
    bias_ref[...] = window_bias((tok * blocks + block) * count, count, starts_ref[...], ends_ref[...])

    def query_of(flip, is_inner_one):
        if flip == 2:
            return query1_ref[...]
        if flip == 3 and not is_inner_one:
            return query2_ref[...]
        slot = min(flip, 2)
        return query0_ref[slot * count : (slot + 1) * count]

    query = jnp.where(inner, query_of(flips[1], True), query_of(flips[0], False))
    for needed, copy in copies:
        pl.when(needed)(copy.wait)
    attend(query, window_ref, bias_ref, scores_ref, weights_ref, out_ref)


def attend_block(place, starts, ends, projected, flips, name, halo=(), spare=0):
    rows, heads_width = projected[-2].shape
    return pl.pallas_call(
        functools.partial(attend_kernel, flips, bool(halo)),
        out_shape=jax.ShapeDtypeStruct((rows + spare, heads_width), BF16),
        in_specs=[SMEM, VMEM, VMEM] + [VMEM, ANY] * 3 + [ANY] * len(halo),
        out_specs=VMEM,
        scratch_shapes=[
            pltpu.VMEM((3 * rows, 2 * heads_width), BF16),
            pltpu.VMEM((rows, 3 * rows), F32),
            pltpu.VMEM((heads_width // HD, rows, 3 * rows), F32),
            pltpu.VMEM((heads_width // HD, rows, 3 * rows), BF16),
            pltpu.SemaphoreType.DMA((3,)),
        ],
        compiler_params=pltpu.CompilerParams(vmem_limit_bytes=12 * MIB),
        cost_estimate=SHORT,
        name=name,
    )(place, starts, ends, *projected, *halo)


def first_norm_kernel(layout, place_ref, own_ref, partner_ref, own_out_ref, gain_ref, bias_ref, *refs):
    parts, pieces = refs[:8], refs[8 : 8 + len(layout)]
    normed_ref, away_ref, all_ref, weight_ref, mixed_ref, sems = refs[8 + len(layout) :]
    tok, kv = place_ref[0], place_ref[1]
    quarters, heads_width, width = weight_ref.shape
    count = own_ref.shape[0]
    copies = [pltpu.make_async_copy(own_out_ref, weight_ref.at[0], sems.at[0])]
    for flips, piece in zip(layout, pieces):
        for index, flip in enumerate(flips):
            depth = piece.shape[2]
            at = pl.multiple_of((tok ^ flip) * depth, depth)
            target = weight_ref.at[1:quarters, pl.ds(at, depth)]
            copies.append(pltpu.make_async_copy(piece.at[index], target, sems.at[len(copies)]))
    for copy in copies:
        copy.start()
    early = jnp.where(is_inner(kv), 0, 1)
    for index, part_ref in enumerate(parts):
        flip = index % 4
        half = early if index < 4 else 1 - early
        at = pl.ds(pl.multiple_of(half * count, count), count)
        all_ref[at, flip * heads_width : (flip + 1) * heads_width] = part_ref[:count]
    for copy in copies:
        copy.wait()
    weight = weight_ref[...].reshape(quarters * heads_width, width)
    mixed_ref[...] = jnp.dot(all_ref[...], weight, preferred_element_type=F32)
    for half, (hidden_ref, result_ref) in enumerate(((own_ref, normed_ref), (partner_ref, away_ref))):
        for row in range(0, count, STRIP):
            at = slice(row, row + STRIP)
            mixed = hidden_ref[at].astype(F32) + mixed_ref[half * count + row : half * count + row + STRIP]
            result_ref[at] = normalized(mixed, gain_ref[...], bias_ref[...]).astype(BF16)


def first_norm(place, own, partner, own_out, gain, bias, parts, pieces):
    rows, width = own.shape
    heads_width = own_out.shape[0]
    layout = tuple(flips for flips, _ in pieces)
    return pl.pallas_call(
        functools.partial(first_norm_kernel, layout),
        out_shape=(jax.ShapeDtypeStruct((rows, width), BF16),) * 2,
        in_specs=[SMEM, VMEM, VMEM, ANY, VMEM, VMEM] + [VMEM] * len(parts) + [ANY] * len(pieces),
        out_specs=(VMEM,) * 2,
        scratch_shapes=[
            pltpu.VMEM((2 * rows, width), BF16),
            pltpu.VMEM((width // heads_width, heads_width, width), BF16),
            pltpu.VMEM((2 * rows, width), F32),
            pltpu.SemaphoreType.DMA((1 + sum(len(flips) for flips in layout),)),
        ],
        compiler_params=pltpu.CompilerParams(vmem_limit_bytes=14 * MIB),
        cost_estimate=SHORT,
        name="first_norm",
    )(place, own, partner, own_out, gain, bias, *parts, *[value for _, value in pieces])


def gelu(values):
    return 0.5 * values * (1.0 + lax.erf(values * math.sqrt(0.5)))


CHUNK = 512


def feed_chunk(rows, up, down_ref, wide_ref, units_ref):
    wide_ref[...] = jnp.dot(rows, up, preferred_element_type=F32)
    for row in range(0, rows.shape[0], STRIP):
        strip = slice(row, row + STRIP)
        units_ref[strip] = gelu(wide_ref[strip]).astype(BF16)
    return jnp.dot(units_ref[...], down_ref[...], preferred_element_type=F32)


def far_copies(tok, held_ref, core_ref, up_ref, down_ref, sems):
    block = 128
    copies = []
    for side, piece in enumerate((held_ref, core_ref)):
        for index in range(4):
            at = pl.ds(pl.multiple_of((tok ^ (2 * index + side)) * block, block), block)
            for part, target in enumerate((up_ref, down_ref)):
                source = piece.at[pl.ds((2 * index + part) * block, block)]
                copies.append(pltpu.make_async_copy(source, target.at[at], sems.at[len(copies)]))
    return copies


def feed_kernel(place_ref, rows_ref, up_near_ref, down_near_ref, held_ref, core_ref, *refs):
    sum_ref, up_ref, down_ref, wide_ref, units_ref, total_ref, sems = refs
    copies = far_copies(place_ref[0], held_ref, core_ref, up_ref, down_ref, sems)
    for copy in copies:
        copy.start()
    rows = rows_ref[...]
    chunks = up_ref.shape[1] // CHUNK
    for index in range(2 * chunks):
        if index == chunks:
            for copy in copies:
                copy.wait()
        up, down = (up_near_ref, down_near_ref) if index < chunks else (up_ref, down_ref)
        at = slice(index % chunks * CHUNK, (index % chunks + 1) * CHUNK)
        product = feed_chunk(rows, up[:, at], down.at[at], wide_ref.at[index % 2], units_ref.at[index % 2])
        if index == 0:
            total_ref[...] = product
        elif index < 2 * chunks - 1:
            total_ref[...] += product
        else:
            sum_ref[...] = (total_ref[...] + product).astype(sum_ref.dtype)


def feed(place, rows, up_weight, down_weight, pieces, dtype, name):
    count, width = rows.shape
    units = up_weight.shape[1]
    return pl.pallas_call(
        feed_kernel,
        out_shape=jax.ShapeDtypeStruct((count, width), dtype),
        in_specs=[SMEM] + [VMEM] * 3 + [ANY] * 2,
        out_specs=VMEM,
        scratch_shapes=[
            pltpu.VMEM((width, units), BF16),
            pltpu.VMEM((units, width), BF16),
            pltpu.VMEM((2, count, CHUNK), F32),
            pltpu.VMEM((2, count, CHUNK), BF16),
            pltpu.VMEM((count, width), F32),
            pltpu.SemaphoreType.DMA((16,)),
        ],
        compiler_params=pltpu.CompilerParams(vmem_limit_bytes=18 * MIB),
        cost_estimate=SHORT,
        name=name,
    )(place, rows, up_weight, down_weight, *pieces)


def finish_kernel(normed_ref, near_ref, far_ref, gain_ref, bias_ref, out_ref):
    for row in range(0, normed_ref.shape[0], STRIP):
        at = slice(row, row + STRIP)
        mixed = normed_ref[at].astype(F32) + near_ref[at] + far_ref[at].astype(F32)
        out_ref[at] = normalized(mixed, gain_ref[...], bias_ref[...]).astype(out_ref.dtype)


def finish(normed, near, far, gain, bias):
    return pl.pallas_call(
        finish_kernel,
        out_shape=jax.ShapeDtypeStruct(normed.shape, BF16),
        in_specs=[VMEM] * 5,
        out_specs=VMEM,
        compiler_params=pltpu.CompilerParams(vmem_limit_bytes=6 * MIB),
        name="finish",
    )(normed, near, far, gain, bias)


def decode_kernel(slot_ref, filled_ref, query_ref, cache_ref, out_ref, high_ref, total_ref, sum_ref):
    step = pl.program_id(0)

    @pl.when(step == 0)
    def _():
        high_ref[...] = jnp.full(high_ref.shape, NEG_FILL, F32)
        total_ref[...] = jnp.zeros_like(total_ref)
        sum_ref[...] = jnp.zeros_like(sum_ref)

    row = slot_ref[step]
    filled = filled_ref[step]
    width = query_ref.shape[1]
    head = lax.broadcasted_iota(jnp.int32, (H, width), 0)
    inside = head == lax.broadcasted_iota(jnp.int32, (H, width), 1) // HD
    query = jnp.where(inside, query_ref[pl.ds(row, 1), :], 0.0).astype(BF16)
    scores = lax.dot_general(query, cache_ref[0, 0, 0], (((1,), (1,)), ((), ())), preferred_element_type=F32)
    live = lax.broadcasted_iota(jnp.int32, scores.shape, 1) < filled
    scores = jnp.where(live, scores * (1.0 / math.sqrt(HD)), NEG_FILL)
    high = jnp.max(scores, axis=1, keepdims=True)
    weights = jnp.where(live, jnp.exp(scores - high), 0.0)
    total = jnp.sum(weights, axis=1, keepdims=True)
    summed = jnp.dot(weights.astype(BF16), cache_ref[1, 0, 0], preferred_element_type=F32)
    along = lambda column: jnp.sum(jnp.where(inside, column, 0.0), axis=0, keepdims=True)
    high, total, summed = along(high), along(total), along(summed)
    used = filled > 0
    at = pl.ds(row, 1)
    old = high_ref[at, :]
    new = jnp.where(used, jnp.maximum(old, high), old)
    left = jnp.exp(old - new)
    right = jnp.where(used, jnp.exp(high - new), 0.0)
    high_ref[at, :] = new
    total_ref[at, :] = total_ref[at, :] * left + total * right
    sum_ref[at, :] = sum_ref[at, :] * left + summed * right

    @pl.when(step == pl.num_programs(0) - 1)
    def _():
        out_ref[0] = high_ref[...]
        out_ref[1] = total_ref[...]
        out_ref[2] = sum_ref[...]


def decode(slots, filled, queries, kv_cache):
    requests, width = queries.shape
    pieces = kv_cache.shape[2]
    state = pltpu.VMEM((requests, width), F32)
    return pl.pallas_call(
        decode_kernel,
        grid=(pieces,),
        out_shape=jax.ShapeDtypeStruct((3, requests, width), F32),
        in_specs=[
            SMEM,
            SMEM,
            pl.BlockSpec((requests, width), lambda i: (0, 0)),
            pl.BlockSpec((2, 1, 1, PLEN, width), lambda i: (0, 0, i, 0, 0)),
        ],
        out_specs=pl.BlockSpec((3, requests, width), lambda i: (0, 0, 0)),
        scratch_shapes=[state, state, state],
        compiler_params=pltpu.CompilerParams(vmem_limit_bytes=8 * MIB),
        cost_estimate=SHORT,
        name="decode",
    )(slots, filled, queries, kv_cache)


def decode_partial(queries, own, kv_cache, piece_req, piece_used):
    owners = piece_req[0]
    slots = ((owners // own) ^ lax.axis_index("kv")) * own + owners % own
    return decode(slots, piece_used[0], queries, kv_cache)


def exchanged_partials(partial, own):
    parts = [partial[:, :own]]
    for flip in range(1, lax.axis_size("kv")):
        parts.append(swapped(partial[:, flip * own : (flip + 1) * own], "kv", flip))
    return parts


def merged_partials(parts):
    high = functools.reduce(jnp.maximum, [part[0] for part in parts])
    factors = [jnp.exp(part[0] - high) for part in parts]
    total = sum(part[1] * factor for part, factor in zip(parts, factors))
    summed = sum(part[2] * factor for part, factor in zip(parts, factors))
    return (summed / total).astype(BF16)


def routed_body(
    hidden_in,
    qkv_weight,
    stretch_len,
    out_weight,
    ln1_gain,
    ln1_bias,
    up_weight,
    down_weight,
    ln2_gain,
    ln2_bias,
    dec_query,
    kv_cache,
    piece_req,
    piece_used,
):
    tok = lax.axis_index("tok")
    kv = lax.axis_index("kv")
    toks, kvs = lax.axis_size("tok"), lax.axis_size("kv")
    rows, width = hidden_in.shape
    heads_width = out_weight.shape[0]
    place = jnp.stack([tok, kv]).astype(jnp.int32)
    eighth = lambda value: lax.dynamic_slice_in_dim(value, tok * (value.shape[0] // toks), value.shape[0] // toks, 0)

    outward = [(1, 0), (2, 3)]
    a1, b1 = over_edges(hidden_in, "kv", 0), over_edges(hidden_in, "kv", 1)
    out_part = eighth(out_weight)
    depth = out_part.shape[0]
    small = jnp.concatenate([out_part, dec_query], axis=0)
    others = [swapped(small, "kv", flip) for flip in range(1, kvs)]
    a2, b2 = lax.ppermute(b1, "kv", outward), over_edges(a1, "kv", 1)
    out_here = after(jnp.stack([other[:depth] for other in others]), b2)
    out_x, out_y = swapped(out_here, "tok", 2), swapped(out_here, "tok", 4)
    weight = jnp.transpose(qkv_weight, (1, 0, 2))
    sizes = (width, heads_width)
    first = project_call(
        project_first_kernel, "project_first", 3 * rows, *sizes, (weight, hidden_in, a1, b1), 0, [pltpu.VMEM((3 * rows, width), BF16)]
    )
    a3 = lax.ppermute(after(b2, first[0]), "kv", outward)
    second = project_call(project_second_kernel, "project_second", rows, *sizes, (place, weight, a2, b2))
    out_far = swapped(out_here, "tok", 6)
    inner = (kv == 1) | (kv == 2)

    order = jnp.arange(stretch_len.shape[0])
    ends = jnp.sum(jnp.where(order[:, None] <= order[None, :], stretch_len[:, None], 0), axis=0, dtype=jnp.int32)
    starts = (ends - stretch_len)[None, :]
    ends = ends[None, :]

    feed_up, feed_down = eighth(up_weight), eighth(down_weight)
    inner_up = lax.ppermute(after(feed_up, second[0]), "kv", [(0, 2), (3, 1)])
    inner_down = lax.ppermute(after(feed_down, second[0]), "kv", [(0, 2), (3, 1)])
    feed_part = after(jnp.concatenate([feed_up, feed_down], axis=0), a3, inner_up, inner_down)
    feed_outer = lax.ppermute(feed_part, "kv", [(1, 3), (2, 0)])
    feed_inner = jnp.concatenate([inner_up, inner_down], axis=0)

    *last, even, odd = project_call(
        project_last_kernel, "project_last", rows, *sizes, (place, weight, first[1], second[1], after(a3, out_x, out_y, out_far)), 2
    )
    halo = over_edges(even, "tok", 0), over_edges(odd, "tok", 1)
    projected = (*first, *second, *last)
    two = attend_block(after(place, halo[0]), starts, ends, projected, (2, 3), "attend_two")
    two_there = swapped(two, "kv", 2)
    out_all = jnp.stack([out_here, out_x, out_y, out_far])
    out_core = swapped(out_all, "tok", 1)
    queries = jnp.concatenate([dec_query] + [other[depth:] for other in others], axis=0)
    queries = after(queries, two, *halo).astype(F32)
    partial = decode_partial(queries, dec_query.shape[0], kv_cache, piece_req, piece_used)
    feed_here = jnp.where(inner, feed_inner, after(feed_outer, partial))
    feed_x, feed_y = swapped(feed_here, "tok", 2), swapped(feed_here, "tok", 4)
    far = attend_block(after(place, feed_here, out_core, partial), starts, ends, projected, (3, 2), "attend_far", halo, 32)
    far_there = swapped(far, "kv", 2)
    two_passed = swapped(after(two_there, far), "kv", 1)
    one = attend_block(after(place, far, two_there), starts, ends, projected, (1, 0), "attend_one")
    one_there = swapped(one, "kv", 1)
    near = attend_block(after(place, one), starts, ends, projected, (0, 1), "attend_near", halo)
    near_there, far_passed = swapped(near, "kv", 1), swapped(far_there, "kv", 1)
    parts = (one, one_there, two_there, two_passed, near, near_there, far_there, far_passed)
    out_pieces = [((0, 2, 4, 6), out_all), ((1, 3, 5, 7), out_core)]
    half = feed_here.shape[0] // 2
    far_up = swapped(after(feed_y, far_there, near_there, two_passed)[:half], "tok", 2)
    far_down = swapped(after(feed_x, far_there, near_there, two_passed)[half:], "tok", 4)
    held = jnp.concatenate([feed_here, feed_x, feed_y, far_up, far_down], axis=0)
    feed_pieces = (held, swapped(after(held, far_passed, two_passed, one_there, near_there), "tok", 1))

    gain, bias = ln1_gain[None, :], ln1_bias[None, :]
    normed, partner = first_norm(place, hidden_in, a1, out_weight, gain, bias, parts, out_pieces)
    away = feed(place, partner, up_weight, down_weight, feed_pieces, BF16, "feed_partner")
    arrived = swapped(away, "kv", 1)
    dec_parts = exchanged_partials(after(partial, away), dec_query.shape[0])
    mine = feed(place, after(normed, away), up_weight, down_weight, feed_pieces, F32, "feed_own")
    prefill_out = finish(normed, mine, arrived, ln2_gain[None, :], ln2_bias[None, :])

    return prefill_out, merged_partials(after(tuple(dec_parts), mine))


def extended(value, sides, width):
    for axis, dim in sides:
        count, length = (lax.axis_size(axis), value.shape[dim])
        up = [(i, (i + 1) % count) for i in range(count - 1)]
        down = [(j, i) for i, j in up]
        last = lax.slice_in_dim(value, length - width, length, axis=dim)
        leading = lax.slice_in_dim(value, 0, width, axis=dim)
        before = lax.ppermute(last, axis, up)
        after = lax.ppermute(leading, axis, down)
        value = jnp.concatenate([before, value, after], axis=dim)
    return value


def merged(value, axis, join):
    pieces = jax.tree.map(lambda part: lax.all_gather(part, axis), value)
    head = jax.tree.map(lambda part: part[0], pieces)
    tail = jax.tree.map(lambda part: part[1:], pieces)
    subtotal, _ = lax.scan(lambda subtotal, section: (join(subtotal, section), None), head, tail)
    return subtotal


def segment_ids(row_ids, stretch_len):
    stretch_ends = jnp.cumsum(stretch_len)
    return jnp.sum((row_ids[:, None] >= stretch_ends[None, :]).astype(jnp.int32), axis=1)


def layer_norm(values, gain, bias):
    center = values - jnp.mean(values, axis=1, keepdims=True)
    spread = jnp.mean(center * center, axis=1, keepdims=True)
    return center * lax.rsqrt(spread + LN_EPS) * gain + bias


def merge_partials(earlier, later):
    highest = jnp.maximum(earlier[0], later[0])
    left_factor = jnp.exp(earlier[0] - highest)
    right_factor = jnp.exp(later[0] - highest)
    totals = earlier[1] * left_factor + later[1] * right_factor
    weighted = earlier[2] * left_factor[..., None] + later[2] * right_factor[..., None]
    return (highest, totals, weighted)


def row_folder(source, shard_rows):
    return jnp.dot(source, shard_rows, preferred_element_type=jnp.float32)


def general_body(
    hidden_in,
    qkv_weight,
    stretch_len,
    out_weight,
    ln1_gain,
    ln1_bias,
    up_weight,
    down_weight,
    ln2_gain,
    ln2_bias,
    dec_query,
    kv_cache,
    piece_req,
    piece_used,
):
    inv_scale = 1.0 / math.sqrt(HD)
    reach = WIN // 2
    local_width = qkv_weight.shape[2]
    head_count = local_width // HD
    flat_weight = qkv_weight.reshape(qkv_weight.shape[0], 3 * local_width)
    qkv_rows = jnp.dot(
        lax.all_gather(hidden_in, "kv", axis=0, tiled=True),
        flat_weight,
        preferred_element_type=jnp.float32,
    ).astype(jnp.bfloat16)
    row_count = qkv_rows.shape[0]
    query_rows = qkv_rows[:, :local_width]
    keyval_rows = qkv_rows[:, local_width:]
    padded = extended(keyval_rows, (("tok", 0),), reach)
    first_row = lax.axis_index("tok") * row_count
    total_rows = row_count * lax.axis_size("tok")
    qblock = min(512, row_count)
    span = qblock + 2 * reach
    block_count = row_count // qblock

    def attend(block_index):
        start = block_index * qblock
        query_ids = first_row + start + jnp.arange(qblock, dtype=jnp.int32)
        key_ids = first_row + start - reach + jnp.arange(span, dtype=jnp.int32)
        query_seg = segment_ids(query_ids, stretch_len)
        inside = (key_ids >= 0) & (key_ids < total_rows)
        key_seg = jnp.where(inside, segment_ids(key_ids, stretch_len), -1)
        allowed = (key_seg[None, :] == query_seg[:, None]) & (
            jnp.abs(key_ids[None, :] - query_ids[:, None]) <= reach
        )
        queries = lax.dynamic_slice_in_dim(query_rows, start, qblock, 0).reshape(
            qblock, head_count, HD
        )
        both = lax.dynamic_slice_in_dim(padded, start, span, 0)
        key_rows = both[:, :local_width].reshape(span, head_count, HD)
        value_rows = both[:, local_width:].reshape(span, head_count, HD)
        scores = (
            jnp.einsum("ihd,jhd->hij", queries, key_rows, preferred_element_type=jnp.float32)
            * inv_scale
        )
        scores = jnp.where(allowed[None], scores, NEG_FILL)
        row_max = jnp.max(scores, axis=2, keepdims=True)
        weights = jnp.where(allowed[None], jnp.exp(scores - row_max), 0.0)
        totals = jnp.sum(weights, axis=2)
        summed = jnp.einsum(
            "hij,jhd->ihd",
            weights.astype(jnp.bfloat16),
            value_rows,
            preferred_element_type=jnp.float32,
        )
        return (
            (summed / jnp.transpose(totals)[:, :, None])
            .astype(jnp.bfloat16)
            .reshape(qblock, local_width)
        )

    attention = lax.map(attend, jnp.arange(block_count, dtype=jnp.int32)).reshape(
        row_count, local_width
    )
    token_major = lax.all_to_all(attention, "kv", split_axis=0, concat_axis=1, tiled=True)
    projected = row_folder(token_major, lax.all_gather(out_weight, "kv", axis=0, tiled=True))
    normed = layer_norm(hidden_in.astype(jnp.float32) + projected, ln1_gain, ln1_bias).astype(
        jnp.bfloat16
    )
    units = jax.nn.gelu(
        jnp.dot(
            lax.all_gather(normed, "kv", axis=0, tiled=True),
            up_weight,
            preferred_element_type=jnp.float32,
        ),
        approximate=False,
    ).astype(jnp.bfloat16)
    ffn = lax.psum_scatter(
        jnp.dot(units, down_weight, preferred_element_type=jnp.float32).astype(jnp.bfloat16),
        "kv",
        scatter_dimension=0,
        tiled=True,
    ).astype(jnp.float32)
    prefill_out = layer_norm(normed.astype(jnp.float32) + ffn, ln2_gain, ln2_bias).astype(
        jnp.bfloat16
    )
    group_queries = lax.all_gather(dec_query, "kv", axis=0, tiled=True)
    request_count = group_queries.shape[0]
    owners = piece_req[0]
    filled = piece_used[0]
    slot_count = owners.shape[0]
    request_ids = jnp.arange(request_count, dtype=jnp.int32)
    selector = (owners[:, None] == request_ids[None, :]).astype(jnp.bfloat16)
    chosen = jnp.dot(selector, group_queries, preferred_element_type=jnp.float32).astype(
        jnp.bfloat16
    )
    chosen = chosen.reshape(slot_count, H, HD)
    cache_keys = kv_cache[0, 0].reshape(slot_count, PLEN, H, HD)
    cache_values = kv_cache[1, 0].reshape(slot_count, PLEN, H, HD)
    piece_scores = (
        jnp.einsum("phd,pthd->pht", chosen, cache_keys, preferred_element_type=jnp.float32)
        * inv_scale
    )
    active = jnp.arange(PLEN, dtype=jnp.int32)[None, :] < filled[:, None]
    piece_scores = jnp.where(active[:, None, :], piece_scores, NEG_FILL)
    piece_max = jnp.max(piece_scores, axis=2)
    piece_weights = jnp.where(
        active[:, None, :], jnp.exp(piece_scores - piece_max[:, :, None]), 0.0
    )
    piece_totals = jnp.sum(piece_weights, axis=2)
    partial_value = jnp.einsum(
        "pht,pthd->phd",
        piece_weights.astype(jnp.bfloat16),
        cache_values,
        preferred_element_type=jnp.float32,
    )
    member = (owners[None, :] == request_ids[:, None]) & (filled[None, :] > 0)
    highest = jnp.max(jnp.where(member[:, :, None], piece_max[None], NEG_FILL), axis=1)
    factor = jnp.where(member[:, :, None], jnp.exp(piece_max[None] - highest[:, None, :]), 0.0)
    denom = jnp.sum(factor * piece_totals[None], axis=1)
    weighted = jnp.einsum("rph,phd->rhd", factor, partial_value)
    own_requests = dec_query.shape[0]
    joined = merged((highest, denom, weighted), "kv", merge_partials)
    begin = lax.axis_index("kv") * own_requests
    final_denom = lax.dynamic_slice_in_dim(joined[1], begin, own_requests, 0)
    final_weighted = lax.dynamic_slice_in_dim(joined[2], begin, own_requests, 0)
    dec_out = (
        (final_weighted / final_denom[:, :, None])
        .astype(jnp.bfloat16)
        .reshape(own_requests, H * HD)
    )
    return (prefill_out, dec_out)


def solution(mesh):
    placed = (
        P(("tok", "kv"), None),
        P(None, None, "kv"),
        P(),
        P("kv", None),
        P(),
        P(),
        P(None, "kv"),
        P("kv", None),
        P(),
        P(),
        P(("tok", "kv"), None),
        P(None, "tok", "kv", None, None),
        P("tok", "kv"),
        P("tok", "kv"),
    )
    routed = mesh.shape["tok"] == 8 and mesh.shape["kv"] == 4
    return jax.shard_map(
        routed_body if routed else general_body,
        mesh=mesh,
        in_specs=placed,
        out_specs=(P(("tok", "kv"), None), P(("tok", "kv"), None)),
        check_vma=False,
    )
```

```python
import functools
import math

import jax
import jax.numpy as jnp
from jax import lax
from jax.experimental import pallas as pl
from jax.experimental.pallas import tpu as pltpu
from jax.sharding import PartitionSpec as P

H = 16
HD = 64
WIN = 512
PLEN = 128


NEG_FILL = -1e30
LN_EPS = 1e-05
BF16 = jnp.bfloat16
F32 = jnp.float32
STRIP = 32
MIB = 1024 * 1024
ANY = pl.BlockSpec(memory_space=pl.ANY)
VMEM = pl.BlockSpec(memory_space=pltpu.VMEM)
SMEM = pl.BlockSpec(memory_space=pltpu.SMEM)
SHORT = pl.CostEstimate(flops=1, bytes_accessed=1, transcendentals=0)


def swapped(value, axis, flip):
    count = lax.axis_size(axis)
    return lax.ppermute(value, axis, [(i, i ^ flip) for i in range(count)])


def over_edges(value, axis, first):
    count = lax.axis_size(axis)
    edges = [(i, i + 1) for i in range(first, count - 1, 2)]
    return lax.ppermute(value, axis, edges + [(j, i) for i, j in edges])


def after(value, *earlier):
    return lax.optimization_barrier((value,) + earlier)[0]


def normalized(values, gain, bias):
    center = values - jnp.mean(values, axis=1, keepdims=True)
    spread = jnp.mean(center * center, axis=1, keepdims=True)
    return center * lax.rsqrt(spread + LN_EPS) * gain + bias


def shard_copies(kv, shards, rows_ref, sems, first, step):
    own, a1, a2, a3, b1, b2 = shards
    count = own.shape[0]
    inner = (kv == 1) | (kv == 2)
    outer = jnp.logical_not(inner)
    always = kv >= 0
    sources = ((own, 0, always), (a1, 1, always), (a2, 2, outer), (b2, 2, inner), (a3, 3, outer), (b1, 3, inner))
    copies = []
    for index, (source, flip, held) in enumerate(sources):
        for slot in range(rows_ref.shape[0] // count):
            needed = held & ((kv ^ flip) == first + slot * step)
            target = rows_ref.at[slot * count : (slot + 1) * count]
            copies.append((needed, pltpu.make_async_copy(source, target, sems.at[index])))
    for needed, copy in copies:
        pl.when(needed)(copy.start)
    for needed, copy in copies:
        pl.when(needed)(copy.wait)


def keys_values(rows, weight_ref, keyval_ref):
    width = weight_ref.shape[2]
    for part in range(2):
        at = slice(part * width, (part + 1) * width)
        keyval_ref[:, at] = jnp.dot(rows, weight_ref[part + 1], preferred_element_type=F32).astype(BF16)


def project_edges_kernel(place_ref, weight_ref, *refs):
    shards, (keyval_ref, even_ref, odd_ref, rows_ref, sems) = refs[:-5], refs[-5:]
    tok, kv = place_ref[0], place_ref[1]
    count = even_ref.shape[0]
    shard_copies(kv, shards, rows_ref, sems, 0, 3)
    keys_values(rows_ref[...], weight_ref, keyval_ref)

    @pl.when(tok % 2 == 0)
    def _():
        even_ref[...] = keyval_ref[count:]
        odd_ref[...] = keyval_ref[:count]

    @pl.when(tok % 2 == 1)
    def _():
        even_ref[...] = keyval_ref[:count]
        odd_ref[...] = keyval_ref[count:]


def project_rest_kernel(place_ref, weight_ref, *refs):
    shards, (query_ref, keyval_ref, rows_ref, sems) = refs[:-4], refs[-4:]
    count = shards[0].shape[0]
    shard_copies(place_ref[1], shards, rows_ref, sems, 0, 1)
    keys_values(rows_ref[count:-count], weight_ref, keyval_ref)
    query = jnp.dot(rows_ref[...], weight_ref[0], preferred_element_type=F32) * (1.0 / math.sqrt(HD))
    query_ref[...] = query.astype(BF16)


def project(place, weight, shards, blocks, edges):
    rows, width = shards[0].shape
    heads_width = weight.shape[2]
    shape = lambda count, columns: jax.ShapeDtypeStruct((count * rows, columns), BF16)
    keyval = shape(2, 2 * heads_width)
    if edges:
        outs = (keyval, shape(1, 2 * heads_width), shape(1, 2 * heads_width))
    else:
        outs = (shape(blocks, heads_width), keyval)
    return pl.pallas_call(
        project_edges_kernel if edges else project_rest_kernel,
        out_shape=outs,
        in_specs=[SMEM, VMEM] + [ANY] * len(shards),
        out_specs=(VMEM,) * len(outs),
        scratch_shapes=[
            pltpu.VMEM((2 * rows if edges else blocks * rows, width), BF16),
            pltpu.SemaphoreType.DMA((len(shards),)),
        ],
        compiler_params=pltpu.CompilerParams(vmem_limit_bytes=12 * MIB),
        cost_estimate=SHORT,
        name="project_edges" if edges else "project_rest",
    )(place, weight, *shards)


def window_bias(first, count, starts, ends):
    reach = WIN // 2
    query = first + lax.broadcasted_iota(jnp.int32, (count, 1), 0)
    low = jnp.max(jnp.where(starts <= query, starts, 0), axis=1, keepdims=True)
    high = jnp.min(jnp.where(ends > query, ends, 1 << 30), axis=1, keepdims=True)
    low = jnp.maximum(low, query - reach)
    high = jnp.minimum(high, query + reach + 1)
    key = first - count + lax.broadcasted_iota(jnp.int32, (count, 3 * count), 1)
    return jnp.where((key >= low) & (key < high), 0.0, NEG_FILL)


def attend(query, keyval_ref, bias_ref, scores_ref, weights_ref, out_ref):
    count, width = query.shape
    lane = lax.broadcasted_iota(jnp.int32, (count, 2 * HD), 1)
    for start in range(0, width, 2 * HD):
        values = keyval_ref[:, width + start : width + start + 2 * HD]
        halves = []
        for side in range(2):
            head = start // HD + side
            inside = (lane < HD) if side == 0 else (lane >= HD)
            only = jnp.where(inside, query[:, start : start + 2 * HD], jnp.zeros((), BF16))
            scores_ref[head] = lax.dot_general(
                only, keyval_ref[:, start : start + 2 * HD], (((1,), (1,)), ((), ())), preferred_element_type=F32
            )
            totals = []
            for row in range(0, count, STRIP):
                at = slice(row, row + STRIP)
                scores = scores_ref[head, at] + bias_ref[at]
                weights = jnp.exp(scores - jnp.max(scores, axis=1, keepdims=True))
                totals.append(jnp.sum(weights, axis=1, keepdims=True))
                weights_ref[head, at] = weights.astype(BF16)
            summed = jnp.dot(weights_ref[head], values, preferred_element_type=F32)
            halves.append(summed / jnp.concatenate(totals, axis=0))
        out_ref[:, start : start + 2 * HD] = jnp.where(lane < HD, halves[0], halves[1]).astype(BF16)


def attend_kernel(flips, place_ref, starts_ref, ends_ref, query_ref, middle_ref, edges_ref, even_ref, odd_ref, *refs):
    out_ref, window_ref, bias_ref, scores_ref, weights_ref, sems = refs
    tok, kv = place_ref[0], place_ref[1]
    count = bias_ref.shape[0]
    out_ref[len(flips) * count :] = jnp.zeros_like(out_ref[len(flips) * count :])
    blocks = query_ref.shape[0] // count
    copies = []
    for index, flip in enumerate(flips):
        block = kv ^ flip
        for part in range(3):
            target = window_ref.at[index, part * count : (part + 1) * count]
            sem = sems.at[index, part]
            at = block + part - 1
            middle = (at > 0) & (at < blocks - 1)
            start = jnp.where(middle, at - 1, 0)
            source = middle_ref.at[pl.ds(pl.multiple_of(start * count, count), count)]
            copies.append((index, middle, pltpu.make_async_copy(source, target, sem)))
            for slot, edge in enumerate((0, blocks - 1)):
                source = edges_ref.at[slot * count : (slot + 1) * count]
                copies.append((index, at == edge, pltpu.make_async_copy(source, target, sem)))
            for first_edge, outside in ((tok % 2 == 1, at < 0), (tok % 2 == 0, at >= blocks)):
                if part != 1:
                    copies.append((index, outside & first_edge, pltpu.make_async_copy(even_ref, target, sem)))
                    other = jnp.logical_not(first_edge)
                    copies.append((index, outside & other, pltpu.make_async_copy(odd_ref, target, sem)))
    for _, needed, copy in copies:
        pl.when(needed)(copy.start)
    for index, flip in enumerate(flips):
        block = kv ^ flip
        first = (tok * blocks + block) * count
        bias_ref[...] = window_bias(first, count, starts_ref[...], ends_ref[...])
        for owner, needed, copy in copies:
            if owner == index:
                pl.when(needed)(copy.wait)
        query = query_ref[pl.ds(pl.multiple_of(block * count, count), count)]
        out = out_ref.at[index * count : (index + 1) * count]
        attend(query, window_ref.at[index], bias_ref, scores_ref, weights_ref, out)


def attend_blocks(place, starts, ends, query, middle, edges, even, odd, rows, flips, name, spare):
    heads_width = query.shape[1]
    return pl.pallas_call(
        functools.partial(attend_kernel, flips),
        out_shape=jax.ShapeDtypeStruct((len(flips) * rows + spare, heads_width), BF16),
        in_specs=[SMEM, VMEM, VMEM, VMEM, ANY, ANY, ANY, ANY],
        out_specs=VMEM,
        scratch_shapes=[
            pltpu.VMEM((len(flips), 3 * rows, 2 * heads_width), BF16),
            pltpu.VMEM((rows, 3 * rows), F32),
            pltpu.VMEM((heads_width // HD, rows, 3 * rows), F32),
            pltpu.VMEM((heads_width // HD, rows, 3 * rows), BF16),
            pltpu.SemaphoreType.DMA((len(flips), 3)),
        ],
        compiler_params=pltpu.CompilerParams(vmem_limit_bytes=14 * MIB),
        cost_estimate=SHORT,
        name=name,
    )(place, starts, ends, query, middle, edges, even, odd)


def first_norm_kernel(layout, place_ref, own_ref, partner_ref, own_out_ref, gain_ref, bias_ref, *refs):
    parts, pieces = refs[:4], refs[4 : 4 + len(layout)]
    normed_ref, away_ref, all_ref, weight_ref, mixed_ref, sems = refs[4 + len(layout) :]
    tok = place_ref[0]
    quarters, heads_width, width = weight_ref.shape
    count = own_ref.shape[0]
    copies = [pltpu.make_async_copy(own_out_ref, weight_ref.at[0], sems.at[0])]
    for flips, piece in zip(layout, pieces):
        for index, flip in enumerate(flips):
            depth = piece.shape[2]
            at = pl.multiple_of((tok ^ flip) * depth, depth)
            target = weight_ref.at[1:quarters, pl.ds(at, depth)]
            copies.append(pltpu.make_async_copy(piece.at[index], target, sems.at[len(copies)]))
    for copy in copies:
        copy.start()
    for flip, part_ref in enumerate(parts):
        columns = slice(flip * heads_width, (flip + 1) * heads_width)
        for half in range(2):
            turned = half ^ (flip % 2)
            all_ref[half * count : (half + 1) * count, columns] = part_ref[turned * count : (turned + 1) * count]
    for copy in copies:
        copy.wait()
    weight = weight_ref[...].reshape(quarters * heads_width, width)
    mixed_ref[...] = jnp.dot(all_ref[...], weight, preferred_element_type=F32)
    for half, (hidden_ref, result_ref) in enumerate(((own_ref, normed_ref), (partner_ref, away_ref))):
        for row in range(0, count, STRIP):
            at = slice(row, row + STRIP)
            mixed = hidden_ref[at].astype(F32) + mixed_ref[half * count + row : half * count + row + STRIP]
            result_ref[at] = normalized(mixed, gain_ref[...], bias_ref[...]).astype(BF16)


def first_norm(place, own, partner, own_out, gain, bias, parts, pieces):
    rows, width = own.shape
    heads_width = own_out.shape[0]
    layout = tuple(flips for flips, _ in pieces)
    return pl.pallas_call(
        functools.partial(first_norm_kernel, layout),
        out_shape=(jax.ShapeDtypeStruct((rows, width), BF16),) * 2,
        in_specs=[SMEM, VMEM, VMEM, ANY, VMEM, VMEM] + [VMEM] * len(parts) + [ANY] * len(pieces),
        out_specs=(VMEM,) * 2,
        scratch_shapes=[
            pltpu.VMEM((2 * rows, width), BF16),
            pltpu.VMEM((len(parts), heads_width, width), BF16),
            pltpu.VMEM((2 * rows, width), F32),
            pltpu.SemaphoreType.DMA((1 + sum(len(flips) for flips in layout),)),
        ],
        compiler_params=pltpu.CompilerParams(vmem_limit_bytes=14 * MIB),
        cost_estimate=SHORT,
        name="first_norm",
    )(place, own, partner, own_out, gain, bias, *parts, *[value for _, value in pieces])


def gelu(values):
    return 0.5 * values * (1.0 + lax.erf(values * math.sqrt(0.5)))


CHUNK = 512


def feed_chunk(rows, up, down_ref, wide_ref, units_ref):
    wide_ref[...] = jnp.dot(rows, up, preferred_element_type=F32)
    for row in range(0, rows.shape[0], STRIP):
        strip = slice(row, row + STRIP)
        units_ref[strip] = gelu(wide_ref[strip]).astype(BF16)
    return jnp.dot(units_ref[...], down_ref[...], preferred_element_type=F32)


def far_copies(tok, held_ref, core_ref, up_ref, down_ref, sems):
    block = 128
    copies = []
    for side, piece in enumerate((held_ref, core_ref)):
        for index in range(4):
            at = pl.ds(pl.multiple_of((tok ^ (2 * index + side)) * block, block), block)
            for part, target in enumerate((up_ref, down_ref)):
                source = piece.at[pl.ds((2 * index + part) * block, block)]
                copies.append(pltpu.make_async_copy(source, target.at[at], sems.at[len(copies)]))
    return copies


def feed_kernel(place_ref, rows_ref, up_near_ref, down_near_ref, held_ref, core_ref, *refs):
    sum_ref, up_ref, down_ref, wide_ref, units_ref, total_ref, sems = refs
    copies = far_copies(place_ref[0], held_ref, core_ref, up_ref, down_ref, sems)
    for copy in copies:
        copy.start()
    rows = rows_ref[...]
    chunks = up_ref.shape[1] // CHUNK
    for index in range(2 * chunks):
        if index == chunks:
            for copy in copies:
                copy.wait()
        up, down = (up_near_ref, down_near_ref) if index < chunks else (up_ref, down_ref)
        at = slice(index % chunks * CHUNK, (index % chunks + 1) * CHUNK)
        product = feed_chunk(rows, up[:, at], down.at[at], wide_ref.at[index % 2], units_ref.at[index % 2])
        if index == 0:
            total_ref[...] = product
        elif index < 2 * chunks - 1:
            total_ref[...] += product
        else:
            sum_ref[...] = (total_ref[...] + product).astype(sum_ref.dtype)


def feed(place, rows, up_weight, down_weight, pieces, dtype, name):
    count, width = rows.shape
    units = up_weight.shape[1]
    return pl.pallas_call(
        feed_kernel,
        out_shape=jax.ShapeDtypeStruct((count, width), dtype),
        in_specs=[SMEM] + [VMEM] * 3 + [ANY] * 2,
        out_specs=VMEM,
        scratch_shapes=[
            pltpu.VMEM((width, units), BF16),
            pltpu.VMEM((units, width), BF16),
            pltpu.VMEM((2, count, CHUNK), F32),
            pltpu.VMEM((2, count, CHUNK), BF16),
            pltpu.VMEM((count, width), F32),
            pltpu.SemaphoreType.DMA((16,)),
        ],
        compiler_params=pltpu.CompilerParams(vmem_limit_bytes=18 * MIB),
        cost_estimate=SHORT,
        name=name,
    )(place, rows, up_weight, down_weight, *pieces)


def finish_kernel(normed_ref, near_ref, far_ref, gain_ref, bias_ref, out_ref):
    for row in range(0, normed_ref.shape[0], STRIP):
        at = slice(row, row + STRIP)
        mixed = normed_ref[at].astype(F32) + near_ref[at] + far_ref[at].astype(F32)
        out_ref[at] = normalized(mixed, gain_ref[...], bias_ref[...]).astype(out_ref.dtype)


def finish(normed, near, far, gain, bias):
    return pl.pallas_call(
        finish_kernel,
        out_shape=jax.ShapeDtypeStruct(normed.shape, BF16),
        in_specs=[VMEM] * 5,
        out_specs=VMEM,
        compiler_params=pltpu.CompilerParams(vmem_limit_bytes=6 * MIB),
        name="finish",
    )(normed, near, far, gain, bias)


def decode_kernel(slot_ref, filled_ref, query_ref, cache_ref, out_ref, high_ref, total_ref, sum_ref):
    step = pl.program_id(0)

    @pl.when(step == 0)
    def _():
        high_ref[...] = jnp.full(high_ref.shape, NEG_FILL, F32)
        total_ref[...] = jnp.zeros_like(total_ref)
        sum_ref[...] = jnp.zeros_like(sum_ref)

    row = slot_ref[step]
    filled = filled_ref[step]
    width = query_ref.shape[1]
    head = lax.broadcasted_iota(jnp.int32, (H, width), 0)
    inside = head == lax.broadcasted_iota(jnp.int32, (H, width), 1) // HD
    query = jnp.where(inside, query_ref[pl.ds(row, 1), :], 0.0).astype(BF16)
    scores = lax.dot_general(query, cache_ref[0, 0, 0], (((1,), (1,)), ((), ())), preferred_element_type=F32)
    live = lax.broadcasted_iota(jnp.int32, scores.shape, 1) < filled
    scores = jnp.where(live, scores * (1.0 / math.sqrt(HD)), NEG_FILL)
    high = jnp.max(scores, axis=1, keepdims=True)
    weights = jnp.where(live, jnp.exp(scores - high), 0.0)
    total = jnp.sum(weights, axis=1, keepdims=True)
    summed = jnp.dot(weights.astype(BF16), cache_ref[1, 0, 0], preferred_element_type=F32)
    along = lambda column: jnp.sum(jnp.where(inside, column, 0.0), axis=0, keepdims=True)
    high, total, summed = along(high), along(total), along(summed)
    used = filled > 0
    at = pl.ds(row, 1)
    old = high_ref[at, :]
    new = jnp.where(used, jnp.maximum(old, high), old)
    left = jnp.exp(old - new)
    right = jnp.where(used, jnp.exp(high - new), 0.0)
    high_ref[at, :] = new
    total_ref[at, :] = total_ref[at, :] * left + total * right
    sum_ref[at, :] = sum_ref[at, :] * left + summed * right

    @pl.when(step == pl.num_programs(0) - 1)
    def _():
        out_ref[0] = high_ref[...]
        out_ref[1] = total_ref[...]
        out_ref[2] = sum_ref[...]


def decode(slots, filled, queries, kv_cache):
    requests, width = queries.shape
    pieces = kv_cache.shape[2]
    state = pltpu.VMEM((requests, width), F32)
    return pl.pallas_call(
        decode_kernel,
        grid=(pieces,),
        out_shape=jax.ShapeDtypeStruct((3, requests, width), F32),
        in_specs=[
            SMEM,
            SMEM,
            pl.BlockSpec((requests, width), lambda i: (0, 0)),
            pl.BlockSpec((2, 1, 1, PLEN, width), lambda i: (0, 0, i, 0, 0)),
        ],
        out_specs=pl.BlockSpec((3, requests, width), lambda i: (0, 0, 0)),
        scratch_shapes=[state, state, state],
        compiler_params=pltpu.CompilerParams(vmem_limit_bytes=8 * MIB),
        cost_estimate=SHORT,
        name="decode",
    )(slots, filled, queries, kv_cache)


def decode_partial(queries, own, kv_cache, piece_req, piece_used):
    owners = piece_req[0]
    slots = ((owners // own) ^ lax.axis_index("kv")) * own + owners % own
    return decode(slots, piece_used[0], queries, kv_cache)


def exchanged_partials(partial, own):
    parts = [partial[:, :own]]
    for flip in range(1, lax.axis_size("kv")):
        parts.append(swapped(partial[:, flip * own : (flip + 1) * own], "kv", flip))
    return parts


def merged_partials(parts):
    high = functools.reduce(jnp.maximum, [part[0] for part in parts])
    factors = [jnp.exp(part[0] - high) for part in parts]
    total = sum(part[1] * factor for part, factor in zip(parts, factors))
    summed = sum(part[2] * factor for part, factor in zip(parts, factors))
    return (summed / total).astype(BF16)


def routed_body(
    hidden_in,
    qkv_weight,
    stretch_len,
    out_weight,
    ln1_gain,
    ln1_bias,
    up_weight,
    down_weight,
    ln2_gain,
    ln2_bias,
    dec_query,
    kv_cache,
    piece_req,
    piece_used,
):
    tok = lax.axis_index("tok")
    kv = lax.axis_index("kv")
    toks, kvs = lax.axis_size("tok"), lax.axis_size("kv")
    rows, width = hidden_in.shape
    place = jnp.stack([tok, kv]).astype(jnp.int32)
    eighth = lambda value: lax.dynamic_slice_in_dim(value, tok * (value.shape[0] // toks), value.shape[0] // toks, 0)

    outward = [(1, 0), (2, 3)]
    a1, b1 = over_edges(hidden_in, "kv", 0), over_edges(hidden_in, "kv", 1)
    out_part = eighth(out_weight)
    depth = out_part.shape[0]
    small = jnp.concatenate([out_part, dec_query], axis=0)
    others = [swapped(small, "kv", flip) for flip in range(1, kvs)]
    a2, b2 = lax.ppermute(b1, "kv", outward), over_edges(a1, "kv", 1)
    queries = jnp.concatenate([dec_query] + [other[depth:] for other in others], axis=0).astype(F32)
    partial = decode_partial(queries, dec_query.shape[0], kv_cache, piece_req, piece_used)
    out_here = jnp.stack([other[:depth] for other in others])
    out_x, out_y = swapped(out_here, "tok", 2), swapped(out_here, "tok", 4)
    a3 = lax.ppermute(after(b2, partial), "kv", outward)
    out_far = swapped(out_here, "tok", 6)
    shards = (after(hidden_in, out_x, out_y, out_far), a1, a2, a3, b1, b2)
    inner = (kv == 1) | (kv == 2)

    feed_part = jnp.concatenate([eighth(up_weight), eighth(down_weight)], axis=0)
    feed_inner = lax.ppermute(after(feed_part, a2, b2), "kv", [(0, 2), (3, 1)])
    feed_outer = lax.ppermute(after(feed_part, a3, feed_inner), "kv", [(1, 3), (2, 0)])

    order = jnp.arange(stretch_len.shape[0])
    ends = jnp.sum(jnp.where(order[:, None] <= order[None, :], stretch_len[:, None], 0), axis=0, dtype=jnp.int32)
    starts = (ends - stretch_len)[None, :]
    ends = ends[None, :]

    weight = jnp.transpose(qkv_weight, (1, 0, 2))
    edges, even, odd = project(place, weight, shards, kvs, True)
    even, odd = over_edges(even, "tok", 0), over_edges(odd, "tok", 1)
    query, middle = project(place, weight, (after(hidden_in, edges),) + shards[1:], kvs, False)
    window = (middle, edges, even, odd, rows)
    out_all = jnp.stack([out_here, out_x, out_y, out_far])
    far = attend_blocks(place, starts, ends, query, *window, (2, 3), "attend_far", 32)
    far_heads = swapped(far, "kv", 2)
    feed_here = jnp.where(inner, feed_inner, after(feed_outer, far))
    feed_x, feed_y = swapped(feed_here, "tok", 2), swapped(feed_here, "tok", 4)
    near = attend_blocks(place, starts, ends, after(query, feed_here), *window, (0, 1), "attend_near", 16)
    partner_heads, passed_heads = swapped(near, "kv", 1), swapped(far_heads, "kv", 1)
    parts = (near, partner_heads, far_heads, passed_heads)
    out_core = swapped(after(out_all, near, far_heads), "tok", 1)
    out_pieces = [((0, 2, 4, 6), out_all), ((1, 3, 5, 7), out_core)]

    half = feed_here.shape[0] // 2
    far_up = swapped(after(feed_y, far_heads, partner_heads)[:half], "tok", 2)
    far_down = swapped(after(feed_x, far_heads, partner_heads)[half:], "tok", 4)
    held = jnp.concatenate([feed_here, feed_x, feed_y, far_up, far_down], axis=0)
    feed_pieces = (held, swapped(after(held, passed_heads, out_core), "tok", 1))

    gain, bias = ln1_gain[None, :], ln1_bias[None, :]
    normed, partner = first_norm(place, hidden_in, a1, out_weight, gain, bias, parts, out_pieces)
    away = feed(place, partner, up_weight, down_weight, feed_pieces, BF16, "feed_partner")
    arrived = swapped(away, "kv", 1)
    dec_parts = exchanged_partials(after(partial, away), dec_query.shape[0])
    mine = feed(place, after(normed, away), up_weight, down_weight, feed_pieces, F32, "feed_own")
    prefill_out = finish(normed, mine, arrived, ln2_gain[None, :], ln2_bias[None, :])

    return prefill_out, merged_partials(after(tuple(dec_parts), mine))


def extended(value, sides, width):
    for axis, dim in sides:
        count, length = (lax.axis_size(axis), value.shape[dim])
        up = [(i, (i + 1) % count) for i in range(count - 1)]
        down = [(j, i) for i, j in up]
        last = lax.slice_in_dim(value, length - width, length, axis=dim)
        leading = lax.slice_in_dim(value, 0, width, axis=dim)
        before = lax.ppermute(last, axis, up)
        after = lax.ppermute(leading, axis, down)
        value = jnp.concatenate([before, value, after], axis=dim)
    return value


def merged(value, axis, join):
    pieces = jax.tree.map(lambda part: lax.all_gather(part, axis), value)
    head = jax.tree.map(lambda part: part[0], pieces)
    tail = jax.tree.map(lambda part: part[1:], pieces)
    subtotal, _ = lax.scan(lambda subtotal, section: (join(subtotal, section), None), head, tail)
    return subtotal


def segment_ids(row_ids, stretch_len):
    stretch_ends = jnp.cumsum(stretch_len)
    return jnp.sum((row_ids[:, None] >= stretch_ends[None, :]).astype(jnp.int32), axis=1)


def layer_norm(values, gain, bias):
    center = values - jnp.mean(values, axis=1, keepdims=True)
    spread = jnp.mean(center * center, axis=1, keepdims=True)
    return center * lax.rsqrt(spread + LN_EPS) * gain + bias


def merge_partials(earlier, later):
    highest = jnp.maximum(earlier[0], later[0])
    left_factor = jnp.exp(earlier[0] - highest)
    right_factor = jnp.exp(later[0] - highest)
    totals = earlier[1] * left_factor + later[1] * right_factor
    weighted = earlier[2] * left_factor[..., None] + later[2] * right_factor[..., None]
    return (highest, totals, weighted)


def row_folder(source, shard_rows):
    return jnp.dot(source, shard_rows, preferred_element_type=jnp.float32)


def general_body(
    hidden_in,
    qkv_weight,
    stretch_len,
    out_weight,
    ln1_gain,
    ln1_bias,
    up_weight,
    down_weight,
    ln2_gain,
    ln2_bias,
    dec_query,
    kv_cache,
    piece_req,
    piece_used,
):
    inv_scale = 1.0 / math.sqrt(HD)
    reach = WIN // 2
    local_width = qkv_weight.shape[2]
    head_count = local_width // HD
    flat_weight = qkv_weight.reshape(qkv_weight.shape[0], 3 * local_width)
    qkv_rows = jnp.dot(
        lax.all_gather(hidden_in, "kv", axis=0, tiled=True),
        flat_weight,
        preferred_element_type=jnp.float32,
    ).astype(jnp.bfloat16)
    row_count = qkv_rows.shape[0]
    query_rows = qkv_rows[:, :local_width]
    keyval_rows = qkv_rows[:, local_width:]
    padded = extended(keyval_rows, (("tok", 0),), reach)
    first_row = lax.axis_index("tok") * row_count
    total_rows = row_count * lax.axis_size("tok")
    qblock = min(512, row_count)
    span = qblock + 2 * reach
    block_count = row_count // qblock

    def attend(block_index):
        start = block_index * qblock
        query_ids = first_row + start + jnp.arange(qblock, dtype=jnp.int32)
        key_ids = first_row + start - reach + jnp.arange(span, dtype=jnp.int32)
        query_seg = segment_ids(query_ids, stretch_len)
        inside = (key_ids >= 0) & (key_ids < total_rows)
        key_seg = jnp.where(inside, segment_ids(key_ids, stretch_len), -1)
        allowed = (key_seg[None, :] == query_seg[:, None]) & (
            jnp.abs(key_ids[None, :] - query_ids[:, None]) <= reach
        )
        queries = lax.dynamic_slice_in_dim(query_rows, start, qblock, 0).reshape(
            qblock, head_count, HD
        )
        both = lax.dynamic_slice_in_dim(padded, start, span, 0)
        key_rows = both[:, :local_width].reshape(span, head_count, HD)
        value_rows = both[:, local_width:].reshape(span, head_count, HD)
        scores = (
            jnp.einsum("ihd,jhd->hij", queries, key_rows, preferred_element_type=jnp.float32)
            * inv_scale
        )
        scores = jnp.where(allowed[None], scores, NEG_FILL)
        row_max = jnp.max(scores, axis=2, keepdims=True)
        weights = jnp.where(allowed[None], jnp.exp(scores - row_max), 0.0)
        totals = jnp.sum(weights, axis=2)
        summed = jnp.einsum(
            "hij,jhd->ihd",
            weights.astype(jnp.bfloat16),
            value_rows,
            preferred_element_type=jnp.float32,
        )
        return (
            (summed / jnp.transpose(totals)[:, :, None])
            .astype(jnp.bfloat16)
            .reshape(qblock, local_width)
        )

    attention = lax.map(attend, jnp.arange(block_count, dtype=jnp.int32)).reshape(
        row_count, local_width
    )
    token_major = lax.all_to_all(attention, "kv", split_axis=0, concat_axis=1, tiled=True)
    projected = row_folder(token_major, lax.all_gather(out_weight, "kv", axis=0, tiled=True))
    normed = layer_norm(hidden_in.astype(jnp.float32) + projected, ln1_gain, ln1_bias).astype(
        jnp.bfloat16
    )
    units = jax.nn.gelu(
        jnp.dot(
            lax.all_gather(normed, "kv", axis=0, tiled=True),
            up_weight,
            preferred_element_type=jnp.float32,
        ),
        approximate=False,
    ).astype(jnp.bfloat16)
    ffn = lax.psum_scatter(
        jnp.dot(units, down_weight, preferred_element_type=jnp.float32).astype(jnp.bfloat16),
        "kv",
        scatter_dimension=0,
        tiled=True,
    ).astype(jnp.float32)
    prefill_out = layer_norm(normed.astype(jnp.float32) + ffn, ln2_gain, ln2_bias).astype(
        jnp.bfloat16
    )
    group_queries = lax.all_gather(dec_query, "kv", axis=0, tiled=True)
    request_count = group_queries.shape[0]
    owners = piece_req[0]
    filled = piece_used[0]
    slot_count = owners.shape[0]
    request_ids = jnp.arange(request_count, dtype=jnp.int32)
    selector = (owners[:, None] == request_ids[None, :]).astype(jnp.bfloat16)
    chosen = jnp.dot(selector, group_queries, preferred_element_type=jnp.float32).astype(
        jnp.bfloat16
    )
    chosen = chosen.reshape(slot_count, H, HD)
    cache_keys = kv_cache[0, 0].reshape(slot_count, PLEN, H, HD)
    cache_values = kv_cache[1, 0].reshape(slot_count, PLEN, H, HD)
    piece_scores = (
        jnp.einsum("phd,pthd->pht", chosen, cache_keys, preferred_element_type=jnp.float32)
        * inv_scale
    )
    active = jnp.arange(PLEN, dtype=jnp.int32)[None, :] < filled[:, None]
    piece_scores = jnp.where(active[:, None, :], piece_scores, NEG_FILL)
    piece_max = jnp.max(piece_scores, axis=2)
    piece_weights = jnp.where(
        active[:, None, :], jnp.exp(piece_scores - piece_max[:, :, None]), 0.0
    )
    piece_totals = jnp.sum(piece_weights, axis=2)
    partial_value = jnp.einsum(
        "pht,pthd->phd",
        piece_weights.astype(jnp.bfloat16),
        cache_values,
        preferred_element_type=jnp.float32,
    )
    member = (owners[None, :] == request_ids[:, None]) & (filled[None, :] > 0)
    highest = jnp.max(jnp.where(member[:, :, None], piece_max[None], NEG_FILL), axis=1)
    factor = jnp.where(member[:, :, None], jnp.exp(piece_max[None] - highest[:, None, :]), 0.0)
    denom = jnp.sum(factor * piece_totals[None], axis=1)
    weighted = jnp.einsum("rph,phd->rhd", factor, partial_value)
    own_requests = dec_query.shape[0]
    joined = merged((highest, denom, weighted), "kv", merge_partials)
    begin = lax.axis_index("kv") * own_requests
    final_denom = lax.dynamic_slice_in_dim(joined[1], begin, own_requests, 0)
    final_weighted = lax.dynamic_slice_in_dim(joined[2], begin, own_requests, 0)
    dec_out = (
        (final_weighted / final_denom[:, :, None])
        .astype(jnp.bfloat16)
        .reshape(own_requests, H * HD)
    )
    return (prefill_out, dec_out)


def solution(mesh):
    placed = (
        P(("tok", "kv"), None),
        P(None, None, "kv"),
        P(),
        P("kv", None),
        P(),
        P(),
        P(None, "kv"),
        P("kv", None),
        P(),
        P(),
        P(("tok", "kv"), None),
        P(None, "tok", "kv", None, None),
        P("tok", "kv"),
        P("tok", "kv"),
    )
    routed = mesh.shape["tok"] == 8 and mesh.shape["kv"] == 4
    return jax.shard_map(
        routed_body if routed else general_body,
        mesh=mesh,
        in_specs=placed,
        out_specs=(P(("tok", "kv"), None), P(("tok", "kv"), None)),
        check_vma=False,
    )
```

```python
import functools
import math

import jax
import jax.numpy as jnp
from jax import lax
from jax.experimental import pallas as pl
from jax.experimental.pallas import tpu as pltpu
from jax.sharding import PartitionSpec as P

H = 16
HD = 64
WIN = 512
PLEN = 128


NEG_FILL = -1e30
LN_EPS = 1e-05
BF16 = jnp.bfloat16
F32 = jnp.float32
STRIP = 32
MIB = 1024 * 1024
ANY = pl.BlockSpec(memory_space=pl.ANY)
VMEM = pl.BlockSpec(memory_space=pltpu.VMEM)
SMEM = pl.BlockSpec(memory_space=pltpu.SMEM)
SHORT = pl.CostEstimate(flops=1, bytes_accessed=1, transcendentals=0)


def swapped(value, axis, flip):
    count = lax.axis_size(axis)
    return lax.ppermute(value, axis, [(i, i ^ flip) for i in range(count)])


def over_edges(value, axis, first):
    count = lax.axis_size(axis)
    edges = [(i, i + 1) for i in range(first, count - 1, 2)]
    return lax.ppermute(value, axis, edges + [(j, i) for i, j in edges])


def after(value, *earlier):
    return lax.optimization_barrier((value,) + earlier)[0]


def normalized(values, gain, bias):
    center = values - jnp.mean(values, axis=1, keepdims=True)
    spread = jnp.mean(center * center, axis=1, keepdims=True)
    return center * lax.rsqrt(spread + LN_EPS) * gain + bias


def shard_copies(kv, shards, rows_ref, sems, first, step):
    own, a1, a2, a3, b1, b2 = shards
    count = own.shape[0]
    inner = (kv == 1) | (kv == 2)
    outer = jnp.logical_not(inner)
    always = kv >= 0
    sources = ((own, 0, always), (a1, 1, always), (a2, 2, outer), (b2, 2, inner), (a3, 3, outer), (b1, 3, inner))
    copies = []
    for index, (source, flip, held) in enumerate(sources):
        for slot in range(rows_ref.shape[0] // count):
            needed = held & ((kv ^ flip) == first + slot * step)
            target = rows_ref.at[slot * count : (slot + 1) * count]
            copies.append((needed, pltpu.make_async_copy(source, target, sems.at[index])))
    for needed, copy in copies:
        pl.when(needed)(copy.start)
    for needed, copy in copies:
        pl.when(needed)(copy.wait)


def keys_values(rows, weight_ref, keyval_ref):
    width = weight_ref.shape[2]
    for part in range(2):
        at = slice(part * width, (part + 1) * width)
        keyval_ref[:, at] = jnp.dot(rows, weight_ref[part + 1], preferred_element_type=F32).astype(BF16)


def project_edges_kernel(place_ref, weight_ref, *refs):
    shards, (keyval_ref, even_ref, odd_ref, rows_ref, sems) = refs[:-5], refs[-5:]
    tok, kv = place_ref[0], place_ref[1]
    count = even_ref.shape[0]
    shard_copies(kv, shards, rows_ref, sems, 0, 3)
    keys_values(rows_ref[...], weight_ref, keyval_ref)

    @pl.when(tok % 2 == 0)
    def _():
        even_ref[...] = keyval_ref[count:]
        odd_ref[...] = keyval_ref[:count]

    @pl.when(tok % 2 == 1)
    def _():
        even_ref[...] = keyval_ref[:count]
        odd_ref[...] = keyval_ref[count:]


def project_rest_kernel(place_ref, weight_ref, *refs):
    shards, (query_ref, keyval_ref, rows_ref, sems) = refs[:-4], refs[-4:]
    count = shards[0].shape[0]
    shard_copies(place_ref[1], shards, rows_ref, sems, 0, 1)
    keys_values(rows_ref[count:-count], weight_ref, keyval_ref)
    query = jnp.dot(rows_ref[...], weight_ref[0], preferred_element_type=F32) * (1.0 / math.sqrt(HD))
    query_ref[...] = query.astype(BF16)


def project(place, weight, shards, blocks, edges):
    rows, width = shards[0].shape
    heads_width = weight.shape[2]
    shape = lambda count, columns: jax.ShapeDtypeStruct((count * rows, columns), BF16)
    keyval = shape(2, 2 * heads_width)
    if edges:
        outs = (keyval, shape(1, 2 * heads_width), shape(1, 2 * heads_width))
    else:
        outs = (shape(blocks, heads_width), keyval)
    return pl.pallas_call(
        project_edges_kernel if edges else project_rest_kernel,
        out_shape=outs,
        in_specs=[SMEM, VMEM] + [ANY] * len(shards),
        out_specs=(VMEM,) * len(outs),
        scratch_shapes=[
            pltpu.VMEM((2 * rows if edges else blocks * rows, width), BF16),
            pltpu.SemaphoreType.DMA((len(shards),)),
        ],
        compiler_params=pltpu.CompilerParams(vmem_limit_bytes=12 * MIB),
        cost_estimate=SHORT,
        name="project_edges" if edges else "project_rest",
    )(place, weight, *shards)


def window_bias(first, count, starts, ends):
    reach = WIN // 2
    query = first + lax.broadcasted_iota(jnp.int32, (count, 1), 0)
    low = jnp.max(jnp.where(starts <= query, starts, 0), axis=1, keepdims=True)
    high = jnp.min(jnp.where(ends > query, ends, 1 << 30), axis=1, keepdims=True)
    low = jnp.maximum(low, query - reach)
    high = jnp.minimum(high, query + reach + 1)
    key = first - count + lax.broadcasted_iota(jnp.int32, (count, 3 * count), 1)
    return jnp.where((key >= low) & (key < high), 0.0, NEG_FILL)


def attend(query, keyval_ref, bias_ref, scores_ref, weights_ref, out_ref):
    count, width = query.shape
    lane = lax.broadcasted_iota(jnp.int32, (count, 2 * HD), 1)
    for start in range(0, width, 2 * HD):
        values = keyval_ref[:, width + start : width + start + 2 * HD]
        halves = []
        for side in range(2):
            head = start // HD + side
            inside = (lane < HD) if side == 0 else (lane >= HD)
            only = jnp.where(inside, query[:, start : start + 2 * HD], jnp.zeros((), BF16))
            scores_ref[head] = lax.dot_general(
                only, keyval_ref[:, start : start + 2 * HD], (((1,), (1,)), ((), ())), preferred_element_type=F32
            )
            totals = []
            for row in range(0, count, STRIP):
                at = slice(row, row + STRIP)
                scores = scores_ref[head, at] + bias_ref[at]
                weights = jnp.exp(scores - jnp.max(scores, axis=1, keepdims=True))
                totals.append(jnp.sum(weights, axis=1, keepdims=True))
                weights_ref[head, at] = weights.astype(BF16)
            summed = jnp.dot(weights_ref[head], values, preferred_element_type=F32)
            halves.append(summed / jnp.concatenate(totals, axis=0))
        out_ref[:, start : start + 2 * HD] = jnp.where(lane < HD, halves[0], halves[1]).astype(BF16)


def attend_kernel(flips, place_ref, starts_ref, ends_ref, query_ref, middle_ref, edges_ref, even_ref, odd_ref, *refs):
    out_ref, window_ref, bias_ref, scores_ref, weights_ref, sems = refs
    tok, kv = place_ref[0], place_ref[1]
    count = bias_ref.shape[0]
    out_ref[len(flips) * count :] = jnp.zeros_like(out_ref[len(flips) * count :])
    blocks = query_ref.shape[0] // count
    copies = []
    for index, flip in enumerate(flips):
        block = kv ^ flip
        for part in range(3):
            target = window_ref.at[index, part * count : (part + 1) * count]
            sem = sems.at[index, part]
            at = block + part - 1
            middle = (at > 0) & (at < blocks - 1)
            start = jnp.where(middle, at - 1, 0)
            source = middle_ref.at[pl.ds(pl.multiple_of(start * count, count), count)]
            copies.append((index, middle, pltpu.make_async_copy(source, target, sem)))
            for slot, edge in enumerate((0, blocks - 1)):
                source = edges_ref.at[slot * count : (slot + 1) * count]
                copies.append((index, at == edge, pltpu.make_async_copy(source, target, sem)))
            for first_edge, outside in ((tok % 2 == 1, at < 0), (tok % 2 == 0, at >= blocks)):
                if part != 1:
                    copies.append((index, outside & first_edge, pltpu.make_async_copy(even_ref, target, sem)))
                    other = jnp.logical_not(first_edge)
                    copies.append((index, outside & other, pltpu.make_async_copy(odd_ref, target, sem)))
    for _, needed, copy in copies:
        pl.when(needed)(copy.start)
    for index, flip in enumerate(flips):
        block = kv ^ flip
        first = (tok * blocks + block) * count
        bias_ref[...] = window_bias(first, count, starts_ref[...], ends_ref[...])
        for owner, needed, copy in copies:
            if owner == index:
                pl.when(needed)(copy.wait)
        query = query_ref[pl.ds(pl.multiple_of(block * count, count), count)]
        out = out_ref.at[index * count : (index + 1) * count]
        attend(query, window_ref.at[index], bias_ref, scores_ref, weights_ref, out)


def attend_blocks(place, starts, ends, query, middle, edges, even, odd, rows, flips, name, spare):
    heads_width = query.shape[1]
    return pl.pallas_call(
        functools.partial(attend_kernel, flips),
        out_shape=jax.ShapeDtypeStruct((len(flips) * rows + spare, heads_width), BF16),
        in_specs=[SMEM, VMEM, VMEM, VMEM, ANY, ANY, ANY, ANY],
        out_specs=VMEM,
        scratch_shapes=[
            pltpu.VMEM((len(flips), 3 * rows, 2 * heads_width), BF16),
            pltpu.VMEM((rows, 3 * rows), F32),
            pltpu.VMEM((heads_width // HD, rows, 3 * rows), F32),
            pltpu.VMEM((heads_width // HD, rows, 3 * rows), BF16),
            pltpu.SemaphoreType.DMA((len(flips), 3)),
        ],
        compiler_params=pltpu.CompilerParams(vmem_limit_bytes=14 * MIB),
        cost_estimate=SHORT,
        name=name,
    )(place, starts, ends, query, middle, edges, even, odd)


def first_norm_kernel(layout, place_ref, own_ref, partner_ref, own_out_ref, gain_ref, bias_ref, *refs):
    parts, pieces = refs[:4], refs[4 : 4 + len(layout)]
    normed_ref, away_ref, all_ref, weight_ref, mixed_ref, sems = refs[4 + len(layout) :]
    tok = place_ref[0]
    quarters, heads_width, width = weight_ref.shape
    count = own_ref.shape[0]
    copies = [pltpu.make_async_copy(own_out_ref, weight_ref.at[0], sems.at[0])]
    for flips, piece in zip(layout, pieces):
        for index, flip in enumerate(flips):
            depth = piece.shape[2]
            at = pl.multiple_of((tok ^ flip) * depth, depth)
            target = weight_ref.at[1:quarters, pl.ds(at, depth)]
            copies.append(pltpu.make_async_copy(piece.at[index], target, sems.at[len(copies)]))
    for copy in copies:
        copy.start()
    for flip, part_ref in enumerate(parts):
        columns = slice(flip * heads_width, (flip + 1) * heads_width)
        for half in range(2):
            turned = half ^ (flip % 2)
            all_ref[half * count : (half + 1) * count, columns] = part_ref[turned * count : (turned + 1) * count]
    for copy in copies:
        copy.wait()
    weight = weight_ref[...].reshape(quarters * heads_width, width)
    mixed_ref[...] = jnp.dot(all_ref[...], weight, preferred_element_type=F32)
    for half, (hidden_ref, result_ref) in enumerate(((own_ref, normed_ref), (partner_ref, away_ref))):
        for row in range(0, count, STRIP):
            at = slice(row, row + STRIP)
            mixed = hidden_ref[at].astype(F32) + mixed_ref[half * count + row : half * count + row + STRIP]
            result_ref[at] = normalized(mixed, gain_ref[...], bias_ref[...]).astype(BF16)


def first_norm(place, own, partner, own_out, gain, bias, parts, pieces):
    rows, width = own.shape
    heads_width = own_out.shape[0]
    layout = tuple(flips for flips, _ in pieces)
    return pl.pallas_call(
        functools.partial(first_norm_kernel, layout),
        out_shape=(jax.ShapeDtypeStruct((rows, width), BF16),) * 2,
        in_specs=[SMEM, VMEM, VMEM, ANY, VMEM, VMEM] + [VMEM] * len(parts) + [ANY] * len(pieces),
        out_specs=(VMEM,) * 2,
        scratch_shapes=[
            pltpu.VMEM((2 * rows, width), BF16),
            pltpu.VMEM((len(parts), heads_width, width), BF16),
            pltpu.VMEM((2 * rows, width), F32),
            pltpu.SemaphoreType.DMA((1 + sum(len(flips) for flips in layout),)),
        ],
        compiler_params=pltpu.CompilerParams(vmem_limit_bytes=14 * MIB),
        cost_estimate=SHORT,
        name="first_norm",
    )(place, own, partner, own_out, gain, bias, *parts, *[value for _, value in pieces])


def gelu(values):
    return 0.5 * values * (1.0 + lax.erf(values * math.sqrt(0.5)))


CHUNK = 512


def feed_chunk(rows, up, down_ref, wide_ref, units_ref):
    wide_ref[...] = jnp.dot(rows, up, preferred_element_type=F32)
    for row in range(0, rows.shape[0], STRIP):
        strip = slice(row, row + STRIP)
        units_ref[strip] = gelu(wide_ref[strip]).astype(BF16)
    return jnp.dot(units_ref[...], down_ref[...], preferred_element_type=F32)


def far_copies(tok, held_ref, core_ref, up_ref, down_ref, sems):
    block = 128
    copies = []
    for side, piece in enumerate((held_ref, core_ref)):
        for index in range(4):
            at = pl.ds(pl.multiple_of((tok ^ (2 * index + side)) * block, block), block)
            for part, target in enumerate((up_ref, down_ref)):
                source = piece.at[pl.ds((2 * index + part) * block, block)]
                copies.append(pltpu.make_async_copy(source, target.at[at], sems.at[len(copies)]))
    return copies


def feed_kernel(place_ref, rows_ref, up_near_ref, down_near_ref, held_ref, core_ref, *refs):
    sum_ref, up_ref, down_ref, wide_ref, units_ref, total_ref, sems = refs
    copies = far_copies(place_ref[0], held_ref, core_ref, up_ref, down_ref, sems)
    for copy in copies:
        copy.start()
    rows = rows_ref[...]
    chunks = up_ref.shape[1] // CHUNK
    for index in range(2 * chunks):
        if index == chunks:
            for copy in copies:
                copy.wait()
        up, down = (up_near_ref, down_near_ref) if index < chunks else (up_ref, down_ref)
        at = slice(index % chunks * CHUNK, (index % chunks + 1) * CHUNK)
        product = feed_chunk(rows, up[:, at], down.at[at], wide_ref.at[index % 2], units_ref.at[index % 2])
        if index == 0:
            total_ref[...] = product
        elif index < 2 * chunks - 1:
            total_ref[...] += product
        else:
            sum_ref[...] = (total_ref[...] + product).astype(sum_ref.dtype)


def feed(place, rows, up_weight, down_weight, pieces, dtype, name):
    count, width = rows.shape
    units = up_weight.shape[1]
    return pl.pallas_call(
        feed_kernel,
        out_shape=jax.ShapeDtypeStruct((count, width), dtype),
        in_specs=[SMEM] + [VMEM] * 3 + [ANY] * 2,
        out_specs=VMEM,
        scratch_shapes=[
            pltpu.VMEM((width, units), BF16),
            pltpu.VMEM((units, width), BF16),
            pltpu.VMEM((2, count, CHUNK), F32),
            pltpu.VMEM((2, count, CHUNK), BF16),
            pltpu.VMEM((count, width), F32),
            pltpu.SemaphoreType.DMA((16,)),
        ],
        compiler_params=pltpu.CompilerParams(vmem_limit_bytes=18 * MIB),
        cost_estimate=SHORT,
        name=name,
    )(place, rows, up_weight, down_weight, *pieces)


def finish_kernel(normed_ref, near_ref, far_ref, gain_ref, bias_ref, out_ref):
    for row in range(0, normed_ref.shape[0], STRIP):
        at = slice(row, row + STRIP)
        mixed = normed_ref[at].astype(F32) + near_ref[at] + far_ref[at].astype(F32)
        out_ref[at] = normalized(mixed, gain_ref[...], bias_ref[...]).astype(out_ref.dtype)


def finish(normed, near, far, gain, bias):
    return pl.pallas_call(
        finish_kernel,
        out_shape=jax.ShapeDtypeStruct(normed.shape, BF16),
        in_specs=[VMEM] * 5,
        out_specs=VMEM,
        compiler_params=pltpu.CompilerParams(vmem_limit_bytes=6 * MIB),
        name="finish",
    )(normed, near, far, gain, bias)


def decode_kernel(slot_ref, filled_ref, query_ref, cache_ref, out_ref, high_ref, total_ref, sum_ref):
    step = pl.program_id(0)

    @pl.when(step == 0)
    def _():
        high_ref[...] = jnp.full(high_ref.shape, NEG_FILL, F32)
        total_ref[...] = jnp.zeros_like(total_ref)
        sum_ref[...] = jnp.zeros_like(sum_ref)

    row = slot_ref[step]
    filled = filled_ref[step]
    width = query_ref.shape[1]
    head = lax.broadcasted_iota(jnp.int32, (H, width), 0)
    inside = head == lax.broadcasted_iota(jnp.int32, (H, width), 1) // HD
    query = jnp.where(inside, query_ref[pl.ds(row, 1), :], 0.0).astype(BF16)
    scores = lax.dot_general(query, cache_ref[0, 0, 0], (((1,), (1,)), ((), ())), preferred_element_type=F32)
    live = lax.broadcasted_iota(jnp.int32, scores.shape, 1) < filled
    scores = jnp.where(live, scores * (1.0 / math.sqrt(HD)), NEG_FILL)
    high = jnp.max(scores, axis=1, keepdims=True)
    weights = jnp.where(live, jnp.exp(scores - high), 0.0)
    total = jnp.sum(weights, axis=1, keepdims=True)
    summed = jnp.dot(weights.astype(BF16), cache_ref[1, 0, 0], preferred_element_type=F32)
    along = lambda column: jnp.sum(jnp.where(inside, column, 0.0), axis=0, keepdims=True)
    high, total, summed = along(high), along(total), along(summed)
    used = filled > 0
    at = pl.ds(row, 1)
    old = high_ref[at, :]
    new = jnp.where(used, jnp.maximum(old, high), old)
    left = jnp.exp(old - new)
    right = jnp.where(used, jnp.exp(high - new), 0.0)
    high_ref[at, :] = new
    total_ref[at, :] = total_ref[at, :] * left + total * right
    sum_ref[at, :] = sum_ref[at, :] * left + summed * right

    @pl.when(step == pl.num_programs(0) - 1)
    def _():
        out_ref[0] = high_ref[...]
        out_ref[1] = total_ref[...]
        out_ref[2] = sum_ref[...]


def decode(slots, filled, queries, kv_cache):
    requests, width = queries.shape
    pieces = kv_cache.shape[2]
    state = pltpu.VMEM((requests, width), F32)
    return pl.pallas_call(
        decode_kernel,
        grid=(pieces,),
        out_shape=jax.ShapeDtypeStruct((3, requests, width), F32),
        in_specs=[
            SMEM,
            SMEM,
            pl.BlockSpec((requests, width), lambda i: (0, 0)),
            pl.BlockSpec((2, 1, 1, PLEN, width), lambda i: (0, 0, i, 0, 0)),
        ],
        out_specs=pl.BlockSpec((3, requests, width), lambda i: (0, 0, 0)),
        scratch_shapes=[state, state, state],
        compiler_params=pltpu.CompilerParams(vmem_limit_bytes=8 * MIB),
        cost_estimate=SHORT,
        name="decode",
    )(slots, filled, queries, kv_cache)


def decode_partial(queries, own, kv_cache, piece_req, piece_used):
    owners = piece_req[0]
    slots = ((owners // own) ^ lax.axis_index("kv")) * own + owners % own
    return decode(slots, piece_used[0], queries, kv_cache)


def exchanged_partials(partial, own):
    parts = [partial[:, :own]]
    for flip in range(1, lax.axis_size("kv")):
        parts.append(swapped(partial[:, flip * own : (flip + 1) * own], "kv", flip))
    return parts


def merged_partials(parts):
    high = functools.reduce(jnp.maximum, [part[0] for part in parts])
    factors = [jnp.exp(part[0] - high) for part in parts]
    total = sum(part[1] * factor for part, factor in zip(parts, factors))
    summed = sum(part[2] * factor for part, factor in zip(parts, factors))
    return (summed / total).astype(BF16)


def routed_body(
    hidden_in,
    qkv_weight,
    stretch_len,
    out_weight,
    ln1_gain,
    ln1_bias,
    up_weight,
    down_weight,
    ln2_gain,
    ln2_bias,
    dec_query,
    kv_cache,
    piece_req,
    piece_used,
):
    tok = lax.axis_index("tok")
    kv = lax.axis_index("kv")
    toks, kvs = lax.axis_size("tok"), lax.axis_size("kv")
    rows, width = hidden_in.shape
    place = jnp.stack([tok, kv]).astype(jnp.int32)
    eighth = lambda value: lax.dynamic_slice_in_dim(value, tok * (value.shape[0] // toks), value.shape[0] // toks, 0)

    outward = [(1, 0), (2, 3)]
    a1, b1 = over_edges(hidden_in, "kv", 0), over_edges(hidden_in, "kv", 1)
    out_part = eighth(out_weight)
    depth = out_part.shape[0]
    small = jnp.concatenate([out_part, dec_query], axis=0)
    others = [swapped(small, "kv", flip) for flip in range(1, kvs)]
    a2, b2 = lax.ppermute(b1, "kv", outward), over_edges(a1, "kv", 1)
    queries = jnp.concatenate([dec_query] + [other[depth:] for other in others], axis=0).astype(F32)
    partial = decode_partial(queries, dec_query.shape[0], kv_cache, piece_req, piece_used)
    out_here = jnp.stack([other[:depth] for other in others])
    out_x, out_y = swapped(out_here, "tok", 2), swapped(out_here, "tok", 4)
    a3 = lax.ppermute(after(b2, partial), "kv", outward)
    out_far = swapped(out_here, "tok", 6)
    shards = (after(hidden_in, out_x, out_y, out_far), a1, a2, a3, b1, b2)
    inner = (kv == 1) | (kv == 2)

    feed_part = jnp.concatenate([eighth(up_weight), eighth(down_weight)], axis=0)
    feed_inner = lax.ppermute(after(feed_part, a2, b2), "kv", [(0, 2), (3, 1)])
    feed_outer = lax.ppermute(after(feed_part, a3, feed_inner), "kv", [(1, 3), (2, 0)])

    order = jnp.arange(stretch_len.shape[0])
    ends = jnp.sum(jnp.where(order[:, None] <= order[None, :], stretch_len[:, None], 0), axis=0, dtype=jnp.int32)
    starts = (ends - stretch_len)[None, :]
    ends = ends[None, :]

    weight = jnp.transpose(qkv_weight, (1, 0, 2))
    edges, even, odd = project(place, weight, shards, kvs, True)
    even, odd = over_edges(even, "tok", 0), over_edges(odd, "tok", 1)
    query, middle = project(place, weight, (after(hidden_in, edges),) + shards[1:], kvs, False)
    window = (middle, edges, even, odd, rows)
    out_all = jnp.stack([out_here, out_x, out_y, out_far])
    far = attend_blocks(place, starts, ends, query, *window, (2, 3), "attend_far", 32)
    far_heads = swapped(far, "kv", 2)
    feed_here = jnp.where(inner, feed_inner, after(feed_outer, far))
    feed_x, feed_y = swapped(feed_here, "tok", 2), swapped(feed_here, "tok", 4)
    near = attend_blocks(place, starts, ends, after(query, feed_here), *window, (0, 1), "attend_near", 16)
    partner_heads, passed_heads = swapped(near, "kv", 1), swapped(far_heads, "kv", 1)
    parts = (near, partner_heads, far_heads, passed_heads)
    out_core = swapped(after(out_all, near, far_heads), "tok", 1)
    out_pieces = [((0, 2, 4, 6), out_all), ((1, 3, 5, 7), out_core)]

    half = feed_here.shape[0] // 2
    far_up = swapped(after(feed_y, far_heads)[:half], "tok", 2)
    far_down = swapped(after(feed_x, far_heads, partner_heads)[half:], "tok", 4)
    held = jnp.concatenate([feed_here, feed_x, feed_y, far_up, far_down], axis=0)
    feed_pieces = (held, swapped(after(held, passed_heads, out_core), "tok", 1))

    gain, bias = ln1_gain[None, :], ln1_bias[None, :]
    normed, partner = first_norm(place, hidden_in, a1, out_weight, gain, bias, parts, out_pieces)
    away = feed(place, partner, up_weight, down_weight, feed_pieces, BF16, "feed_partner")
    arrived = swapped(away, "kv", 1)
    dec_parts = exchanged_partials(after(partial, away), dec_query.shape[0])
    mine = feed(place, after(normed, away), up_weight, down_weight, feed_pieces, F32, "feed_own")
    prefill_out = finish(normed, mine, arrived, ln2_gain[None, :], ln2_bias[None, :])

    return prefill_out, merged_partials(after(tuple(dec_parts), mine))


def extended(value, sides, width):
    for axis, dim in sides:
        count, length = (lax.axis_size(axis), value.shape[dim])
        up = [(i, (i + 1) % count) for i in range(count - 1)]
        down = [(j, i) for i, j in up]
        last = lax.slice_in_dim(value, length - width, length, axis=dim)
        leading = lax.slice_in_dim(value, 0, width, axis=dim)
        before = lax.ppermute(last, axis, up)
        after = lax.ppermute(leading, axis, down)
        value = jnp.concatenate([before, value, after], axis=dim)
    return value


def merged(value, axis, join):
    pieces = jax.tree.map(lambda part: lax.all_gather(part, axis), value)
    head = jax.tree.map(lambda part: part[0], pieces)
    tail = jax.tree.map(lambda part: part[1:], pieces)
    subtotal, _ = lax.scan(lambda subtotal, section: (join(subtotal, section), None), head, tail)
    return subtotal


def segment_ids(row_ids, stretch_len):
    stretch_ends = jnp.cumsum(stretch_len)
    return jnp.sum((row_ids[:, None] >= stretch_ends[None, :]).astype(jnp.int32), axis=1)


def layer_norm(values, gain, bias):
    center = values - jnp.mean(values, axis=1, keepdims=True)
    spread = jnp.mean(center * center, axis=1, keepdims=True)
    return center * lax.rsqrt(spread + LN_EPS) * gain + bias


def merge_partials(earlier, later):
    highest = jnp.maximum(earlier[0], later[0])
    left_factor = jnp.exp(earlier[0] - highest)
    right_factor = jnp.exp(later[0] - highest)
    totals = earlier[1] * left_factor + later[1] * right_factor
    weighted = earlier[2] * left_factor[..., None] + later[2] * right_factor[..., None]
    return (highest, totals, weighted)


def row_folder(source, shard_rows):
    return jnp.dot(source, shard_rows, preferred_element_type=jnp.float32)


def general_body(
    hidden_in,
    qkv_weight,
    stretch_len,
    out_weight,
    ln1_gain,
    ln1_bias,
    up_weight,
    down_weight,
    ln2_gain,
    ln2_bias,
    dec_query,
    kv_cache,
    piece_req,
    piece_used,
):
    inv_scale = 1.0 / math.sqrt(HD)
    reach = WIN // 2
    local_width = qkv_weight.shape[2]
    head_count = local_width // HD
    flat_weight = qkv_weight.reshape(qkv_weight.shape[0], 3 * local_width)
    qkv_rows = jnp.dot(
        lax.all_gather(hidden_in, "kv", axis=0, tiled=True),
        flat_weight,
        preferred_element_type=jnp.float32,
    ).astype(jnp.bfloat16)
    row_count = qkv_rows.shape[0]
    query_rows = qkv_rows[:, :local_width]
    keyval_rows = qkv_rows[:, local_width:]
    padded = extended(keyval_rows, (("tok", 0),), reach)
    first_row = lax.axis_index("tok") * row_count
    total_rows = row_count * lax.axis_size("tok")
    qblock = min(512, row_count)
    span = qblock + 2 * reach
    block_count = row_count // qblock

    def attend(block_index):
        start = block_index * qblock
        query_ids = first_row + start + jnp.arange(qblock, dtype=jnp.int32)
        key_ids = first_row + start - reach + jnp.arange(span, dtype=jnp.int32)
        query_seg = segment_ids(query_ids, stretch_len)
        inside = (key_ids >= 0) & (key_ids < total_rows)
        key_seg = jnp.where(inside, segment_ids(key_ids, stretch_len), -1)
        allowed = (key_seg[None, :] == query_seg[:, None]) & (
            jnp.abs(key_ids[None, :] - query_ids[:, None]) <= reach
        )
        queries = lax.dynamic_slice_in_dim(query_rows, start, qblock, 0).reshape(
            qblock, head_count, HD
        )
        both = lax.dynamic_slice_in_dim(padded, start, span, 0)
        key_rows = both[:, :local_width].reshape(span, head_count, HD)
        value_rows = both[:, local_width:].reshape(span, head_count, HD)
        scores = (
            jnp.einsum("ihd,jhd->hij", queries, key_rows, preferred_element_type=jnp.float32)
            * inv_scale
        )
        scores = jnp.where(allowed[None], scores, NEG_FILL)
        row_max = jnp.max(scores, axis=2, keepdims=True)
        weights = jnp.where(allowed[None], jnp.exp(scores - row_max), 0.0)
        totals = jnp.sum(weights, axis=2)
        summed = jnp.einsum(
            "hij,jhd->ihd",
            weights.astype(jnp.bfloat16),
            value_rows,
            preferred_element_type=jnp.float32,
        )
        return (
            (summed / jnp.transpose(totals)[:, :, None])
            .astype(jnp.bfloat16)
            .reshape(qblock, local_width)
        )

    attention = lax.map(attend, jnp.arange(block_count, dtype=jnp.int32)).reshape(
        row_count, local_width
    )
    token_major = lax.all_to_all(attention, "kv", split_axis=0, concat_axis=1, tiled=True)
    projected = row_folder(token_major, lax.all_gather(out_weight, "kv", axis=0, tiled=True))
    normed = layer_norm(hidden_in.astype(jnp.float32) + projected, ln1_gain, ln1_bias).astype(
        jnp.bfloat16
    )
    units = jax.nn.gelu(
        jnp.dot(
            lax.all_gather(normed, "kv", axis=0, tiled=True),
            up_weight,
            preferred_element_type=jnp.float32,
        ),
        approximate=False,
    ).astype(jnp.bfloat16)
    ffn = lax.psum_scatter(
        jnp.dot(units, down_weight, preferred_element_type=jnp.float32).astype(jnp.bfloat16),
        "kv",
        scatter_dimension=0,
        tiled=True,
    ).astype(jnp.float32)
    prefill_out = layer_norm(normed.astype(jnp.float32) + ffn, ln2_gain, ln2_bias).astype(
        jnp.bfloat16
    )
    group_queries = lax.all_gather(dec_query, "kv", axis=0, tiled=True)
    request_count = group_queries.shape[0]
    owners = piece_req[0]
    filled = piece_used[0]
    slot_count = owners.shape[0]
    request_ids = jnp.arange(request_count, dtype=jnp.int32)
    selector = (owners[:, None] == request_ids[None, :]).astype(jnp.bfloat16)
    chosen = jnp.dot(selector, group_queries, preferred_element_type=jnp.float32).astype(
        jnp.bfloat16
    )
    chosen = chosen.reshape(slot_count, H, HD)
    cache_keys = kv_cache[0, 0].reshape(slot_count, PLEN, H, HD)
    cache_values = kv_cache[1, 0].reshape(slot_count, PLEN, H, HD)
    piece_scores = (
        jnp.einsum("phd,pthd->pht", chosen, cache_keys, preferred_element_type=jnp.float32)
        * inv_scale
    )
    active = jnp.arange(PLEN, dtype=jnp.int32)[None, :] < filled[:, None]
    piece_scores = jnp.where(active[:, None, :], piece_scores, NEG_FILL)
    piece_max = jnp.max(piece_scores, axis=2)
    piece_weights = jnp.where(
        active[:, None, :], jnp.exp(piece_scores - piece_max[:, :, None]), 0.0
    )
    piece_totals = jnp.sum(piece_weights, axis=2)
    partial_value = jnp.einsum(
        "pht,pthd->phd",
        piece_weights.astype(jnp.bfloat16),
        cache_values,
        preferred_element_type=jnp.float32,
    )
    member = (owners[None, :] == request_ids[:, None]) & (filled[None, :] > 0)
    highest = jnp.max(jnp.where(member[:, :, None], piece_max[None], NEG_FILL), axis=1)
    factor = jnp.where(member[:, :, None], jnp.exp(piece_max[None] - highest[:, None, :]), 0.0)
    denom = jnp.sum(factor * piece_totals[None], axis=1)
    weighted = jnp.einsum("rph,phd->rhd", factor, partial_value)
    own_requests = dec_query.shape[0]
    joined = merged((highest, denom, weighted), "kv", merge_partials)
    begin = lax.axis_index("kv") * own_requests
    final_denom = lax.dynamic_slice_in_dim(joined[1], begin, own_requests, 0)
    final_weighted = lax.dynamic_slice_in_dim(joined[2], begin, own_requests, 0)
    dec_out = (
        (final_weighted / final_denom[:, :, None])
        .astype(jnp.bfloat16)
        .reshape(own_requests, H * HD)
    )
    return (prefill_out, dec_out)


def solution(mesh):
    placed = (
        P(("tok", "kv"), None),
        P(None, None, "kv"),
        P(),
        P("kv", None),
        P(),
        P(),
        P(None, "kv"),
        P("kv", None),
        P(),
        P(),
        P(("tok", "kv"), None),
        P(None, "tok", "kv", None, None),
        P("tok", "kv"),
        P("tok", "kv"),
    )
    routed = mesh.shape["tok"] == 8 and mesh.shape["kv"] == 4
    return jax.shard_map(
        routed_body if routed else general_body,
        mesh=mesh,
        in_specs=placed,
        out_specs=(P(("tok", "kv"), None), P(("tok", "kv"), None)),
        check_vma=False,
    )
```
